32 devices in a mesh: reader: 4 (over y, x), blk: 8 (over z, core).
Axes of the slice: x: 2, y: 2, z: 4, core: 2. Of those that a mesh axis runs over, the one named last changes fastest.
Arguments:
- features: bfloat16 [4096, 512], P(('reader', 'blk')), may hold values from -40 to 40
- cotangent: bfloat16 [4096, 512], P(('reader', 'blk')), may hold values from -6 to 6
- w_query: bfloat16 [512, 512], replicated, may hold values from -0.25 to 0.25
- w_key: bfloat16 [512, 512], replicated, may hold values from -0.25 to 0.25
- w_value: bfloat16 [512, 512], replicated, may hold values from -0.25 to 0.25
- tile_coords: int32 [4, 8, 8, 3], P('reader', 'blk'), may hold values from 0 to 239, as said below
- tile_count: int32 [4, 8], P('reader', 'blk'), may hold values from 1 to 8, as said below
- mask_table: int32 [240, 128, 4], replicated, may hold values from -2147483648 to 2147483647, as said below
Outputs:
- attn_out: bfloat16 [4096, 512], P(('reader', 'blk'))
- grad_features: bfloat16 [4096, 512], P(('reader', 'blk'))
The draws below stay inside these ranges and needn't reach their ends.
Inputs may be any that keep to these rules, and one draw needn't show every extreme that they name: `tile_coords`: for every r and b the 8 slots name distinct (qb, kb) pairs with qb < 8, kb < 4, p < 240; the first 1 slots are the tiles in which the nodes of segment r * 8 + b meet themselves. `tile_count`: some pair (r, b) uses all 8 slots, and some pair uses the fewest. `mask_table`: each word packs 32 edge bits as a signed int32; each bit is set with probability 1/32.
All inputs are finite; a program needn't handle non-finite values.
Results may differ from the reference program's by a relative error of at most 0.01265.
The reference program's roundings to bfloat16 on the way count: a program that leaves them out, or rounds other values in their place, can miss the bound.
Values may be sent and summed in bfloat16 or wider, within the bound.
No kernel may reach another device: no remote copies, remote signals or barrier semaphores. Data moves between devices by JAX's collectives and lax.ppermute only.
A program may use at most 128 MiB of HBM per device.

```python
import jax
import jax.numpy as jnp
from jax import lax

D = 512
HEADS = 8
BLOCK = 128
PATTERNS = 240
NODE_DEV = 128
NODES = 4096
SEG_BLOCKS = 1
QBLK = 8
KBLK = 4
CAP = 8
N_READER = 4
N_BLK = 8


def draw_features(key, part):
    key_base = jax.random.fold_in(key, 0)
    base = jax.random.normal(key_base, (NODES, D), jnp.float32)
    return jnp.clip(base, -40.0, 40.0).astype(jnp.bfloat16)


def draw_tile_coords(key, part):
    key_order, key_pattern = jax.random.split(key)
    pair_count = QBLK * KBLK
    device_keys = jax.random.split(key_order, N_READER * N_BLK)
    pair_ranks = jax.vmap(lambda one: jax.random.permutation(one, pair_count))(device_keys)
    pair_ranks = pair_ranks.reshape(N_READER, N_BLK, pair_count).astype(jnp.int32)
    pair_ids = jnp.arange(pair_count, dtype=jnp.int32)[None, None, :]
    query_blk = pair_ids // KBLK
    key_blk = pair_ids % KBLK
    reader_ids = jnp.arange(N_READER, dtype=jnp.int32)[:, None, None]
    blk_ids = jnp.arange(N_BLK, dtype=jnp.int32)[None, :, None]
    on_diag = (query_blk // SEG_BLOCKS == blk_ids) & (key_blk // SEG_BLOCKS == reader_ids) & (query_blk % SEG_BLOCKS == key_blk % SEG_BLOCKS)
    ordered = jnp.argsort(pair_ranks - pair_count * on_diag.astype(jnp.int32), axis=-1)[..., :CAP].astype(jnp.int32)
    patterns = jax.random.randint(key_pattern, (N_READER, N_BLK, CAP), 0, PATTERNS, dtype=jnp.int32)
    return jnp.stack([ordered // KBLK, ordered % KBLK, patterns], axis=-1).astype(jnp.int32)


def draw_tile_count(key, part):
    key_draw, key_place = jax.random.split(key)
    floor_count = max(SEG_BLOCKS, CAP // 8)
    drawn = jax.random.randint(key_draw, (N_READER * N_BLK,), floor_count, CAP // 2 + 1, dtype=jnp.int32)
    counts = jnp.maximum(floor_count, drawn)
    order_ids = jax.random.permutation(key_place, N_READER * N_BLK)
    counts = counts.at[order_ids[0]].set(CAP).at[order_ids[1]].set(floor_count)
    return counts.reshape(N_READER, N_BLK).astype(jnp.int32)


def draw_mask_table(key, part):
    word_keys = jax.random.split(key, 5)
    shape = (PATTERNS, BLOCK, BLOCK // 32)
    words = jax.random.randint(word_keys[0], shape, -2147483648, 2147483647, dtype=jnp.int32)
    for index in range(1, 5):
        words = words & jax.random.randint(word_keys[index], shape, -2147483648, 2147483647, dtype=jnp.int32)
    return words


def steps_of(key, shape, pieces, low, largest):
    loudness = 1.0
    for axis_at, shards_of in pieces:
        draws = jax.random.uniform(jax.random.fold_in(jax.random.fold_in(key, 6), axis_at), (shards_of,), jnp.float32, low / len(pieces), largest / len(pieces))
        loudness = loudness * jnp.repeat(jnp.exp(draws), shape[axis_at] // shards_of).reshape((-1,) + (1,) * (len(shape) - 1 - axis_at))
    return loudness


def scatter_about(key, shape, scale, limit, pieces=(), kind=jnp.bfloat16):
    entries = scale * jax.random.normal(key, shape, jnp.float32)
    if pieces:
        entries = entries * steps_of(key, shape, pieces, -0.22, 0.18)
    return jnp.clip(entries, -limit, limit).astype(kind)


def setup_inputs(seed: int = 0) -> dict:
    keys = jax.random.split(jax.random.key(seed), 9)
    return {
        "features": draw_features(jax.random.fold_in(keys[8], 71), 0),
        "cotangent": scatter_about(keys[1], (NODES, D), 1.0, 6.0, ((0, 32),)),
        "w_query": scatter_about(keys[2], (D, D), D ** -0.5, 0.25),
        "w_key": scatter_about(keys[3], (D, D), D ** -0.5, 0.25),
        "w_value": scatter_about(keys[4], (D, D), D ** -0.5, 0.25),
        "tile_coords": draw_tile_coords(jax.random.fold_in(keys[8], 71), 0),
        "tile_count": draw_tile_count(jax.random.fold_in(keys[8], 71), 0),
        "mask_table": draw_mask_table(jax.random.fold_in(keys[8], 71), 0),
    }


NEG_FILL = -1.0e30


def unpack(mask_words):
    shifts = jnp.arange(32, dtype=jnp.int32)
    mask_bits = jnp.right_shift(mask_words[..., None], shifts) & 1
    return mask_bits.reshape(mask_words.shape[:-1] + (mask_words.shape[-1] * 32,)) > 0


def project(rows, weight):
    return jnp.dot(rows, weight, preferred_element_type=jnp.float32).astype(jnp.bfloat16)


def key_layout(node_rows):
    moved = node_rows.reshape(N_READER, N_BLK, NODE_DEV, D).transpose(1, 0, 2, 3)
    return moved.reshape(N_BLK * KBLK, BLOCK, HEADS, D // HEADS)


def node_layout(key_tiles):
    moved = key_tiles.reshape(N_BLK, N_READER, NODE_DEV, D).transpose(1, 0, 2, 3)
    return moved.reshape(NODES, D)


def rounded_low(values_in):
    return lax.optimization_barrier(values_in.astype(jnp.bfloat16)).astype(jnp.float32)


def reference(features, cotangent, w_query, w_key, w_value, tile_coords, tile_count, mask_table):
    head_dim = D // HEADS
    scale = float(head_dim) ** -0.5
    tile_batch = 32
    query_tiles = project(features, w_query).reshape(N_READER * QBLK, BLOCK, HEADS, head_dim).astype(jnp.float32)
    key_tiles = key_layout(project(features, w_key)).astype(jnp.float32)
    value_tiles = key_layout(project(features, w_value)).astype(jnp.float32)
    grad_tiles = cotangent.reshape(N_READER * QBLK, BLOCK, HEADS, head_dim).astype(jnp.float32)
    reader_ids = jnp.arange(N_READER, dtype=jnp.int32)[:, None, None]
    blk_ids = jnp.arange(N_BLK, dtype=jnp.int32)[None, :, None]
    slot_ids = jnp.arange(CAP, dtype=jnp.int32)[None, None, :]
    query_blk = tile_coords[..., 0].astype(jnp.int32)
    key_blk = tile_coords[..., 1].astype(jnp.int32)
    usable = slot_ids < tile_count[:, :, None]
    on_diag = (query_blk // SEG_BLOCKS == blk_ids) & (key_blk // SEG_BLOCKS == reader_ids) & (query_blk % SEG_BLOCKS == key_blk % SEG_BLOCKS)
    global_query = (reader_ids * QBLK + query_blk).reshape(-1, tile_batch)
    global_key = (blk_ids * KBLK + key_blk).reshape(-1, tile_batch)
    items = (global_query, global_key, tile_coords[..., 2].astype(jnp.int32).reshape(-1, tile_batch),
             usable.reshape(-1, tile_batch), on_diag.reshape(-1, tile_batch))
    diagonal_cells = jnp.eye(BLOCK, dtype=bool)

    def tile_scores(item):
        g_query, g_key, patterns, usable_now, diag_now = item
        allowed = (unpack(mask_table[patterns]) | (diag_now[:, None, None] & diagonal_cells)) & usable_now[:, None, None]
        scores = jnp.einsum("gqhd,gkhd->ghqk", query_tiles[g_query], key_tiles[g_key]) * scale
        return allowed[:, None], scores

    def max_step(row_max, item):
        allowed, scores = tile_scores(item)
        tile_max = jnp.max(jnp.where(allowed, scores, NEG_FILL), axis=-1)
        return row_max.at[item[0]].max(tile_max), None

    start_max = jnp.full((N_READER * QBLK, HEADS, BLOCK), NEG_FILL, jnp.float32)
    row_max = lax.scan(max_step, start_max, items)[0]

    def sum_step(state_now, item):
        totals, weighted = state_now
        allowed, scores = tile_scores(item)
        expo = jnp.exp(jnp.where(allowed, scores - row_max[item[0]][..., None], NEG_FILL))
        totals = totals.at[item[0]].add(jnp.sum(expo, axis=-1))
        weighted = weighted.at[item[0]].add(jnp.einsum("ghqk,gkhd->gqhd", rounded_low(expo), value_tiles[item[1]]))
        return (totals, weighted), None

    start_sums = (jnp.zeros((N_READER * QBLK, HEADS, BLOCK), jnp.float32),
                  jnp.zeros((N_READER * QBLK, BLOCK, HEADS, head_dim), jnp.float32))
    totals, weighted = lax.scan(sum_step, start_sums, items)[0]
    outputs = weighted / totals.transpose(0, 2, 1)[..., None]
    attn_out = outputs.reshape(NODES, D).astype(jnp.bfloat16)
    delta = jnp.sum(grad_tiles * outputs, axis=-1).transpose(0, 2, 1)

    def grad_step(state_now, item):
        grad_query, grad_key, grad_value = state_now
        allowed, scores = tile_scores(item)
        probs = jnp.exp(jnp.where(allowed, scores - row_max[item[0]][..., None], NEG_FILL)) / totals[item[0]][..., None]
        d_rows = grad_tiles[item[0]]
        grad_value = grad_value.at[item[1]].add(jnp.einsum("ghqk,gqhd->gkhd", rounded_low(probs), d_rows))
        d_probs = jnp.einsum("gqhd,gkhd->ghqk", d_rows, value_tiles[item[1]])
        d_scores = rounded_low(probs * (d_probs - delta[item[0]][..., None]) * scale)
        grad_query = grad_query.at[item[0]].add(jnp.einsum("ghqk,gkhd->gqhd", d_scores, key_tiles[item[1]]))
        grad_key = grad_key.at[item[1]].add(jnp.einsum("ghqk,gqhd->gkhd", d_scores, query_tiles[item[0]]))
        return (grad_query, grad_key, grad_value), None

    start_grads = (jnp.zeros((N_READER * QBLK, BLOCK, HEADS, head_dim), jnp.float32),
                   jnp.zeros((N_BLK * KBLK, BLOCK, HEADS, head_dim), jnp.float32),
                   jnp.zeros((N_BLK * KBLK, BLOCK, HEADS, head_dim), jnp.float32))
    grad_query, grad_key, grad_value = lax.scan(grad_step, start_grads, items)[0]
    query_low = grad_query.reshape(NODES, D).astype(jnp.bfloat16)
    key_low = node_layout(grad_key).astype(jnp.bfloat16)
    value_low = node_layout(grad_value).astype(jnp.bfloat16)
    grad_total = jnp.dot(query_low, w_query.T, preferred_element_type=jnp.float32)
    grad_total = grad_total + jnp.dot(key_low, w_key.T, preferred_element_type=jnp.float32)
    grad_total = grad_total + jnp.dot(value_low, w_value.T, preferred_element_type=jnp.float32)
    return attn_out, grad_total.astype(jnp.bfloat16)
```

```python
import functools

import jax
import jax.numpy as jnp
from jax import lax
from jax.experimental import pallas as pl
from jax.experimental.pallas import tpu as pltpu
from jax.sharding import PartitionSpec as P

HEADS = 8
NEG_FILL = -1e30
NT = (((1,), (1,)), ((), ()))
NN = (((1,), (0,)), ((), ()))
EXTRA = 16
VMEM_LIMIT = 48 * 1024 * 1024


def dot(a, b, dims=NN):
    return lax.dot_general(a, b, dims, preferred_element_type=jnp.float32)


def pair_stack(rows):
    lane = lax.broadcasted_iota(jnp.int32, rows.shape, 1)
    half = rows.shape[1] // 2
    zero = jnp.zeros_like(rows)
    return jnp.concatenate([jnp.where(lane < half, rows, zero), jnp.where(lane >= half, rows, zero)], 0)


def tile_bias(mask_ref, pattern, diag):
    words = mask_ref[pattern]
    count, size = words.shape
    keys = lax.broadcasted_iota(jnp.int32, (size, size), 0)
    queries = lax.broadcasted_iota(jnp.int32, (size, size), 1)
    spread = jnp.concatenate(
        [jnp.broadcast_to(words[g : g + 1], (size // count, size)) for g in range(count)], 0
    )
    bits = jnp.right_shift(spread, keys & 31) & 1
    same = keys - queries == jnp.where(diag, 0, 2 * size)
    return jnp.where((bits == 1) | same, 0.0, NEG_FILL)


def list_tiles(coords_ref, counts_ref, list_ref, first, step, lists, cap, column, own):
    def one_list(index, found):
        owner = first + step * index

        def one_slot(slot, found):
            base = (owner * cap + slot) * 3
            other = coords_ref[base + 1 - column]
            list_ref[found * 2] = other * lists + index if column == 0 else index * step + other
            list_ref[found * 2 + 1] = coords_ref[base + 2]
            return found + jnp.where(coords_ref[base + column] == own, 1, 0)

        return lax.fori_loop(0, counts_ref[owner], one_slot, found)

    return lax.fori_loop(0, lists, one_list, 0)


def stream_tiles(total, list_ref, sources, buffers, sems, body):
    def copies(index):
        block = list_ref[index * 2]
        slot = lax.rem(index, 2)
        return [
            pltpu.make_async_copy(
                src.at[block, pl.ds(0, buf.shape[1])], buf.at[slot], sems.at[slot, which]
            )
            for which, (src, buf) in enumerate(zip(sources, buffers))
        ]

    @pl.when(total > 0)
    def _():
        for copy in copies(0):
            copy.start()

    def step(index, carry):
        @pl.when(index + 1 < total)
        def _():
            for copy in copies(index + 1):
                copy.start()

        for copy in copies(index):
            copy.wait()
        body(lax.rem(index, 2), list_ref[index * 2], list_ref[index * 2 + 1])
        return carry

    lax.fori_loop(0, total, step, 0)


def forward_kernel(
    sizes, coords_ref, counts_ref, own_ref, cot_ref, wq_ref, wk_ref, wvt_ref, mask_ref, all_ref,
    out_ref, stats_ref, list_ref, buf_ref, bias_ref, max_ref, sum_ref, acc_ref, sems,
):
    readers, blks, cap = sizes
    reader, blk = lax.axis_index("reader"), lax.axis_index("blk")
    me = reader * blks + blk
    total = list_tiles(coords_ref, counts_ref, list_ref, reader * blks, 1, blks, cap, 0, blk)
    block, width = own_ref.shape
    head = width // HEADS
    queries = dot(own_ref[...], wq_ref[...]).astype(jnp.bfloat16) * jnp.bfloat16(head**-0.5)
    stacks = [pair_stack(queries[:, 2 * head * p : 2 * head * (p + 1)]) for p in range(HEADS // 2)]
    max_ref[...] = jnp.full(max_ref.shape, NEG_FILL, jnp.float32)
    sum_ref[...] = jnp.zeros(sum_ref.shape, jnp.float32)
    acc_ref[...] = jnp.zeros(acc_ref.shape, jnp.float32)

    def tile(slot, other, pattern):
        rows = buf_ref[slot]
        keys = dot(rows, wk_ref[...]).astype(jnp.bfloat16)
        values = dot(wvt_ref[...], rows, NT).astype(jnp.bfloat16)
        bias_ref[...] = tile_bias(mask_ref, pattern, other == me)
        for p in range(HEADS // 2):
            scores = dot(keys[:, 2 * head * p : 2 * head * (p + 1)], stacks[p], NT)
            for e in range(2):
                h = 2 * p + e
                s = scores[:, block * e : block * (e + 1)] + bias_ref[...]
                old = max_ref[h : h + 1]
                new = jnp.maximum(old, jnp.max(s, axis=0, keepdims=True))
                fade = jnp.exp(old - new)
                expo = jnp.exp(s - new)
                max_ref[h : h + 1] = new
                sum_ref[h : h + 1] = sum_ref[h : h + 1] * fade + jnp.sum(expo, axis=0, keepdims=True)
                at = slice(head * h, head * (h + 1))
                acc_ref[at] = acc_ref[at] * fade + dot(values[at], expo.astype(jnp.bfloat16))

    stream_tiles(total, list_ref, [all_ref], [buf_ref], sems, tile)
    inverse = 1.0 / sum_ref[...]
    cot = cot_ref[...].astype(jnp.float32).T
    stats_ref[0:HEADS] = max_ref[...]
    stats_ref[HEADS : 2 * HEADS] = inverse
    for h in range(HEADS):
        at = slice(head * h, head * (h + 1))
        outputs = acc_ref[at] * inverse[h : h + 1]
        acc_ref[at] = outputs
        stats_ref[2 * HEADS + h : 2 * HEADS + h + 1] = jnp.sum(outputs * cot[at], axis=0, keepdims=True)
    out_ref[...] = acc_ref[...].T.astype(out_ref.dtype)


def tile_grads(scores, d_probs, bias, stats, block, p):
    probs, d_scores = [], []
    for e in range(2):
        h = 2 * p + e
        at = slice(block * e, block * (e + 1))
        prob = jnp.exp(scores[:, at] + bias - stats[h : h + 1]) * stats[HEADS + h : HEADS + h + 1]
        probs.append(prob.astype(jnp.bfloat16))
        d_scores.append((prob * (d_probs[:, at] - stats[2 * HEADS + h : 2 * HEADS + h + 1])).astype(jnp.bfloat16))
    return probs, d_scores


def query_grad_kernel(
    sizes, coords_ref, counts_ref, own_ref, cot_ref, wq_ref, wk_ref, wkt_ref, wv_ref, mask_ref, stats_ref, all_ref,
    out_ref, list_ref, buf_ref, bias_ref, acc_ref, sems,
):
    readers, blks, cap = sizes
    reader, blk = lax.axis_index("reader"), lax.axis_index("blk")
    me = reader * blks + blk
    total = list_tiles(coords_ref, counts_ref, list_ref, reader * blks, 1, blks, cap, 0, blk)
    block, width = own_ref.shape
    head = width // HEADS
    queries = dot(own_ref[...], wq_ref[...]).astype(jnp.bfloat16) * jnp.bfloat16(head**-0.5)
    pairs = [slice(2 * head * p, 2 * head * (p + 1)) for p in range(HEADS // 2)]
    query_stacks = [pair_stack(queries[:, pair]) for pair in pairs]
    cot_stacks = [pair_stack(cot_ref[:, pair]) for pair in pairs]
    acc_ref[...] = jnp.zeros(acc_ref.shape, jnp.float32)

    def tile(slot, other, pattern):
        rows = buf_ref[slot]
        keys = dot(rows, wk_ref[...]).astype(jnp.bfloat16)
        keys_t = dot(wkt_ref[...], rows, NT).astype(jnp.bfloat16)
        values = dot(rows, wv_ref[...]).astype(jnp.bfloat16)
        bias_ref[...] = tile_bias(mask_ref, pattern, other == me)
        for p, pair in enumerate(pairs):
            scores = dot(keys[:, pair], query_stacks[p], NT)
            d_probs = dot(values[:, pair], cot_stacks[p], NT)
            _, d_scores = tile_grads(scores, d_probs, bias_ref[...], stats_ref, block, p)
            for e in range(2):
                at = slice(head * (2 * p + e), head * (2 * p + e + 1))
                acc_ref[at] += dot(keys_t[at], d_scores[e])

    stream_tiles(total, list_ref, [all_ref], [buf_ref], sems, tile)
    grad = (acc_ref[...].T * (head**-0.5)).astype(jnp.bfloat16)
    out_ref[...] = dot(grad, wq_ref[...], NT)


def key_grad_kernel(
    sizes, coords_ref, counts_ref, own_ref, wq_ref, wk_ref, wv_ref, mask_ref, part_ref, all_ref, cots_ref, stats_all_ref,
    out_ref, list_ref, buf_ref, cot_buf_ref, stats_buf_ref, bias_ref, key_acc_ref, value_acc_ref, sems,
):
    readers, blks, cap = sizes
    reader, blk = lax.axis_index("reader"), lax.axis_index("blk")
    me = reader * blks + blk
    total = list_tiles(coords_ref, counts_ref, list_ref, blk, blks, readers, cap, 1, reader)
    block, width = own_ref.shape
    head = width // HEADS
    pairs = [slice(2 * head * p, 2 * head * (p + 1)) for p in range(HEADS // 2)]
    keys = dot(own_ref[...], wk_ref[...]).astype(jnp.bfloat16)
    values = dot(own_ref[...], wv_ref[...]).astype(jnp.bfloat16)
    key_acc_ref[...] = jnp.zeros(key_acc_ref.shape, jnp.float32)
    value_acc_ref[...] = jnp.zeros(value_acc_ref.shape, jnp.float32)

    def tile(slot, other, pattern):
        queries = dot(buf_ref[slot], wq_ref[...]).astype(jnp.bfloat16) * jnp.bfloat16(head**-0.5)
        cot = cot_buf_ref[slot]
        stats = stats_buf_ref[slot]
        bias_ref[...] = tile_bias(mask_ref, pattern, other == me)
        for p, pair in enumerate(pairs):
            query_stack = pair_stack(queries[:, pair])
            cot_stack = pair_stack(cot[:, pair])
            scores = dot(keys[:, pair], query_stack, NT)
            d_probs = dot(values[:, pair], cot_stack, NT)
            probs, d_scores = tile_grads(scores, d_probs, bias_ref[...], stats, block, p)
            value_acc_ref[:, pair] += dot(jnp.concatenate(probs, 1), cot_stack)
            key_acc_ref[:, pair] += dot(jnp.concatenate(d_scores, 1), query_stack)

    stream_tiles(
        total, list_ref, [all_ref, cots_ref, stats_all_ref], [buf_ref, cot_buf_ref, stats_buf_ref], sems, tile
    )
    grad = part_ref[...] + dot(key_acc_ref[...].astype(jnp.bfloat16), wk_ref[...], NT)
    grad = grad + dot(value_acc_ref[...].astype(jnp.bfloat16), wv_ref[...], NT)
    out_ref[...] = grad.astype(out_ref.dtype)


VMEM = pl.BlockSpec(memory_space=pltpu.VMEM)
SMEM = pl.BlockSpec(memory_space=pltpu.SMEM)
ANY = pl.BlockSpec(memory_space=pl.ANY)


def local(features, cotangent, w_query, w_key, w_value, tile_coords, tile_count, mask_table):
    block, width = features.shape
    assert block == mask_table.shape[1]
    readers, blks, cap = lax.axis_size("reader"), lax.axis_size("blk"), tile_coords.shape[2]
    devices = readers * blks
    sizes = (readers, blks, cap)
    f32, bf16, i32 = jnp.float32, jnp.bfloat16, jnp.int32
    masks = mask_table.transpose(0, 2, 1)
    axes = ("reader", "blk")

    listing = jnp.concatenate([tile_coords.reshape(-1), tile_count.reshape(-1)]).astype(bf16)
    listing = jnp.pad(listing, (0, EXTRA * width - listing.shape[0])).reshape(EXTRA, width)
    packed = jnp.concatenate([features, listing], 0)
    rows_all = lax.all_gather(packed[None], axes, axis=0, tiled=True)
    cots_all = lax.all_gather(cotangent[None], axes, axis=0, tiled=True)
    numbers = rows_all[:, block, : 3 * cap + 1].astype(i32)
    coords = numbers[:, : 3 * cap].reshape(-1)
    counts = numbers[:, 3 * cap]

    params = pltpu.CompilerParams(vmem_limit_bytes=VMEM_LIMIT)
    list_space = pltpu.SMEM((2 * (devices * cap + 1),), i32)
    buffer = pltpu.VMEM((2, block, width), bf16)
    bias = pltpu.VMEM((block, block), f32)

    def cost(tiles):
        return pl.CostEstimate(flops=tiles * 200_000_000, bytes_accessed=4_000_000, transcendentals=tiles * 131072)

    attn_out, stats = pl.pallas_call(
        functools.partial(forward_kernel, sizes),
        out_shape=(
            jax.ShapeDtypeStruct((block, width), bf16),
            jax.ShapeDtypeStruct((3 * HEADS, block), f32),
        ),
        in_specs=[SMEM, SMEM, VMEM, VMEM, VMEM, VMEM, VMEM, VMEM, ANY],
        out_specs=(VMEM, VMEM),
        scratch_shapes=[
            list_space, buffer, bias,
            pltpu.VMEM((HEADS, block), f32), pltpu.VMEM((HEADS, block), f32), pltpu.VMEM((width, block), f32),
            pltpu.SemaphoreType.DMA((2, 1)),
        ],
        compiler_params=params,
        cost_estimate=cost(5),
        name="forward",
    )(coords, counts, features, cotangent, w_query, w_key, w_value.T, masks, rows_all)

    stats_all = lax.all_gather(stats[None], axes, axis=0, tiled=True)

    query_part = pl.pallas_call(
        functools.partial(query_grad_kernel, sizes),
        out_shape=jax.ShapeDtypeStruct((block, width), f32),
        in_specs=[SMEM, SMEM] + [VMEM] * 8 + [ANY],
        out_specs=VMEM,
        scratch_shapes=[
            list_space, buffer, bias, pltpu.VMEM((width, block), f32), pltpu.SemaphoreType.DMA((2, 1)),
        ],
        compiler_params=params,
        cost_estimate=cost(5),
        name="query_grad",
    )(coords, counts, features, cotangent, w_query, w_key, w_key.T, w_value, masks, stats, rows_all)

    grad_features = pl.pallas_call(
        functools.partial(key_grad_kernel, sizes),
        out_shape=jax.ShapeDtypeStruct((block, width), bf16),
        in_specs=[SMEM, SMEM] + [VMEM] * 6 + [ANY] * 3,
        out_specs=VMEM,
        scratch_shapes=[
            list_space, buffer, buffer, pltpu.VMEM((2, 3 * HEADS, block), f32), bias,
            pltpu.VMEM((block, width), f32), pltpu.VMEM((block, width), f32), pltpu.SemaphoreType.DMA((2, 3)),
        ],
        compiler_params=params,
        cost_estimate=cost(5),
        name="key_grad",
    )(coords, counts, features, w_query, w_key, w_value, masks, query_part, rows_all, cots_all, stats_all)
    return attn_out, grad_features


def solution(mesh):
    return jax.shard_map(
        local,
        mesh=mesh,
        in_specs=(
            P(("reader", "blk"), None),
            P(("reader", "blk"), None),
            P(),
            P(),
            P(),
            P("reader", "blk", None, None),
            P("reader", "blk"),
            P(),
        ),
        out_specs=(P(("reader", "blk"), None), P(("reader", "blk"), None)),
        check_vma=False,
    )
```

```python
import functools

import jax
import jax.numpy as jnp
from jax import lax
from jax.experimental import pallas as pl
from jax.experimental.pallas import tpu as pltpu
from jax.sharding import PartitionSpec as P

HEADS = 8
NEG_FILL = -1e30
NT = (((1,), (1,)), ((), ()))
NN = (((1,), (0,)), ((), ()))
VMEM_LIMIT = 48 * 1024 * 1024


def dot(a, b, dims=NN):
    return lax.dot_general(a, b, dims, preferred_element_type=jnp.float32)


def pair_stack(rows):
    lane = lax.broadcasted_iota(jnp.int32, rows.shape, 1)
    half = rows.shape[1] // 2
    zero = jnp.zeros_like(rows)
    return jnp.concatenate([jnp.where(lane < half, rows, zero), jnp.where(lane >= half, rows, zero)], 0)


def tile_bias(mask_ref, pattern, diag):
    words = mask_ref[pattern]
    count, size = words.shape
    keys = lax.broadcasted_iota(jnp.int32, (size, size), 0)
    queries = lax.broadcasted_iota(jnp.int32, (size, size), 1)
    spread = jnp.concatenate(
        [jnp.broadcast_to(words[g : g + 1], (size // count, size)) for g in range(count)], 0
    )
    bits = jnp.right_shift(spread, keys & 31) & 1
    same = keys - queries == jnp.where(diag, 0, 2 * size)
    return jnp.where((bits == 1) | same, 0.0, NEG_FILL)


def list_tiles(lists_ref, list_ref, count, own_list, column, own, block_of):
    cap = (lists_ref.shape[1] - 1) // 3

    def one_list(index, found):
        def one_slot(slot, found):
            list_ref[found * 2] = block_of(jnp.bitwise_xor(index, own_list), lists_ref[index, 3 * slot + 1 - column])
            list_ref[found * 2 + 1] = lists_ref[index, 3 * slot + 2]
            return found + jnp.where(lists_ref[index, 3 * slot + column] == own, 1, 0)

        return lax.fori_loop(0, lists_ref[index, 3 * cap], one_slot, found)

    return lax.fori_loop(0, count, one_list, 0)


def stream_tiles(total, list_ref, sources, sems, body):
    def copy_of(which, ref, where, slot):
        _, _, buf, rows = sources[which]
        return pltpu.make_async_copy(ref.at[where], buf.at[slot, rows], sems.at[slot, which])

    def start(index):
        block = list_ref[index * 2]
        slot = lax.rem(index, 2)
        for which, (refs, place, _, _) in enumerate(sources):
            group, where = place(block)
            for g, ref in enumerate(refs):

                @pl.when(group == g)
                def _():
                    copy_of(which, ref, where, slot).start()

    @pl.when(total > 0)
    def _():
        start(0)

    def step(index, carry):
        @pl.when(index + 1 < total)
        def _():
            start(index + 1)

        slot = lax.rem(index, 2)
        for which, (refs, _, _, _) in enumerate(sources):
            copy_of(which, refs[0], 0, slot).wait()
        body(slot, list_ref[index * 2], list_ref[index * 2 + 1])
        return carry

    lax.fori_loop(0, total, step, 0)


def bits_of(size):
    return size.bit_length() - 1


def swap(block, mask):
    axes = ("reader", "blk")
    count = lax.axis_size("reader") * lax.axis_size("blk")
    return lax.ppermute(block, axes, [(i, i ^ mask) for i in range(count)])


def gather_line(block):
    return jnp.concatenate([block] + [swap(block, 2 * k) for k in range(1, lax.axis_size("blk") // 2)], 0)


def gather_plane(chunk, order):
    blks = lax.axis_size("blk")
    for bit in order[:-1]:
        chunk = jnp.concatenate([chunk, swap(chunk, blks << bit)], 0)
    return [chunk, swap(chunk, blks << order[-1])]


def other_core(groups):
    return groups + [swap(group, 1) for group in groups]


def place_in(order, blks, me):
    def place(block):
        apart = jnp.bitwise_xor(block, me)
        reader, blk = apart // blks, lax.rem(apart, blks)
        where = blk // 2
        for at, bit in enumerate(order[:-1]):
            where = where + (jnp.right_shift(reader, bit) & 1) * ((blks // 2) << at)
        return (jnp.right_shift(reader, order[-1]) & 1) + 2 * (blk & 1), where

    return place


def orders(readers):
    rising = tuple(range(bits_of(readers)))
    return rising, rising[::-1]


def halves(groups, sizes, me, buffer):
    readers, blks, _ = sizes
    rows = buffer.shape[1] // 2
    return [
        (refs, place_in(order, blks, me), buffer, pl.ds(rows * k, rows))
        for k, (refs, order) in enumerate(zip((groups[:4], groups[4:]), orders(readers)))
    ]


def forward_kernel(
    sizes, lists_ref, own_ref, cot_ref, wq_ref, wk_ref, wvt_ref, mask_ref, *refs,
):
    groups, (out_ref, stats_ref, list_ref, buf_ref, bias_ref, max_ref, sum_ref, acc_ref, sems) = refs[:8], refs[8:]
    readers, blks, cap = sizes
    reader, blk = lax.axis_index("reader"), lax.axis_index("blk")
    me = reader * blks + blk
    total = list_tiles(lists_ref, list_ref, blks, blk, 0, blk, lambda b, k: k * blks + b)
    block, width = own_ref.shape
    head = width // HEADS
    queries = dot(own_ref[...], wq_ref[...]).astype(jnp.bfloat16) * jnp.bfloat16(head**-0.5)
    stacks = [pair_stack(queries[:, 2 * head * p : 2 * head * (p + 1)]) for p in range(HEADS // 2)]
    max_ref[...] = jnp.full(max_ref.shape, NEG_FILL, jnp.float32)
    sum_ref[...] = jnp.zeros(sum_ref.shape, jnp.float32)
    acc_ref[...] = jnp.zeros(acc_ref.shape, jnp.float32)

    def tile(slot, other, pattern):
        rows = buf_ref[slot]
        keys = dot(rows, wk_ref[...]).astype(jnp.bfloat16)
        values = dot(wvt_ref[...], rows, NT).astype(jnp.bfloat16)
        bias_ref[...] = tile_bias(mask_ref, pattern, other == me)
        for p in range(HEADS // 2):
            scores = dot(keys[:, 2 * head * p : 2 * head * (p + 1)], stacks[p], NT)
            for e in range(2):
                h = 2 * p + e
                s = scores[:, block * e : block * (e + 1)] + bias_ref[...]
                old = max_ref[h : h + 1]
                new = jnp.maximum(old, jnp.max(s, axis=0, keepdims=True))
                fade = jnp.exp(old - new)
                expo = jnp.exp(s - new)
                max_ref[h : h + 1] = new
                sum_ref[h : h + 1] = sum_ref[h : h + 1] * fade + jnp.sum(expo, axis=0, keepdims=True)
                at = slice(head * h, head * (h + 1))
                acc_ref[at] = acc_ref[at] * fade + dot(values[at], expo.astype(jnp.bfloat16))

    stream_tiles(total, list_ref, halves(groups, sizes, me, buf_ref), sems, tile)
    inverse = 1.0 / sum_ref[...]
    cot = cot_ref[...].astype(jnp.float32).T
    stats_ref[0:HEADS] = max_ref[...]
    stats_ref[HEADS : 2 * HEADS] = inverse
    for h in range(HEADS):
        at = slice(head * h, head * (h + 1))
        outputs = acc_ref[at] * inverse[h : h + 1]
        acc_ref[at] = outputs
        stats_ref[2 * HEADS + h : 2 * HEADS + h + 1] = jnp.sum(outputs * cot[at], axis=0, keepdims=True)
    out_ref[...] = acc_ref[...].T.astype(out_ref.dtype)


def tile_grads(scores, d_probs, bias, stats, block, p):
    probs, d_scores = [], []
    for e in range(2):
        h = 2 * p + e
        at = slice(block * e, block * (e + 1))
        prob = jnp.exp(scores[:, at] + bias - stats[h : h + 1]) * stats[HEADS + h : HEADS + h + 1]
        probs.append(prob.astype(jnp.bfloat16))
        d_scores.append((prob * (d_probs[:, at] - stats[2 * HEADS + h : 2 * HEADS + h + 1])).astype(jnp.bfloat16))
    return probs, d_scores


def query_grad_kernel(
    sizes, lists_ref, own_ref, cot_ref, wq_ref, wk_ref, wkt_ref, wv_ref, mask_ref, stats_ref, *refs,
):
    groups, (out_ref, list_ref, buf_ref, bias_ref, acc_ref, sems) = refs[:8], refs[8:]
    readers, blks, cap = sizes
    reader, blk = lax.axis_index("reader"), lax.axis_index("blk")
    me = reader * blks + blk
    total = list_tiles(lists_ref, list_ref, blks, blk, 0, blk, lambda b, k: k * blks + b)
    block, width = own_ref.shape
    head = width // HEADS
    queries = dot(own_ref[...], wq_ref[...]).astype(jnp.bfloat16) * jnp.bfloat16(head**-0.5)
    pairs = [slice(2 * head * p, 2 * head * (p + 1)) for p in range(HEADS // 2)]
    query_stacks = [pair_stack(queries[:, pair]) for pair in pairs]
    cot_stacks = [pair_stack(cot_ref[:, pair]) for pair in pairs]
    acc_ref[...] = jnp.zeros(acc_ref.shape, jnp.float32)

    def tile(slot, other, pattern):
        rows = buf_ref[slot]
        keys = dot(rows, wk_ref[...]).astype(jnp.bfloat16)
        keys_t = dot(wkt_ref[...], rows, NT).astype(jnp.bfloat16)
        values = dot(rows, wv_ref[...]).astype(jnp.bfloat16)
        bias_ref[...] = tile_bias(mask_ref, pattern, other == me)
        for p, pair in enumerate(pairs):
            scores = dot(keys[:, pair], query_stacks[p], NT)
            d_probs = dot(values[:, pair], cot_stacks[p], NT)
            _, d_scores = tile_grads(scores, d_probs, bias_ref[...], stats_ref, block, p)
            for e in range(2):
                at = slice(head * (2 * p + e), head * (2 * p + e + 1))
                acc_ref[at] += dot(keys_t[at], d_scores[e])

    stream_tiles(total, list_ref, halves(groups, sizes, me, buf_ref), sems, tile)
    grad = (acc_ref[...].T * (head**-0.5)).astype(jnp.bfloat16)
    out_ref[...] = dot(grad, wq_ref[...], NT)


def key_grad_kernel(
    sizes, lists_ref, own_ref, wq_ref, wk_ref, wv_ref, mask_ref, part_ref, stats_all_ref, *refs,
):
    groups, cot_groups, refs = refs[:8], refs[8:16], refs[16:]
    out_ref, list_ref, buf_ref, cot_buf_ref, bias_ref, key_acc_ref, value_acc_ref, sems = refs
    readers, blks, cap = sizes
    reader, blk = lax.axis_index("reader"), lax.axis_index("blk")
    me = reader * blks + blk
    total = list_tiles(lists_ref, list_ref, readers, reader, 1, reader, lambda r, q: r * blks + q)
    block, width = own_ref.shape
    head = width // HEADS
    pairs = [slice(2 * head * p, 2 * head * (p + 1)) for p in range(HEADS // 2)]
    keys = dot(own_ref[...], wk_ref[...]).astype(jnp.bfloat16)
    values = dot(own_ref[...], wv_ref[...]).astype(jnp.bfloat16)
    key_acc_ref[...] = jnp.zeros(key_acc_ref.shape, jnp.float32)
    value_acc_ref[...] = jnp.zeros(value_acc_ref.shape, jnp.float32)

    def tile(slot, other, pattern):
        queries = dot(buf_ref[slot], wq_ref[...]).astype(jnp.bfloat16) * jnp.bfloat16(head**-0.5)
        cot = cot_buf_ref[slot]
        apart = jnp.bitwise_xor(other, me)
        stats = stats_all_ref.at[apart // blks * blks + lax.rem(apart, blks)]
        bias_ref[...] = tile_bias(mask_ref, pattern, other == me)
        for p, pair in enumerate(pairs):
            query_stack = pair_stack(queries[:, pair])
            cot_stack = pair_stack(cot[:, pair])
            scores = dot(keys[:, pair], query_stack, NT)
            d_probs = dot(values[:, pair], cot_stack, NT)
            probs, d_scores = tile_grads(scores, d_probs, bias_ref[...], stats, block, p)
            value_acc_ref[:, pair] += dot(jnp.concatenate(probs, 1), cot_stack)
            key_acc_ref[:, pair] += dot(jnp.concatenate(d_scores, 1), query_stack)

    sources = halves(groups, sizes, me, buf_ref) + halves(cot_groups, sizes, me, cot_buf_ref)
    stream_tiles(total, list_ref, sources, sems, tile)
    grad = part_ref[...] + dot(key_acc_ref[...].astype(jnp.bfloat16), wk_ref[...], NT)
    grad = grad + dot(value_acc_ref[...].astype(jnp.bfloat16), wv_ref[...], NT)
    out_ref[...] = grad.astype(out_ref.dtype)


VMEM = pl.BlockSpec(memory_space=pltpu.VMEM)
SMEM = pl.BlockSpec(memory_space=pltpu.SMEM)
ANY = pl.BlockSpec(memory_space=pl.ANY)


def after(value, *others):
    return lax.optimization_barrier((value, *others))[0]


def local(features, cotangent, w_query, w_key, w_value, tile_coords, tile_count, mask_table):
    block, width = features.shape
    assert block == mask_table.shape[1]
    readers, blks, cap = lax.axis_size("reader"), lax.axis_size("blk"), tile_coords.shape[2]
    sizes = (readers, blks, cap)
    f32, bf16, i32 = jnp.float32, jnp.bfloat16, jnp.int32
    masks = mask_table.transpose(0, 2, 1)

    listing = jnp.concatenate([tile_coords.reshape(1, -1), tile_count.reshape(1, 1)], 1)
    row_lists = jnp.concatenate([listing] + [swap(listing, k) for k in range(1, blks)], 0)
    column_lists = jnp.concatenate([listing] + [swap(listing, blks * k) for k in range(1, readers)], 0)

    half = block // 2
    pair = lambda array: (array[None, :half], array[None, half:])
    lines = [gather_line(part) for part in pair(features)]
    planes = [gather_plane(part, order) for part, order in zip(lines, orders(readers))]
    rows_all = [other_core(groups) for groups in planes]
    cot_pair = after(pair(cotangent), lines)
    cot_lines = after([gather_line(part) for part in cot_pair], planes)
    cots_all = [other_core(gather_plane(part, order)) for part, order in zip(cot_lines, orders(readers))]

    params = pltpu.CompilerParams(vmem_limit_bytes=VMEM_LIMIT)
    buffer = pltpu.VMEM((2, block, width), bf16)
    bias = pltpu.VMEM((block, block), f32)

    def list_space(lists):
        return pltpu.SMEM((2 * (lists * cap + 1),), i32)

    def cost(tiles):
        return pl.CostEstimate(flops=tiles * 200_000_000, bytes_accessed=4_000_000, transcendentals=tiles * 131072)

    attn_out, stats = pl.pallas_call(
        functools.partial(forward_kernel, sizes),
        out_shape=(
            jax.ShapeDtypeStruct((block, width), bf16),
            jax.ShapeDtypeStruct((3 * HEADS, block), f32),
        ),
        in_specs=[SMEM] + [VMEM] * 6 + [ANY] * 8,
        out_specs=(VMEM, VMEM),
        scratch_shapes=[
            list_space(blks), buffer, bias,
            pltpu.VMEM((HEADS, block), f32), pltpu.VMEM((HEADS, block), f32), pltpu.VMEM((width, block), f32),
            pltpu.SemaphoreType.DMA((2, 2)),
        ],
        compiler_params=params,
        cost_estimate=cost(5),
        name="forward",
    )(row_lists, features, cotangent, w_query, w_key, w_value.T, masks, *rows_all[0], *rows_all[1])

    stats_row = jnp.concatenate([stats[None]] + [swap(stats[None], k) for k in range(1, blks)], 0)
    stats_all = jnp.concatenate([stats_row] + [swap(stats_row, blks * k) for k in range(1, readers)], 0)

    query_part = pl.pallas_call(
        functools.partial(query_grad_kernel, sizes),
        out_shape=jax.ShapeDtypeStruct((block, width), f32),
        in_specs=[SMEM] + [VMEM] * 8 + [ANY] * 8,
        out_specs=VMEM,
        scratch_shapes=[
            list_space(blks), buffer, bias, pltpu.VMEM((width, block), f32), pltpu.SemaphoreType.DMA((2, 2)),
        ],
        compiler_params=params,
        cost_estimate=cost(5),
        name="query_grad",
    )(row_lists, features, cotangent, w_query, w_key, w_key.T, w_value, masks, stats, *rows_all[0], *rows_all[1])

    grad_features = pl.pallas_call(
        functools.partial(key_grad_kernel, sizes),
        out_shape=jax.ShapeDtypeStruct((block, width), bf16),
        in_specs=[SMEM] + [VMEM] * 7 + [ANY] * 16,
        out_specs=VMEM,
        scratch_shapes=[
            list_space(readers), buffer, buffer, bias,
            pltpu.VMEM((block, width), f32), pltpu.VMEM((block, width), f32), pltpu.SemaphoreType.DMA((2, 4)),
        ],
        compiler_params=params,
        cost_estimate=cost(5),
        name="key_grad",
    )(
        column_lists, features, w_query, w_key, w_value, masks, query_part, stats_all,
        *rows_all[0], *rows_all[1], *cots_all[0], *cots_all[1],
    )
    return attn_out, grad_features


def solution(mesh):
    return jax.shard_map(
        local,
        mesh=mesh,
        in_specs=(
            P(("reader", "blk"), None),
            P(("reader", "blk"), None),
            P(),
            P(),
            P(),
            P("reader", "blk", None, None),
            P("reader", "blk"),
            P(),
        ),
        out_specs=(P(("reader", "blk"), None), P(("reader", "blk"), None)),
        check_vma=False,
    )
```

```python
import functools

import jax
import jax.numpy as jnp
from jax import lax
from jax.experimental import pallas as pl
from jax.experimental.pallas import tpu as pltpu
from jax.sharding import PartitionSpec as P

HEADS = 8
NEG_FILL = -1e30
NT = (((1,), (1,)), ((), ()))
NN = (((1,), (0,)), ((), ()))
LIST_ROWS = 16
VMEM_LIMIT = 48 * 1024 * 1024


def dot(a, b, dims=NN):
    return lax.dot_general(a, b, dims, preferred_element_type=jnp.float32)


def pair_stack(rows):
    lane = lax.broadcasted_iota(jnp.int32, rows.shape, 1)
    half = rows.shape[1] // 2
    zero = jnp.zeros_like(rows)
    return jnp.concatenate([jnp.where(lane < half, rows, zero), jnp.where(lane >= half, rows, zero)], 0)


def tile_bias(mask_ref, pattern, diag):
    words = mask_ref[pattern]
    count, size = words.shape
    keys = lax.broadcasted_iota(jnp.int32, (size, size), 0)
    queries = lax.broadcasted_iota(jnp.int32, (size, size), 1)
    spread = jnp.concatenate(
        [jnp.broadcast_to(words[g : g + 1], (size // count, size)) for g in range(count)], 0
    )
    bits = jnp.right_shift(spread, keys & 31) & 1
    same = keys - queries == jnp.where(diag, 0, 2 * size)
    return jnp.where((bits == 1) | same, 0.0, NEG_FILL)


class Layout:
    def __init__(self, readers, blks, cap):
        self.readers, self.blks, self.cap = readers, blks, cap
        self.reader, self.blk = lax.axis_index("reader"), lax.axis_index("blk")
        self.me = self.reader * blks + self.blk

    def apart(self, device):
        far = jnp.bitwise_xor(device, self.me)
        reader, blk = far // self.blks, lax.rem(far, self.blks)
        return reader, blk // 2, blk & 1

    def row_place(self, device):
        reader, line, core = self.apart(device)
        return reader + self.readers * core, line

    def list_place(self, device):
        group, line = self.row_place(device)
        return group * (self.blks // 2) + line

    def half_place(self, bit, device):
        reader, line, core = self.apart(device)
        first = jnp.right_shift(reader, bit) & 1
        low = reader & ((1 << bit) - 1)
        rest = low + (jnp.right_shift(reader, bit + 1) << bit)
        return rest + self.readers // 2 * core, 2 * line + first


def start_copy(place, refs, make):
    group, where = place
    for g, ref in enumerate(refs):

        @pl.when(group == g)
        def _():
            make(ref.at[where]).start()


def scan_list(layout, lists_ref, device, column, wanted, found, write):
    row, cap = layout.list_place(device), layout.cap

    def one_slot(slot, found):
        write(found, lists_ref[row, (1 - column) * cap + slot], lists_ref[row, 2 * cap + slot])
        return found + jnp.where(lists_ref[row, column * cap + slot] == wanted, 1, 0)

    return lax.fori_loop(0, lists_ref[row, 3 * cap], one_slot, found)


def scan_queries(layout, lists_ref, target, write):
    blks = layout.blks
    reader, wanted = target // blks, lax.rem(target, blks)

    def one(b, found):
        put = lambda found, other, pattern: write(found, other * blks + b, pattern)
        return scan_list(layout, lists_ref, reader * blks + b, 0, wanted, found, put)

    return one


def scan_keys(layout, lists_ref, write):
    def one(r, found):
        put = lambda found, other, pattern: write(found, r * layout.blks + other, pattern)
        return scan_list(layout, lists_ref, r * layout.blks + layout.blk, 1, layout.reader, found, put)

    return lax.fori_loop(0, layout.readers, one, 0)


def pack_kernel(own_ref, coords_ref, count_ref, out_ref):
    block = own_ref.shape[0]
    cap = coords_ref.shape[1]
    out_ref[0:block] = own_ref[...]
    lane = lax.broadcasted_iota(jnp.int32, (LIST_ROWS, out_ref.shape[1]), 1)
    row = jnp.zeros(lane.shape, jnp.int32)
    for column in range(3):
        for slot in range(cap):
            row = jnp.where(lane == column * cap + slot, coords_ref[column, slot], row)
    row = jnp.where(lane == 3 * cap, count_ref[0, 0], row)
    out_ref[block:] = row.astype(jnp.float32).astype(jnp.bfloat16)


def forward_kernel(sizes, lists_ref, cot_ref, wq_ref, wk_ref, wvt_ref, mask_ref, *refs):
    readers, blks, cap = sizes
    groups, refs = refs[: 2 * readers], refs[2 * readers :]
    out_ref, stats_ref, stats_all_ref, o_all_ref, target_ref, work_ref = refs[:6]
    key_buf, query_buf, stack_ref, bias_ref, max_ref, sum_ref, acc_ref, o_buf, sems, o_sem = refs[6:]
    layout = Layout(*sizes)
    block, width = cot_ref.shape
    head = width // HEADS

    def write_target(found, device, pattern):
        target_ref[found] = device

    targets = scan_keys(layout, lists_ref, write_target)

    def one_target(index, found):
        target = target_ref[index]

        def write_work(found, key, pattern):
            work_ref[4 * found] = target
            work_ref[4 * found + 1] = key
            work_ref[4 * found + 2] = pattern
            work_ref[4 * found + 3] = index

        return lax.fori_loop(0, blks, scan_queries(layout, lists_ref, target, write_work), found)

    total = lax.fori_loop(0, targets, one_target, 0)
    work_ref[4 * total + 3] = -1

    def key_copy(index):
        slot = lax.rem(index, 2)
        return lambda src: pltpu.make_async_copy(src.at[pl.ds(0, block)], key_buf.at[slot], sems.at[0, slot])

    def query_copy(order):
        slot = lax.rem(order, 2)
        return lambda src: pltpu.make_async_copy(src.at[pl.ds(0, block)], query_buf.at[slot], sems.at[1, slot])

    def is_first(index):
        return jnp.logical_or(index == 0, work_ref[4 * jnp.maximum(index - 1, 0) + 3] != work_ref[4 * index + 3])

    def fetch(index):
        start_copy(layout.row_place(work_ref[4 * index + 1]), groups, key_copy(index))

        @pl.when(is_first(index))
        def _():
            start_copy(layout.row_place(work_ref[4 * index]), groups, query_copy(work_ref[4 * index + 3]))

    fetch(0)

    def tile(index, carry):
        target, key = work_ref[4 * index], work_ref[4 * index + 1]
        pattern, order = work_ref[4 * index + 2], work_ref[4 * index + 3]

        @pl.when(index + 1 < total)
        def _():
            fetch(index + 1)

        key_copy(index)(groups[0].at[0]).wait()

        @pl.when(is_first(index))
        def _():
            query_copy(order)(groups[0].at[0]).wait()
            rows = query_buf[lax.rem(order, 2)]
            queries = dot(rows, wq_ref[...]).astype(jnp.bfloat16) * jnp.bfloat16(head**-0.5)
            for p in range(HEADS // 2):
                stack_ref[p] = pair_stack(queries[:, 2 * head * p : 2 * head * (p + 1)])
            max_ref[...] = jnp.full(max_ref.shape, NEG_FILL, jnp.float32)
            sum_ref[...] = jnp.zeros(sum_ref.shape, jnp.float32)
            acc_ref[...] = jnp.zeros(acc_ref.shape, jnp.float32)

        rows = key_buf[lax.rem(index, 2)]
        keys = dot(rows, wk_ref[...]).astype(jnp.bfloat16)
        values = dot(wvt_ref[...], rows, NT).astype(jnp.bfloat16)
        bias_ref[...] = tile_bias(mask_ref, pattern, key == target)
        for p in range(HEADS // 2):
            scores = dot(keys[:, 2 * head * p : 2 * head * (p + 1)], stack_ref[p], NT)
            for e in range(2):
                h = 2 * p + e
                s = scores[:, block * e : block * (e + 1)] + bias_ref[...]
                old = max_ref[h : h + 1]
                new = jnp.maximum(old, jnp.max(s, axis=0, keepdims=True))
                fade = jnp.exp(old - new)
                expo = jnp.exp(s - new)
                max_ref[h : h + 1] = new
                sum_ref[h : h + 1] = sum_ref[h : h + 1] * fade + jnp.sum(expo, axis=0, keepdims=True)
                at = slice(head * h, head * (h + 1))
                acc_ref[at] = acc_ref[at] * fade + dot(values[at], expo.astype(jnp.bfloat16))

        @pl.when(work_ref[4 * index + 7] != order)
        def _():
            o_copy = pltpu.make_async_copy(o_buf, o_all_ref.at[order], o_sem)

            @pl.when(order > 0)
            def _():
                o_copy.wait()

            inverse = 1.0 / sum_ref[...]
            stats_all_ref[order, 0:HEADS] = max_ref[...]
            stats_all_ref[order, HEADS : 2 * HEADS] = inverse
            for h in range(HEADS):
                at = slice(head * h, head * (h + 1))
                o_buf[at] = acc_ref[at] * inverse[h : h + 1]
            o_copy.start()

            @pl.when(target == layout.me)
            def _():
                cot = cot_ref[...].astype(jnp.float32).T
                stats_ref[0:HEADS] = max_ref[...]
                stats_ref[HEADS : 2 * HEADS] = inverse
                for h in range(HEADS):
                    at = slice(head * h, head * (h + 1))
                    stats_ref[2 * HEADS + h : 2 * HEADS + h + 1] = jnp.sum(o_buf[at] * cot[at], axis=0, keepdims=True)
                out_ref[...] = o_buf[...].T.astype(out_ref.dtype)

        return carry

    lax.fori_loop(0, total, tile, 0)
    pltpu.make_async_copy(o_buf, o_all_ref.at[0], o_sem).wait()


def tile_grads(scores, d_probs, bias, maxima, inverse, delta, block, p):
    probs, d_scores = [], []
    for e in range(2):
        h = 2 * p + e
        at = slice(block * e, block * (e + 1))
        prob = jnp.exp(scores[:, at] + bias - maxima[h : h + 1]) * inverse[h : h + 1]
        probs.append(prob.astype(jnp.bfloat16))
        d_scores.append((prob * (d_probs[:, at] - delta[h : h + 1])).astype(jnp.bfloat16))
    return probs, d_scores


def query_grad_kernel(
    sizes, lists_ref, own_ref, cot_ref, wq_ref, wk_ref, wkt_ref, wv_ref, mask_ref, stats_ref, *refs
):
    groups, refs = refs[: 2 * sizes[0]], refs[2 * sizes[0] :]
    out_ref, work_ref, key_buf, bias_ref, acc_ref, sems = refs
    layout = Layout(*sizes)
    block, width = own_ref.shape
    head = width // HEADS

    def write_work(found, key, pattern):
        work_ref[2 * found] = key
        work_ref[2 * found + 1] = pattern

    total = lax.fori_loop(0, layout.blks, scan_queries(layout, lists_ref, layout.me, write_work), 0)

    def key_copy(index):
        slot = lax.rem(index, 2)
        return lambda src: pltpu.make_async_copy(src.at[pl.ds(0, block)], key_buf.at[slot], sems.at[slot])

    def fetch(index):
        start_copy(layout.row_place(work_ref[2 * index]), groups, key_copy(index))

    fetch(0)
    queries = dot(own_ref[...], wq_ref[...]).astype(jnp.bfloat16) * jnp.bfloat16(head**-0.5)
    pairs = [slice(2 * head * p, 2 * head * (p + 1)) for p in range(HEADS // 2)]
    query_stacks = [pair_stack(queries[:, pair]) for pair in pairs]
    cot_stacks = [pair_stack(cot_ref[:, pair]) for pair in pairs]
    maxima, inverse, delta = (stats_ref[HEADS * k : HEADS * (k + 1)] for k in range(3))
    acc_ref[...] = jnp.zeros(acc_ref.shape, jnp.float32)

    def tile(index, carry):
        @pl.when(index + 1 < total)
        def _():
            fetch(index + 1)

        key_copy(index)(groups[0].at[0]).wait()
        rows = key_buf[lax.rem(index, 2)]
        keys = dot(rows, wk_ref[...]).astype(jnp.bfloat16)
        keys_t = dot(wkt_ref[...], rows, NT).astype(jnp.bfloat16)
        values = dot(rows, wv_ref[...]).astype(jnp.bfloat16)
        bias_ref[...] = tile_bias(mask_ref, work_ref[2 * index + 1], work_ref[2 * index] == layout.me)
        for p, pair in enumerate(pairs):
            scores = dot(keys[:, pair], query_stacks[p], NT)
            d_probs = dot(values[:, pair], cot_stacks[p], NT)
            _, d_scores = tile_grads(scores, d_probs, bias_ref[...], maxima, inverse, delta, block, p)
            for e in range(2):
                at = slice(head * (2 * p + e), head * (2 * p + e + 1))
                acc_ref[at] += dot(keys_t[at], d_scores[e])
        return carry

    lax.fori_loop(0, total, tile, 0)
    grad = (acc_ref[...].T * (head**-0.5)).astype(jnp.bfloat16)
    out_ref[...] = dot(grad, wq_ref[...], NT)


def key_grad_kernel(
    sizes, bits, lists_ref, own_ref, wq_ref, wk_ref, wv_ref, mask_ref, part_ref, stats_all_ref, o_all_ref, *refs
):
    readers = sizes[0]
    groups, halves, refs = refs[: 2 * readers], (refs[2 * readers : 3 * readers], refs[3 * readers : 4 * readers]), refs[4 * readers :]
    out_ref, work_ref, query_buf, cot_buf, o_buf, bias_ref, delta_ref, key_acc, value_acc, sems = refs
    layout = Layout(*sizes)
    block, width = own_ref.shape
    head = width // HEADS

    def write_work(found, query, pattern):
        work_ref[2 * found] = query
        work_ref[2 * found + 1] = pattern

    total = scan_keys(layout, lists_ref, write_work)

    def query_copy(slot):
        return lambda src: pltpu.make_async_copy(src.at[pl.ds(0, block)], query_buf.at[slot], sems.at[slot, 0])

    def o_copy(slot, index):
        return pltpu.make_async_copy(o_all_ref.at[index], o_buf.at[slot], sems.at[slot, 1])

    def half_copy(slot, k):
        rows = pl.ds(block // 2 * k, block // 2)
        return lambda src: pltpu.make_async_copy(src, cot_buf.at[slot, rows], sems.at[slot, 2 + k])

    def fetch(index):
        slot, query = lax.rem(index, 2), work_ref[2 * index]
        start_copy(layout.row_place(query), groups, query_copy(slot))
        o_copy(slot, index).start()
        for k in range(2):
            start_copy(layout.half_place(bits[k], query), halves[k], half_copy(slot, k))

    fetch(0)
    pairs = [slice(2 * head * p, 2 * head * (p + 1)) for p in range(HEADS // 2)]
    keys = dot(own_ref[...], wk_ref[...]).astype(jnp.bfloat16)
    values = dot(own_ref[...], wv_ref[...]).astype(jnp.bfloat16)
    key_acc[...] = jnp.zeros(key_acc.shape, jnp.float32)
    value_acc[...] = jnp.zeros(value_acc.shape, jnp.float32)

    def tile(index, carry):
        @pl.when(index + 1 < total)
        def _():
            fetch(index + 1)

        slot = lax.rem(index, 2)
        query_copy(slot)(groups[0].at[0]).wait()
        o_copy(slot, 0).wait()
        for k in range(2):
            half_copy(slot, k)(halves[k][0].at[0]).wait()
        queries = dot(query_buf[slot], wq_ref[...]).astype(jnp.bfloat16) * jnp.bfloat16(head**-0.5)
        cot = cot_buf[slot]
        cot_t = cot.astype(jnp.float32).T
        for h in range(HEADS):
            at = slice(head * h, head * (h + 1))
            delta_ref[h : h + 1] = jnp.sum(o_buf[slot, at] * cot_t[at], axis=0, keepdims=True)
        maxima, inverse = stats_all_ref[index, 0:HEADS], stats_all_ref[index, HEADS : 2 * HEADS]
        bias_ref[...] = tile_bias(mask_ref, work_ref[2 * index + 1], work_ref[2 * index] == layout.me)
        for p, pair in enumerate(pairs):
            query_stack = pair_stack(queries[:, pair])
            cot_stack = pair_stack(cot[:, pair])
            scores = dot(keys[:, pair], query_stack, NT)
            d_probs = dot(values[:, pair], cot_stack, NT)
            probs, d_scores = tile_grads(
                scores, d_probs, bias_ref[...], maxima, inverse, delta_ref[...], block, p
            )
            value_acc[:, pair] += dot(jnp.concatenate(probs, 1), cot_stack)
            key_acc[:, pair] += dot(jnp.concatenate(d_scores, 1), query_stack)
        return carry

    lax.fori_loop(0, total, tile, 0)
    grad = part_ref[...] + dot(key_acc[...].astype(jnp.bfloat16), wk_ref[...], NT)
    grad = grad + dot(value_acc[...].astype(jnp.bfloat16), wv_ref[...], NT)
    out_ref[...] = grad.astype(out_ref.dtype)


VMEM = pl.BlockSpec(memory_space=pltpu.VMEM)
SMEM = pl.BlockSpec(memory_space=pltpu.SMEM)
ANY = pl.BlockSpec(memory_space=pl.ANY)


def swap(block, mask):
    axes = ("reader", "blk")
    count = lax.axis_size("reader") * lax.axis_size("blk")
    return lax.ppermute(block, axes, [(i, i ^ mask) for i in range(count)])


def after(value, *others):
    return lax.optimization_barrier((value, *others))[0]


def local(features, cotangent, w_query, w_key, w_value, tile_coords, tile_count, mask_table):
    block, width = features.shape
    readers, blks, cap = lax.axis_size("reader"), lax.axis_size("blk"), tile_coords.shape[2]
    assert block == mask_table.shape[1] and 3 * cap < 128
    sizes = (readers, blks, cap)
    devices, lines = readers * blks, blks // 2
    f32, bf16, i32 = jnp.float32, jnp.bfloat16, jnp.int32
    masks = mask_table.transpose(0, 2, 1)
    params = pltpu.CompilerParams(vmem_limit_bytes=VMEM_LIMIT)

    packed = pl.pallas_call(
        pack_kernel,
        out_shape=jax.ShapeDtypeStruct((block + LIST_ROWS, width), bf16),
        in_specs=[VMEM, SMEM, SMEM],
        out_specs=VMEM,
        compiler_params=params,
        name="pack",
    )(features, tile_coords.transpose(0, 3, 1, 2).reshape(3, cap), tile_count)[None]

    line = [packed] + [swap(packed, 2 * k) for k in range(1, lines)]
    chunk = jnp.concatenate(line, 0)
    rows_here = [chunk] + [swap(chunk, blks * k) for k in range(1, readers)]
    rows_all = rows_here + [swap(group, 1) for group in rows_here]

    half = block // 2
    bits = (0, (readers - 1).bit_length() - 1)
    pairs = []
    for k in range(2):
        part = cotangent[None, half * k : half * (k + 1)]
        pairs += [part, swap(part, blks << bits[k])]
    both = jnp.concatenate(pairs, 0)
    cot_line = [both] + [swap(after(both, *line), 2 * k) for k in range(1, lines)]
    cots_all = []
    for k in range(2):
        part = jnp.concatenate([entry[2 * k : 2 * k + 2] for entry in cot_line], 0)
        masks_left = [m for m in range(1, readers) if not m >> bits[k] & 1]
        here = [part] + [swap(after(part, *rows_here), blks * m) for m in masks_left]
        cots_all.append(here + [swap(group, 1) for group in here])

    lists = jnp.concatenate([group[:, block, :128] for group in rows_all], 0).astype(i32)

    buffer = pltpu.VMEM((2, block, width), bf16)
    bias = pltpu.VMEM((block, block), f32)
    turned = pltpu.VMEM((width, block), f32)
    per_head = pltpu.VMEM((HEADS, block), f32)
    targets = min(readers * cap, devices)

    def cost(tiles):
        return pl.CostEstimate(flops=tiles * 200_000_000, bytes_accessed=4_000_000, transcendentals=tiles * 131072)

    attn_out, stats, stats_all, o_all = pl.pallas_call(
        functools.partial(forward_kernel, sizes),
        out_shape=(
            jax.ShapeDtypeStruct((block, width), bf16),
            jax.ShapeDtypeStruct((3 * HEADS, block), f32),
            jax.ShapeDtypeStruct((targets, 2 * HEADS, block), f32),
            jax.ShapeDtypeStruct((targets, width, block), f32),
        ),
        in_specs=[SMEM] + [VMEM] * 5 + [ANY] * (2 * readers),
        out_specs=(VMEM, VMEM, VMEM, ANY),
        scratch_shapes=[
            pltpu.SMEM((targets + 1,), i32), pltpu.SMEM((4 * (targets * min(blks * cap, devices) + 2),), i32),
            buffer, buffer, pltpu.VMEM((HEADS // 2, 2 * block, width // HEADS * 2), bf16),
            bias, per_head, per_head, turned, turned,
            pltpu.SemaphoreType.DMA((2, 2)), pltpu.SemaphoreType.DMA,
        ],
        compiler_params=params,
        cost_estimate=cost(12),
        name="forward",
    )(lists, cotangent, w_query, w_key, w_value.T, masks, *rows_all)

    query_part = pl.pallas_call(
        functools.partial(query_grad_kernel, sizes),
        out_shape=jax.ShapeDtypeStruct((block, width), f32),
        in_specs=[SMEM] + [VMEM] * 8 + [ANY] * (2 * readers),
        out_specs=VMEM,
        scratch_shapes=[
            pltpu.SMEM((2 * (blks * cap + 1),), i32), buffer, bias, turned, pltpu.SemaphoreType.DMA((2,)),
        ],
        compiler_params=params,
        cost_estimate=cost(5),
        name="query_grad",
    )(lists, features, cotangent, w_query, w_key, w_key.T, w_value, masks, stats, *rows_all)

    grad_features = pl.pallas_call(
        functools.partial(key_grad_kernel, sizes, bits),
        out_shape=jax.ShapeDtypeStruct((block, width), bf16),
        in_specs=[SMEM] + [VMEM] * 7 + [ANY] * (1 + 4 * readers),
        out_specs=VMEM,
        scratch_shapes=[
            pltpu.SMEM((2 * (readers * cap + 1),), i32), buffer, buffer, pltpu.VMEM((2, width, block), f32),
            bias, per_head, pltpu.VMEM((block, width), f32), pltpu.VMEM((block, width), f32),
            pltpu.SemaphoreType.DMA((2, 4)),
        ],
        compiler_params=params,
        cost_estimate=cost(5),
        name="key_grad",
    )(
        lists, features, w_query, w_key, w_value, masks, query_part, stats_all, o_all,
        *rows_all, *cots_all[0], *cots_all[1],
    )
    return attn_out, grad_features


def solution(mesh):
    return jax.shard_map(
        local,
        mesh=mesh,
        in_specs=(
            P(("reader", "blk"), None),
            P(("reader", "blk"), None),
            P(),
            P(),
            P(),
            P("reader", "blk", None, None),
            P("reader", "blk"),
            P(),
        ),
        out_specs=(P(("reader", "blk"), None), P(("reader", "blk"), None)),
        check_vma=False,
    )
```

```python
import functools

import jax
import jax.numpy as jnp
from jax import lax
from jax.experimental import pallas as pl
from jax.experimental.pallas import tpu as pltpu
from jax.sharding import PartitionSpec as P

HEADS = 8
NEG_FILL = -1e30
NT = (((1,), (1,)), ((), ()))
NN = (((1,), (0,)), ((), ()))
LIST_ROWS = 16
TILES = 2
KEPT = 4
VMEM_LIMIT = 40 * 1024 * 1024


def dot(a, b, dims=NN):
    return lax.dot_general(a, b, dims, preferred_element_type=jnp.float32)


def pair_stack(rows):
    lane = lax.broadcasted_iota(jnp.int32, rows.shape, 1)
    half = rows.shape[1] // 2
    zero = jnp.zeros_like(rows)
    return jnp.concatenate([jnp.where(lane < half, rows, zero), jnp.where(lane >= half, rows, zero)], 0)


def tile_bias(words, pattern, diag):
    count, size = words.shape
    keys = lax.broadcasted_iota(jnp.int32, (size, size), 0)
    queries = lax.broadcasted_iota(jnp.int32, (size, size), 1)
    spread = jnp.concatenate(
        [jnp.broadcast_to(words[g : g + 1], (size // count, size)) for g in range(count)], 0
    )
    bits = jnp.right_shift(spread, keys & 31) & 1
    same = keys - queries == jnp.where(diag, 0, 2 * size)
    return jnp.where((bits == 1) | same, jnp.where(pattern < 0, NEG_FILL, 0.0), NEG_FILL)


class Layout:
    def __init__(self, readers, blks, cap):
        self.readers, self.blks, self.cap = readers, blks, cap
        self.reader, self.blk = lax.axis_index("reader"), lax.axis_index("blk")
        self.me = self.reader * blks + self.blk

    def apart(self, device):
        far = jnp.bitwise_xor(device, self.me)
        reader, blk = far // self.blks, lax.rem(far, self.blks)
        return reader, blk // 2, blk & 1

    def row_place(self, order, device):
        reader, line, core = self.apart(device)
        for at, bit in enumerate(order[:-1]):
            line = line + (jnp.right_shift(reader, bit) & 1) * ((self.blks // 2) << at)
        return (jnp.right_shift(reader, order[-1]) & 1) + 2 * core, line

    def orders(self):
        return orders(self.readers)

    def half_place(self, bit, device):
        reader, line, core = self.apart(device)
        first = jnp.right_shift(reader, bit) & 1
        low = reader & ((1 << bit) - 1)
        rest = low + (jnp.right_shift(reader, bit + 1) << bit)
        return rest + self.readers // 2 * core, 2 * line + first


def orders(readers):
    rising = tuple(range((readers - 1).bit_length()))
    return rising, rising[::-1]


def start_copy(place, refs, make):
    group, where = place
    for g, ref in enumerate(refs):

        @pl.when(group == g)
        def _():
            make(ref.at[where]).start()


def pack_kernel(own_ref, coords_hbm, count_hbm, out_ref, coords_ref, count_ref, sems):
    block = own_ref.shape[0]
    cap = coords_ref.shape[3]
    copies = [
        pltpu.make_async_copy(coords_hbm, coords_ref, sems.at[0]),
        pltpu.make_async_copy(count_hbm, count_ref, sems.at[1]),
        pltpu.make_async_copy(own_ref, out_ref.at[0, pl.ds(0, block)], sems.at[2]),
    ]
    for copy in copies:
        copy.start()
    copies[0].wait()
    copies[1].wait()
    lane = lax.broadcasted_iota(jnp.int32, (LIST_ROWS, out_ref.shape[2]), 1)
    row = jnp.zeros(lane.shape, jnp.int32)
    for column in range(3):
        for slot in range(cap):
            row = jnp.where(lane == column * cap + slot, coords_ref[0, column, 0, slot], row)
    row = jnp.where(lane == 3 * cap, count_ref[0, 0], row)
    out_ref[0, block:] = row.astype(jnp.float32).astype(jnp.bfloat16)
    copies[2].wait()


def load_lists(refs, half, low_ref, wide_ref, lists_ref, sems):
    copies = []
    for ref, indices in refs:
        for index in indices:
            src = ref.at[index, pl.ds(half, LIST_ROWS), pl.ds(0, 128)]
            copies.append(pltpu.make_async_copy(src, low_ref.at[len(copies)], sems.at[len(copies)]))
    for copy in copies:
        copy.start()
    for copy in copies:
        copy.wait()
    for k in range(low_ref.shape[0]):
        wide_ref[8 * k : 8 * k + 8] = low_ref[k].astype(jnp.float32).astype(jnp.int32)[0:8]
    move = pltpu.make_async_copy(wide_ref, lists_ref, sems.at[0])
    move.start()
    return move


def scan_list(lists_ref, cap, row, column, wanted, found, out_ref, block_of):
    def one_slot(slot, found):
        out_ref[2 * found + 1] = block_of(lists_ref[8 * row, (1 - column) * cap + slot])
        out_ref[2 * found + 2] = lists_ref[8 * row, 2 * cap + slot]
        return found + jnp.where(lists_ref[8 * row, column * cap + slot] == wanted, 1, 0)

    return lax.fori_loop(0, lists_ref[8 * row, 3 * cap], one_slot, found)


def close_work(found, out_ref):
    out_ref[2 * found + 1] = out_ref[2 * found - 1]
    out_ref[2 * found + 2] = -1
    out_ref[0] = (found + 1) // 2


def prepare_kernel(
    sizes, own_ref, cot_ref, wq_ref, wk_ref, wv_ref, line_ref, line_other_ref,
    work_ref, query_stack_ref, cot_stack_ref, key_ref, value_ref, wkt_ref, wvt_ref,
    low_ref, wide_ref, lists_ref, sems,
):
    readers, blks, cap = sizes
    layout = Layout(*sizes)
    block, width = own_ref.shape
    head = width // HEADS
    lines = blks // 2
    refs = [(line_ref, range(lines)), (line_other_ref, range(lines))]
    move = load_lists(refs, block // 2, low_ref, wide_ref, lists_ref, sems)
    queries = dot(own_ref[...], wq_ref[...]).astype(jnp.bfloat16) * jnp.bfloat16(head**-0.5)
    for p in range(HEADS // 2):
        pair = slice(2 * head * p, 2 * head * (p + 1))
        query_stack_ref[p] = pair_stack(queries[:, pair])
        cot_stack_ref[p] = pair_stack(cot_ref[:, pair])
    key_ref[...] = dot(own_ref[...], wk_ref[...]).astype(jnp.bfloat16)
    value_ref[...] = dot(own_ref[...], wv_ref[...]).astype(jnp.bfloat16)
    wkt_ref[...] = wk_ref[...].T
    wvt_ref[...] = wv_ref[...].T
    move.wait()

    def query_side(k, found):
        blk = jnp.bitwise_xor(k, layout.blk)
        row = k // 2 + (k & 1) * lines
        return scan_list(lists_ref, cap, row, 0, layout.blk, found, work_ref, lambda other: other * blks + blk)

    close_work(lax.fori_loop(0, blks, query_side, 0), work_ref)


def key_list_kernel(sizes, here_ref, there_ref, work_ref, low_ref, wide_ref, lists_ref, sems):
    readers, blks, cap = sizes
    layout = Layout(*sizes)
    lines = blks // 2
    starts = range(0, lines * readers // 2, lines)
    half = here_ref.shape[1] - LIST_ROWS
    load_lists([(here_ref, starts), (there_ref, starts)], half, low_ref, wide_ref, lists_ref, sems).wait()
    order = layout.orders()[1]

    def key_side(k, found):
        reader = jnp.bitwise_xor(k, layout.reader)
        row = sum((jnp.right_shift(k, bit) & 1) << at for at, bit in enumerate(order))
        return scan_list(lists_ref, cap, row, 1, layout.reader, found, work_ref, lambda other: reader * blks + other)

    close_work(lax.fori_loop(0, readers, key_side, 0), work_ref)


def step_entry(work_ref, index):
    at = 1 + 2 * TILES * index
    return [work_ref[at + 2 * t] for t in range(TILES)], [work_ref[at + 2 * t + 1] for t in range(TILES)]


def run_steps(work_ref, start, wait, body):
    total = work_ref[0]

    def step(index, carry):
        @pl.when(index + 1 < total)
        def _():
            start(lax.rem(index + 1, 2), *step_entry(work_ref, index + 1))

        slot = lax.rem(index, 2)
        wait(slot)
        body(slot, *step_entry(work_ref, index), index)
        return carry

    lax.fori_loop(0, total, step, 0)


def first_step(work_ref, start):
    start(0, *step_entry(work_ref, 0))


class Rows:
    def __init__(self, layout, groups, mask_ref, buf, words, sems, block):
        self.layout, self.halves, self.mask_ref = layout, (groups[:4], groups[4:]), mask_ref
        self.buf, self.words, self.sems, self.block = buf, words, sems, block

    def rows(self, slot, t, k):
        half = self.block // 2
        into = self.buf.at[slot, pl.ds(t * self.block + k * half, half)]
        return lambda src: pltpu.make_async_copy(src.at[pl.ds(0, half)], into, self.sems.at[slot, t, k])

    def mask(self, slot, t, pattern):
        return pltpu.make_async_copy(self.mask_ref.at[pattern], self.words.at[slot, t], self.sems.at[slot, t, 2])

    def start(self, slot, blocks, patterns):
        for t in range(TILES):
            for k, order in enumerate(self.layout.orders()):
                start_copy(self.layout.row_place(order, blocks[t]), self.halves[k], self.rows(slot, t, k))
            self.mask(slot, t, jnp.maximum(patterns[t], 0)).start()

    def wait(self, slot):
        for t in range(TILES):
            for k in range(2):
                self.rows(slot, t, k)(self.halves[k][0].at[0]).wait()
            self.mask(slot, t, 0).wait()

    def bias(self, slot, blocks, patterns):
        parts = [
            tile_bias(self.words[slot, t], patterns[t], blocks[t] == self.layout.me) for t in range(TILES)
        ]
        return jnp.concatenate(parts, 0)


def query_kernel(
    sizes, work_ref, stack_ref, cot_stack_ref, cot_ref, wq_ref, wk_hbm, wkt_hbm, wv_hbm, wvt_hbm, mask_ref, *refs
):
    groups, refs = refs[:8], refs[8:]
    out_ref, stats_ref, part_ref, wk_ref, wkt_ref, wv_ref, wvt_ref = refs[:7]
    buf, words, bias_ref, max_ref, sum_ref, acc_ref, score_ref, d_prob_ref, key_ref, sems, w_sems = refs[7:]
    layout = Layout(*sizes)
    block, width = cot_ref.shape
    head = width // HEADS
    rows_in = Rows(layout, groups, mask_ref, buf, words, sems, block)
    kept = score_ref.shape[0] - 1
    first_step(work_ref, rows_in.start)
    loads = [
        pltpu.make_async_copy(src, into, w_sems.at[k])
        for k, (src, into) in enumerate(
            ((wk_hbm, wk_ref), (wvt_hbm, wvt_ref), (wv_hbm, wv_ref), (wkt_hbm, wkt_ref))
        )
    ]
    for load in loads:
        load.start()
    max_ref[...] = jnp.full(max_ref.shape, NEG_FILL, jnp.float32)
    sum_ref[...] = jnp.zeros(sum_ref.shape, jnp.float32)
    acc_ref[...] = jnp.zeros(acc_ref.shape, jnp.float32)
    for load in loads:
        load.wait()

    def meet(slot, place, blocks, patterns):
        rows = buf[slot]
        keys = dot(rows, wk_ref[...]).astype(jnp.bfloat16)
        values = dot(rows, wv_ref[...]).astype(jnp.bfloat16)
        key_ref[place] = dot(wkt_ref[...], rows, NT).astype(jnp.bfloat16)
        bias_ref[...] = rows_in.bias(slot, blocks, patterns)
        for p in range(HEADS // 2):
            pair = slice(2 * head * p, 2 * head * (p + 1))
            scores = dot(keys[:, pair], stack_ref[p], NT)
            d_probs = dot(values[:, pair], cot_stack_ref[p], NT)
            for e in range(2):
                of = slice(block * e, block * (e + 1))
                score_ref[place, 2 * p + e] = scores[:, of] + bias_ref[...]
                d_prob_ref[place, 2 * p + e] = d_probs[:, of]

    def soften(slot, blocks, patterns, index):
        place = jnp.minimum(index, kept)
        meet(slot, place, blocks, patterns)
        values = dot(wvt_ref[...], buf[slot], NT).astype(jnp.bfloat16)
        for h in range(HEADS):
            s = score_ref[place, h]
            old = max_ref[h : h + 1]
            new = jnp.maximum(old, jnp.max(s, axis=0, keepdims=True))
            fade = jnp.exp(old - new)
            expo = jnp.exp(s - new)
            max_ref[h : h + 1] = new
            sum_ref[h : h + 1] = sum_ref[h : h + 1] * fade + jnp.sum(expo, axis=0, keepdims=True)
            at = slice(head * h, head * (h + 1))
            acc_ref[at] = acc_ref[at] * fade + dot(values[at], expo.astype(jnp.bfloat16))

    run_steps(work_ref, rows_in.start, rows_in.wait, soften)
    inverse = 1.0 / sum_ref[...]
    cot = cot_ref[...].astype(jnp.float32).T
    stats_ref[0:HEADS] = max_ref[...] + jnp.log(sum_ref[...])
    for h in range(HEADS):
        at = slice(head * h, head * (h + 1))
        outputs = acc_ref[at] * inverse[h : h + 1]
        acc_ref[at] = outputs
        stats_ref[HEADS + h : HEADS + h + 1] = jnp.sum(outputs * cot[at], axis=0, keepdims=True)
    out_ref[...] = acc_ref[...].T.astype(out_ref.dtype)
    acc_ref[...] = jnp.zeros(acc_ref.shape, jnp.float32)

    def slope(index, carry):
        place = jnp.minimum(index, kept)

        @pl.when(index >= kept)
        def _():
            blocks, patterns = step_entry(work_ref, index)
            rows_in.start(0, blocks, patterns)
            rows_in.wait(0)
            meet(0, place, blocks, patterns)

        for h in range(HEADS):
            _, d_scores = tile_grads(
                score_ref[place, h], d_prob_ref[place, h], stats_ref[h : h + 1], stats_ref[HEADS + h : HEADS + h + 1]
            )
            at = slice(head * h, head * (h + 1))
            acc_ref[at] += dot(key_ref[place, at], d_scores)
        return carry

    lax.fori_loop(0, work_ref[0], slope, 0)
    grad = (acc_ref[...].T * (head**-0.5)).astype(jnp.bfloat16)
    part_ref[...] = dot(grad, wq_ref[...], NT)


def tile_grads(scores, d_probs, lse, delta):
    prob = jnp.exp(scores - lse)
    return prob.astype(jnp.bfloat16), (prob * (d_probs - delta)).astype(jnp.bfloat16)


def key_grad_kernel(
    sizes, bits, work_ref, key_ref, value_ref, wq_hbm, wk_hbm, wv_hbm, part_ref, mask_ref, stats_all_ref, *refs
):
    readers = sizes[0]
    groups, refs = refs[:8], refs[8:]
    halves, refs = (refs[:readers], refs[readers : 2 * readers]), refs[2 * readers :]
    out_ref, wq_ref, wk_ref, wv_ref, buf, words, cot_buf, stats, bias_ref = refs[:9]
    key_acc, value_acc, sems, c_sems, w_sems = refs[9:]
    layout = Layout(*sizes)
    block, width = out_ref.shape
    head = width // HEADS
    rows_in = Rows(layout, groups, mask_ref, buf, words, sems, block)

    def half_copy(slot, t, k):
        into = cot_buf.at[slot, pl.ds(t * block + block // 2 * k, block // 2)]
        return lambda src: pltpu.make_async_copy(src, into, c_sems.at[slot, t, k])

    def stats_copy(slot, t, query):
        return pltpu.make_async_copy(stats_all_ref.at[query], stats.at[slot, t], c_sems.at[slot, t, 2])

    def start(slot, blocks, patterns):
        rows_in.start(slot, blocks, patterns)
        for t in range(TILES):
            stats_copy(slot, t, blocks[t]).start()
            for k in range(2):
                start_copy(layout.half_place(bits[k], blocks[t]), halves[k], half_copy(slot, t, k))

    def wait(slot):
        rows_in.wait(slot)
        for t in range(TILES):
            stats_copy(slot, t, 0).wait()
            for k in range(2):
                half_copy(slot, t, k)(halves[k][0].at[0]).wait()

    first_step(work_ref, start)
    loads = [
        pltpu.make_async_copy(src, into, w_sems.at[k])
        for k, (src, into) in enumerate(((wq_hbm, wq_ref), (wk_hbm, wk_ref), (wv_hbm, wv_ref)))
    ]
    for load in loads:
        load.start()
    key_acc[...] = jnp.zeros(key_acc.shape, jnp.float32)
    value_acc[...] = jnp.zeros(value_acc.shape, jnp.float32)
    loads[0].wait()

    def tiles(slot, blocks, patterns, index):
        queries = dot(buf[slot], wq_ref[...]).astype(jnp.bfloat16) * jnp.bfloat16(head**-0.5)
        bias_ref[...] = rows_in.bias(slot, blocks, patterns)
        cots = cot_buf[slot]
        for p in range(HEADS // 2):
            pair = slice(2 * head * p, 2 * head * (p + 1))
            of_tile = [slice(block * t, block * (t + 1)) for t in range(TILES)]
            query_stack = jnp.concatenate([pair_stack(queries[of, pair]) for of in of_tile], 0)
            cot_stack = jnp.concatenate([pair_stack(cots[of, pair]) for of in of_tile], 0)
            scores = dot(key_ref[:, pair], query_stack, NT)
            d_probs = dot(value_ref[:, pair], cot_stack, NT)
            probs, d_scores = [], []
            for t in range(TILES):
                for e in range(2):
                    h = 2 * p + e
                    of = slice(block * (2 * t + e), block * (2 * t + e + 1))
                    prob, d_score = tile_grads(
                        scores[:, of] + bias_ref[of_tile[t]], d_probs[:, of], stats[slot, t, h : h + 1],
                        stats[slot, t, HEADS + h : HEADS + h + 1],
                    )
                    probs.append(prob)
                    d_scores.append(d_score)
            value_acc[:, pair] += dot(jnp.concatenate(probs, 1), cot_stack)
            key_acc[:, pair] += dot(jnp.concatenate(d_scores, 1), query_stack)

    run_steps(work_ref, start, wait, tiles)
    loads[1].wait()
    loads[2].wait()
    grad = part_ref[...] + dot(key_acc[...].astype(jnp.bfloat16), wk_ref[...], NT)
    grad = grad + dot(value_acc[...].astype(jnp.bfloat16), wv_ref[...], NT)
    out_ref[...] = grad.astype(out_ref.dtype)


VMEM = pl.BlockSpec(memory_space=pltpu.VMEM)
SMEM = pl.BlockSpec(memory_space=pltpu.SMEM)
HBM = pl.BlockSpec(memory_space=pltpu.HBM)


def swap(block, mask):
    axes = ("reader", "blk")
    count = lax.axis_size("reader") * lax.axis_size("blk")
    return lax.ppermute(block, axes, [(i, i ^ mask) for i in range(count)])


def after(value, *others):
    return lax.optimization_barrier((value, *others))[0]


def over_readers(chunk, order, blks):
    for bit in order[:-1]:
        chunk = jnp.concatenate([chunk, swap(chunk, blks << bit)], 0)
    return [chunk, swap(chunk, blks << order[-1])]


def other_core(groups):
    return groups + [swap(group, 1) for group in groups]


def local(features, cotangent, w_query, w_key, w_value, tile_coords, tile_count, mask_table):
    block, width = features.shape
    readers, blks, cap = lax.axis_size("reader"), lax.axis_size("blk"), tile_coords.shape[2]
    assert block == mask_table.shape[1] and 3 * cap < 128
    sizes = (readers, blks, cap)
    devices, lines = readers * blks, blks // 2
    f32, bf16, i32 = jnp.float32, jnp.bfloat16, jnp.int32
    shape = jax.ShapeDtypeStruct
    masks = mask_table.transpose(0, 2, 1)
    words = masks.shape[1]
    head = width // HEADS
    half = block // 2
    params = pltpu.CompilerParams(vmem_limit_bytes=VMEM_LIMIT)
    masks_off = [2 * k for k in range(1, lines)]

    packed = pl.pallas_call(
        pack_kernel,
        out_shape=shape((1, block + LIST_ROWS, width), bf16),
        in_specs=[HBM, HBM, HBM],
        out_specs=VMEM,
        scratch_shapes=[
            pltpu.SMEM((1, 3, 1, cap), i32), pltpu.SMEM((1, 1), i32), pltpu.SemaphoreType.DMA((3,)),
        ],
        compiler_params=params,
        name="pack",
    )(features, tile_coords.transpose(0, 3, 1, 2), tile_count)

    lined = [packed] + [swap(packed, m) for m in masks_off]
    chunks = [
        jnp.concatenate([entry[:, :half] for entry in lined], 0),
        jnp.concatenate([entry[:, half:] for entry in lined], 0),
    ]
    here = [over_readers(chunk, order, blks) for chunk, order in zip(chunks, orders(readers))]
    rows_all = [group for groups in here for group in other_core(groups)]

    bits = (0, (readers - 1).bit_length() - 1)
    pairs = []
    for k in range(2):
        part = cotangent[None, half * k : half * (k + 1)]
        pairs += [part, swap(part, blks << bits[k])]
    both = jnp.concatenate(pairs, 0)
    cot_line = [both] + [swap(after(both, *chunks), m) for m in masks_off]
    cots_all = []
    for k in range(2):
        part = jnp.concatenate([entry[2 * k : 2 * k + 2] for entry in cot_line], 0)
        masks_left = [m for m in range(1, readers) if not m >> bits[k] & 1]
        cot_here = [part] + [swap(after(part, here), blks * m) for m in masks_left]
        cots_all += other_core(cot_here)

    def list_scratch(count):
        return [
            pltpu.VMEM((count, LIST_ROWS, 128), bf16), pltpu.VMEM((8 * count, 128), i32),
            pltpu.SMEM((8 * count, 128), i32), pltpu.SemaphoreType.DMA((count,)),
        ]

    def cost(tiles):
        return pl.CostEstimate(flops=tiles * 200_000_000, bytes_accessed=4_000_000, transcendentals=tiles * 131072)

    stacks = shape((HEADS // 2, 2 * block, 2 * head), bf16)
    own = shape((block, width), bf16)
    square = shape((width, width), bf16)
    query_work, query_stack, cot_stack, keys, values, w_key_t, w_value_t = pl.pallas_call(
        functools.partial(prepare_kernel, sizes),
        out_shape=(shape((2 * blks * cap + 5,), i32), stacks, stacks, own, own, square, square),
        in_specs=[VMEM] * 5 + [HBM] * 2,
        out_specs=(SMEM,) + (VMEM,) * 6,
        scratch_shapes=list_scratch(blks),
        compiler_params=params,
        cost_estimate=cost(2),
        name="prepare",
    )(features, cotangent, w_query, w_key, w_value, rows_all[4], rows_all[6])

    key_work = pl.pallas_call(
        functools.partial(key_list_kernel, sizes),
        out_shape=shape((2 * readers * cap + 5,), i32),
        in_specs=[HBM] * 2,
        out_specs=SMEM,
        scratch_shapes=list_scratch(readers),
        compiler_params=params,
        cost_estimate=cost(1),
        name="key_list",
    )(rows_all[4], rows_all[5])

    weight = pltpu.VMEM((width, width), bf16)
    buffer = pltpu.VMEM((2, TILES * block, width), bf16)
    word_buffer = pltpu.VMEM((2, TILES, words, block), i32)
    bias = pltpu.VMEM((TILES * block, block), f32)
    turned = pltpu.VMEM((width, block), f32)
    per_head = pltpu.VMEM((HEADS, block), f32)
    met = pltpu.VMEM((KEPT + 1, HEADS, TILES * block, block), f32)
    row_sems = pltpu.SemaphoreType.DMA((2, TILES, 3))

    attn_out, stats, query_part = pl.pallas_call(
        functools.partial(query_kernel, sizes),
        out_shape=(own, shape((2 * HEADS, block), f32), shape((block, width), f32)),
        in_specs=[SMEM, VMEM, VMEM, VMEM, VMEM] + [HBM] * 13,
        out_specs=(VMEM, VMEM, VMEM),
        scratch_shapes=[
            weight, weight, weight, weight, buffer, word_buffer, bias, per_head, per_head, turned, met, met,
            pltpu.VMEM((KEPT + 1, width, TILES * block), bf16), row_sems, pltpu.SemaphoreType.DMA((4,)),
        ],
        compiler_params=params,
        cost_estimate=cost(10),
        name="query_side",
    )(query_work, query_stack, cot_stack, cotangent, w_query, w_key, w_key_t, w_value, w_value_t, masks, *rows_all)

    sent = jnp.broadcast_to(stats[None], (devices, *stats.shape))
    stats_all = lax.all_to_all(sent, ("reader", "blk"), 0, 0, tiled=True)

    grad_features = pl.pallas_call(
        functools.partial(key_grad_kernel, sizes, bits),
        out_shape=own,
        in_specs=[SMEM, VMEM, VMEM, HBM, HBM, HBM, VMEM, HBM, HBM] + [HBM] * (8 + 2 * readers),
        out_specs=VMEM,
        scratch_shapes=[
            weight, weight, weight, buffer, word_buffer, buffer, pltpu.VMEM((2, TILES, 2 * HEADS, block), f32),
            bias, pltpu.VMEM((block, width), f32), pltpu.VMEM((block, width), f32),
            row_sems, pltpu.SemaphoreType.DMA((2, TILES, 3)), pltpu.SemaphoreType.DMA((3,)),
        ],
        compiler_params=params,
        cost_estimate=cost(5),
        name="key_grad",
    )(key_work, keys, values, w_query, w_key, w_value, query_part, masks, stats_all, *rows_all, *cots_all)
    return attn_out, grad_features


def solution(mesh):
    return jax.shard_map(
        local,
        mesh=mesh,
        in_specs=(
            P(("reader", "blk"), None),
            P(("reader", "blk"), None),
            P(),
            P(),
            P(),
            P("reader", "blk", None, None),
            P("reader", "blk"),
            P(),
        ),
        out_specs=(P(("reader", "blk"), None), P(("reader", "blk"), None)),
        check_vma=False,
    )
```

```python
import functools

import jax
import jax.numpy as jnp
from jax import lax
from jax.experimental import pallas as pl
from jax.experimental.pallas import tpu as pltpu
from jax.sharding import PartitionSpec as P

HEADS = 8
NEG_FILL = -1e30
NT = (((1,), (1,)), ((), ()))
NN = (((1,), (0,)), ((), ()))
LIST_ROWS = 16
TILES = 2
KEPT = 4
VMEM_LIMIT = 58 * 1024 * 1024


def dot(a, b, dims=NN):
    return lax.dot_general(a, b, dims, preferred_element_type=jnp.float32)


def pair_stack(rows):
    lane = lax.broadcasted_iota(jnp.int32, rows.shape, 1)
    half = rows.shape[1] // 2
    zero = jnp.zeros_like(rows)
    return jnp.concatenate([jnp.where(lane < half, rows, zero), jnp.where(lane >= half, rows, zero)], 0)


def tile_bias(words, pattern, diag):
    count, size = words.shape
    keys = lax.broadcasted_iota(jnp.int32, (size, size), 0)
    queries = lax.broadcasted_iota(jnp.int32, (size, size), 1)
    spread = jnp.concatenate(
        [jnp.broadcast_to(words[g : g + 1], (size // count, size)) for g in range(count)], 0
    )
    bits = jnp.right_shift(spread, keys & 31) & 1
    same = keys - queries == jnp.where(diag, 0, 2 * size)
    return jnp.where((bits == 1) | same, jnp.where(pattern < 0, NEG_FILL, 0.0), NEG_FILL)


class Layout:
    def __init__(self, readers, blks, cap):
        self.readers, self.blks, self.cap = readers, blks, cap
        self.reader, self.blk = lax.axis_index("reader"), lax.axis_index("blk")
        self.me = self.reader * blks + self.blk

    def apart(self, device):
        far = jnp.bitwise_xor(device, self.me)
        reader, blk = far // self.blks, lax.rem(far, self.blks)
        return reader, blk // 2, blk & 1

    def row_place(self, order, device):
        reader, line, core = self.apart(device)
        for at, bit in enumerate(order[:-1]):
            line = line + (jnp.right_shift(reader, bit) & 1) * ((self.blks // 2) << at)
        return (jnp.right_shift(reader, order[-1]) & 1) + 2 * core, line

    def orders(self):
        return orders(self.readers)

    def half_place(self, bit, device):
        reader, line, core = self.apart(device)
        first = jnp.right_shift(reader, bit) & 1
        top = (self.blks // 2 - 1).bit_length() - 1
        line = sum((jnp.right_shift(line, top - at) & 1) << at for at in range(top + 1))
        low = reader & ((1 << bit) - 1)
        rest = low + (jnp.right_shift(reader, bit + 1) << bit)
        return rest + self.readers // 2 * core, 2 * line + first


def orders(readers):
    rising = tuple(range((readers - 1).bit_length()))
    return rising, rising[::-1]


def start_copy(place, refs, make):
    group, where = place
    for g, ref in enumerate(refs):

        @pl.when(group == g)
        def _():
            make(ref.at[where]).start()


def pack_kernel(own_ref, coords_hbm, count_hbm, out_ref, coords_ref, count_ref, sems):
    block = own_ref.shape[0]
    cap = coords_ref.shape[3]
    copies = [
        pltpu.make_async_copy(coords_hbm, coords_ref, sems.at[0]),
        pltpu.make_async_copy(count_hbm, count_ref, sems.at[1]),
        pltpu.make_async_copy(own_ref, out_ref.at[0, pl.ds(0, block)], sems.at[2]),
    ]
    for copy in copies:
        copy.start()
    copies[0].wait()
    copies[1].wait()
    lane = lax.broadcasted_iota(jnp.int32, (LIST_ROWS, out_ref.shape[2]), 1)
    row = jnp.zeros(lane.shape, jnp.int32)
    for column in range(3):
        for slot in range(cap):
            row = jnp.where(lane == column * cap + slot, coords_ref[0, column, 0, slot], row)
    row = jnp.where(lane == 3 * cap, count_ref[0, 0], row)
    out_ref[0, block:] = row.astype(jnp.float32).astype(jnp.bfloat16)
    copies[2].wait()


def load_lists(refs, half, low_ref, wide_ref, lists_ref, sems):
    copies = []
    for ref, indices in refs:
        for index in indices:
            src = ref.at[index, pl.ds(half, LIST_ROWS), pl.ds(0, 128)]
            copies.append(pltpu.make_async_copy(src, low_ref.at[len(copies)], sems.at[len(copies)]))
    for copy in copies:
        copy.start()
    for copy in copies:
        copy.wait()
    for k in range(low_ref.shape[0]):
        wide_ref[8 * k : 8 * k + 8] = low_ref[k].astype(jnp.float32).astype(jnp.int32)[0:8]
    move = pltpu.make_async_copy(wide_ref, lists_ref, sems.at[0])
    move.start()
    return move


def scan_list(lists_ref, cap, row, column, wanted, found, out_ref, block_of):
    def one_slot(slot, found):
        out_ref[2 * found + 1] = block_of(lists_ref[8 * row, (1 - column) * cap + slot])
        out_ref[2 * found + 2] = lists_ref[8 * row, 2 * cap + slot]
        return found + jnp.where(lists_ref[8 * row, column * cap + slot] == wanted, 1, 0)

    return lax.fori_loop(0, lists_ref[8 * row, 3 * cap], one_slot, found)


def close_work(found, out_ref):
    out_ref[2 * found + 1] = out_ref[2 * found - 1]
    out_ref[2 * found + 2] = -1
    out_ref[0] = (found + 1) // 2


def prepare_kernel(
    sizes, own_ref, cot_ref, wq_ref, wk_ref, wv_ref, line_ref, line_other_ref,
    work_ref, query_stack_ref, cot_stack_ref, key_ref, value_ref, wkt_ref, wvt_ref,
    low_ref, wide_ref, lists_ref, sems,
):
    readers, blks, cap = sizes
    layout = Layout(*sizes)
    block, width = own_ref.shape
    head = width // HEADS
    lines = blks // 2
    refs = [(line_ref, range(lines)), (line_other_ref, range(lines))]
    move = load_lists(refs, block // 2, low_ref, wide_ref, lists_ref, sems)
    queries = dot(own_ref[...], wq_ref[...]).astype(jnp.bfloat16) * jnp.bfloat16(head**-0.5)
    for p in range(HEADS // 2):
        pair = slice(2 * head * p, 2 * head * (p + 1))
        query_stack_ref[p] = pair_stack(queries[:, pair])
        cot_stack_ref[p] = pair_stack(cot_ref[:, pair])
    key_ref[...] = dot(own_ref[...], wk_ref[...]).astype(jnp.bfloat16)
    value_ref[...] = dot(own_ref[...], wv_ref[...]).astype(jnp.bfloat16)
    wkt_ref[...] = wk_ref[...].T
    wvt_ref[...] = wv_ref[...].T
    move.wait()

    def query_side(k, found):
        blk = jnp.bitwise_xor(k, layout.blk)
        row = k // 2 + (k & 1) * lines
        return scan_list(lists_ref, cap, row, 0, layout.blk, found, work_ref, lambda other: other * blks + blk)

    close_work(lax.fori_loop(0, blks, query_side, 0), work_ref)


def key_list_kernel(sizes, here_ref, there_ref, work_ref, low_ref, wide_ref, lists_ref, sems):
    readers, blks, cap = sizes
    layout = Layout(*sizes)
    lines = blks // 2
    starts = range(0, lines * readers // 2, lines)
    half = here_ref.shape[1] - LIST_ROWS
    load_lists([(here_ref, starts), (there_ref, starts)], half, low_ref, wide_ref, lists_ref, sems).wait()
    order = layout.orders()[1]

    def key_side(k, found):
        reader = jnp.bitwise_xor(k, layout.reader)
        row = sum((jnp.right_shift(k, bit) & 1) << at for at, bit in enumerate(order))
        return scan_list(lists_ref, cap, row, 1, layout.reader, found, work_ref, lambda other: reader * blks + other)

    close_work(lax.fori_loop(0, readers, key_side, 0), work_ref)


def step_entry(work_ref, index):
    at = 1 + 2 * TILES * index
    return [work_ref[at + 2 * t] for t in range(TILES)], [work_ref[at + 2 * t + 1] for t in range(TILES)]


def run_steps(work_ref, start, wait, body):
    total = work_ref[0]

    def step(index, carry):
        @pl.when(index + 1 < total)
        def _():
            start(lax.rem(index + 1, 2), *step_entry(work_ref, index + 1))

        slot = lax.rem(index, 2)
        wait(slot)
        body(slot, *step_entry(work_ref, index), index)
        return carry

    lax.fori_loop(0, total, step, 0)


def first_step(work_ref, start):
    start(0, *step_entry(work_ref, 0))


class Rows:
    def __init__(self, layout, groups, mask_ref, buf, words, sems, block):
        self.layout, self.halves, self.mask_ref = layout, (groups[:4], groups[4:]), mask_ref
        self.buf, self.words, self.sems, self.block = buf, words, sems, block

    def rows(self, slot, t, k):
        half = self.block // 2
        into = self.buf.at[slot, pl.ds(t * self.block + k * half, half)]
        return lambda src: pltpu.make_async_copy(src.at[pl.ds(0, half)], into, self.sems.at[slot, t, k])

    def mask(self, slot, t, pattern):
        return pltpu.make_async_copy(self.mask_ref.at[pattern], self.words.at[slot, t], self.sems.at[slot, t, 2])

    def start(self, slot, blocks, patterns):
        for t in range(TILES):
            for k, order in enumerate(self.layout.orders()):
                start_copy(self.layout.row_place(order, blocks[t]), self.halves[k], self.rows(slot, t, k))
            self.mask(slot, t, jnp.maximum(patterns[t], 0)).start()

    def wait(self, slot):
        for t in range(TILES):
            for k in range(2):
                self.rows(slot, t, k)(self.halves[k][0].at[0]).wait()
            self.mask(slot, t, 0).wait()

    def bias(self, slot, blocks, patterns):
        parts = [
            tile_bias(self.words[slot, t], patterns[t], blocks[t] == self.layout.me) for t in range(TILES)
        ]
        return jnp.concatenate(parts, 0)


def query_kernel(
    sizes, work_ref, stack_hbm, cot_stack_hbm, cot_hbm, wq_hbm, wk_hbm, wkt_hbm, wv_hbm, wvt_hbm, mask_ref, *refs
):
    groups, refs = refs[:8], refs[8:]
    out_ref, sent_ref, part_ref, stack_ref, cot_stack_ref, cot_ref, wq_ref, wk_ref, wkt_ref, wv_ref, wvt_ref = refs[:11]
    stats_ref, buf, words, bias_ref, max_ref, sum_ref, acc_ref, score_ref, d_prob_ref, key_ref, sems, w_sems = refs[11:]
    layout = Layout(*sizes)
    block, width = cot_ref.shape
    head = width // HEADS
    rows_in = Rows(layout, groups, mask_ref, buf, words, sems, block)
    kept = score_ref.shape[0] - 1
    first_step(work_ref, rows_in.start)
    loads = [
        pltpu.make_async_copy(src, into, w_sems.at[k])
        for k, (src, into) in enumerate((
            (wk_hbm, wk_ref), (stack_hbm, stack_ref), (wv_hbm, wv_ref), (cot_stack_hbm, cot_stack_ref),
            (wkt_hbm, wkt_ref), (wvt_hbm, wvt_ref), (cot_hbm, cot_ref), (wq_hbm, wq_ref),
        ))
    ]
    for load in loads:
        load.start()
    max_ref[...] = jnp.full(max_ref.shape, NEG_FILL, jnp.float32)
    sum_ref[...] = jnp.zeros(sum_ref.shape, jnp.float32)
    acc_ref[...] = jnp.zeros(acc_ref.shape, jnp.float32)
    for load in loads[:6]:
        load.wait()

    def meet(slot, place, blocks, patterns):
        rows = buf[slot]
        keys = dot(rows, wk_ref[...]).astype(jnp.bfloat16)
        values = dot(rows, wv_ref[...]).astype(jnp.bfloat16)
        key_ref[place] = dot(wkt_ref[...], rows, NT).astype(jnp.bfloat16)
        bias_ref[...] = rows_in.bias(slot, blocks, patterns)
        for p in range(HEADS // 2):
            pair = slice(2 * head * p, 2 * head * (p + 1))
            scores = dot(keys[:, pair], stack_ref[p], NT)
            d_probs = dot(values[:, pair], cot_stack_ref[p], NT)
            for e in range(2):
                of = slice(block * e, block * (e + 1))
                score_ref[place, 2 * p + e] = scores[:, of] + bias_ref[...]
                d_prob_ref[place, 2 * p + e] = d_probs[:, of]

    def soften(slot, blocks, patterns, index):
        place = jnp.minimum(index, kept)
        meet(slot, place, blocks, patterns)
        values = dot(wvt_ref[...], buf[slot], NT).astype(jnp.bfloat16)
        for h in range(HEADS):
            s = score_ref[place, h]
            old = max_ref[h : h + 1]
            new = jnp.maximum(old, jnp.max(s, axis=0, keepdims=True))
            fade = jnp.exp(old - new)
            expo = jnp.exp(s - new)
            max_ref[h : h + 1] = new
            sum_ref[h : h + 1] = sum_ref[h : h + 1] * fade + jnp.sum(expo, axis=0, keepdims=True)
            at = slice(head * h, head * (h + 1))
            acc_ref[at] = acc_ref[at] * fade + dot(values[at], expo.astype(jnp.bfloat16))

    run_steps(work_ref, rows_in.start, rows_in.wait, soften)
    for load in loads[6:]:
        load.wait()
    inverse = 1.0 / sum_ref[...]
    cot = cot_ref[...].astype(jnp.float32).T
    stats_ref[0:HEADS] = max_ref[...] + jnp.log(sum_ref[...])
    for h in range(HEADS):
        at = slice(head * h, head * (h + 1))
        outputs = acc_ref[at] * inverse[h : h + 1]
        acc_ref[at] = outputs
        stats_ref[HEADS + h : HEADS + h + 1] = jnp.sum(outputs * cot[at], axis=0, keepdims=True)
    sent_ref[...] = jnp.broadcast_to(stats_ref[...], sent_ref.shape)
    out_ref[...] = acc_ref[...].T.astype(out_ref.dtype)
    acc_ref[...] = jnp.zeros(acc_ref.shape, jnp.float32)

    def slope(index, carry):
        place = jnp.minimum(index, kept)

        @pl.when(index >= kept)
        def _():
            blocks, patterns = step_entry(work_ref, index)
            rows_in.start(0, blocks, patterns)
            rows_in.wait(0)
            meet(0, place, blocks, patterns)

        for h in range(HEADS):
            _, d_scores = tile_grads(
                score_ref[place, h], d_prob_ref[place, h], stats_ref[h : h + 1], stats_ref[HEADS + h : HEADS + h + 1]
            )
            at = slice(head * h, head * (h + 1))
            acc_ref[at] += dot(key_ref[place, at], d_scores)
        return carry

    lax.fori_loop(0, work_ref[0], slope, 0)
    grad = (acc_ref[...].T * (head**-0.5)).astype(jnp.bfloat16)
    part_ref[...] = dot(grad, wq_ref[...], NT)


def tile_grads(scores, d_probs, lse, delta):
    prob = jnp.exp(scores - lse)
    return prob.astype(jnp.bfloat16), (prob * (d_probs - delta)).astype(jnp.bfloat16)


def key_grad_kernel(
    sizes, bits, work_ref, key_hbm, value_hbm, wq_hbm, wk_hbm, wv_hbm, part_hbm, mask_ref, stats_all_ref, *refs
):
    readers = sizes[0]
    groups, refs = refs[:8], refs[8:]
    halves, refs = (refs[:readers], refs[readers : 2 * readers]), refs[2 * readers :]
    out_ref, key_ref, value_ref, part_ref, wq_ref, wk_ref, wv_ref, buf, words, cot_buf, stats, bias_ref = refs[:12]
    key_acc, value_acc, sems, c_sems, w_sems = refs[12:]
    layout = Layout(*sizes)
    block, width = out_ref.shape
    head = width // HEADS
    rows_in = Rows(layout, groups, mask_ref, buf, words, sems, block)

    def half_copy(slot, t, k):
        into = cot_buf.at[slot, pl.ds(t * block + block // 2 * k, block // 2)]
        return lambda src: pltpu.make_async_copy(src, into, c_sems.at[slot, t, k])

    def stats_copy(slot, t, query):
        return pltpu.make_async_copy(stats_all_ref.at[query], stats.at[slot, t], c_sems.at[slot, t, 2])

    def start(slot, blocks, patterns):
        rows_in.start(slot, blocks, patterns)
        for t in range(TILES):
            stats_copy(slot, t, blocks[t]).start()
            for k in range(2):
                start_copy(layout.half_place(bits[k], blocks[t]), halves[k], half_copy(slot, t, k))

    def wait(slot):
        rows_in.wait(slot)
        for t in range(TILES):
            stats_copy(slot, t, 0).wait()
            for k in range(2):
                half_copy(slot, t, k)(halves[k][0].at[0]).wait()

    first_step(work_ref, start)
    loads = [
        pltpu.make_async_copy(src, into, w_sems.at[k])
        for k, (src, into) in enumerate((
            (wq_hbm, wq_ref), (key_hbm, key_ref), (value_hbm, value_ref),
            (wk_hbm, wk_ref), (wv_hbm, wv_ref), (part_hbm, part_ref),
        ))
    ]
    for load in loads:
        load.start()
    key_acc[...] = jnp.zeros(key_acc.shape, jnp.float32)
    value_acc[...] = jnp.zeros(value_acc.shape, jnp.float32)
    for load in loads[:3]:
        load.wait()

    def tiles(slot, blocks, patterns, index):
        queries = dot(buf[slot], wq_ref[...]).astype(jnp.bfloat16) * jnp.bfloat16(head**-0.5)
        bias_ref[...] = rows_in.bias(slot, blocks, patterns)
        cots = cot_buf[slot]
        for p in range(HEADS // 2):
            pair = slice(2 * head * p, 2 * head * (p + 1))
            of_tile = [slice(block * t, block * (t + 1)) for t in range(TILES)]
            query_stack = jnp.concatenate([pair_stack(queries[of, pair]) for of in of_tile], 0)
            cot_stack = jnp.concatenate([pair_stack(cots[of, pair]) for of in of_tile], 0)
            scores = dot(key_ref[:, pair], query_stack, NT)
            d_probs = dot(value_ref[:, pair], cot_stack, NT)
            probs, d_scores = [], []
            for t in range(TILES):
                for e in range(2):
                    h = 2 * p + e
                    of = slice(block * (2 * t + e), block * (2 * t + e + 1))
                    prob, d_score = tile_grads(
                        scores[:, of] + bias_ref[of_tile[t]], d_probs[:, of], stats[slot, t, h : h + 1],
                        stats[slot, t, HEADS + h : HEADS + h + 1],
                    )
                    probs.append(prob)
                    d_scores.append(d_score)
            value_acc[:, pair] += dot(jnp.concatenate(probs, 1), cot_stack)
            key_acc[:, pair] += dot(jnp.concatenate(d_scores, 1), query_stack)

    run_steps(work_ref, start, wait, tiles)
    for load in loads[3:]:
        load.wait()
    grad = part_ref[...] + dot(key_acc[...].astype(jnp.bfloat16), wk_ref[...], NT)
    grad = grad + dot(value_acc[...].astype(jnp.bfloat16), wv_ref[...], NT)
    out_ref[...] = grad.astype(out_ref.dtype)


VMEM = pl.BlockSpec(memory_space=pltpu.VMEM)
SMEM = pl.BlockSpec(memory_space=pltpu.SMEM)
HBM = pl.BlockSpec(memory_space=pltpu.HBM)


def swap(block, mask):
    axes = ("reader", "blk")
    count = lax.axis_size("reader") * lax.axis_size("blk")
    return lax.ppermute(block, axes, [(i, i ^ mask) for i in range(count)])


def after(value, *others):
    return lax.optimization_barrier((value, *others))[0]


def over_readers(chunk, order, blks):
    for bit in order[:-1]:
        chunk = jnp.concatenate([chunk, swap(chunk, blks << bit)], 0)
    return [chunk, swap(chunk, blks << order[-1])]


def other_core(groups):
    return groups + [swap(group, 1) for group in groups]


def local(features, cotangent, w_query, w_key, w_value, tile_coords, tile_count, mask_table):
    block, width = features.shape
    readers, blks, cap = lax.axis_size("reader"), lax.axis_size("blk"), tile_coords.shape[2]
    assert block == mask_table.shape[1] and 3 * cap < 128
    sizes = (readers, blks, cap)
    devices, lines = readers * blks, blks // 2
    f32, bf16, i32 = jnp.float32, jnp.bfloat16, jnp.int32
    shape = jax.ShapeDtypeStruct
    masks = mask_table.transpose(0, 2, 1)
    words = masks.shape[1]
    head = width // HEADS
    half = block // 2
    params = pltpu.CompilerParams(vmem_limit_bytes=VMEM_LIMIT)
    masks_off = [2 * k for k in range(1, lines)]

    packed = pl.pallas_call(
        pack_kernel,
        out_shape=shape((1, block + LIST_ROWS, width), bf16),
        in_specs=[HBM, HBM, HBM],
        out_specs=VMEM,
        scratch_shapes=[
            pltpu.SMEM((1, 3, 1, cap), i32), pltpu.SMEM((1, 1), i32), pltpu.SemaphoreType.DMA((3,)),
        ],
        compiler_params=params,
        name="pack",
    )(features, tile_coords.transpose(0, 3, 1, 2), tile_count)

    lined = [packed] + [swap(packed, m) for m in masks_off]
    chunks = [
        jnp.concatenate([entry[:, :half] for entry in lined], 0),
        jnp.concatenate([entry[:, half:] for entry in lined], 0),
    ]
    here = [over_readers(chunk, order, blks) for chunk, order in zip(chunks, orders(readers))]
    rows_all = [group for groups in here for group in other_core(groups)]

    bits = (0, (readers - 1).bit_length() - 1)
    pairs = []
    for k in range(2):
        part = cotangent[None, half * k : half * (k + 1)]
        pairs += [part, swap(part, blks << bits[k])]
    both = jnp.concatenate(pairs, 0)
    cot_line = after(both, *chunks)[None]
    mask = blks // 2
    while mask > 1:
        cot_line = jnp.concatenate([cot_line, swap(cot_line, mask)], 0)
        mask //= 2
    cots_here, cots_all = [], []
    for k in range(2):
        part = cot_line[:, 2 * k : 2 * k + 2].reshape(2 * lines, half, width)
        masks_left = [m for m in range(1, readers) if not m >> bits[k] & 1]
        cots_here.append([part] + [swap(after(part, here), blks * m) for m in masks_left])

    def list_scratch(count):
        return [
            pltpu.VMEM((count, LIST_ROWS, 128), bf16), pltpu.VMEM((8 * count, 128), i32),
            pltpu.SMEM((8 * count, 128), i32), pltpu.SemaphoreType.DMA((count,)),
        ]

    def cost(tiles):
        return pl.CostEstimate(flops=tiles * 200_000_000, bytes_accessed=4_000_000, transcendentals=tiles * 131072)

    stacks = shape((HEADS // 2, 2 * block, 2 * head), bf16)
    own = shape((block, width), bf16)
    square = shape((width, width), bf16)
    query_work, query_stack, cot_stack, keys, values, w_key_t, w_value_t = pl.pallas_call(
        functools.partial(prepare_kernel, sizes),
        out_shape=(shape((2 * blks * cap + 5,), i32), stacks, stacks, own, own, square, square),
        in_specs=[VMEM] * 5 + [HBM] * 2,
        out_specs=(SMEM,) + (VMEM,) * 6,
        scratch_shapes=list_scratch(blks),
        compiler_params=params,
        cost_estimate=cost(2),
        name="prepare",
    )(features, cotangent, w_query, w_key, w_value, rows_all[4], rows_all[6])

    key_work = pl.pallas_call(
        functools.partial(key_list_kernel, sizes),
        out_shape=shape((2 * readers * cap + 5,), i32),
        in_specs=[HBM] * 2,
        out_specs=SMEM,
        scratch_shapes=list_scratch(readers),
        compiler_params=params,
        cost_estimate=cost(1),
        name="key_list",
    )(rows_all[4], rows_all[5])

    weight = pltpu.VMEM((width, width), bf16)
    stack_space = pltpu.VMEM(stacks.shape, bf16)
    rows_low, rows_wide = pltpu.VMEM((block, width), bf16), pltpu.VMEM((block, width), f32)
    buffer = pltpu.VMEM((2, TILES * block, width), bf16)
    word_buffer = pltpu.VMEM((2, TILES, words, block), i32)
    bias = pltpu.VMEM((TILES * block, block), f32)
    turned = pltpu.VMEM((width, block), f32)
    per_head = pltpu.VMEM((HEADS, block), f32)
    met = pltpu.VMEM((KEPT + 1, HEADS, TILES * block, block), f32)
    row_sems = pltpu.SemaphoreType.DMA((2, TILES, 3))

    attn_out, stats, query_part = pl.pallas_call(
        functools.partial(query_kernel, sizes),
        out_shape=(own, shape((devices, 2 * HEADS, block), f32), shape((block, width), f32)),
        in_specs=[SMEM] + [HBM] * 17,
        out_specs=(VMEM, VMEM, VMEM),
        scratch_shapes=[
            stack_space, stack_space, rows_low, weight, weight, weight, weight, weight, pltpu.VMEM((2 * HEADS, block), f32),
            buffer, word_buffer, bias, per_head, per_head, turned, met, met,
            pltpu.VMEM((KEPT + 1, width, TILES * block), bf16), row_sems, pltpu.SemaphoreType.DMA((8,)),
        ],
        compiler_params=params,
        cost_estimate=cost(10),
        name="query_side",
    )(query_work, query_stack, cot_stack, cotangent, w_query, w_key, w_key_t, w_value, w_value_t, masks, *rows_all)

    for first, *rest in cots_here:
        cots_all += [first, *rest, swap(after(first, rows_all), 1)] + [swap(after(part, stats), 1) for part in rest]
    stats_all = lax.all_to_all(stats, ("reader", "blk"), 0, 0, tiled=True)

    grad_features = pl.pallas_call(
        functools.partial(key_grad_kernel, sizes, bits),
        out_shape=own,
        in_specs=[SMEM] + [HBM] * (16 + 2 * readers),
        out_specs=VMEM,
        scratch_shapes=[
            rows_low, rows_low, rows_wide, weight, weight, weight,
            buffer, word_buffer, buffer, pltpu.VMEM((2, TILES, 2 * HEADS, block), f32), bias, rows_wide, rows_wide,
            row_sems, pltpu.SemaphoreType.DMA((2, TILES, 3)), pltpu.SemaphoreType.DMA((6,)),
        ],
        compiler_params=params,
        cost_estimate=cost(5),
        name="key_grad",
    )(key_work, keys, values, w_query, w_key, w_value, query_part, masks, stats_all, *rows_all, *cots_all)
    return attn_out, grad_features


def solution(mesh):
    return jax.shard_map(
        local,
        mesh=mesh,
        in_specs=(
            P(("reader", "blk"), None),
            P(("reader", "blk"), None),
            P(),
            P(),
            P(),
            P("reader", "blk", None, None),
            P("reader", "blk"),
            P(),
        ),
        out_specs=(P(("reader", "blk"), None), P(("reader", "blk"), None)),
        check_vma=False,
    )
```

```python
import functools

import jax
import jax.numpy as jnp
from jax import lax
from jax.experimental import pallas as pl
from jax.experimental.pallas import tpu as pltpu
from jax.sharding import PartitionSpec as P

HEADS = 8
NEG_FILL = -1e30
NT = (((1,), (1,)), ((), ()))
NN = (((1,), (0,)), ((), ()))
TILES = 2
VMEM_SOME = 40 * 1024 * 1024
VMEM_MOST = 58 * 1024 * 1024


def dot(a, b, dims=NN):
    return lax.dot_general(a, b, dims, preferred_element_type=jnp.float32)


def pair_stack(rows):
    lane = lax.broadcasted_iota(jnp.int32, rows.shape, 1)
    half = rows.shape[1] // 2
    zero = jnp.zeros_like(rows)
    return jnp.concatenate([jnp.where(lane < half, rows, zero), jnp.where(lane >= half, rows, zero)], 0)


def tile_bias(words, pattern, diag):
    count, size = words.shape
    keys = lax.broadcasted_iota(jnp.int32, (size, size), 0)
    queries = lax.broadcasted_iota(jnp.int32, (size, size), 1)
    spread = jnp.concatenate(
        [jnp.broadcast_to(words[g : g + 1], (size // count, size)) for g in range(count)], 0
    )
    bits = jnp.right_shift(spread, keys & 31) & 1
    same = keys - queries == jnp.where(diag, 0, 2 * size)
    return jnp.where((bits == 1) | same, jnp.where(pattern < 0, NEG_FILL, 0.0), NEG_FILL)


class Layout:
    def __init__(self, readers, blks, cap):
        self.readers, self.blks, self.cap = readers, blks, cap
        self.reader, self.blk = lax.axis_index("reader"), lax.axis_index("blk")
        self.me = self.reader * blks + self.blk

    def apart(self, device):
        far = jnp.bitwise_xor(device, self.me)
        reader, blk = far // self.blks, lax.rem(far, self.blks)
        return reader, blk // 2, blk & 1

    def row_place(self, order, device):
        reader, line, core = self.apart(device)
        for at, bit in enumerate(order[:-1]):
            line = line + (jnp.right_shift(reader, bit) & 1) * ((self.blks // 2) << at)
        return (jnp.right_shift(reader, order[-1]) & 1) + 2 * core, line

    def orders(self):
        return orders(self.readers)

    def half_place(self, bit, device):
        reader, line, core = self.apart(device)
        first = jnp.right_shift(reader, bit) & 1
        top = (self.blks // 2 - 1).bit_length() - 1
        line = sum((jnp.right_shift(line, top - at) & 1) << at for at in range(top + 1))
        low = reader & ((1 << bit) - 1)
        rest = low + (jnp.right_shift(reader, bit + 1) << bit)
        return rest + self.readers // 2 * core, 2 * line + first


def orders(readers):
    rising = tuple(range((readers - 1).bit_length()))
    return rising, rising[::-1]


def start_copy(place, refs, make):
    group, where = place
    for g, ref in enumerate(refs):

        @pl.when(group == g)
        def _():
            make(ref.at[where]).start()


def send_list_kernel(coords_hbm, count_hbm, out_ref, coords_ref, count_ref, sems):
    cap = coords_ref.shape[3]
    copies = [
        pltpu.make_async_copy(coords_hbm, coords_ref, sems.at[0]),
        pltpu.make_async_copy(count_hbm, count_ref, sems.at[1]),
    ]
    for copy in copies:
        copy.start()
    for copy in copies:
        copy.wait()
    lane = lax.broadcasted_iota(jnp.int32, out_ref.shape[1:], 1)
    row = jnp.zeros(lane.shape, jnp.int32)
    for column in range(3):
        for slot in range(cap):
            row = jnp.where(lane == column * cap + slot, coords_ref[0, column, 0, slot], row)
    row = jnp.where(lane == 3 * cap, count_ref[0, 0], row)
    out_ref[...] = jnp.broadcast_to(row[None], out_ref.shape)


def scan_list(lists_ref, cap, row, column, wanted, found, out_ref, block_of):
    def one_slot(slot, found):
        out_ref[2 * found + 1] = block_of(lists_ref[row, (1 - column) * cap + slot])
        out_ref[2 * found + 2] = lists_ref[row, 2 * cap + slot]
        return found + jnp.where(lists_ref[row, column * cap + slot] == wanted, 1, 0)

    return lax.fori_loop(0, lists_ref[row, 3 * cap], one_slot, found)


def close_work(found, out_ref):
    out_ref[2 * found + 1] = out_ref[2 * found - 1]
    out_ref[2 * found + 2] = -1
    out_ref[0] = (found + 1) // 2


def work_kernel(sizes, lists_hbm, query_work_ref, key_work_ref, lists_ref, sem):
    readers, blks, cap = sizes
    layout = Layout(*sizes)
    copy = pltpu.make_async_copy(lists_hbm, lists_ref, sem)
    copy.start()
    copy.wait()

    def query_side(blk, found):
        row = layout.reader * blks + blk
        put = lambda other: other * blks + blk
        return scan_list(lists_ref, cap, row, 0, layout.blk, found, query_work_ref, put)

    close_work(lax.fori_loop(0, blks, query_side, 0), query_work_ref)

    def key_side(reader, found):
        row = reader * blks + layout.blk
        put = lambda other: reader * blks + other
        return scan_list(lists_ref, cap, row, 1, layout.reader, found, key_work_ref, put)

    close_work(lax.fori_loop(0, readers, key_side, 0), key_work_ref)


def prepare_kernel(
    own_ref, cot_ref, wq_ref, wk_ref, wv_ref, query_stack_ref, cot_stack_ref, key_ref, value_ref, wkt_ref, wvt_ref
):
    head = own_ref.shape[1] // HEADS
    queries = dot(own_ref[...], wq_ref[...]).astype(jnp.bfloat16) * jnp.bfloat16(head**-0.5)
    for p in range(HEADS // 2):
        pair = slice(2 * head * p, 2 * head * (p + 1))
        query_stack_ref[p] = pair_stack(queries[:, pair])
        cot_stack_ref[p] = pair_stack(cot_ref[:, pair])
    key_ref[...] = dot(own_ref[...], wk_ref[...]).astype(jnp.bfloat16)
    value_ref[...] = dot(own_ref[...], wv_ref[...]).astype(jnp.bfloat16)
    wkt_ref[...] = wk_ref[...].T
    wvt_ref[...] = wv_ref[...].T


def step_entry(work_ref, index):
    at = 1 + 2 * TILES * index
    return [work_ref[at + 2 * t] for t in range(TILES)], [work_ref[at + 2 * t + 1] for t in range(TILES)]


def run_steps(work_ref, start, wait, body):
    total = work_ref[0]

    def step(index, carry):
        @pl.when(index + 1 < total)
        def _():
            start(lax.rem(index + 1, 2), *step_entry(work_ref, index + 1))

        slot = lax.rem(index, 2)
        wait(slot)
        body(slot, *step_entry(work_ref, index), index)
        return carry

    lax.fori_loop(0, total, step, 0)


def first_step(work_ref, start):
    start(0, *step_entry(work_ref, 0))


class Rows:
    def __init__(self, layout, groups, mask_ref, buf, words, sems, block):
        self.layout, self.halves, self.mask_ref = layout, (groups[:4], groups[4:]), mask_ref
        self.buf, self.words, self.sems, self.block = buf, words, sems, block

    def rows(self, slot, t, k):
        half = self.block // 2
        into = self.buf.at[slot, pl.ds(t * self.block + k * half, half)]
        return lambda src: pltpu.make_async_copy(src.at[pl.ds(0, half)], into, self.sems.at[slot, t, k])

    def mask(self, slot, t, pattern):
        return pltpu.make_async_copy(self.mask_ref.at[pattern], self.words.at[slot, t], self.sems.at[slot, t, 2])

    def start(self, slot, blocks, patterns):
        for t in range(TILES):
            for k, order in enumerate(self.layout.orders()):
                start_copy(self.layout.row_place(order, blocks[t]), self.halves[k], self.rows(slot, t, k))
            self.mask(slot, t, jnp.maximum(patterns[t], 0)).start()

    def wait(self, slot):
        for t in range(TILES):
            for k in range(2):
                self.rows(slot, t, k)(self.halves[k][0].at[0]).wait()
            self.mask(slot, t, 0).wait()

    def bias(self, slot, blocks, patterns):
        parts = [
            tile_bias(self.words[slot, t], patterns[t], blocks[t] == self.layout.me) for t in range(TILES)
        ]
        return jnp.concatenate(parts, 0)


def load(pairs, sems):
    copies = [pltpu.make_async_copy(src, into, sems.at[k]) for k, (src, into) in enumerate(pairs)]
    for copy in copies:
        copy.start()
    return copies


def forward_kernel(sizes, work_ref, stack_ref, cot_ref, wk_ref, wvt_ref, mask_ref, *refs):
    groups, refs = refs[:8], refs[8:]
    out_ref, sent_ref, stats_ref, buf, words, bias_ref, max_ref, sum_ref, acc_ref, score_ref, sems = refs
    layout = Layout(*sizes)
    block, width = cot_ref.shape
    head = width // HEADS
    rows_in = Rows(layout, groups, mask_ref, buf, words, sems, block)
    first_step(work_ref, rows_in.start)
    max_ref[...] = jnp.full(max_ref.shape, NEG_FILL, jnp.float32)
    sum_ref[...] = jnp.zeros(sum_ref.shape, jnp.float32)
    acc_ref[...] = jnp.zeros(acc_ref.shape, jnp.float32)

    def tiles(slot, blocks, patterns, index):
        rows = buf[slot]
        keys = dot(rows, wk_ref[...]).astype(jnp.bfloat16)
        values = dot(wvt_ref[...], rows, NT).astype(jnp.bfloat16)
        bias_ref[...] = rows_in.bias(slot, blocks, patterns)
        for p in range(HEADS // 2):
            scores = dot(keys[:, 2 * head * p : 2 * head * (p + 1)], stack_ref[p], NT)
            for e in range(2):
                score_ref[2 * p + e] = scores[:, block * e : block * (e + 1)] + bias_ref[...]
        for h in range(HEADS):
            s = score_ref[h]
            old = max_ref[h : h + 1]
            new = jnp.maximum(old, jnp.max(s, axis=0, keepdims=True))
            fade = jnp.exp(old - new)
            expo = jnp.exp(s - new)
            max_ref[h : h + 1] = new
            sum_ref[h : h + 1] = sum_ref[h : h + 1] * fade + jnp.sum(expo, axis=0, keepdims=True)
            at = slice(head * h, head * (h + 1))
            acc_ref[at] = acc_ref[at] * fade + dot(values[at], expo.astype(jnp.bfloat16))

    run_steps(work_ref, rows_in.start, rows_in.wait, tiles)
    inverse = 1.0 / sum_ref[...]
    cot = cot_ref[...].astype(jnp.float32).T
    stats_ref[0:HEADS] = max_ref[...] + jnp.log(sum_ref[...])
    for h in range(HEADS):
        at = slice(head * h, head * (h + 1))
        outputs = acc_ref[at] * inverse[h : h + 1]
        acc_ref[at] = outputs
        stats_ref[HEADS + h : HEADS + h + 1] = jnp.sum(outputs * cot[at], axis=0, keepdims=True)
    sent_ref[...] = jnp.broadcast_to(stats_ref[...], sent_ref.shape)
    out_ref[...] = acc_ref[...].T.astype(out_ref.dtype)


def tile_grads(scores, d_probs, lse, delta):
    prob = jnp.exp(scores - lse)
    return prob.astype(jnp.bfloat16), (prob * (d_probs - delta)).astype(jnp.bfloat16)


def query_grad_kernel(
    sizes, work_ref, stack_hbm, cot_stack_hbm, stats_hbm, wq_hbm, wk_hbm, wkt_hbm, wv_hbm, mask_ref, *refs
):
    groups, refs = refs[:8], refs[8:]
    part_ref, stack_ref, cot_stack_ref, stats_ref, wq_ref, wk_ref, wkt_ref, wv_ref = refs[:8]
    buf, words, bias_ref, acc_ref, score_ref, d_prob_ref, sems, w_sems = refs[8:]
    layout = Layout(*sizes)
    block, width = part_ref.shape
    head = width // HEADS
    rows_in = Rows(layout, groups, mask_ref, buf, words, sems, block)
    first_step(work_ref, rows_in.start)
    loads = load((
        (wk_hbm, wk_ref), (stack_hbm, stack_ref), (wv_hbm, wv_ref), (cot_stack_hbm, cot_stack_ref),
        (wkt_hbm, wkt_ref), (stats_hbm.at[0], stats_ref), (wq_hbm, wq_ref),
    ), w_sems)
    acc_ref[...] = jnp.zeros(acc_ref.shape, jnp.float32)
    for copy in loads[:6]:
        copy.wait()

    def tiles(slot, blocks, patterns, index):
        rows = buf[slot]
        keys = dot(rows, wk_ref[...]).astype(jnp.bfloat16)
        values = dot(rows, wv_ref[...]).astype(jnp.bfloat16)
        keys_t = dot(wkt_ref[...], rows, NT).astype(jnp.bfloat16)
        bias_ref[...] = rows_in.bias(slot, blocks, patterns)
        for p in range(HEADS // 2):
            pair = slice(2 * head * p, 2 * head * (p + 1))
            scores = dot(keys[:, pair], stack_ref[p], NT)
            d_probs = dot(values[:, pair], cot_stack_ref[p], NT)
            for e in range(2):
                of = slice(block * e, block * (e + 1))
                score_ref[2 * p + e] = scores[:, of] + bias_ref[...]
                d_prob_ref[2 * p + e] = d_probs[:, of]
        for h in range(HEADS):
            _, d_scores = tile_grads(
                score_ref[h], d_prob_ref[h], stats_ref[h : h + 1], stats_ref[HEADS + h : HEADS + h + 1]
            )
            at = slice(head * h, head * (h + 1))
            acc_ref[at] += dot(keys_t[at], d_scores)

    run_steps(work_ref, rows_in.start, rows_in.wait, tiles)
    loads[6].wait()
    grad = (acc_ref[...].T * (head**-0.5)).astype(jnp.bfloat16)
    part_ref[...] = dot(grad, wq_ref[...], NT)


def key_grad_kernel(
    sizes, bits, work_ref, key_hbm, value_hbm, wq_hbm, wk_hbm, wv_hbm, part_hbm, mask_ref, stats_all_ref, *refs
):
    readers = sizes[0]
    groups, refs = refs[:8], refs[8:]
    halves, refs = (refs[:readers], refs[readers : 2 * readers]), refs[2 * readers :]
    out_ref, key_ref, value_ref, part_ref, wq_ref, wk_ref, wv_ref, buf, words, cot_buf, stats, bias_ref = refs[:12]
    query_stack_ref, cot_stack_ref, score_ref, d_prob_ref, key_acc, value_acc, sems, c_sems, w_sems = refs[12:]
    layout = Layout(*sizes)
    block, width = out_ref.shape
    head = width // HEADS
    rows_in = Rows(layout, groups, mask_ref, buf, words, sems, block)

    def half_copy(slot, t, k):
        into = cot_buf.at[slot, pl.ds(t * block + block // 2 * k, block // 2)]
        return lambda src: pltpu.make_async_copy(src, into, c_sems.at[slot, t, k])

    def stats_copy(slot, t, query):
        return pltpu.make_async_copy(stats_all_ref.at[query], stats.at[slot, t], c_sems.at[slot, t, 2])

    def start(slot, blocks, patterns):
        rows_in.start(slot, blocks, patterns)
        for t in range(TILES):
            stats_copy(slot, t, blocks[t]).start()
            for k in range(2):
                start_copy(layout.half_place(bits[k], blocks[t]), halves[k], half_copy(slot, t, k))

    def wait(slot):
        rows_in.wait(slot)
        for t in range(TILES):
            stats_copy(slot, t, 0).wait()
            for k in range(2):
                half_copy(slot, t, k)(halves[k][0].at[0]).wait()

    first_step(work_ref, start)
    loads = load((
        (wq_hbm, wq_ref), (key_hbm, key_ref), (value_hbm, value_ref),
        (wk_hbm, wk_ref), (wv_hbm, wv_ref), (part_hbm, part_ref),
    ), w_sems)
    key_acc[...] = jnp.zeros(key_acc.shape, jnp.float32)
    value_acc[...] = jnp.zeros(value_acc.shape, jnp.float32)
    for copy in loads[:3]:
        copy.wait()

    def tiles(slot, blocks, patterns, index):
        queries = dot(buf[slot], wq_ref[...]).astype(jnp.bfloat16) * jnp.bfloat16(head**-0.5)
        bias_ref[...] = rows_in.bias(slot, blocks, patterns)
        cots = cot_buf[slot]
        pairs = [slice(2 * head * p, 2 * head * (p + 1)) for p in range(HEADS // 2)]
        of_tile = [slice(block * t, block * (t + 1)) for t in range(TILES)]
        for p, pair in enumerate(pairs):
            query_stack_ref[p] = jnp.concatenate([pair_stack(queries[of, pair]) for of in of_tile], 0)
            cot_stack_ref[p] = jnp.concatenate([pair_stack(cots[of, pair]) for of in of_tile], 0)
            score_ref[p] = dot(key_ref[:, pair], query_stack_ref[p], NT)
            d_prob_ref[p] = dot(value_ref[:, pair], cot_stack_ref[p], NT)
        for p, pair in enumerate(pairs):
            probs, d_scores = [], []
            for t in range(TILES):
                for e in range(2):
                    h = 2 * p + e
                    of = slice(block * (2 * t + e), block * (2 * t + e + 1))
                    prob, d_score = tile_grads(
                        score_ref[p, :, of] + bias_ref[of_tile[t]], d_prob_ref[p, :, of], stats[slot, t, h : h + 1],
                        stats[slot, t, HEADS + h : HEADS + h + 1],
                    )
                    probs.append(prob)
                    d_scores.append(d_score)
            value_acc[:, pair] += dot(jnp.concatenate(probs, 1), cot_stack_ref[p])
            key_acc[:, pair] += dot(jnp.concatenate(d_scores, 1), query_stack_ref[p])

    run_steps(work_ref, start, wait, tiles)
    for copy in loads[3:]:
        copy.wait()
    grad = part_ref[...] + dot(key_acc[...].astype(jnp.bfloat16), wk_ref[...], NT)
    grad = grad + dot(value_acc[...].astype(jnp.bfloat16), wv_ref[...], NT)
    out_ref[...] = grad.astype(out_ref.dtype)


VMEM = pl.BlockSpec(memory_space=pltpu.VMEM)
SMEM = pl.BlockSpec(memory_space=pltpu.SMEM)
HBM = pl.BlockSpec(memory_space=pltpu.HBM)


def swap(block, mask):
    axes = ("reader", "blk")
    count = lax.axis_size("reader") * lax.axis_size("blk")
    return lax.ppermute(block, axes, [(i, i ^ mask) for i in range(count)])


def after(value, *others):
    return lax.optimization_barrier((value, *others))[0]


def over_readers(chunk, order, blks):
    for bit in order[:-1]:
        chunk = jnp.concatenate([chunk, swap(chunk, blks << bit)], 0)
    return [chunk, swap(chunk, blks << order[-1])]


def local(features, cotangent, w_query, w_key, w_value, tile_coords, tile_count, mask_table):
    block, width = features.shape
    readers, blks, cap = lax.axis_size("reader"), lax.axis_size("blk"), tile_coords.shape[2]
    assert block == mask_table.shape[1] and 3 * cap < 128
    sizes = (readers, blks, cap)
    devices, lines = readers * blks, blks // 2
    f32, bf16, i32 = jnp.float32, jnp.bfloat16, jnp.int32
    shape = jax.ShapeDtypeStruct
    masks = mask_table.transpose(0, 2, 1)
    words = masks.shape[1]
    head = width // HEADS
    half = block // 2
    some = pltpu.CompilerParams(vmem_limit_bytes=VMEM_SOME)
    most = pltpu.CompilerParams(vmem_limit_bytes=VMEM_MOST)
    axes = ("reader", "blk")

    def cost(tiles):
        return pl.CostEstimate(flops=tiles * 200_000_000, bytes_accessed=4_000_000, transcendentals=tiles * 131072)

    rows = features[None]
    lined = [rows] + [swap(rows, 2 * k) for k in range(1, lines)]

    bits = (0, (readers - 1).bit_length() - 1)
    cot_parts = [cotangent[None, half * k : half * (k + 1)] for k in range(2)]
    cot_other = [swap(part, blks << bit) for part, bit in zip(cot_parts, bits)]

    sent = pl.pallas_call(
        send_list_kernel,
        out_shape=shape((devices, 8, 128), i32),
        in_specs=[HBM, HBM],
        out_specs=VMEM,
        scratch_shapes=[
            pltpu.SMEM((1, 3, 1, cap), i32), pltpu.SMEM((1, 1), i32), pltpu.SemaphoreType.DMA((2,)),
        ],
        compiler_params=some,
        name="send_list",
    )(tile_coords.transpose(0, 3, 1, 2), tile_count)
    lists = lax.all_to_all(after(sent, *cot_other), axes, 0, 0, tiled=True)[:, 0]
    query_work, key_work = pl.pallas_call(
        functools.partial(work_kernel, sizes),
        out_shape=(shape((2 * blks * cap + 5,), i32), shape((2 * readers * cap + 5,), i32)),
        in_specs=[HBM],
        out_specs=(SMEM, SMEM),
        scratch_shapes=[pltpu.SMEM((devices, 128), i32), pltpu.SemaphoreType.DMA],
        compiler_params=some,
        cost_estimate=cost(2),
        name="work",
    )(lists)

    stacks = shape((HEADS // 2, 2 * block, 2 * head), bf16)
    own = shape((block, width), bf16)
    square = shape((width, width), bf16)
    prepared = pl.pallas_call(
        prepare_kernel,
        out_shape=(stacks, stacks, own, own, square, square),
        in_specs=[VMEM] * 5,
        out_specs=(VMEM,) * 6,
        compiler_params=some,
        cost_estimate=cost(2),
        name="prepare",
    )(features, cotangent, w_query, w_key, w_value)
    query_stack, cot_stack, keys, values, w_key_t, w_value_t = prepared

    lined = after(lined, prepared)
    chunks = [jnp.concatenate([entry[:, half * k : half * (k + 1)] for entry in lined], 0) for k in range(2)]
    here = [over_readers(chunk, order, blks) for chunk, order in zip(chunks, orders(readers))]
    rows_all = []
    for first, last in here:
        rows_all += [first, last, swap(after(first, query_work), 1), swap(last, 1)]

    both = jnp.concatenate([cot_parts[0], cot_other[0], cot_parts[1], cot_other[1]], 0)
    cot_line = after(both, *chunks)[None]
    mask = blks // 2
    while mask > 1:
        cot_line = jnp.concatenate([cot_line, swap(cot_line, mask)], 0)
        mask //= 2

    weight = pltpu.VMEM((width, width), bf16)
    stack_space = pltpu.VMEM(stacks.shape, bf16)
    rows_low, rows_wide = pltpu.VMEM((block, width), bf16), pltpu.VMEM((block, width), f32)
    buffer = pltpu.VMEM((2, TILES * block, width), bf16)
    word_buffer = pltpu.VMEM((2, TILES, words, block), i32)
    bias = pltpu.VMEM((TILES * block, block), f32)
    turned = pltpu.VMEM((width, block), f32)
    per_head = pltpu.VMEM((HEADS, block), f32)
    own_stats = pltpu.VMEM((2 * HEADS, block), f32)
    met = pltpu.VMEM((HEADS, TILES * block, block), f32)
    pair_met = pltpu.VMEM((HEADS // 2, block, 2 * TILES * block), f32)
    pair_rows = pltpu.VMEM((HEADS // 2, 2 * TILES * block, 2 * head), bf16)
    row_sems = pltpu.SemaphoreType.DMA((2, TILES, 3))

    attn_out, stats = pl.pallas_call(
        functools.partial(forward_kernel, sizes),
        out_shape=(own, shape((devices, 2 * HEADS, block), f32)),
        in_specs=[SMEM] + [VMEM] * 4 + [HBM] * 9,
        out_specs=(VMEM, VMEM),
        scratch_shapes=[own_stats, buffer, word_buffer, bias, per_head, per_head, turned, met, row_sems],
        compiler_params=some,
        cost_estimate=cost(5),
        name="forward",
    )(query_work, query_stack, cotangent, w_key, w_value_t, masks, *rows_all)

    cots_here = []
    for k in range(2):
        part = after(cot_line[:, 2 * k : 2 * k + 2].reshape(2 * lines, half, width), stats)
        masks_left = [m for m in range(1, readers) if not m >> bits[k] & 1]
        cots_here.append((part, [swap(part, blks * m) for m in masks_left], swap(part, 1)))
    stats_all = lax.all_to_all(stats, axes, 0, 0, tiled=True)

    query_part = pl.pallas_call(
        functools.partial(query_grad_kernel, sizes),
        out_shape=shape((block, width), f32),
        in_specs=[SMEM] + [HBM] * 16,
        out_specs=VMEM,
        scratch_shapes=[
            stack_space, stack_space, own_stats, weight, weight, weight, weight, buffer, word_buffer, bias, turned,
            met, met, row_sems, pltpu.SemaphoreType.DMA((7,)),
        ],
        compiler_params=most,
        cost_estimate=cost(5),
        name="query_grad",
    )(query_work, query_stack, cot_stack, stats, w_query, w_key, w_key_t, w_value, masks, *rows_all)

    cots_all = []
    for first, rest, other in cots_here:
        cots_all += [first, *rest, other] + [swap(after(part, stats_all, query_part), 1) for part in rest]

    grad_features = pl.pallas_call(
        functools.partial(key_grad_kernel, sizes, bits),
        out_shape=own,
        in_specs=[SMEM] + [HBM] * (16 + 2 * readers),
        out_specs=VMEM,
        scratch_shapes=[
            rows_low, rows_low, rows_wide, weight, weight, weight,
            buffer, word_buffer, buffer, pltpu.VMEM((2, TILES, 2 * HEADS, block), f32), bias,
            pair_rows, pair_rows, pair_met, pair_met, rows_wide, rows_wide,
            row_sems, pltpu.SemaphoreType.DMA((2, TILES, 3)), pltpu.SemaphoreType.DMA((6,)),
        ],
        compiler_params=most,
        cost_estimate=cost(5),
        name="key_grad",
    )(key_work, keys, values, w_query, w_key, w_value, query_part, masks, stats_all, *rows_all, *cots_all)
    return attn_out, grad_features


def solution(mesh):
    return jax.shard_map(
        local,
        mesh=mesh,
        in_specs=(
            P(("reader", "blk"), None),
            P(("reader", "blk"), None),
            P(),
            P(),
            P(),
            P("reader", "blk", None, None),
            P("reader", "blk"),
            P(),
        ),
        out_specs=(P(("reader", "blk"), None), P(("reader", "blk"), None)),
        check_vma=False,
    )
```

```python
import functools

import jax
import jax.numpy as jnp
from jax import lax
from jax.experimental import pallas as pl
from jax.experimental.pallas import tpu as pltpu
from jax.sharding import PartitionSpec as P

HEADS = 8
NEG_FILL = -1e30
NT = (((1,), (1,)), ((), ()))
NN = (((1,), (0,)), ((), ()))
TILES = 2
VMEM_SOME = 40 * 1024 * 1024
VMEM_MOST = 58 * 1024 * 1024


def dot(a, b, dims=NN):
    return lax.dot_general(a, b, dims, preferred_element_type=jnp.float32)


def pair_stack(rows):
    lane = lax.broadcasted_iota(jnp.int32, rows.shape, 1)
    half = rows.shape[1] // 2
    zero = jnp.zeros_like(rows)
    return jnp.concatenate([jnp.where(lane < half, rows, zero), jnp.where(lane >= half, rows, zero)], 0)


def tile_bias(words, pattern, diag):
    count, size = words.shape
    keys = lax.broadcasted_iota(jnp.int32, (size, size), 0)
    queries = lax.broadcasted_iota(jnp.int32, (size, size), 1)
    spread = jnp.concatenate(
        [jnp.broadcast_to(words[g : g + 1], (size // count, size)) for g in range(count)], 0
    )
    bits = jnp.right_shift(spread, keys & 31) & 1
    same = keys - queries == jnp.where(diag, 0, 2 * size)
    return jnp.where((bits == 1) | same, jnp.where(pattern < 0, NEG_FILL, 0.0), NEG_FILL)


class Layout:
    def __init__(self, readers, blks, cap):
        self.readers, self.blks, self.cap = readers, blks, cap
        self.reader, self.blk = lax.axis_index("reader"), lax.axis_index("blk")
        self.me = self.reader * blks + self.blk

    def apart(self, device):
        far = jnp.bitwise_xor(device, self.me)
        reader, blk = far // self.blks, lax.rem(far, self.blks)
        return reader, blk // 2, blk & 1

    def row_place(self, order, device):
        reader, line, core = self.apart(device)
        for at, bit in enumerate(order[:-1]):
            line = line + (jnp.right_shift(reader, bit) & 1) * ((self.blks // 2) << at)
        return (jnp.right_shift(reader, order[-1]) & 1) + 2 * core, line

    def orders(self):
        return orders(self.readers)

    def half_place(self, bit, device):
        reader, line, core = self.apart(device)
        first = jnp.right_shift(reader, bit) & 1
        top = (self.blks // 2 - 1).bit_length() - 1
        line = sum((jnp.right_shift(line, top - at) & 1) << at for at in range(top + 1))
        low = reader & ((1 << bit) - 1)
        rest = low + (jnp.right_shift(reader, bit + 1) << bit)
        return rest + self.readers // 2 * core, 2 * line + first


def orders(readers):
    rising = tuple(range((readers - 1).bit_length()))
    return rising, rising[::-1]


def start_copy(place, refs, make):
    group, where = place
    for g, ref in enumerate(refs):

        @pl.when(group == g)
        def _():
            make(ref.at[where]).start()


def send_list_kernel(coords_hbm, count_hbm, out_ref, coords_ref, count_ref, sems):
    cap = coords_ref.shape[3]
    copies = [
        pltpu.make_async_copy(coords_hbm, coords_ref, sems.at[0]),
        pltpu.make_async_copy(count_hbm, count_ref, sems.at[1]),
    ]
    for copy in copies:
        copy.start()
    for copy in copies:
        copy.wait()
    lane = lax.broadcasted_iota(jnp.int32, out_ref.shape[1:], 1)
    row = jnp.zeros(lane.shape, jnp.int32)
    for column in range(3):
        for slot in range(cap):
            row = jnp.where(lane == column * cap + slot, coords_ref[0, column, 0, slot], row)
    row = jnp.where(lane == 3 * cap, count_ref[0, 0], row)
    out_ref[0] = row


def scan_list(lists_ref, cap, row, column, wanted, found, out_ref, block_of):
    def one_slot(slot, found):
        out_ref[2 * found + 1] = block_of(lists_ref[row, (1 - column) * cap + slot])
        out_ref[2 * found + 2] = lists_ref[row, 2 * cap + slot]
        return found + jnp.where(lists_ref[row, column * cap + slot] == wanted, 1, 0)

    return lax.fori_loop(0, lists_ref[row, 3 * cap], one_slot, found)


def close_work(found, out_ref):
    out_ref[2 * found + 1] = out_ref[2 * found - 1]
    out_ref[2 * found + 2] = -1
    out_ref[0] = (found + 1) // 2


def query_work_kernel(sizes, lists_hbm, work_ref, lists_ref, sem):
    readers, blks, cap = sizes
    layout = Layout(*sizes)
    copy = pltpu.make_async_copy(lists_hbm, lists_ref, sem)
    copy.start()
    copy.wait()

    def one(k, found):
        blk = jnp.bitwise_xor(k, layout.blk)
        row = k // 2 + (k & 1) * (blks // 2)
        put = lambda other: other * blks + blk
        return scan_list(lists_ref, cap, row, 0, layout.blk, found, work_ref, put)

    close_work(lax.fori_loop(0, blks, one, 0), work_ref)


def key_work_kernel(sizes, lists_hbm, work_ref, lists_ref, sem):
    readers, blks, cap = sizes
    layout = Layout(*sizes)
    copy = pltpu.make_async_copy(lists_hbm, lists_ref, sem)
    copy.start()
    copy.wait()

    def one(k, found):
        reader = jnp.bitwise_xor(k, layout.reader)
        put = lambda other: reader * blks + other
        return scan_list(lists_ref, cap, k, 1, layout.reader, found, work_ref, put)

    close_work(lax.fori_loop(0, readers, one, 0), work_ref)


def prepare_kernel(
    own_ref, cot_ref, wq_ref, wk_ref, wv_ref,
    query_stack_ref, cot_stack_ref, key_ref, value_ref, wqt_ref, wkt_ref, wvt_ref,
):
    head = own_ref.shape[1] // HEADS
    queries = dot(own_ref[...], wq_ref[...]).astype(jnp.bfloat16) * jnp.bfloat16(head**-0.5)
    for p in range(HEADS // 2):
        pair = slice(2 * head * p, 2 * head * (p + 1))
        query_stack_ref[p] = pair_stack(queries[:, pair]).T
        cot_stack_ref[p] = pair_stack(cot_ref[:, pair]).T
    key_ref[...] = dot(own_ref[...], wk_ref[...]).astype(jnp.bfloat16)
    value_ref[...] = dot(own_ref[...], wv_ref[...]).astype(jnp.bfloat16)
    wqt_ref[...] = wq_ref[...].T
    wkt_ref[...] = wk_ref[...].T
    wvt_ref[...] = wv_ref[...].T


def step_entry(work_ref, index):
    at = 1 + 2 * TILES * index
    return [work_ref[at + 2 * t] for t in range(TILES)], [work_ref[at + 2 * t + 1] for t in range(TILES)]


def run_steps(work_ref, start, wait, body):
    total = work_ref[0]

    def step(index, carry):
        @pl.when(index + 1 < total)
        def _():
            start(lax.rem(index + 1, 2), *step_entry(work_ref, index + 1))

        slot = lax.rem(index, 2)
        wait(slot)
        body(slot, *step_entry(work_ref, index), index)
        return carry

    lax.fori_loop(0, total, step, 0)


def first_step(work_ref, start):
    start(0, *step_entry(work_ref, 0))


class Rows:
    def __init__(self, layout, groups, mask_ref, buf, words, sems, block):
        self.layout, self.halves, self.mask_ref = layout, (groups[:4], groups[4:]), mask_ref
        self.buf, self.words, self.sems, self.block = buf, words, sems, block

    def rows(self, slot, t, k):
        half = self.block // 2
        into = self.buf.at[slot, pl.ds(t * self.block + k * half, half)]
        return lambda src: pltpu.make_async_copy(src.at[pl.ds(0, half)], into, self.sems.at[slot, t, k])

    def mask(self, slot, t, pattern):
        return pltpu.make_async_copy(self.mask_ref.at[pattern], self.words.at[slot, t], self.sems.at[slot, t, 2])

    def start(self, slot, blocks, patterns):
        for t in range(TILES):
            for k, order in enumerate(self.layout.orders()):
                start_copy(self.layout.row_place(order, blocks[t]), self.halves[k], self.rows(slot, t, k))
            self.mask(slot, t, jnp.maximum(patterns[t], 0)).start()

    def wait(self, slot):
        for t in range(TILES):
            for k in range(2):
                self.rows(slot, t, k)(self.halves[k][0].at[0]).wait()
            self.mask(slot, t, 0).wait()

    def bias(self, slot, blocks, patterns):
        parts = [
            tile_bias(self.words[slot, t], patterns[t], blocks[t] == self.layout.me) for t in range(TILES)
        ]
        return jnp.concatenate(parts, 0)


def load(pairs, sems):
    copies = [pltpu.make_async_copy(src, into, sems.at[k]) for k, (src, into) in enumerate(pairs)]
    for copy in copies:
        copy.start()
    return copies


def forward_kernel(sizes, work_ref, stack_ref, cot_ref, wk_ref, wvt_ref, mask_ref, *refs):
    groups, refs = refs[:8], refs[8:]
    out_ref, sent_ref, stats_ref, buf, words, bias_ref, max_ref, sum_ref, acc_ref, score_ref, sems = refs
    layout = Layout(*sizes)
    block, width = cot_ref.shape
    head = width // HEADS
    rows_in = Rows(layout, groups, mask_ref, buf, words, sems, block)
    first_step(work_ref, rows_in.start)
    max_ref[...] = jnp.full(max_ref.shape, NEG_FILL, jnp.float32)
    sum_ref[...] = jnp.zeros(sum_ref.shape, jnp.float32)
    acc_ref[...] = jnp.zeros(acc_ref.shape, jnp.float32)

    def tiles(slot, blocks, patterns, index):
        rows = buf[slot]
        keys = dot(rows, wk_ref[...]).astype(jnp.bfloat16)
        values = dot(wvt_ref[...], rows, NT).astype(jnp.bfloat16)
        bias_ref[...] = rows_in.bias(slot, blocks, patterns)
        for p in range(HEADS // 2):
            scores = dot(keys[:, 2 * head * p : 2 * head * (p + 1)], stack_ref[p])
            for e in range(2):
                score_ref[2 * p + e] = scores[:, block * e : block * (e + 1)] + bias_ref[...]
        for h in range(HEADS):
            s = score_ref[h]
            old = max_ref[h : h + 1]
            new = jnp.maximum(old, jnp.max(s, axis=0, keepdims=True))
            fade = jnp.exp(old - new)
            expo = jnp.exp(s - new)
            max_ref[h : h + 1] = new
            sum_ref[h : h + 1] = sum_ref[h : h + 1] * fade + jnp.sum(expo, axis=0, keepdims=True)
            at = slice(head * h, head * (h + 1))
            acc_ref[at] = acc_ref[at] * fade + dot(values[at], expo.astype(jnp.bfloat16))

    run_steps(work_ref, rows_in.start, rows_in.wait, tiles)
    inverse = 1.0 / sum_ref[...]
    cot = cot_ref[...].astype(jnp.float32).T
    stats_ref[0:HEADS] = max_ref[...] + jnp.log(sum_ref[...])
    for h in range(HEADS):
        at = slice(head * h, head * (h + 1))
        outputs = acc_ref[at] * inverse[h : h + 1]
        acc_ref[at] = outputs
        stats_ref[HEADS + h : HEADS + h + 1] = jnp.sum(outputs * cot[at], axis=0, keepdims=True)
    sent_ref[...] = jnp.broadcast_to(stats_ref[...], sent_ref.shape)
    out_ref[...] = acc_ref[...].T.astype(out_ref.dtype)


def tile_grads(scores, d_probs, lse, delta):
    prob = jnp.exp(scores - lse)
    return prob.astype(jnp.bfloat16), (prob * (d_probs - delta)).astype(jnp.bfloat16)


def query_grad_kernel(
    sizes, work_ref, stack_hbm, cot_stack_hbm, stats_hbm, wqt_hbm, wk_hbm, wkt_hbm, wv_hbm, mask_ref, *refs
):
    groups, refs = refs[:8], refs[8:]
    part_ref, stack_ref, cot_stack_ref, stats_ref, wqt_ref, wk_ref, wkt_ref, wv_ref = refs[:8]
    buf, words, bias_ref, acc_ref, score_ref, d_prob_ref, sems, w_sems = refs[8:]
    layout = Layout(*sizes)
    block, width = part_ref.shape
    head = width // HEADS
    rows_in = Rows(layout, groups, mask_ref, buf, words, sems, block)
    first_step(work_ref, rows_in.start)
    loads = load((
        (wk_hbm, wk_ref), (stack_hbm, stack_ref), (wv_hbm, wv_ref), (cot_stack_hbm, cot_stack_ref),
        (wkt_hbm, wkt_ref), (stats_hbm.at[0], stats_ref), (wqt_hbm, wqt_ref),
    ), w_sems)
    acc_ref[...] = jnp.zeros(acc_ref.shape, jnp.float32)
    for copy in loads[:6]:
        copy.wait()

    def tiles(slot, blocks, patterns, index):
        rows = buf[slot]
        keys = dot(rows, wk_ref[...]).astype(jnp.bfloat16)
        values = dot(rows, wv_ref[...]).astype(jnp.bfloat16)
        keys_t = dot(wkt_ref[...], rows, NT).astype(jnp.bfloat16)
        bias_ref[...] = rows_in.bias(slot, blocks, patterns)
        for p in range(HEADS // 2):
            pair = slice(2 * head * p, 2 * head * (p + 1))
            scores = dot(keys[:, pair], stack_ref[p])
            d_probs = dot(values[:, pair], cot_stack_ref[p])
            for e in range(2):
                of = slice(block * e, block * (e + 1))
                score_ref[2 * p + e] = scores[:, of] + bias_ref[...]
                d_prob_ref[2 * p + e] = d_probs[:, of]
        for h in range(HEADS):
            _, d_scores = tile_grads(
                score_ref[h], d_prob_ref[h], stats_ref[h : h + 1], stats_ref[HEADS + h : HEADS + h + 1]
            )
            at = slice(head * h, head * (h + 1))
            acc_ref[at] += dot(keys_t[at], d_scores)

    run_steps(work_ref, rows_in.start, rows_in.wait, tiles)
    loads[6].wait()
    grad = (acc_ref[...].T * (head**-0.5)).astype(jnp.bfloat16)
    part_ref[...] = dot(grad, wqt_ref[...])


def key_grad_kernel(
    sizes, bits, work_ref, key_hbm, value_hbm, wq_hbm, wkt_hbm, wvt_hbm, part_hbm, mask_ref, stats_all_ref, *refs
):
    readers = sizes[0]
    groups, refs = refs[:8], refs[8:]
    halves, refs = (refs[:readers], refs[readers : 2 * readers]), refs[2 * readers :]
    out_ref, key_ref, value_ref, part_ref, wq_ref, wkt_ref, wvt_ref, buf, words, cot_buf, stats, bias_ref = refs[:12]
    query_stack_ref, cot_stack_ref, score_ref, d_prob_ref, key_acc, value_acc, sems, c_sems, w_sems = refs[12:]
    layout = Layout(*sizes)
    block, width = out_ref.shape
    head = width // HEADS
    rows_in = Rows(layout, groups, mask_ref, buf, words, sems, block)

    def half_copy(slot, t, k):
        into = cot_buf.at[slot, pl.ds(t * block + block // 2 * k, block // 2)]
        return lambda src: pltpu.make_async_copy(src, into, c_sems.at[slot, t, k])

    def stats_copy(slot, t, query):
        return pltpu.make_async_copy(stats_all_ref.at[query], stats.at[slot, t], c_sems.at[slot, t, 2])

    def start(slot, blocks, patterns):
        rows_in.start(slot, blocks, patterns)
        for t in range(TILES):
            stats_copy(slot, t, blocks[t]).start()
            for k in range(2):
                start_copy(layout.half_place(bits[k], blocks[t]), halves[k], half_copy(slot, t, k))

    def wait(slot):
        rows_in.wait(slot)
        for t in range(TILES):
            stats_copy(slot, t, 0).wait()
            for k in range(2):
                half_copy(slot, t, k)(halves[k][0].at[0]).wait()

    first_step(work_ref, start)
    loads = load((
        (wq_hbm, wq_ref), (key_hbm, key_ref), (value_hbm, value_ref),
        (wkt_hbm, wkt_ref), (wvt_hbm, wvt_ref), (part_hbm, part_ref),
    ), w_sems)
    key_acc[...] = jnp.zeros(key_acc.shape, jnp.float32)
    value_acc[...] = jnp.zeros(value_acc.shape, jnp.float32)
    for copy in loads[:3]:
        copy.wait()

    def tiles(slot, blocks, patterns, index):
        queries = dot(buf[slot], wq_ref[...]).astype(jnp.bfloat16) * jnp.bfloat16(head**-0.5)
        bias_ref[...] = rows_in.bias(slot, blocks, patterns)
        cots = cot_buf[slot]
        pairs = [slice(2 * head * p, 2 * head * (p + 1)) for p in range(HEADS // 2)]
        of_tile = [slice(block * t, block * (t + 1)) for t in range(TILES)]
        for p, pair in enumerate(pairs):
            query_stack_ref[p] = jnp.concatenate([pair_stack(queries[of, pair]) for of in of_tile], 0)
            cot_stack_ref[p] = jnp.concatenate([pair_stack(cots[of, pair]) for of in of_tile], 0)
            score_ref[p] = dot(key_ref[:, pair], query_stack_ref[p], NT)
            d_prob_ref[p] = dot(value_ref[:, pair], cot_stack_ref[p], NT)
        for p, pair in enumerate(pairs):
            probs, d_scores = [], []
            for t in range(TILES):
                for e in range(2):
                    h = 2 * p + e
                    of = slice(block * (2 * t + e), block * (2 * t + e + 1))
                    prob, d_score = tile_grads(
                        score_ref[p, :, of] + bias_ref[of_tile[t]], d_prob_ref[p, :, of], stats[slot, t, h : h + 1],
                        stats[slot, t, HEADS + h : HEADS + h + 1],
                    )
                    probs.append(prob)
                    d_scores.append(d_score)
            value_acc[:, pair] += dot(jnp.concatenate(probs, 1), cot_stack_ref[p])
            key_acc[:, pair] += dot(jnp.concatenate(d_scores, 1), query_stack_ref[p])

    run_steps(work_ref, start, wait, tiles)
    for copy in loads[3:]:
        copy.wait()
    grad = part_ref[...] + dot(key_acc[...].astype(jnp.bfloat16), wkt_ref[...])
    grad = grad + dot(value_acc[...].astype(jnp.bfloat16), wvt_ref[...])
    out_ref[...] = grad.astype(out_ref.dtype)


VMEM = pl.BlockSpec(memory_space=pltpu.VMEM)
SMEM = pl.BlockSpec(memory_space=pltpu.SMEM)
HBM = pl.BlockSpec(memory_space=pltpu.HBM)


def swap(block, mask):
    axes = ("reader", "blk")
    count = lax.axis_size("reader") * lax.axis_size("blk")
    return lax.ppermute(block, axes, [(i, i ^ mask) for i in range(count)])


def after(value, *others):
    return lax.optimization_barrier((value, *others))[0]


def over_readers(chunk, order, blks, *others):
    for bit in order[:-1]:
        chunk = jnp.concatenate([chunk, swap(chunk, blks << bit)], 0)
    chunk = after(chunk, *others)
    return [chunk, swap(chunk, blks << order[-1])]


def local(features, cotangent, w_query, w_key, w_value, tile_coords, tile_count, mask_table):
    block, width = features.shape
    readers, blks, cap = lax.axis_size("reader"), lax.axis_size("blk"), tile_coords.shape[2]
    assert block == mask_table.shape[1] and 3 * cap < 128
    sizes = (readers, blks, cap)
    devices, lines = readers * blks, blks // 2
    f32, bf16, i32 = jnp.float32, jnp.bfloat16, jnp.int32
    shape = jax.ShapeDtypeStruct
    masks = mask_table.transpose(0, 2, 1)
    words = masks.shape[1]
    head = width // HEADS
    half = block // 2
    some = pltpu.CompilerParams(vmem_limit_bytes=VMEM_SOME)
    most = pltpu.CompilerParams(vmem_limit_bytes=VMEM_MOST)
    axes = ("reader", "blk")

    def cost(tiles):
        return pl.CostEstimate(flops=tiles * 200_000_000, bytes_accessed=4_000_000, transcendentals=tiles * 131072)

    rows = features[None]
    lined = [rows] + [swap(rows, 2 * k) for k in range(1, lines)]

    bits = (0, (readers - 1).bit_length() - 1)
    cot_parts = [cotangent[None, half * k : half * (k + 1)] for k in range(2)]
    cot_other = [swap(part, blks << bit) for part, bit in zip(cot_parts, bits)]

    sent = pl.pallas_call(
        send_list_kernel,
        out_shape=shape((1, 8, 128), i32),
        in_specs=[HBM, HBM],
        out_specs=VMEM,
        scratch_shapes=[
            pltpu.SMEM((1, 3, 1, cap), i32), pltpu.SMEM((1, 1), i32), pltpu.SemaphoreType.DMA((2,)),
        ],
        compiler_params=some,
        name="send_list",
    )(tile_coords.transpose(0, 3, 1, 2), tile_count)
    sent = after(sent, *cot_other)
    line_lists = jnp.concatenate([sent] + [swap(sent, 2 * k) for k in range(1, lines)], 0)
    row_lists = jnp.concatenate([line_lists, swap(line_lists, 1)], 0)
    sent = after(sent, line_lists)
    column_lists = jnp.concatenate([sent] + [swap(sent, blks * k) for k in range(1, readers)], 0)

    def work(kernel, lists, count, name):
        return pl.pallas_call(
            functools.partial(kernel, sizes),
            out_shape=shape((2 * count * cap + 5,), i32),
            in_specs=[HBM],
            out_specs=SMEM,
            scratch_shapes=[pltpu.SMEM((count, 128), i32), pltpu.SemaphoreType.DMA],
            compiler_params=some,
            cost_estimate=cost(1),
            name=name,
        )(lists[:, 0])

    query_work = work(query_work_kernel, row_lists, blks, "query_work")
    key_work = work(key_work_kernel, column_lists, readers, "key_work")

    stacks = shape((HEADS // 2, 2 * head, 2 * block), bf16)
    own = shape((block, width), bf16)
    square = shape((width, width), bf16)
    prepared = pl.pallas_call(
        prepare_kernel,
        out_shape=(stacks, stacks, own, own, square, square, square),
        in_specs=[VMEM] * 5,
        out_specs=(VMEM,) * 7,
        compiler_params=some,
        cost_estimate=cost(2),
        name="prepare",
    )(features, cotangent, w_query, w_key, w_value)
    query_stack, cot_stack, keys, values, w_query_t, w_key_t, w_value_t = prepared

    lined = after(lined, prepared)
    chunks = [jnp.concatenate([entry[:, half * k : half * (k + 1)] for entry in lined], 0) for k in range(2)]
    here = [over_readers(chunk, order, blks, row_lists) for chunk, order in zip(chunks, orders(readers))]
    rows_all = []
    for first, last in here:
        rows_all += [first, last, swap(after(first, query_work, key_work), 1), swap(last, 1)]

    both = jnp.concatenate([cot_parts[0], cot_other[0], cot_parts[1], cot_other[1]], 0)
    cot_line = after(both, *chunks)[None]
    mask = blks // 2
    while mask > 1:
        cot_line = jnp.concatenate([cot_line, swap(cot_line, mask)], 0)
        mask //= 2

    weight = pltpu.VMEM((width, width), bf16)
    stack_space = pltpu.VMEM(stacks.shape, bf16)
    rows_low, rows_wide = pltpu.VMEM((block, width), bf16), pltpu.VMEM((block, width), f32)
    buffer = pltpu.VMEM((2, TILES * block, width), bf16)
    word_buffer = pltpu.VMEM((2, TILES, words, block), i32)
    bias = pltpu.VMEM((TILES * block, block), f32)
    turned = pltpu.VMEM((width, block), f32)
    per_head = pltpu.VMEM((HEADS, block), f32)
    own_stats = pltpu.VMEM((2 * HEADS, block), f32)
    met = pltpu.VMEM((HEADS, TILES * block, block), f32)
    pair_met = pltpu.VMEM((HEADS // 2, block, 2 * TILES * block), f32)
    pair_rows = pltpu.VMEM((HEADS // 2, 2 * TILES * block, 2 * head), bf16)
    row_sems = pltpu.SemaphoreType.DMA((2, TILES, 3))

    attn_out, stats = pl.pallas_call(
        functools.partial(forward_kernel, sizes),
        out_shape=(own, shape((devices, 2 * HEADS, block), f32)),
        in_specs=[SMEM] + [VMEM] * 4 + [HBM] * 9,
        out_specs=(VMEM, VMEM),
        scratch_shapes=[own_stats, buffer, word_buffer, bias, per_head, per_head, turned, met, row_sems],
        compiler_params=some,
        cost_estimate=cost(5),
        name="forward",
    )(query_work, query_stack, cotangent, w_key, w_value_t, masks, *rows_all)

    cots_here = []
    for k in range(2):
        part = after(cot_line[:, 2 * k : 2 * k + 2].reshape(2 * lines, half, width), stats)
        masks_left = [m for m in range(1, readers) if not m >> bits[k] & 1]
        cots_here.append((part, [swap(part, blks * m) for m in masks_left], swap(part, 1)))
    stats_all = lax.all_to_all(stats, axes, 0, 0, tiled=True)

    query_part = pl.pallas_call(
        functools.partial(query_grad_kernel, sizes),
        out_shape=shape((block, width), f32),
        in_specs=[SMEM] + [HBM] * 16,
        out_specs=VMEM,
        scratch_shapes=[
            stack_space, stack_space, own_stats, weight, weight, weight, weight, buffer, word_buffer, bias, turned,
            met, met, row_sems, pltpu.SemaphoreType.DMA((7,)),
        ],
        compiler_params=most,
        cost_estimate=cost(5),
        name="query_grad",
    )(query_work, query_stack, cot_stack, stats, w_query_t, w_key, w_key_t, w_value, masks, *rows_all)

    cots_all = []
    for first, rest, other in cots_here:
        cots_all += [first, *rest, other] + [swap(after(part, stats_all, query_part), 1) for part in rest]

    grad_features = pl.pallas_call(
        functools.partial(key_grad_kernel, sizes, bits),
        out_shape=own,
        in_specs=[SMEM] + [HBM] * (16 + 2 * readers),
        out_specs=VMEM,
        scratch_shapes=[
            rows_low, rows_low, rows_wide, weight, weight, weight,
            buffer, word_buffer, buffer, pltpu.VMEM((2, TILES, 2 * HEADS, block), f32), bias,
            pair_rows, pair_rows, pair_met, pair_met, rows_wide, rows_wide,
            row_sems, pltpu.SemaphoreType.DMA((2, TILES, 3)), pltpu.SemaphoreType.DMA((6,)),
        ],
        compiler_params=most,
        cost_estimate=cost(5),
        name="key_grad",
    )(key_work, keys, values, w_query, w_key_t, w_value_t, query_part, masks, stats_all, *rows_all, *cots_all)
    return attn_out, grad_features


def solution(mesh):
    return jax.shard_map(
        local,
        mesh=mesh,
        in_specs=(
            P(("reader", "blk"), None),
            P(("reader", "blk"), None),
            P(),
            P(),
            P(),
            P("reader", "blk", None, None),
            P("reader", "blk"),
            P(),
        ),
        out_specs=(P(("reader", "blk"), None), P(("reader", "blk"), None)),
        check_vma=False,
    )
```

```python
import functools

import jax
import jax.numpy as jnp
from jax import lax
from jax.experimental import pallas as pl
from jax.experimental.pallas import tpu as pltpu
from jax.sharding import PartitionSpec as P

HEADS = 8
NEG_FILL = -1e30
NT = (((1,), (1,)), ((), ()))
NN = (((1,), (0,)), ((), ()))
TILES = 2
VMEM_SOME = 40 * 1024 * 1024
VMEM_MOST = 58 * 1024 * 1024


def dot(a, b, dims=NN):
    return lax.dot_general(a, b, dims, preferred_element_type=jnp.float32)


def pair_stack(rows):
    lane = lax.broadcasted_iota(jnp.int32, rows.shape, 1)
    half = rows.shape[1] // 2
    zero = jnp.zeros_like(rows)
    return jnp.concatenate([jnp.where(lane < half, rows, zero), jnp.where(lane >= half, rows, zero)], 0)


def tile_bias(words, pattern, diag):
    count, size = words.shape
    keys = lax.broadcasted_iota(jnp.int32, (size, size), 0)
    queries = lax.broadcasted_iota(jnp.int32, (size, size), 1)
    spread = jnp.concatenate(
        [jnp.broadcast_to(words[g : g + 1], (size // count, size)) for g in range(count)], 0
    )
    bits = jnp.right_shift(spread, keys & 31) & 1
    same = keys - queries == jnp.where(diag, 0, 2 * size)
    return jnp.where((bits == 1) | same, jnp.where(pattern < 0, NEG_FILL, 0.0), NEG_FILL)


class Layout:
    def __init__(self, readers, blks, cap):
        self.readers, self.blks, self.cap = readers, blks, cap
        self.reader, self.blk = lax.axis_index("reader"), lax.axis_index("blk")
        self.me = self.reader * blks + self.blk

    def apart(self, device):
        far = jnp.bitwise_xor(device, self.me)
        reader, blk = far // self.blks, lax.rem(far, self.blks)
        return reader, blk // 2, blk & 1

    def row_place(self, order, device):
        reader, line, core = self.apart(device)
        for at, bit in enumerate(order[:-1]):
            line = line + (jnp.right_shift(reader, bit) & 1) * ((self.blks // 2) << at)
        return (jnp.right_shift(reader, order[-1]) & 1) + 2 * core, line

    def orders(self):
        return orders(self.readers)

    def half_place(self, bit, device):
        reader, line, core = self.apart(device)
        first = jnp.right_shift(reader, bit) & 1
        top = (self.blks // 2 - 1).bit_length() - 1
        line = sum((jnp.right_shift(line, top - at) & 1) << at for at in range(top + 1))
        low = reader & ((1 << bit) - 1)
        rest = low + (jnp.right_shift(reader, bit + 1) << bit)
        return rest + self.readers // 2 * core, 2 * line + first


def orders(readers):
    rising = tuple(range((readers - 1).bit_length()))
    return rising, rising[::-1]


def start_copy(place, refs, make):
    group, where = place
    for g, ref in enumerate(refs):

        @pl.when(group == g)
        def _():
            make(ref.at[where]).start()


def send_list_kernel(coords_hbm, count_hbm, out_ref, coords_ref, count_ref, sems):
    cap = coords_ref.shape[3]
    copies = [
        pltpu.make_async_copy(coords_hbm, coords_ref, sems.at[0]),
        pltpu.make_async_copy(count_hbm, count_ref, sems.at[1]),
    ]
    for copy in copies:
        copy.start()
    for copy in copies:
        copy.wait()
    lane = lax.broadcasted_iota(jnp.int32, out_ref.shape[1:], 1)
    row = jnp.zeros(lane.shape, jnp.int32)
    for column in range(3):
        for slot in range(cap):
            row = jnp.where(lane == column * cap + slot, coords_ref[0, column, 0, slot], row)
    row = jnp.where(lane == 3 * cap, count_ref[0, 0], row)
    out_ref[...] = jnp.broadcast_to(row[None], out_ref.shape)


def scan_list(lists_ref, cap, row, column, wanted, found, out_ref, block_of):
    def one_slot(slot, found):
        out_ref[2 * found + 1] = block_of(lists_ref[row, (1 - column) * cap + slot])
        out_ref[2 * found + 2] = lists_ref[row, 2 * cap + slot]
        return found + jnp.where(lists_ref[row, column * cap + slot] == wanted, 1, 0)

    return lax.fori_loop(0, lists_ref[row, 3 * cap], one_slot, found)


def close_work(found, out_ref):
    out_ref[2 * found + 1] = out_ref[2 * found - 1]
    out_ref[2 * found + 2] = -1
    out_ref[0] = (found + 1) // 2


def query_work_kernel(sizes, lists_hbm, work_ref, lists_ref, sem):
    readers, blks, cap = sizes
    layout = Layout(*sizes)
    copy = pltpu.make_async_copy(lists_hbm, lists_ref, sem)
    copy.start()
    copy.wait()

    def one(k, found):
        put = lambda other: other * blks + k
        return scan_list(lists_ref, cap, k, 0, layout.blk, found, work_ref, put)

    close_work(lax.fori_loop(0, blks, one, 0), work_ref)


def key_work_kernel(sizes, lists_hbm, work_ref, lists_ref, sem):
    readers, blks, cap = sizes
    layout = Layout(*sizes)
    copy = pltpu.make_async_copy(lists_hbm, lists_ref, sem)
    copy.start()
    copy.wait()

    def one(k, found):
        put = lambda other: k * blks + other
        return scan_list(lists_ref, cap, k, 1, layout.reader, found, work_ref, put)

    close_work(lax.fori_loop(0, readers, one, 0), work_ref)


def load(pairs, sems):
    copies = [pltpu.make_async_copy(src, into, sems.at[k]) for k, (src, into) in enumerate(pairs)]
    for copy in copies:
        copy.start()
    return copies


def prepare_kernel(
    own_hbm, cot_hbm, wq_hbm, wk_hbm, wv_hbm,
    query_stack_ref, cot_stack_ref, key_ref, value_ref, wqt_ref, wkt_ref, wvt_ref,
    own_ref, cot_ref, wq_ref, wk_ref, wv_ref, sems,
):
    loads = load((
        (own_hbm, own_ref), (wq_hbm, wq_ref), (wk_hbm, wk_ref), (wv_hbm, wv_ref), (cot_hbm, cot_ref),
    ), sems)
    for copy in loads:
        copy.wait()
    head = own_ref.shape[1] // HEADS
    queries = dot(own_ref[...], wq_ref[...]).astype(jnp.bfloat16) * jnp.bfloat16(head**-0.5)
    for p in range(HEADS // 2):
        pair = slice(2 * head * p, 2 * head * (p + 1))
        query_stack_ref[p] = pair_stack(queries[:, pair]).T
        cot_stack_ref[p] = pair_stack(cot_ref[:, pair]).T
    key_ref[...] = dot(own_ref[...], wk_ref[...]).astype(jnp.bfloat16)
    value_ref[...] = dot(own_ref[...], wv_ref[...]).astype(jnp.bfloat16)
    wqt_ref[...] = wq_ref[...].T
    wkt_ref[...] = wk_ref[...].T
    wvt_ref[...] = wv_ref[...].T


def step_entry(work_ref, index):
    at = 1 + 2 * TILES * index
    return [work_ref[at + 2 * t] for t in range(TILES)], [work_ref[at + 2 * t + 1] for t in range(TILES)]


def run_steps(work_ref, start, wait, body):
    total = work_ref[0]

    def step(index, carry):
        @pl.when(index + 1 < total)
        def _():
            start(lax.rem(index + 1, 2), *step_entry(work_ref, index + 1))

        slot = lax.rem(index, 2)
        wait(slot)
        body(slot, *step_entry(work_ref, index), index)
        return carry

    lax.fori_loop(0, total, step, 0)


def first_step(work_ref, start):
    start(0, *step_entry(work_ref, 0))


class Rows:
    def __init__(self, layout, groups, mask_ref, buf, words, sems, block):
        self.layout, self.halves, self.mask_ref = layout, (groups[:4], groups[4:]), mask_ref
        self.buf, self.words, self.sems, self.block = buf, words, sems, block

    def rows(self, slot, t, k):
        half = self.block // 2
        into = self.buf.at[slot, pl.ds(t * self.block + k * half, half)]
        return lambda src: pltpu.make_async_copy(src.at[pl.ds(0, half)], into, self.sems.at[slot, t, k])

    def mask(self, slot, t, pattern):
        return pltpu.make_async_copy(self.mask_ref.at[pattern], self.words.at[slot, t], self.sems.at[slot, t, 2])

    def start(self, slot, blocks, patterns):
        for t in range(TILES):
            for k, order in enumerate(self.layout.orders()):
                start_copy(self.layout.row_place(order, blocks[t]), self.halves[k], self.rows(slot, t, k))
            self.mask(slot, t, jnp.maximum(patterns[t], 0)).start()

    def wait(self, slot):
        for t in range(TILES):
            for k in range(2):
                self.rows(slot, t, k)(self.halves[k][0].at[0]).wait()
            self.mask(slot, t, 0).wait()

    def bias(self, slot, blocks, patterns):
        parts = [
            tile_bias(self.words[slot, t], patterns[t], blocks[t] == self.layout.me) for t in range(TILES)
        ]
        return jnp.concatenate(parts, 0)


def forward_kernel(sizes, work_ref, stack_ref, cot_ref, wk_ref, wvt_ref, mask_ref, *refs):
    groups, refs = refs[:8], refs[8:]
    out_ref, sent_ref, stats_ref, buf, words, bias_ref, max_ref, sum_ref, acc_ref, score_ref, sems = refs
    layout = Layout(*sizes)
    block, width = cot_ref.shape
    head = width // HEADS
    rows_in = Rows(layout, groups, mask_ref, buf, words, sems, block)
    first_step(work_ref, rows_in.start)
    max_ref[...] = jnp.full(max_ref.shape, NEG_FILL, jnp.float32)
    sum_ref[...] = jnp.zeros(sum_ref.shape, jnp.float32)
    acc_ref[...] = jnp.zeros(acc_ref.shape, jnp.float32)

    def tiles(slot, blocks, patterns, index):
        rows = buf[slot]
        keys = dot(rows, wk_ref[...]).astype(jnp.bfloat16)
        values = dot(wvt_ref[...], rows, NT).astype(jnp.bfloat16)
        bias_ref[...] = rows_in.bias(slot, blocks, patterns)
        for p in range(HEADS // 2):
            scores = dot(keys[:, 2 * head * p : 2 * head * (p + 1)], stack_ref[p])
            for e in range(2):
                score_ref[2 * p + e] = scores[:, block * e : block * (e + 1)] + bias_ref[...]
        for h in range(HEADS):
            s = score_ref[h]
            old = max_ref[h : h + 1]
            new = jnp.maximum(old, jnp.max(s, axis=0, keepdims=True))
            fade = jnp.exp(old - new)
            expo = jnp.exp(s - new)
            max_ref[h : h + 1] = new
            sum_ref[h : h + 1] = sum_ref[h : h + 1] * fade + jnp.sum(expo, axis=0, keepdims=True)
            at = slice(head * h, head * (h + 1))
            acc_ref[at] = acc_ref[at] * fade + dot(values[at], expo.astype(jnp.bfloat16))

    run_steps(work_ref, rows_in.start, rows_in.wait, tiles)
    inverse = 1.0 / sum_ref[...]
    cot = cot_ref[...].astype(jnp.float32).T
    stats_ref[0:HEADS] = max_ref[...] + jnp.log(sum_ref[...])
    for h in range(HEADS):
        at = slice(head * h, head * (h + 1))
        outputs = acc_ref[at] * inverse[h : h + 1]
        acc_ref[at] = outputs
        stats_ref[HEADS + h : HEADS + h + 1] = jnp.sum(outputs * cot[at], axis=0, keepdims=True)
    sent_ref[...] = jnp.broadcast_to(stats_ref[...], sent_ref.shape)
    out_ref[...] = acc_ref[...].T.astype(out_ref.dtype)


def tile_grads(scores, d_probs, lse, delta):
    prob = jnp.exp(scores - lse)
    return prob.astype(jnp.bfloat16), (prob * (d_probs - delta)).astype(jnp.bfloat16)


def query_grad_kernel(
    sizes, work_ref, stack_hbm, cot_stack_hbm, stats_hbm, wqt_hbm, wk_hbm, wkt_hbm, wv_hbm, mask_ref, *refs
):
    groups, refs = refs[:8], refs[8:]
    part_ref, stack_ref, cot_stack_ref, stats_ref, wqt_ref, wk_ref, wkt_ref, wv_ref = refs[:8]
    buf, words, bias_ref, acc_ref, score_ref, d_prob_ref, sems, w_sems = refs[8:]
    layout = Layout(*sizes)
    block, width = part_ref.shape
    head = width // HEADS
    rows_in = Rows(layout, groups, mask_ref, buf, words, sems, block)
    first_step(work_ref, rows_in.start)
    loads = load((
        (wk_hbm, wk_ref), (stack_hbm, stack_ref), (wv_hbm, wv_ref), (cot_stack_hbm, cot_stack_ref),
        (wkt_hbm, wkt_ref), (stats_hbm.at[0], stats_ref), (wqt_hbm, wqt_ref),
    ), w_sems)
    acc_ref[...] = jnp.zeros(acc_ref.shape, jnp.float32)
    for copy in loads[:6]:
        copy.wait()

    def tiles(slot, blocks, patterns, index):
        rows = buf[slot]
        keys = dot(rows, wk_ref[...]).astype(jnp.bfloat16)
        values = dot(rows, wv_ref[...]).astype(jnp.bfloat16)
        keys_t = dot(wkt_ref[...], rows, NT).astype(jnp.bfloat16)
        bias_ref[...] = rows_in.bias(slot, blocks, patterns)
        for p in range(HEADS // 2):
            pair = slice(2 * head * p, 2 * head * (p + 1))
            scores = dot(keys[:, pair], stack_ref[p])
            d_probs = dot(values[:, pair], cot_stack_ref[p])
            for e in range(2):
                of = slice(block * e, block * (e + 1))
                score_ref[2 * p + e] = scores[:, of] + bias_ref[...]
                d_prob_ref[2 * p + e] = d_probs[:, of]
        for h in range(HEADS):
            _, d_scores = tile_grads(
                score_ref[h], d_prob_ref[h], stats_ref[h : h + 1], stats_ref[HEADS + h : HEADS + h + 1]
            )
            at = slice(head * h, head * (h + 1))
            acc_ref[at] += dot(keys_t[at], d_scores)

    run_steps(work_ref, rows_in.start, rows_in.wait, tiles)
    loads[6].wait()
    grad = (acc_ref[...].T * (head**-0.5)).astype(jnp.bfloat16)
    part_ref[...] = dot(grad, wqt_ref[...])


def key_grad_kernel(
    sizes, bits, work_ref, key_hbm, value_hbm, wq_hbm, wkt_hbm, wvt_hbm, part_hbm, mask_ref, stats_all_ref, *refs
):
    readers = sizes[0]
    groups, refs = refs[:8], refs[8:]
    halves, refs = (refs[:readers], refs[readers : 2 * readers]), refs[2 * readers :]
    out_ref, key_ref, value_ref, part_ref, wq_ref, wkt_ref, wvt_ref, buf, words, cot_buf, stats, bias_ref = refs[:12]
    query_stack_ref, cot_stack_ref, score_ref, d_prob_ref, key_acc, value_acc, sems, c_sems, w_sems = refs[12:]
    layout = Layout(*sizes)
    block, width = out_ref.shape
    head = width // HEADS
    rows_in = Rows(layout, groups, mask_ref, buf, words, sems, block)

    def half_copy(slot, t, k):
        into = cot_buf.at[slot, pl.ds(t * block + block // 2 * k, block // 2)]
        return lambda src: pltpu.make_async_copy(src, into, c_sems.at[slot, t, k])

    def stats_copy(slot, t, query):
        return pltpu.make_async_copy(stats_all_ref.at[query], stats.at[slot, t], c_sems.at[slot, t, 2])

    def start(slot, blocks, patterns):
        rows_in.start(slot, blocks, patterns)
        for t in range(TILES):
            stats_copy(slot, t, blocks[t]).start()
            for k in range(2):
                start_copy(layout.half_place(bits[k], blocks[t]), halves[k], half_copy(slot, t, k))

    def wait(slot):
        rows_in.wait(slot)
        for t in range(TILES):
            stats_copy(slot, t, 0).wait()
            for k in range(2):
                half_copy(slot, t, k)(halves[k][0].at[0]).wait()

    first_step(work_ref, start)
    loads = load((
        (wq_hbm, wq_ref), (key_hbm, key_ref), (value_hbm, value_ref),
        (wkt_hbm, wkt_ref), (wvt_hbm, wvt_ref), (part_hbm, part_ref),
    ), w_sems)
    key_acc[...] = jnp.zeros(key_acc.shape, jnp.float32)
    value_acc[...] = jnp.zeros(value_acc.shape, jnp.float32)
    for copy in loads[:3]:
        copy.wait()

    def tiles(slot, blocks, patterns, index):
        queries = dot(buf[slot], wq_ref[...]).astype(jnp.bfloat16) * jnp.bfloat16(head**-0.5)
        bias_ref[...] = rows_in.bias(slot, blocks, patterns)
        cots = cot_buf[slot]
        pairs = [slice(2 * head * p, 2 * head * (p + 1)) for p in range(HEADS // 2)]
        of_tile = [slice(block * t, block * (t + 1)) for t in range(TILES)]
        for p, pair in enumerate(pairs):
            query_stack_ref[p] = jnp.concatenate([pair_stack(queries[of, pair]) for of in of_tile], 0)
            cot_stack_ref[p] = jnp.concatenate([pair_stack(cots[of, pair]) for of in of_tile], 0)
            score_ref[p] = dot(key_ref[:, pair], query_stack_ref[p], NT)
            d_prob_ref[p] = dot(value_ref[:, pair], cot_stack_ref[p], NT)
        for p, pair in enumerate(pairs):
            probs, d_scores = [], []
            for t in range(TILES):
                for e in range(2):
                    h = 2 * p + e
                    of = slice(block * (2 * t + e), block * (2 * t + e + 1))
                    prob, d_score = tile_grads(
                        score_ref[p, :, of] + bias_ref[of_tile[t]], d_prob_ref[p, :, of], stats[slot, t, h : h + 1],
                        stats[slot, t, HEADS + h : HEADS + h + 1],
                    )
                    probs.append(prob)
                    d_scores.append(d_score)
            value_acc[:, pair] += dot(jnp.concatenate(probs, 1), cot_stack_ref[p])
            key_acc[:, pair] += dot(jnp.concatenate(d_scores, 1), query_stack_ref[p])

    run_steps(work_ref, start, wait, tiles)
    for copy in loads[3:]:
        copy.wait()
    grad = part_ref[...] + dot(key_acc[...].astype(jnp.bfloat16), wkt_ref[...])
    grad = grad + dot(value_acc[...].astype(jnp.bfloat16), wvt_ref[...])
    out_ref[...] = grad.astype(out_ref.dtype)


VMEM = pl.BlockSpec(memory_space=pltpu.VMEM)
SMEM = pl.BlockSpec(memory_space=pltpu.SMEM)
HBM = pl.BlockSpec(memory_space=pltpu.HBM)


def swap(block, mask):
    axes = ("reader", "blk")
    count = lax.axis_size("reader") * lax.axis_size("blk")
    return lax.ppermute(block, axes, [(i, i ^ mask) for i in range(count)])


def after(value, *others):
    return lax.optimization_barrier((value, *others))[0]


def over_readers(chunk, order, blks):
    for bit in order[:-1]:
        chunk = jnp.concatenate([chunk, swap(chunk, blks << bit)], 0)
    return [chunk, swap(chunk, blks << order[-1])]


def local(features, cotangent, w_query, w_key, w_value, tile_coords, tile_count, mask_table):
    block, width = features.shape
    readers, blks, cap = lax.axis_size("reader"), lax.axis_size("blk"), tile_coords.shape[2]
    assert block == mask_table.shape[1] and 3 * cap < 128
    sizes = (readers, blks, cap)
    devices, lines = readers * blks, blks // 2
    f32, bf16, i32 = jnp.float32, jnp.bfloat16, jnp.int32
    shape = jax.ShapeDtypeStruct
    masks = mask_table.transpose(0, 2, 1)
    words = masks.shape[1]
    head = width // HEADS
    half = block // 2
    some = pltpu.CompilerParams(vmem_limit_bytes=VMEM_SOME)
    most = pltpu.CompilerParams(vmem_limit_bytes=VMEM_MOST)
    axes = ("reader", "blk")

    def cost(tiles):
        return pl.CostEstimate(flops=tiles * 200_000_000, bytes_accessed=4_000_000, transcendentals=tiles * 131072)

    rows = features[None]
    lined = [rows] + [swap(rows, 2 * k) for k in range(1, lines)]

    bits = (0, (readers - 1).bit_length() - 1)
    cot_parts = [cotangent[None, half * k : half * (k + 1)] for k in range(2)]
    cot_other = [swap(part, blks << bit) for part, bit in zip(cot_parts, bits)]

    sent = pl.pallas_call(
        send_list_kernel,
        out_shape=shape((blks, 8, 128), i32),
        in_specs=[HBM, HBM],
        out_specs=VMEM,
        scratch_shapes=[
            pltpu.SMEM((1, 3, 1, cap), i32), pltpu.SMEM((1, 1), i32), pltpu.SemaphoreType.DMA((2,)),
        ],
        compiler_params=some,
        name="send_list",
    )(tile_coords.transpose(0, 3, 1, 2), tile_count)
    row_lists = lax.all_to_all(after(sent, *lined), "blk", 0, 0, tiled=True)

    def work(kernel, lists, count, name):
        return pl.pallas_call(
            functools.partial(kernel, sizes),
            out_shape=shape((2 * count * cap + 5,), i32),
            in_specs=[HBM],
            out_specs=SMEM,
            scratch_shapes=[pltpu.SMEM((count, 128), i32), pltpu.SemaphoreType.DMA],
            compiler_params=some,
            cost_estimate=cost(1),
            name=name,
        )(lists[:, 0])

    query_work = work(query_work_kernel, row_lists, blks, "query_work")

    stacks = shape((HEADS // 2, 2 * head, 2 * block), bf16)
    own = shape((block, width), bf16)
    square = shape((width, width), bf16)
    weight = pltpu.VMEM((width, width), bf16)
    rows_low, rows_wide = pltpu.VMEM((block, width), bf16), pltpu.VMEM((block, width), f32)
    prepared = pl.pallas_call(
        prepare_kernel,
        out_shape=(stacks, stacks, own, own, square, square, square),
        in_specs=[HBM] * 5,
        out_specs=(VMEM,) * 7,
        scratch_shapes=[rows_low, rows_low, weight, weight, weight, pltpu.SemaphoreType.DMA((5,))],
        compiler_params=most,
        cost_estimate=cost(2),
        name="prepare",
    )(features, cotangent, w_query, w_key, w_value)
    query_stack, cot_stack, keys, values, w_query_t, w_key_t, w_value_t = prepared

    lined = after(lined, prepared)
    chunks = [jnp.concatenate([entry[:, half * k : half * (k + 1)] for entry in lined], 0) for k in range(2)]
    here = [over_readers(chunk, order, blks) for chunk, order in zip(chunks, orders(readers))]
    rows_all = []
    for first, last in here:
        rows_all += [first, last, swap(first, 1), swap(last, 1)]

    both = jnp.concatenate([cot_parts[0], cot_other[0], cot_parts[1], cot_other[1]], 0)
    cot_line = after(both, *chunks)[None]
    mask = blks // 2
    while mask > 1:
        cot_line = after(jnp.concatenate([cot_line, swap(cot_line, mask)], 0), query_work)
        mask //= 2

    stack_space = pltpu.VMEM(stacks.shape, bf16)
    buffer = pltpu.VMEM((2, TILES * block, width), bf16)
    word_buffer = pltpu.VMEM((2, TILES, words, block), i32)
    bias = pltpu.VMEM((TILES * block, block), f32)
    turned = pltpu.VMEM((width, block), f32)
    per_head = pltpu.VMEM((HEADS, block), f32)
    own_stats = pltpu.VMEM((2 * HEADS, block), f32)
    met = pltpu.VMEM((HEADS, TILES * block, block), f32)
    pair_met = pltpu.VMEM((HEADS // 2, block, 2 * TILES * block), f32)
    pair_rows = pltpu.VMEM((HEADS // 2, 2 * TILES * block, 2 * head), bf16)
    row_sems = pltpu.SemaphoreType.DMA((2, TILES, 3))

    attn_out, stats = pl.pallas_call(
        functools.partial(forward_kernel, sizes),
        out_shape=(own, shape((devices, 2 * HEADS, block), f32)),
        in_specs=[SMEM] + [VMEM] * 4 + [HBM] * 9,
        out_specs=(VMEM, VMEM),
        scratch_shapes=[own_stats, buffer, word_buffer, bias, per_head, per_head, turned, met, row_sems],
        compiler_params=some,
        cost_estimate=cost(5),
        name="forward",
    )(query_work, query_stack, cotangent, w_key, w_value_t, masks, *rows_all)

    cots_here = []
    for k in range(2):
        part = after(cot_line[:, 2 * k : 2 * k + 2].reshape(2 * lines, half, width), stats)
        masks_left = [m for m in range(1, readers) if not m >> bits[k] & 1]
        cots_here.append((part, [swap(part, blks * m) for m in masks_left], swap(part, 1)))
    stats_all = lax.all_to_all(stats, axes, 0, 0, tiled=True)

    column_lists = lax.all_to_all(after(sent, stats)[:readers], "reader", 0, 0, tiled=True)
    key_work = work(key_work_kernel, column_lists, readers, "key_work")

    query_part = pl.pallas_call(
        functools.partial(query_grad_kernel, sizes),
        out_shape=shape((block, width), f32),
        in_specs=[SMEM] + [HBM] * 16,
        out_specs=VMEM,
        scratch_shapes=[
            stack_space, stack_space, own_stats, weight, weight, weight, weight, buffer, word_buffer, bias, turned,
            met, met, row_sems, pltpu.SemaphoreType.DMA((7,)),
        ],
        compiler_params=most,
        cost_estimate=cost(5),
        name="query_grad",
    )(query_work, query_stack, cot_stack, stats, w_query_t, w_key, w_key_t, w_value, masks, *rows_all)

    cots_all = []
    for first, rest, other in cots_here:
        cots_all += [first, *rest, other] + [swap(after(part, stats_all, query_part, key_work), 1) for part in rest]

    grad_features = pl.pallas_call(
        functools.partial(key_grad_kernel, sizes, bits),
        out_shape=own,
        in_specs=[SMEM] + [HBM] * (16 + 2 * readers),
        out_specs=VMEM,
        scratch_shapes=[
            rows_low, rows_low, rows_wide, weight, weight, weight,
            buffer, word_buffer, buffer, pltpu.VMEM((2, TILES, 2 * HEADS, block), f32), bias,
            pair_rows, pair_rows, pair_met, pair_met, rows_wide, rows_wide,
            row_sems, pltpu.SemaphoreType.DMA((2, TILES, 3)), pltpu.SemaphoreType.DMA((6,)),
        ],
        compiler_params=most,
        cost_estimate=cost(5),
        name="key_grad",
    )(key_work, keys, values, w_query, w_key_t, w_value_t, query_part, masks, stats_all, *rows_all, *cots_all)
    return attn_out, grad_features


def solution(mesh):
    return jax.shard_map(
        local,
        mesh=mesh,
        in_specs=(
            P(("reader", "blk"), None),
            P(("reader", "blk"), None),
            P(),
            P(),
            P(),
            P("reader", "blk", None, None),
            P("reader", "blk"),
            P(),
        ),
        out_specs=(P(("reader", "blk"), None), P(("reader", "blk"), None)),
        check_vma=False,
    )
```

```python
import functools

import jax
import jax.numpy as jnp
from jax import lax
from jax.experimental import pallas as pl
from jax.experimental.pallas import tpu as pltpu
from jax.sharding import PartitionSpec as P

HEADS = 8
NEG_FILL = -1e30
NT = (((1,), (1,)), ((), ()))
NN = (((1,), (0,)), ((), ()))
TILES = 2
LIST_ROWS = 16
VMEM_SOME = 40 * 1024 * 1024
VMEM_MOST = 58 * 1024 * 1024


def dot(a, b, dims=NN):
    return lax.dot_general(a, b, dims, preferred_element_type=jnp.float32)


def pair_stack(rows):
    lane = lax.broadcasted_iota(jnp.int32, rows.shape, 1)
    half = rows.shape[1] // 2
    zero = jnp.zeros_like(rows)
    return jnp.concatenate([jnp.where(lane < half, rows, zero), jnp.where(lane >= half, rows, zero)], 0)


def tile_bias(words, pattern, diag):
    count, size = words.shape
    keys = lax.broadcasted_iota(jnp.int32, (size, size), 0)
    queries = lax.broadcasted_iota(jnp.int32, (size, size), 1)
    spread = jnp.concatenate(
        [jnp.broadcast_to(words[g : g + 1], (size // count, size)) for g in range(count)], 0
    )
    bits = jnp.right_shift(spread, keys & 31) & 1
    same = keys - queries == jnp.where(diag, 0, 2 * size)
    return jnp.where((bits == 1) | same, jnp.where(pattern < 0, NEG_FILL, 0.0), NEG_FILL)


class Layout:
    def __init__(self, readers, blks, cap):
        self.readers, self.blks, self.cap = readers, blks, cap
        self.reader, self.blk = lax.axis_index("reader"), lax.axis_index("blk")
        self.me = self.reader * blks + self.blk

    def apart(self, device):
        far = jnp.bitwise_xor(device, self.me)
        reader, blk = far // self.blks, lax.rem(far, self.blks)
        return reader, blk // 2, blk & 1

    def row_place(self, order, device):
        reader, line, core = self.apart(device)
        for at, bit in enumerate(order[:-1]):
            line = line + (jnp.right_shift(reader, bit) & 1) * ((self.blks // 2) << at)
        return (jnp.right_shift(reader, order[-1]) & 1) + 2 * core, line

    def orders(self):
        return orders(self.readers)

    def half_place(self, bit, device):
        reader, line, core = self.apart(device)
        first = jnp.right_shift(reader, bit) & 1
        top = (self.blks // 2 - 1).bit_length() - 1
        line = sum((jnp.right_shift(line, top - at) & 1) << at for at in range(top + 1))
        low = reader & ((1 << bit) - 1)
        rest = low + (jnp.right_shift(reader, bit + 1) << bit)
        return rest + self.readers // 2 * core, 2 * line + first


def orders(readers):
    rising = tuple(range((readers - 1).bit_length()))
    return rising, rising[::-1]


def start_copy(place, refs, make):
    group, where = place
    for g, ref in enumerate(refs):

        @pl.when(group == g)
        def _():
            make(ref.at[where]).start()


def pack_kernel(own_hbm, coords_hbm, count_hbm, out_hbm, row_ref, coords_ref, count_ref, sems):
    block = own_hbm.shape[0]
    cap = coords_ref.shape[3]
    rows = pltpu.make_async_copy(own_hbm, out_hbm.at[0, pl.ds(0, block)], sems.at[2])
    rows.start()
    copies = [
        pltpu.make_async_copy(coords_hbm, coords_ref, sems.at[0]),
        pltpu.make_async_copy(count_hbm, count_ref, sems.at[1]),
    ]
    for copy in copies:
        copy.start()
    for copy in copies:
        copy.wait()
    lane = lax.broadcasted_iota(jnp.int32, row_ref.shape, 1)
    row = jnp.zeros(lane.shape, jnp.int32)
    for column in range(3):
        for slot in range(cap):
            row = jnp.where(lane == column * cap + slot, coords_ref[0, column, 0, slot], row)
    row = jnp.where(lane == 3 * cap, count_ref[0, 0], row)
    row_ref[...] = row.astype(jnp.float32).astype(jnp.bfloat16)
    more = pltpu.make_async_copy(row_ref, out_hbm.at[0, pl.ds(block, LIST_ROWS)], sems.at[0])
    more.start()
    more.wait()
    rows.wait()


def scan_list(lists_ref, cap, row, column, wanted, found, out_ref, block_of):
    def one_slot(slot, found):
        out_ref[2 * found + 1] = block_of(lists_ref[row, (1 - column) * cap + slot])
        out_ref[2 * found + 2] = lists_ref[row, 2 * cap + slot]
        return found + jnp.where(lists_ref[row, column * cap + slot] == wanted, 1, 0)

    return lax.fori_loop(0, lists_ref[row, 3 * cap], one_slot, found)


def close_work(found, out_ref):
    out_ref[2 * found + 1] = out_ref[2 * found - 1]
    out_ref[2 * found + 2] = -1
    out_ref[0] = (found + 1) // 2


def query_work_kernel(sizes, lists_hbm, work_ref, lists_ref, sem):
    readers, blks, cap = sizes
    layout = Layout(*sizes)
    copy = pltpu.make_async_copy(lists_hbm, lists_ref, sem)
    copy.start()
    copy.wait()

    def one(k, found):
        blk = jnp.bitwise_xor(k, layout.blk)
        row = k // 2 + (k & 1) * (blks // 2)
        put = lambda other: other * blks + blk
        return scan_list(lists_ref, cap, row, 0, layout.blk, found, work_ref, put)

    close_work(lax.fori_loop(0, blks, one, 0), work_ref)


def key_work_kernel(sizes, lists_hbm, work_ref, lists_ref, sem):
    readers, blks, cap = sizes
    layout = Layout(*sizes)
    copy = pltpu.make_async_copy(lists_hbm, lists_ref, sem)
    copy.start()
    copy.wait()

    def one(k, found):
        reader = jnp.bitwise_xor(k, layout.reader)
        put = lambda other: reader * blks + other
        return scan_list(lists_ref, cap, k, 1, layout.reader, found, work_ref, put)

    close_work(lax.fori_loop(0, readers, one, 0), work_ref)


def load(pairs, sems):
    copies = [pltpu.make_async_copy(src, into, sems.at[k]) for k, (src, into) in enumerate(pairs)]
    for copy in copies:
        copy.start()
    return copies


def prepare_kernel(
    own_hbm, cot_hbm, wq_hbm, wk_hbm, wv_hbm,
    query_stack_ref, cot_stack_ref, key_ref, value_ref, wqt_ref, wkt_ref, wvt_ref,
    own_ref, cot_ref, wq_ref, wk_ref, wv_ref, sems,
):
    loads = load((
        (own_hbm, own_ref), (wq_hbm, wq_ref), (wk_hbm, wk_ref), (wv_hbm, wv_ref), (cot_hbm, cot_ref),
    ), sems)
    for copy in loads:
        copy.wait()
    head = own_ref.shape[1] // HEADS
    queries = dot(own_ref[...], wq_ref[...]).astype(jnp.bfloat16) * jnp.bfloat16(head**-0.5)
    for p in range(HEADS // 2):
        pair = slice(2 * head * p, 2 * head * (p + 1))
        query_stack_ref[p] = pair_stack(queries[:, pair]).T
        cot_stack_ref[p] = pair_stack(cot_ref[:, pair]).T
    key_ref[...] = dot(own_ref[...], wk_ref[...]).astype(jnp.bfloat16)
    value_ref[...] = dot(own_ref[...], wv_ref[...]).astype(jnp.bfloat16)
    wqt_ref[...] = wq_ref[...].T
    wkt_ref[...] = wk_ref[...].T
    wvt_ref[...] = wv_ref[...].T


def step_entry(work_ref, index):
    at = 1 + 2 * TILES * index
    return [work_ref[at + 2 * t] for t in range(TILES)], [work_ref[at + 2 * t + 1] for t in range(TILES)]


def run_steps(work_ref, start, wait, body):
    total = work_ref[0]

    def step(index, carry):
        @pl.when(index + 1 < total)
        def _():
            start(lax.rem(index + 1, 2), *step_entry(work_ref, index + 1))

        slot = lax.rem(index, 2)
        wait(slot)
        body(slot, *step_entry(work_ref, index), index)
        return carry

    lax.fori_loop(0, total, step, 0)


def first_step(work_ref, start):
    start(0, *step_entry(work_ref, 0))


class Rows:
    def __init__(self, layout, groups, mask_ref, buf, words, sems, block):
        self.layout, self.halves, self.mask_ref = layout, (groups[:4], groups[4:]), mask_ref
        self.buf, self.words, self.sems, self.block = buf, words, sems, block

    def rows(self, slot, t, k):
        half = self.block // 2
        into = self.buf.at[slot, pl.ds(t * self.block + k * half, half)]
        return lambda src: pltpu.make_async_copy(src.at[pl.ds(0, half)], into, self.sems.at[slot, t, k])

    def mask(self, slot, t, pattern):
        return pltpu.make_async_copy(self.mask_ref.at[pattern], self.words.at[slot, t], self.sems.at[slot, t, 2])

    def start(self, slot, blocks, patterns):
        for t in range(TILES):
            for k, order in enumerate(self.layout.orders()):
                start_copy(self.layout.row_place(order, blocks[t]), self.halves[k], self.rows(slot, t, k))
            self.mask(slot, t, jnp.maximum(patterns[t], 0)).start()

    def wait(self, slot):
        for t in range(TILES):
            for k in range(2):
                self.rows(slot, t, k)(self.halves[k][0].at[0]).wait()
            self.mask(slot, t, 0).wait()

    def bias(self, slot, blocks, patterns):
        parts = [
            tile_bias(self.words[slot, t], patterns[t], blocks[t] == self.layout.me) for t in range(TILES)
        ]
        return jnp.concatenate(parts, 0)


def forward_kernel(sizes, work_ref, stack_ref, cot_ref, wk_ref, wvt_ref, mask_ref, *refs):
    groups, refs = refs[:8], refs[8:]
    out_ref, sent_ref, stats_ref, buf, words, bias_ref, max_ref, sum_ref, acc_ref, score_ref, sems = refs
    layout = Layout(*sizes)
    block, width = cot_ref.shape
    head = width // HEADS
    rows_in = Rows(layout, groups, mask_ref, buf, words, sems, block)
    first_step(work_ref, rows_in.start)
    max_ref[...] = jnp.full(max_ref.shape, NEG_FILL, jnp.float32)
    sum_ref[...] = jnp.zeros(sum_ref.shape, jnp.float32)
    acc_ref[...] = jnp.zeros(acc_ref.shape, jnp.float32)

    def tiles(slot, blocks, patterns, index):
        rows = buf[slot]
        keys = dot(rows, wk_ref[...]).astype(jnp.bfloat16)
        values = dot(wvt_ref[...], rows, NT).astype(jnp.bfloat16)
        bias_ref[...] = rows_in.bias(slot, blocks, patterns)
        for p in range(HEADS // 2):
            scores = dot(keys[:, 2 * head * p : 2 * head * (p + 1)], stack_ref[p])
            for e in range(2):
                score_ref[2 * p + e] = scores[:, block * e : block * (e + 1)] + bias_ref[...]
        for h in range(HEADS):
            s = score_ref[h]
            old = max_ref[h : h + 1]
            new = jnp.maximum(old, jnp.max(s, axis=0, keepdims=True))
            fade = jnp.exp(old - new)
            expo = jnp.exp(s - new)
            max_ref[h : h + 1] = new
            sum_ref[h : h + 1] = sum_ref[h : h + 1] * fade + jnp.sum(expo, axis=0, keepdims=True)
            at = slice(head * h, head * (h + 1))
            acc_ref[at] = acc_ref[at] * fade + dot(values[at], expo.astype(jnp.bfloat16))

    run_steps(work_ref, rows_in.start, rows_in.wait, tiles)
    inverse = 1.0 / sum_ref[...]
    cot = cot_ref[...].astype(jnp.float32).T
    stats_ref[0:HEADS] = max_ref[...] + jnp.log(sum_ref[...])
    for h in range(HEADS):
        at = slice(head * h, head * (h + 1))
        outputs = acc_ref[at] * inverse[h : h + 1]
        acc_ref[at] = outputs
        stats_ref[HEADS + h : HEADS + h + 1] = jnp.sum(outputs * cot[at], axis=0, keepdims=True)
    sent_ref[...] = jnp.broadcast_to(stats_ref[...], sent_ref.shape)
    out_ref[...] = acc_ref[...].T.astype(out_ref.dtype)


def tile_grads(scores, d_probs, lse, delta):
    prob = jnp.exp(scores - lse)
    return prob.astype(jnp.bfloat16), (prob * (d_probs - delta)).astype(jnp.bfloat16)


def query_grad_kernel(
    sizes, work_ref, stack_hbm, cot_stack_hbm, stats_hbm, wqt_hbm, wk_hbm, wkt_hbm, wv_hbm, mask_ref, *refs
):
    groups, refs = refs[:8], refs[8:]
    part_ref, stack_ref, cot_stack_ref, stats_ref, wqt_ref, wk_ref, wkt_ref, wv_ref = refs[:8]
    buf, words, bias_ref, acc_ref, score_ref, d_prob_ref, sems, w_sems = refs[8:]
    layout = Layout(*sizes)
    block, width = part_ref.shape
    head = width // HEADS
    rows_in = Rows(layout, groups, mask_ref, buf, words, sems, block)
    first_step(work_ref, rows_in.start)
    loads = load((
        (wk_hbm, wk_ref), (stack_hbm, stack_ref), (wv_hbm, wv_ref), (cot_stack_hbm, cot_stack_ref),
        (wkt_hbm, wkt_ref), (stats_hbm.at[0], stats_ref), (wqt_hbm, wqt_ref),
    ), w_sems)
    acc_ref[...] = jnp.zeros(acc_ref.shape, jnp.float32)
    for copy in loads[:6]:
        copy.wait()

    def tiles(slot, blocks, patterns, index):
        rows = buf[slot]
        keys = dot(rows, wk_ref[...]).astype(jnp.bfloat16)
        values = dot(rows, wv_ref[...]).astype(jnp.bfloat16)
        keys_t = dot(wkt_ref[...], rows, NT).astype(jnp.bfloat16)
        bias_ref[...] = rows_in.bias(slot, blocks, patterns)
        for p in range(HEADS // 2):
            pair = slice(2 * head * p, 2 * head * (p + 1))
            scores = dot(keys[:, pair], stack_ref[p])
            d_probs = dot(values[:, pair], cot_stack_ref[p])
            for e in range(2):
                of = slice(block * e, block * (e + 1))
                score_ref[2 * p + e] = scores[:, of] + bias_ref[...]
                d_prob_ref[2 * p + e] = d_probs[:, of]
        for h in range(HEADS):
            _, d_scores = tile_grads(
                score_ref[h], d_prob_ref[h], stats_ref[h : h + 1], stats_ref[HEADS + h : HEADS + h + 1]
            )
            at = slice(head * h, head * (h + 1))
            acc_ref[at] += dot(keys_t[at], d_scores)

    run_steps(work_ref, rows_in.start, rows_in.wait, tiles)
    loads[6].wait()
    grad = (acc_ref[...].T * (head**-0.5)).astype(jnp.bfloat16)
    part_ref[...] = dot(grad, wqt_ref[...])


def key_grad_kernel(
    sizes, bits, work_ref, key_hbm, value_hbm, wq_hbm, wkt_hbm, wvt_hbm, part_hbm, mask_ref, stats_all_ref, *refs
):
    readers = sizes[0]
    groups, refs = refs[:8], refs[8:]
    halves, refs = (refs[:readers], refs[readers : 2 * readers]), refs[2 * readers :]
    out_ref, key_ref, value_ref, part_ref, wq_ref, wkt_ref, wvt_ref, buf, words, cot_buf, stats, bias_ref = refs[:12]
    query_stack_ref, cot_stack_ref, score_ref, d_prob_ref, key_acc, value_acc, sems, c_sems, w_sems = refs[12:]
    layout = Layout(*sizes)
    block, width = out_ref.shape
    head = width // HEADS
    rows_in = Rows(layout, groups, mask_ref, buf, words, sems, block)

    def half_copy(slot, t, k):
        into = cot_buf.at[slot, pl.ds(t * block + block // 2 * k, block // 2)]
        return lambda src: pltpu.make_async_copy(src, into, c_sems.at[slot, t, k])

    def stats_copy(slot, t, query):
        return pltpu.make_async_copy(stats_all_ref.at[query], stats.at[slot, t], c_sems.at[slot, t, 2])

    def start(slot, blocks, patterns):
        rows_in.start(slot, blocks, patterns)
        for t in range(TILES):
            stats_copy(slot, t, blocks[t]).start()
            for k in range(2):
                start_copy(layout.half_place(bits[k], blocks[t]), halves[k], half_copy(slot, t, k))

    def wait(slot):
        rows_in.wait(slot)
        for t in range(TILES):
            stats_copy(slot, t, 0).wait()
            for k in range(2):
                half_copy(slot, t, k)(halves[k][0].at[0]).wait()

    first_step(work_ref, start)
    loads = load((
        (wq_hbm, wq_ref), (key_hbm, key_ref), (value_hbm, value_ref),
        (wkt_hbm, wkt_ref), (wvt_hbm, wvt_ref), (part_hbm, part_ref),
    ), w_sems)
    key_acc[...] = jnp.zeros(key_acc.shape, jnp.float32)
    value_acc[...] = jnp.zeros(value_acc.shape, jnp.float32)
    for copy in loads[:3]:
        copy.wait()

    def tiles(slot, blocks, patterns, index):
        queries = dot(buf[slot], wq_ref[...]).astype(jnp.bfloat16) * jnp.bfloat16(head**-0.5)
        bias_ref[...] = rows_in.bias(slot, blocks, patterns)
        cots = cot_buf[slot]
        pairs = [slice(2 * head * p, 2 * head * (p + 1)) for p in range(HEADS // 2)]
        of_tile = [slice(block * t, block * (t + 1)) for t in range(TILES)]
        for p, pair in enumerate(pairs):
            query_stack_ref[p] = jnp.concatenate([pair_stack(queries[of, pair]) for of in of_tile], 0)
            cot_stack_ref[p] = jnp.concatenate([pair_stack(cots[of, pair]) for of in of_tile], 0)
            score_ref[p] = dot(key_ref[:, pair], query_stack_ref[p], NT)
            d_prob_ref[p] = dot(value_ref[:, pair], cot_stack_ref[p], NT)
        for p, pair in enumerate(pairs):
            probs, d_scores = [], []
            for t in range(TILES):
                for e in range(2):
                    h = 2 * p + e
                    of = slice(block * (2 * t + e), block * (2 * t + e + 1))
                    prob, d_score = tile_grads(
                        score_ref[p, :, of] + bias_ref[of_tile[t]], d_prob_ref[p, :, of], stats[slot, t, h : h + 1],
                        stats[slot, t, HEADS + h : HEADS + h + 1],
                    )
                    probs.append(prob)
                    d_scores.append(d_score)
            value_acc[:, pair] += dot(jnp.concatenate(probs, 1), cot_stack_ref[p])
            key_acc[:, pair] += dot(jnp.concatenate(d_scores, 1), query_stack_ref[p])

    run_steps(work_ref, start, wait, tiles)
    for copy in loads[3:]:
        copy.wait()
    grad = part_ref[...] + dot(key_acc[...].astype(jnp.bfloat16), wkt_ref[...])
    grad = grad + dot(value_acc[...].astype(jnp.bfloat16), wvt_ref[...])
    out_ref[...] = grad.astype(out_ref.dtype)


VMEM = pl.BlockSpec(memory_space=pltpu.VMEM)
SMEM = pl.BlockSpec(memory_space=pltpu.SMEM)
HBM = pl.BlockSpec(memory_space=pltpu.HBM)


def swap(block, mask):
    axes = ("reader", "blk")
    count = lax.axis_size("reader") * lax.axis_size("blk")
    return lax.ppermute(block, axes, [(i, i ^ mask) for i in range(count)])


def after(value, *others):
    return lax.optimization_barrier((value, *others))[0]


def over_readers(chunk, order, blks):
    for bit in order[:-1]:
        chunk = jnp.concatenate([chunk, swap(chunk, blks << bit)], 0)
    return [chunk, swap(chunk, blks << order[-1])]


def local(features, cotangent, w_query, w_key, w_value, tile_coords, tile_count, mask_table):
    block, width = features.shape
    readers, blks, cap = lax.axis_size("reader"), lax.axis_size("blk"), tile_coords.shape[2]
    assert block == mask_table.shape[1] and 3 * cap < 128
    sizes = (readers, blks, cap)
    devices, lines = readers * blks, blks // 2
    f32, bf16, i32 = jnp.float32, jnp.bfloat16, jnp.int32
    shape = jax.ShapeDtypeStruct
    masks = mask_table.transpose(0, 2, 1)
    words = masks.shape[1]
    head = width // HEADS
    half = block // 2
    some = pltpu.CompilerParams(vmem_limit_bytes=VMEM_SOME)
    most = pltpu.CompilerParams(vmem_limit_bytes=VMEM_MOST)
    axes = ("reader", "blk")

    def cost(tiles):
        return pl.CostEstimate(flops=tiles * 200_000_000, bytes_accessed=4_000_000, transcendentals=tiles * 131072)

    packed = pl.pallas_call(
        pack_kernel,
        out_shape=shape((1, block + LIST_ROWS, width), bf16),
        in_specs=[HBM, HBM, HBM],
        out_specs=HBM,
        scratch_shapes=[
            pltpu.VMEM((LIST_ROWS, width), bf16), pltpu.SMEM((1, 3, 1, cap), i32), pltpu.SMEM((1, 1), i32),
            pltpu.SemaphoreType.DMA((3,)),
        ],
        compiler_params=most,
        name="pack",
    )(features, tile_coords.transpose(0, 3, 1, 2), tile_count)
    lined = [packed] + [swap(packed, 2 * k) for k in range(1, lines)]

    bits = (0, (readers - 1).bit_length() - 1)
    cot_parts = [
        jnp.concatenate([cotangent[None, half * k : half * (k + 1)], packed[:, block:]], 1) for k in range(2)
    ]
    cot_other = [swap(part, blks << bit) for part, bit in zip(cot_parts, bits)]

    own_list = packed[:, block:, :128]
    columns = {1 << bit: other[:, half:, :128] for bit, other in zip(bits, cot_other)}
    far_list = after(own_list, *cot_other)
    columns = {k: columns[k] if k in columns else swap(far_list, blks * k) for k in range(1, readers)}
    column_lists = jnp.concatenate([own_list] + [columns[k] for k in range(1, readers)], 0)
    line_lists = jnp.concatenate([entry[:, block:, :128] for entry in lined], 0)
    row_lists = jnp.concatenate([line_lists, swap(line_lists, 1)], 0)

    def work(kernel, lists, count, name):
        return pl.pallas_call(
            functools.partial(kernel, sizes),
            out_shape=shape((2 * count * cap + 5,), i32),
            in_specs=[HBM],
            out_specs=SMEM,
            scratch_shapes=[pltpu.SMEM((count, 128), i32), pltpu.SemaphoreType.DMA],
            compiler_params=some,
            cost_estimate=cost(1),
            name=name,
        )(lists[:, 0].astype(i32))

    query_work = work(query_work_kernel, row_lists, blks, "query_work")
    key_work = work(key_work_kernel, column_lists, readers, "key_work")

    stacks = shape((HEADS // 2, 2 * head, 2 * block), bf16)
    own = shape((block, width), bf16)
    square = shape((width, width), bf16)
    weight = pltpu.VMEM((width, width), bf16)
    rows_low, rows_wide = pltpu.VMEM((block, width), bf16), pltpu.VMEM((block, width), f32)
    prepared = pl.pallas_call(
        prepare_kernel,
        out_shape=(stacks, stacks, own, own, square, square, square),
        in_specs=[HBM] * 5,
        out_specs=(VMEM,) * 7,
        scratch_shapes=[rows_low, rows_low, weight, weight, weight, pltpu.SemaphoreType.DMA((5,))],
        compiler_params=most,
        cost_estimate=cost(2),
        name="prepare",
    )(features, cotangent, w_query, w_key, w_value)
    query_stack, cot_stack, keys, values, w_query_t, w_key_t, w_value_t = prepared

    lined = after(lined, prepared)
    chunks = [jnp.concatenate([entry[:, half * k : half * (k + 1)] for entry in lined], 0) for k in range(2)]
    here = [over_readers(chunk, order, blks) for chunk, order in zip(chunks, orders(readers))]
    rows_all = []
    for first, last in here:
        rows_all += [first, last, swap(first, 1), swap(last, 1)]

    pairs = [part[:, :half] for k in range(2) for part in (cot_parts[k], cot_other[k])]
    pieces = [after(jnp.concatenate(pairs, 0), *chunks)]
    mask = blks // 2
    while mask > 1:
        pieces += [swap(after(piece, query_work, key_work) if at else piece, mask) for at, piece in enumerate(pieces)]
        mask //= 2

    cots_here = []
    for k in range(2):
        part = jnp.concatenate([piece[2 * k : 2 * k + 2] for piece in pieces], 0)
        masks_left = [m for m in range(1, readers) if not m >> bits[k] & 1]
        cots_here.append((part, [swap(after(part, here), blks * m) for m in masks_left]))

    stack_space = pltpu.VMEM(stacks.shape, bf16)
    buffer = pltpu.VMEM((2, TILES * block, width), bf16)
    word_buffer = pltpu.VMEM((2, TILES, words, block), i32)
    bias = pltpu.VMEM((TILES * block, block), f32)
    turned = pltpu.VMEM((width, block), f32)
    per_head = pltpu.VMEM((HEADS, block), f32)
    own_stats = pltpu.VMEM((2 * HEADS, block), f32)
    met = pltpu.VMEM((HEADS, TILES * block, block), f32)
    pair_met = pltpu.VMEM((HEADS // 2, block, 2 * TILES * block), f32)
    pair_rows = pltpu.VMEM((HEADS // 2, 2 * TILES * block, 2 * head), bf16)
    row_sems = pltpu.SemaphoreType.DMA((2, TILES, 3))

    attn_out, stats = pl.pallas_call(
        functools.partial(forward_kernel, sizes),
        out_shape=(own, shape((devices, 2 * HEADS, block), f32)),
        in_specs=[SMEM] + [VMEM] * 4 + [HBM] * 9,
        out_specs=(VMEM, VMEM),
        scratch_shapes=[own_stats, buffer, word_buffer, bias, per_head, per_head, turned, met, row_sems],
        compiler_params=some,
        cost_estimate=cost(5),
        name="forward",
    )(query_work, query_stack, cotangent, w_key, w_value_t, masks, *rows_all)

    stats_all = lax.all_to_all(stats, axes, 0, 0, tiled=True)

    query_part = pl.pallas_call(
        functools.partial(query_grad_kernel, sizes),
        out_shape=shape((block, width), f32),
        in_specs=[SMEM] + [HBM] * 16,
        out_specs=VMEM,
        scratch_shapes=[
            stack_space, stack_space, own_stats, weight, weight, weight, weight, buffer, word_buffer, bias, turned,
            met, met, row_sems, pltpu.SemaphoreType.DMA((7,)),
        ],
        compiler_params=most,
        cost_estimate=cost(5),
        name="query_grad",
    )(query_work, query_stack, cot_stack, stats, w_query_t, w_key, w_key_t, w_value, masks, *rows_all)

    cots_all = []
    for first, rest in cots_here:
        cots_all += [first, *rest, swap(after(first, stats), 1)]
        cots_all += [swap(after(part, stats_all, query_part), 1) for part in rest]

    grad_features = pl.pallas_call(
        functools.partial(key_grad_kernel, sizes, bits),
        out_shape=own,
        in_specs=[SMEM] + [HBM] * (16 + 2 * readers),
        out_specs=VMEM,
        scratch_shapes=[
            rows_low, rows_low, rows_wide, weight, weight, weight,
            buffer, word_buffer, buffer, pltpu.VMEM((2, TILES, 2 * HEADS, block), f32), bias,
            pair_rows, pair_rows, pair_met, pair_met, rows_wide, rows_wide,
            row_sems, pltpu.SemaphoreType.DMA((2, TILES, 3)), pltpu.SemaphoreType.DMA((6,)),
        ],
        compiler_params=most,
        cost_estimate=cost(5),
        name="key_grad",
    )(key_work, keys, values, w_query, w_key_t, w_value_t, query_part, masks, stats_all, *rows_all, *cots_all)
    return attn_out, grad_features


def solution(mesh):
    return jax.shard_map(
        local,
        mesh=mesh,
        in_specs=(
            P(("reader", "blk"), None),
            P(("reader", "blk"), None),
            P(),
            P(),
            P(),
            P("reader", "blk", None, None),
            P("reader", "blk"),
            P(),
        ),
        out_specs=(P(("reader", "blk"), None), P(("reader", "blk"), None)),
        check_vma=False,
    )
```

```python
import functools

import jax
import jax.numpy as jnp
from jax import lax
from jax.experimental import pallas as pl
from jax.experimental.pallas import tpu as pltpu
from jax.sharding import PartitionSpec as P

HEADS = 8
NEG_FILL = -1e30
NT = (((1,), (1,)), ((), ()))
NN = (((1,), (0,)), ((), ()))
TILES = 2
LIST_ROWS = 16
VMEM_SOME = 40 * 1024 * 1024
VMEM_MOST = 58 * 1024 * 1024


def dot(a, b, dims=NN):
    return lax.dot_general(a, b, dims, preferred_element_type=jnp.float32)


def pair_stack(rows):
    lane = lax.broadcasted_iota(jnp.int32, rows.shape, 1)
    half = rows.shape[1] // 2
    zero = jnp.zeros_like(rows)
    return jnp.concatenate([jnp.where(lane < half, rows, zero), jnp.where(lane >= half, rows, zero)], 0)


def tile_bias(words, pattern, diag):
    count, size = words.shape
    keys = lax.broadcasted_iota(jnp.int32, (size, size), 0)
    queries = lax.broadcasted_iota(jnp.int32, (size, size), 1)
    spread = jnp.concatenate(
        [jnp.broadcast_to(words[g : g + 1], (size // count, size)) for g in range(count)], 0
    )
    bits = jnp.right_shift(spread, keys & 31) & 1
    same = keys - queries == jnp.where(diag, 0, 2 * size)
    return jnp.where((bits == 1) | same, jnp.where(pattern < 0, NEG_FILL, 0.0), NEG_FILL)


class Layout:
    def __init__(self, readers, blks, cap):
        self.readers, self.blks, self.cap = readers, blks, cap
        self.reader, self.blk = lax.axis_index("reader"), lax.axis_index("blk")
        self.me = self.reader * blks + self.blk

    def apart(self, device):
        far = jnp.bitwise_xor(device, self.me)
        reader, blk = far // self.blks, lax.rem(far, self.blks)
        return reader, blk // 2, blk & 1

    def row_place(self, order, device):
        reader, line, core = self.apart(device)
        for at, bit in enumerate(order[:-1]):
            line = line + (jnp.right_shift(reader, bit) & 1) * ((self.blks // 2) << at)
        return (jnp.right_shift(reader, order[-1]) & 1) + 2 * core, line

    def orders(self):
        return orders(self.readers)

    def half_place(self, bit, device):
        reader, line, core = self.apart(device)
        first = jnp.right_shift(reader, bit) & 1
        top = (self.blks // 2 - 1).bit_length() - 1
        line = sum((jnp.right_shift(line, top - at) & 1) << at for at in range(top + 1))
        low = reader & ((1 << bit) - 1)
        rest = low + (jnp.right_shift(reader, bit + 1) << bit)
        return rest + self.readers // 2 * core, 2 * line + first


def orders(readers):
    rising = tuple(range((readers - 1).bit_length()))
    return rising, rising[::-1]


def start_copy(place, refs, make):
    group, where = place
    for g, ref in enumerate(refs):

        @pl.when(group == g)
        def _():
            make(ref.at[where]).start()


def pack_kernel(own_hbm, coords_hbm, count_hbm, out_ref, coords_ref, count_ref, sems):
    block = own_hbm.shape[0]
    cap = coords_ref.shape[3]
    copies = [
        pltpu.make_async_copy(coords_hbm, coords_ref, sems.at[0]),
        pltpu.make_async_copy(count_hbm, count_ref, sems.at[1]),
        pltpu.make_async_copy(own_hbm, out_ref.at[0, pl.ds(0, block)], sems.at[2]),
    ]
    for copy in copies:
        copy.start()
    copies[0].wait()
    copies[1].wait()
    lane = lax.broadcasted_iota(jnp.int32, (LIST_ROWS, out_ref.shape[2]), 1)
    row = jnp.zeros(lane.shape, jnp.int32)
    for column in range(3):
        for slot in range(cap):
            row = jnp.where(lane == column * cap + slot, coords_ref[0, column, 0, slot], row)
    row = jnp.where(lane == 3 * cap, count_ref[0, 0], row)
    out_ref[0, block:] = row.astype(jnp.float32).astype(jnp.bfloat16)
    copies[2].wait()


def scan_list(lists_ref, cap, row, column, wanted, found, out_ref, block_of):
    def one_slot(slot, found):
        out_ref[2 * found + 1] = block_of(lists_ref[row, (1 - column) * cap + slot])
        out_ref[2 * found + 2] = lists_ref[row, 2 * cap + slot]
        return found + jnp.where(lists_ref[row, column * cap + slot] == wanted, 1, 0)

    return lax.fori_loop(0, lists_ref[row, 3 * cap], one_slot, found)


def close_work(found, out_ref):
    out_ref[2 * found + 1] = out_ref[2 * found - 1]
    out_ref[2 * found + 2] = -1
    out_ref[0] = (found + 1) // 2


def query_work_kernel(sizes, lists_hbm, work_ref, lists_ref, sem):
    readers, blks, cap = sizes
    layout = Layout(*sizes)
    copy = pltpu.make_async_copy(lists_hbm, lists_ref, sem)
    copy.start()
    copy.wait()

    def one(k, found):
        blk = jnp.bitwise_xor(k, layout.blk)
        row = k // 2 + (k & 1) * (blks // 2)
        put = lambda other: other * blks + blk
        return scan_list(lists_ref, cap, row, 0, layout.blk, found, work_ref, put)

    close_work(lax.fori_loop(0, blks, one, 0), work_ref)


def key_work_kernel(sizes, lists_hbm, work_ref, lists_ref, sem):
    readers, blks, cap = sizes
    layout = Layout(*sizes)
    copy = pltpu.make_async_copy(lists_hbm, lists_ref, sem)
    copy.start()
    copy.wait()

    def one(k, found):
        reader = jnp.bitwise_xor(k, layout.reader)
        put = lambda other: reader * blks + other
        return scan_list(lists_ref, cap, k, 1, layout.reader, found, work_ref, put)

    close_work(lax.fori_loop(0, readers, one, 0), work_ref)


def load(pairs, sems):
    copies = [pltpu.make_async_copy(src, into, sems.at[k]) for k, (src, into) in enumerate(pairs)]
    for copy in copies:
        copy.start()
    return copies


def prepare_kernel(
    own_hbm, cot_hbm, wq_hbm, wk_hbm, wv_hbm,
    query_stack_ref, cot_stack_ref, key_ref, value_ref, wqt_ref, wkt_ref, wvt_ref,
    own_ref, cot_ref, wq_ref, wk_ref, wv_ref, sems,
):
    loads = load((
        (own_hbm, own_ref), (wq_hbm, wq_ref), (wk_hbm, wk_ref), (wv_hbm, wv_ref), (cot_hbm, cot_ref),
    ), sems)
    for copy in loads:
        copy.wait()
    head = own_ref.shape[1] // HEADS
    queries = dot(own_ref[...], wq_ref[...]).astype(jnp.bfloat16) * jnp.bfloat16(head**-0.5)
    for p in range(HEADS // 2):
        pair = slice(2 * head * p, 2 * head * (p + 1))
        query_stack_ref[p] = pair_stack(queries[:, pair]).T
        cot_stack_ref[p] = pair_stack(cot_ref[:, pair]).T
    key_ref[...] = dot(own_ref[...], wk_ref[...]).astype(jnp.bfloat16)
    value_ref[...] = dot(own_ref[...], wv_ref[...]).astype(jnp.bfloat16)
    wqt_ref[...] = wq_ref[...].T
    wkt_ref[...] = wk_ref[...].T
    wvt_ref[...] = wv_ref[...].T


def step_entry(work_ref, index):
    at = 1 + 2 * TILES * index
    return [work_ref[at + 2 * t] for t in range(TILES)], [work_ref[at + 2 * t + 1] for t in range(TILES)]


def run_steps(work_ref, start, wait, body):
    total = work_ref[0]

    def step(index, carry):
        @pl.when(index + 1 < total)
        def _():
            start(lax.rem(index + 1, 2), *step_entry(work_ref, index + 1))

        slot = lax.rem(index, 2)
        wait(slot)
        body(slot, *step_entry(work_ref, index), index)
        return carry

    lax.fori_loop(0, total, step, 0)


def first_step(work_ref, start):
    start(0, *step_entry(work_ref, 0))


class Rows:
    def __init__(self, layout, groups, mask_ref, buf, words, sems, block):
        self.layout, self.halves, self.mask_ref = layout, (groups[:4], groups[4:]), mask_ref
        self.buf, self.words, self.sems, self.block = buf, words, sems, block

    def rows(self, slot, t, k):
        half = self.block // 2
        into = self.buf.at[slot, pl.ds(t * self.block + k * half, half)]
        return lambda src: pltpu.make_async_copy(src.at[pl.ds(0, half)], into, self.sems.at[slot, t, k])

    def mask(self, slot, t, pattern):
        return pltpu.make_async_copy(self.mask_ref.at[pattern], self.words.at[slot, t], self.sems.at[slot, t, 2])

    def start(self, slot, blocks, patterns):
        for t in range(TILES):
            for k, order in enumerate(self.layout.orders()):
                start_copy(self.layout.row_place(order, blocks[t]), self.halves[k], self.rows(slot, t, k))
            self.mask(slot, t, jnp.maximum(patterns[t], 0)).start()

    def wait(self, slot):
        for t in range(TILES):
            for k in range(2):
                self.rows(slot, t, k)(self.halves[k][0].at[0]).wait()
            self.mask(slot, t, 0).wait()

    def bias(self, slot, blocks, patterns):
        parts = [
            tile_bias(self.words[slot, t], patterns[t], blocks[t] == self.layout.me) for t in range(TILES)
        ]
        return jnp.concatenate(parts, 0)


def forward_kernel(sizes, work_ref, stack_ref, cot_ref, wk_ref, wvt_ref, mask_ref, *refs):
    groups, refs = refs[:8], refs[8:]
    out_ref, sent_ref, stats_ref, buf, words, bias_ref, max_ref, sum_ref, acc_ref, score_ref, sems = refs
    layout = Layout(*sizes)
    block, width = cot_ref.shape
    head = width // HEADS
    rows_in = Rows(layout, groups, mask_ref, buf, words, sems, block)
    first_step(work_ref, rows_in.start)
    max_ref[...] = jnp.full(max_ref.shape, NEG_FILL, jnp.float32)
    sum_ref[...] = jnp.zeros(sum_ref.shape, jnp.float32)
    acc_ref[...] = jnp.zeros(acc_ref.shape, jnp.float32)

    def tiles(slot, blocks, patterns, index):
        rows = buf[slot]
        keys = dot(rows, wk_ref[...]).astype(jnp.bfloat16)
        values = dot(wvt_ref[...], rows, NT).astype(jnp.bfloat16)
        bias_ref[...] = rows_in.bias(slot, blocks, patterns)
        for p in range(HEADS // 2):
            scores = dot(keys[:, 2 * head * p : 2 * head * (p + 1)], stack_ref[p])
            for e in range(2):
                score_ref[2 * p + e] = scores[:, block * e : block * (e + 1)] + bias_ref[...]
        for h in range(HEADS):
            s = score_ref[h]
            old = max_ref[h : h + 1]
            new = jnp.maximum(old, jnp.max(s, axis=0, keepdims=True))
            fade = jnp.exp(old - new)
            expo = jnp.exp(s - new)
            max_ref[h : h + 1] = new
            sum_ref[h : h + 1] = sum_ref[h : h + 1] * fade + jnp.sum(expo, axis=0, keepdims=True)
            at = slice(head * h, head * (h + 1))
            acc_ref[at] = acc_ref[at] * fade + dot(values[at], expo.astype(jnp.bfloat16))

    run_steps(work_ref, rows_in.start, rows_in.wait, tiles)
    inverse = 1.0 / sum_ref[...]
    cot = cot_ref[...].astype(jnp.float32).T
    stats_ref[0:HEADS] = max_ref[...] + jnp.log(sum_ref[...])
    for h in range(HEADS):
        at = slice(head * h, head * (h + 1))
        outputs = acc_ref[at] * inverse[h : h + 1]
        acc_ref[at] = outputs
        stats_ref[HEADS + h : HEADS + h + 1] = jnp.sum(outputs * cot[at], axis=0, keepdims=True)
    sent_ref[...] = jnp.broadcast_to(stats_ref[...], sent_ref.shape)
    out_ref[...] = acc_ref[...].T.astype(out_ref.dtype)


def tile_grads(scores, d_probs, lse, delta):
    prob = jnp.exp(scores - lse)
    return prob.astype(jnp.bfloat16), (prob * (d_probs - delta)).astype(jnp.bfloat16)


def query_grad_kernel(
    sizes, work_ref, stack_hbm, cot_stack_hbm, stats_hbm, wqt_hbm, wk_hbm, wkt_hbm, wv_hbm, mask_ref, *refs
):
    groups, refs = refs[:8], refs[8:]
    part_ref, stack_ref, cot_stack_ref, stats_ref, wqt_ref, wk_ref, wkt_ref, wv_ref = refs[:8]
    buf, words, bias_ref, acc_ref, score_ref, d_prob_ref, sems, w_sems = refs[8:]
    layout = Layout(*sizes)
    block, width = part_ref.shape
    head = width // HEADS
    rows_in = Rows(layout, groups, mask_ref, buf, words, sems, block)
    first_step(work_ref, rows_in.start)
    loads = load((
        (wk_hbm, wk_ref), (stack_hbm, stack_ref), (wv_hbm, wv_ref), (cot_stack_hbm, cot_stack_ref),
        (wkt_hbm, wkt_ref), (stats_hbm.at[0], stats_ref), (wqt_hbm, wqt_ref),
    ), w_sems)
    acc_ref[...] = jnp.zeros(acc_ref.shape, jnp.float32)
    for copy in loads[:6]:
        copy.wait()

    def tiles(slot, blocks, patterns, index):
        rows = buf[slot]
        keys = dot(rows, wk_ref[...]).astype(jnp.bfloat16)
        values = dot(rows, wv_ref[...]).astype(jnp.bfloat16)
        keys_t = dot(wkt_ref[...], rows, NT).astype(jnp.bfloat16)
        bias_ref[...] = rows_in.bias(slot, blocks, patterns)
        for p in range(HEADS // 2):
            pair = slice(2 * head * p, 2 * head * (p + 1))
            scores = dot(keys[:, pair], stack_ref[p])
            d_probs = dot(values[:, pair], cot_stack_ref[p])
            for e in range(2):
                of = slice(block * e, block * (e + 1))
                score_ref[2 * p + e] = scores[:, of] + bias_ref[...]
                d_prob_ref[2 * p + e] = d_probs[:, of]
        for h in range(HEADS):
            _, d_scores = tile_grads(
                score_ref[h], d_prob_ref[h], stats_ref[h : h + 1], stats_ref[HEADS + h : HEADS + h + 1]
            )
            at = slice(head * h, head * (h + 1))
            acc_ref[at] += dot(keys_t[at], d_scores)

    run_steps(work_ref, rows_in.start, rows_in.wait, tiles)
    loads[6].wait()
    grad = (acc_ref[...].T * (head**-0.5)).astype(jnp.bfloat16)
    part_ref[...] = dot(grad, wqt_ref[...])


def key_grad_kernel(
    sizes, bits, work_ref, key_hbm, value_hbm, wq_hbm, wkt_hbm, wvt_hbm, part_hbm, mask_ref, stats_all_ref, *refs
):
    readers = sizes[0]
    groups, refs = refs[:8], refs[8:]
    halves, refs = (refs[:readers], refs[readers : 2 * readers]), refs[2 * readers :]
    out_ref, key_ref, value_ref, part_ref, wq_ref, wkt_ref, wvt_ref, buf, words, cot_buf, stats, bias_ref = refs[:12]
    query_stack_ref, cot_stack_ref, score_ref, d_prob_ref, key_acc, value_acc, sems, c_sems, w_sems = refs[12:]
    layout = Layout(*sizes)
    block, width = out_ref.shape
    head = width // HEADS
    rows_in = Rows(layout, groups, mask_ref, buf, words, sems, block)

    def half_copy(slot, t, k):
        into = cot_buf.at[slot, pl.ds(t * block + block // 2 * k, block // 2)]
        return lambda src: pltpu.make_async_copy(src, into, c_sems.at[slot, t, k])

    def stats_copy(slot, t, query):
        return pltpu.make_async_copy(stats_all_ref.at[query], stats.at[slot, t], c_sems.at[slot, t, 2])

    def start(slot, blocks, patterns):
        rows_in.start(slot, blocks, patterns)
        for t in range(TILES):
            stats_copy(slot, t, blocks[t]).start()
            for k in range(2):
                start_copy(layout.half_place(bits[k], blocks[t]), halves[k], half_copy(slot, t, k))

    def wait(slot):
        rows_in.wait(slot)
        for t in range(TILES):
            stats_copy(slot, t, 0).wait()
            for k in range(2):
                half_copy(slot, t, k)(halves[k][0].at[0]).wait()

    first_step(work_ref, start)
    loads = load((
        (wq_hbm, wq_ref), (key_hbm, key_ref), (value_hbm, value_ref),
        (wkt_hbm, wkt_ref), (wvt_hbm, wvt_ref), (part_hbm, part_ref),
    ), w_sems)
    key_acc[...] = jnp.zeros(key_acc.shape, jnp.float32)
    value_acc[...] = jnp.zeros(value_acc.shape, jnp.float32)
    for copy in loads[:3]:
        copy.wait()

    def tiles(slot, blocks, patterns, index):
        queries = dot(buf[slot], wq_ref[...]).astype(jnp.bfloat16) * jnp.bfloat16(head**-0.5)
        bias_ref[...] = rows_in.bias(slot, blocks, patterns)
        cots = cot_buf[slot]
        pairs = [slice(2 * head * p, 2 * head * (p + 1)) for p in range(HEADS // 2)]
        of_tile = [slice(block * t, block * (t + 1)) for t in range(TILES)]
        for p, pair in enumerate(pairs):
            query_stack_ref[p] = jnp.concatenate([pair_stack(queries[of, pair]) for of in of_tile], 0)
            cot_stack_ref[p] = jnp.concatenate([pair_stack(cots[of, pair]) for of in of_tile], 0)
            score_ref[p] = dot(key_ref[:, pair], query_stack_ref[p], NT)
            d_prob_ref[p] = dot(value_ref[:, pair], cot_stack_ref[p], NT)
        for p, pair in enumerate(pairs):
            probs, d_scores = [], []
            for t in range(TILES):
                for e in range(2):
                    h = 2 * p + e
                    of = slice(block * (2 * t + e), block * (2 * t + e + 1))
                    prob, d_score = tile_grads(
                        score_ref[p, :, of] + bias_ref[of_tile[t]], d_prob_ref[p, :, of], stats[slot, t, h : h + 1],
                        stats[slot, t, HEADS + h : HEADS + h + 1],
                    )
                    probs.append(prob)
                    d_scores.append(d_score)
            value_acc[:, pair] += dot(jnp.concatenate(probs, 1), cot_stack_ref[p])
            key_acc[:, pair] += dot(jnp.concatenate(d_scores, 1), query_stack_ref[p])

    run_steps(work_ref, start, wait, tiles)
    for copy in loads[3:]:
        copy.wait()
    grad = part_ref[...] + dot(key_acc[...].astype(jnp.bfloat16), wkt_ref[...])
    grad = grad + dot(value_acc[...].astype(jnp.bfloat16), wvt_ref[...])
    out_ref[...] = grad.astype(out_ref.dtype)


VMEM = pl.BlockSpec(memory_space=pltpu.VMEM)
SMEM = pl.BlockSpec(memory_space=pltpu.SMEM)
HBM = pl.BlockSpec(memory_space=pltpu.HBM)


def swap(block, mask):
    axes = ("reader", "blk")
    count = lax.axis_size("reader") * lax.axis_size("blk")
    return lax.ppermute(block, axes, [(i, i ^ mask) for i in range(count)])


def after(value, *others):
    return lax.optimization_barrier((value, *others))[0]


def over_readers(chunk, order, blks):
    for bit in order[:-1]:
        chunk = jnp.concatenate([chunk, swap(chunk, blks << bit)], 0)
    return [chunk, swap(chunk, blks << order[-1])]


def local(features, cotangent, w_query, w_key, w_value, tile_coords, tile_count, mask_table):
    block, width = features.shape
    readers, blks, cap = lax.axis_size("reader"), lax.axis_size("blk"), tile_coords.shape[2]
    assert block == mask_table.shape[1] and 3 * cap < 128
    sizes = (readers, blks, cap)
    devices, lines = readers * blks, blks // 2
    f32, bf16, i32 = jnp.float32, jnp.bfloat16, jnp.int32
    shape = jax.ShapeDtypeStruct
    masks = mask_table.transpose(0, 2, 1)
    words = masks.shape[1]
    head = width // HEADS
    half = block // 2
    some = pltpu.CompilerParams(vmem_limit_bytes=VMEM_SOME)
    most = pltpu.CompilerParams(vmem_limit_bytes=VMEM_MOST)
    axes = ("reader", "blk")

    def cost(tiles):
        return pl.CostEstimate(flops=tiles * 200_000_000, bytes_accessed=4_000_000, transcendentals=tiles * 131072)

    packed = pl.pallas_call(
        pack_kernel,
        out_shape=shape((1, block + LIST_ROWS, width), bf16),
        in_specs=[HBM, HBM, HBM],
        out_specs=VMEM,
        scratch_shapes=[
            pltpu.SMEM((1, 3, 1, cap), i32), pltpu.SMEM((1, 1), i32), pltpu.SemaphoreType.DMA((3,)),
        ],
        compiler_params=most,
        name="pack",
    )(features, tile_coords.transpose(0, 3, 1, 2), tile_count)
    lined = [packed] + [swap(packed, 2 * k) for k in range(1, lines)]

    bits = (0, (readers - 1).bit_length() - 1)
    cot_parts = [
        jnp.concatenate([cotangent[None, half * k : half * (k + 1)], packed[:, block:]], 1) for k in range(2)
    ]
    cot_other = [swap(part, blks << bit) for part, bit in zip(cot_parts, bits)]

    own_list = packed[:, block:, :128]
    columns = {1 << bit: other[:, half:, :128] for bit, other in zip(bits, cot_other)}
    line_lists = jnp.concatenate([entry[:, block:, :128] for entry in lined], 0)
    row_lists = jnp.concatenate([line_lists, swap(line_lists, 1)], 0)
    far_list = after(own_list, row_lists)
    columns = {k: columns[k] if k in columns else swap(far_list, blks * k) for k in range(1, readers)}
    column_lists = jnp.concatenate([own_list] + [columns[k] for k in range(1, readers)], 0)

    def work(kernel, lists, count, name):
        return pl.pallas_call(
            functools.partial(kernel, sizes),
            out_shape=shape((2 * count * cap + 5,), i32),
            in_specs=[HBM],
            out_specs=SMEM,
            scratch_shapes=[pltpu.SMEM((count, 128), i32), pltpu.SemaphoreType.DMA],
            compiler_params=some,
            cost_estimate=cost(1),
            name=name,
        )(lists[:, 0].astype(i32))

    query_work = work(query_work_kernel, row_lists, blks, "query_work")
    key_work = work(key_work_kernel, column_lists, readers, "key_work")

    stacks = shape((HEADS // 2, 2 * head, 2 * block), bf16)
    own = shape((block, width), bf16)
    square = shape((width, width), bf16)
    weight = pltpu.VMEM((width, width), bf16)
    rows_low, rows_wide = pltpu.VMEM((block, width), bf16), pltpu.VMEM((block, width), f32)
    prepared = pl.pallas_call(
        prepare_kernel,
        out_shape=(stacks, stacks, own, own, square, square, square),
        in_specs=[HBM] * 5,
        out_specs=(VMEM,) * 7,
        scratch_shapes=[rows_low, rows_low, weight, weight, weight, pltpu.SemaphoreType.DMA((5,))],
        compiler_params=most,
        cost_estimate=cost(2),
        name="prepare",
    )(features, cotangent, w_query, w_key, w_value)
    query_stack, cot_stack, keys, values, w_query_t, w_key_t, w_value_t = prepared

    lined = after(lined, prepared)
    chunks = [jnp.concatenate([entry[:, half * k : half * (k + 1)] for entry in lined], 0) for k in range(2)]
    here = [over_readers(chunk, order, blks) for chunk, order in zip(chunks, orders(readers))]
    rows_all = []
    for first, last in here:
        rows_all += [first, last, swap(first, 1), swap(last, 1)]

    pairs = [part[:, :half] for k in range(2) for part in (cot_parts[k], cot_other[k])]
    pieces = [after(jnp.concatenate(pairs, 0), *chunks, row_lists)]
    mask = blks // 2
    while mask > 1:
        pieces += [swap(after(piece, query_work, key_work) if at else piece, mask) for at, piece in enumerate(pieces)]
        mask //= 2

    cots_here = []
    for k in range(2):
        part = jnp.concatenate([piece[2 * k : 2 * k + 2] for piece in pieces], 0)
        masks_left = [m for m in range(1, readers) if not m >> bits[k] & 1]
        cots_here.append((part, [swap(after(part, here), blks * m) for m in masks_left]))

    stack_space = pltpu.VMEM(stacks.shape, bf16)
    buffer = pltpu.VMEM((2, TILES * block, width), bf16)
    word_buffer = pltpu.VMEM((2, TILES, words, block), i32)
    bias = pltpu.VMEM((TILES * block, block), f32)
    turned = pltpu.VMEM((width, block), f32)
    per_head = pltpu.VMEM((HEADS, block), f32)
    own_stats = pltpu.VMEM((2 * HEADS, block), f32)
    met = pltpu.VMEM((HEADS, TILES * block, block), f32)
    pair_met = pltpu.VMEM((HEADS // 2, block, 2 * TILES * block), f32)
    pair_rows = pltpu.VMEM((HEADS // 2, 2 * TILES * block, 2 * head), bf16)
    row_sems = pltpu.SemaphoreType.DMA((2, TILES, 3))

    attn_out, stats = pl.pallas_call(
        functools.partial(forward_kernel, sizes),
        out_shape=(own, shape((devices, 2 * HEADS, block), f32)),
        in_specs=[SMEM] + [VMEM] * 4 + [HBM] * 9,
        out_specs=(VMEM, VMEM),
        scratch_shapes=[own_stats, buffer, word_buffer, bias, per_head, per_head, turned, met, row_sems],
        compiler_params=some,
        cost_estimate=cost(5),
        name="forward",
    )(query_work, query_stack, cotangent, w_key, w_value_t, masks, *rows_all)

    stats_all = lax.all_to_all(stats, axes, 0, 0, tiled=True)

    query_part = pl.pallas_call(
        functools.partial(query_grad_kernel, sizes),
        out_shape=shape((block, width), f32),
        in_specs=[SMEM] + [HBM] * 16,
        out_specs=VMEM,
        scratch_shapes=[
            stack_space, stack_space, own_stats, weight, weight, weight, weight, buffer, word_buffer, bias, turned,
            met, met, row_sems, pltpu.SemaphoreType.DMA((7,)),
        ],
        compiler_params=most,
        cost_estimate=cost(5),
        name="query_grad",
    )(query_work, query_stack, cot_stack, stats, w_query_t, w_key, w_key_t, w_value, masks, *rows_all)

    cots_all = []
    for first, rest in cots_here:
        cots_all += [first, *rest, swap(after(first, stats), 1)]
        cots_all += [swap(after(part, stats_all, query_part), 1) for part in rest]

    grad_features = pl.pallas_call(
        functools.partial(key_grad_kernel, sizes, bits),
        out_shape=own,
        in_specs=[SMEM] + [HBM] * (16 + 2 * readers),
        out_specs=VMEM,
        scratch_shapes=[
            rows_low, rows_low, rows_wide, weight, weight, weight,
            buffer, word_buffer, buffer, pltpu.VMEM((2, TILES, 2 * HEADS, block), f32), bias,
            pair_rows, pair_rows, pair_met, pair_met, rows_wide, rows_wide,
            row_sems, pltpu.SemaphoreType.DMA((2, TILES, 3)), pltpu.SemaphoreType.DMA((6,)),
        ],
        compiler_params=most,
        cost_estimate=cost(5),
        name="key_grad",
    )(key_work, keys, values, w_query, w_key_t, w_value_t, query_part, masks, stats_all, *rows_all, *cots_all)
    return attn_out, grad_features


def solution(mesh):
    return jax.shard_map(
        local,
        mesh=mesh,
        in_specs=(
            P(("reader", "blk"), None),
            P(("reader", "blk"), None),
            P(),
            P(),
            P(),
            P("reader", "blk", None, None),
            P("reader", "blk"),
            P(),
        ),
        out_specs=(P(("reader", "blk"), None), P(("reader", "blk"), None)),
        check_vma=False,
    )
```

```python
import functools

import jax
import jax.numpy as jnp
from jax import lax
from jax.experimental import pallas as pl
from jax.experimental.pallas import tpu as pltpu
from jax.sharding import PartitionSpec as P

HEADS = 8
NEG_FILL = -1e30
NT = (((1,), (1,)), ((), ()))
NN = (((1,), (0,)), ((), ()))
TILES = 2
LIST_ROWS = 16
VMEM_SOME = 40 * 1024 * 1024
VMEM_MOST = 58 * 1024 * 1024


def dot(a, b, dims=NN):
    return lax.dot_general(a, b, dims, preferred_element_type=jnp.float32)


def pair_stack(rows):
    lane = lax.broadcasted_iota(jnp.int32, rows.shape, 1)
    half = rows.shape[1] // 2
    zero = jnp.zeros_like(rows)
    return jnp.concatenate([jnp.where(lane < half, rows, zero), jnp.where(lane >= half, rows, zero)], 0)


def tile_bias(words, pattern, diag):
    count, size = words.shape
    keys = lax.broadcasted_iota(jnp.int32, (size, size), 0)
    queries = lax.broadcasted_iota(jnp.int32, (size, size), 1)
    spread = jnp.concatenate(
        [jnp.broadcast_to(words[g : g + 1], (size // count, size)) for g in range(count)], 0
    )
    bits = jnp.right_shift(spread, keys & 31) & 1
    same = keys - queries == jnp.where(diag, 0, 2 * size)
    return jnp.where((bits == 1) | same, jnp.where(pattern < 0, NEG_FILL, 0.0), NEG_FILL)


class Layout:
    def __init__(self, readers, blks, cap):
        self.readers, self.blks, self.cap = readers, blks, cap
        self.reader, self.blk = lax.axis_index("reader"), lax.axis_index("blk")
        self.me = self.reader * blks + self.blk

    def apart(self, device):
        far = jnp.bitwise_xor(device, self.me)
        reader, blk = far // self.blks, lax.rem(far, self.blks)
        return reader, blk // 2, blk & 1

    def row_place(self, device):
        reader, line, core = self.apart(device)
        near = line == 0
        group = jnp.where(near, core, 2 + reader + self.readers * core)
        return group, jnp.where(near, reader, line - 1)

    def half_place(self, bit, device):
        reader, line, core = self.apart(device)
        first = jnp.right_shift(reader, bit) & 1
        top = (self.blks // 2 - 1).bit_length() - 1
        line = sum((jnp.right_shift(line, top - at) & 1) << at for at in range(top + 1))
        low = reader & ((1 << bit) - 1)
        rest = low + (jnp.right_shift(reader, bit + 1) << bit)
        return rest + self.readers // 2 * core, 2 * line + first


def start_copy(place, refs, make):
    group, where = place
    for g, ref in enumerate(refs):

        @pl.when(group == g)
        def _():
            make(ref.at[where]).start()


def pack_kernel(own_hbm, coords_hbm, count_hbm, out_ref, coords_ref, count_ref, sems):
    block = own_hbm.shape[0]
    cap = coords_ref.shape[3]
    copies = [
        pltpu.make_async_copy(coords_hbm, coords_ref, sems.at[0]),
        pltpu.make_async_copy(count_hbm, count_ref, sems.at[1]),
        pltpu.make_async_copy(own_hbm, out_ref.at[0, pl.ds(0, block)], sems.at[2]),
    ]
    for copy in copies:
        copy.start()
    copies[0].wait()
    copies[1].wait()
    lane = lax.broadcasted_iota(jnp.int32, (LIST_ROWS, out_ref.shape[2]), 1)
    row = jnp.zeros(lane.shape, jnp.int32)
    for column in range(3):
        for slot in range(cap):
            row = jnp.where(lane == column * cap + slot, coords_ref[0, column, 0, slot], row)
    row = jnp.where(lane == 3 * cap, count_ref[0, 0], row)
    out_ref[0, block:] = row.astype(jnp.float32).astype(jnp.bfloat16)
    copies[2].wait()


def scan_list(lists_ref, cap, row, column, wanted, found, out_ref, block_of):
    def one_slot(slot, found):
        out_ref[2 * found + 1] = block_of(lists_ref[row, (1 - column) * cap + slot])
        out_ref[2 * found + 2] = lists_ref[row, 2 * cap + slot]
        return found + jnp.where(lists_ref[row, column * cap + slot] == wanted, 1, 0)

    return lax.fori_loop(0, lists_ref[row, 3 * cap], one_slot, found)


def close_work(found, out_ref):
    out_ref[2 * found + 1] = out_ref[2 * found - 1]
    out_ref[2 * found + 2] = -1
    out_ref[0] = (found + 1) // 2


def query_work_kernel(sizes, lists_hbm, work_ref, lists_ref, sem):
    readers, blks, cap = sizes
    layout = Layout(*sizes)
    copy = pltpu.make_async_copy(lists_hbm, lists_ref, sem)
    copy.start()
    copy.wait()

    def one(k, found):
        blk = jnp.bitwise_xor(k, layout.blk)
        row = k // 2 + (k & 1) * (blks // 2)
        put = lambda other: other * blks + blk
        return scan_list(lists_ref, cap, row, 0, layout.blk, found, work_ref, put)

    close_work(lax.fori_loop(0, blks, one, 0), work_ref)


def key_work_kernel(sizes, lists_hbm, work_ref, lists_ref, sem):
    readers, blks, cap = sizes
    layout = Layout(*sizes)
    copy = pltpu.make_async_copy(lists_hbm, lists_ref, sem)
    copy.start()
    copy.wait()

    def one(k, found):
        reader = jnp.bitwise_xor(k, layout.reader)
        put = lambda other: reader * blks + other
        return scan_list(lists_ref, cap, k, 1, layout.reader, found, work_ref, put)

    close_work(lax.fori_loop(0, readers, one, 0), work_ref)


def load(pairs, sems):
    copies = [pltpu.make_async_copy(src, into, sems.at[k]) for k, (src, into) in enumerate(pairs)]
    for copy in copies:
        copy.start()
    return copies


def prepare_kernel(
    own_hbm, cot_hbm, wq_hbm, wk_hbm, wv_hbm,
    query_stack_ref, cot_stack_ref, key_ref, value_ref, wqt_ref, wkt_ref, wvt_ref,
    own_ref, cot_ref, wq_ref, wk_ref, wv_ref, sems,
):
    loads = load((
        (own_hbm, own_ref), (wq_hbm, wq_ref), (wk_hbm, wk_ref), (wv_hbm, wv_ref), (cot_hbm, cot_ref),
    ), sems)
    for copy in loads:
        copy.wait()
    head = own_ref.shape[1] // HEADS
    queries = dot(own_ref[...], wq_ref[...]).astype(jnp.bfloat16) * jnp.bfloat16(head**-0.5)
    for p in range(HEADS // 2):
        pair = slice(2 * head * p, 2 * head * (p + 1))
        query_stack_ref[p] = pair_stack(queries[:, pair]).T
        cot_stack_ref[p] = pair_stack(cot_ref[:, pair]).T
    key_ref[...] = dot(own_ref[...], wk_ref[...]).astype(jnp.bfloat16)
    value_ref[...] = dot(own_ref[...], wv_ref[...]).astype(jnp.bfloat16)
    wqt_ref[...] = wq_ref[...].T
    wkt_ref[...] = wk_ref[...].T
    wvt_ref[...] = wv_ref[...].T


def step_entry(work_ref, index):
    at = 1 + 2 * TILES * index
    return [work_ref[at + 2 * t] for t in range(TILES)], [work_ref[at + 2 * t + 1] for t in range(TILES)]


def run_steps(work_ref, start, wait, body):
    total = work_ref[0]

    def step(index, carry):
        @pl.when(index + 1 < total)
        def _():
            start(lax.rem(index + 1, 2), *step_entry(work_ref, index + 1))

        slot = lax.rem(index, 2)
        wait(slot)
        body(slot, *step_entry(work_ref, index), index)
        return carry

    lax.fori_loop(0, total, step, 0)


def first_step(work_ref, start):
    start(0, *step_entry(work_ref, 0))


class Rows:
    def __init__(self, layout, groups, mask_ref, buf, words, sems, block):
        self.layout, self.groups, self.mask_ref = layout, groups, mask_ref
        self.buf, self.words, self.sems, self.block = buf, words, sems, block

    def rows(self, slot, t):
        into = self.buf.at[slot, pl.ds(t * self.block, self.block)]
        return lambda src: pltpu.make_async_copy(src, into, self.sems.at[slot, t, 0])

    def mask(self, slot, t, pattern):
        return pltpu.make_async_copy(self.mask_ref.at[pattern], self.words.at[slot, t], self.sems.at[slot, t, 1])

    def start(self, slot, blocks, patterns):
        for t in range(TILES):
            start_copy(self.layout.row_place(blocks[t]), self.groups, self.rows(slot, t))
            self.mask(slot, t, jnp.maximum(patterns[t], 0)).start()

    def wait(self, slot):
        for t in range(TILES):
            self.rows(slot, t)(self.groups[0].at[0]).wait()
            self.mask(slot, t, 0).wait()

    def bias(self, slot, blocks, patterns):
        parts = [
            tile_bias(self.words[slot, t], patterns[t], blocks[t] == self.layout.me) for t in range(TILES)
        ]
        return jnp.concatenate(parts, 0)


def forward_kernel(sizes, work_ref, stack_ref, cot_ref, wk_ref, wvt_ref, mask_ref, *refs):
    count = 2 + 2 * sizes[0]
    groups, refs = refs[:count], refs[count:]
    out_ref, sent_ref, stats_ref, buf, words, bias_ref, max_ref, sum_ref, acc_ref, score_ref, sems = refs
    layout = Layout(*sizes)
    block, width = cot_ref.shape
    head = width // HEADS
    rows_in = Rows(layout, groups, mask_ref, buf, words, sems, block)
    first_step(work_ref, rows_in.start)
    max_ref[...] = jnp.full(max_ref.shape, NEG_FILL, jnp.float32)
    sum_ref[...] = jnp.zeros(sum_ref.shape, jnp.float32)
    acc_ref[...] = jnp.zeros(acc_ref.shape, jnp.float32)

    def tiles(slot, blocks, patterns, index):
        rows = buf[slot]
        keys = dot(rows, wk_ref[...]).astype(jnp.bfloat16)
        values = dot(wvt_ref[...], rows, NT).astype(jnp.bfloat16)
        bias_ref[...] = rows_in.bias(slot, blocks, patterns)
        for p in range(HEADS // 2):
            scores = dot(keys[:, 2 * head * p : 2 * head * (p + 1)], stack_ref[p])
            for e in range(2):
                score_ref[2 * p + e] = scores[:, block * e : block * (e + 1)] + bias_ref[...]
        for h in range(HEADS):
            s = score_ref[h]
            old = max_ref[h : h + 1]
            new = jnp.maximum(old, jnp.max(s, axis=0, keepdims=True))
            fade = jnp.exp(old - new)
            expo = jnp.exp(s - new)
            max_ref[h : h + 1] = new
            sum_ref[h : h + 1] = sum_ref[h : h + 1] * fade + jnp.sum(expo, axis=0, keepdims=True)
            at = slice(head * h, head * (h + 1))
            acc_ref[at] = acc_ref[at] * fade + dot(values[at], expo.astype(jnp.bfloat16))

    run_steps(work_ref, rows_in.start, rows_in.wait, tiles)
    inverse = 1.0 / sum_ref[...]
    cot = cot_ref[...].astype(jnp.float32).T
    stats_ref[0:HEADS] = max_ref[...] + jnp.log(sum_ref[...])
    for h in range(HEADS):
        at = slice(head * h, head * (h + 1))
        outputs = acc_ref[at] * inverse[h : h + 1]
        acc_ref[at] = outputs
        stats_ref[HEADS + h : HEADS + h + 1] = jnp.sum(outputs * cot[at], axis=0, keepdims=True)
    sent_ref[...] = jnp.broadcast_to(stats_ref[...], sent_ref.shape)
    out_ref[...] = acc_ref[...].T.astype(out_ref.dtype)


def tile_grads(scores, d_probs, lse, delta):
    prob = jnp.exp(scores - lse)
    return prob.astype(jnp.bfloat16), (prob * (d_probs - delta)).astype(jnp.bfloat16)


def query_grad_kernel(
    sizes, work_ref, stack_hbm, cot_stack_hbm, stats_hbm, wqt_hbm, wk_hbm, wkt_hbm, wv_hbm, mask_ref, *refs
):
    count = 2 + 2 * sizes[0]
    groups, refs = refs[:count], refs[count:]
    part_ref, stack_ref, cot_stack_ref, stats_ref, wqt_ref, wk_ref, wkt_ref, wv_ref = refs[:8]
    buf, words, bias_ref, acc_ref, score_ref, d_prob_ref, sems, w_sems = refs[8:]
    layout = Layout(*sizes)
    block, width = part_ref.shape
    head = width // HEADS
    rows_in = Rows(layout, groups, mask_ref, buf, words, sems, block)
    first_step(work_ref, rows_in.start)
    loads = load((
        (wk_hbm, wk_ref), (stack_hbm, stack_ref), (wv_hbm, wv_ref), (cot_stack_hbm, cot_stack_ref),
        (wkt_hbm, wkt_ref), (stats_hbm.at[0], stats_ref), (wqt_hbm, wqt_ref),
    ), w_sems)
    acc_ref[...] = jnp.zeros(acc_ref.shape, jnp.float32)
    for copy in loads[:6]:
        copy.wait()

    def tiles(slot, blocks, patterns, index):
        rows = buf[slot]
        keys = dot(rows, wk_ref[...]).astype(jnp.bfloat16)
        values = dot(rows, wv_ref[...]).astype(jnp.bfloat16)
        keys_t = dot(wkt_ref[...], rows, NT).astype(jnp.bfloat16)
        bias_ref[...] = rows_in.bias(slot, blocks, patterns)
        for p in range(HEADS // 2):
            pair = slice(2 * head * p, 2 * head * (p + 1))
            scores = dot(keys[:, pair], stack_ref[p])
            d_probs = dot(values[:, pair], cot_stack_ref[p])
            for e in range(2):
                of = slice(block * e, block * (e + 1))
                score_ref[2 * p + e] = scores[:, of] + bias_ref[...]
                d_prob_ref[2 * p + e] = d_probs[:, of]
        for h in range(HEADS):
            _, d_scores = tile_grads(
                score_ref[h], d_prob_ref[h], stats_ref[h : h + 1], stats_ref[HEADS + h : HEADS + h + 1]
            )
            at = slice(head * h, head * (h + 1))
            acc_ref[at] += dot(keys_t[at], d_scores)

    run_steps(work_ref, rows_in.start, rows_in.wait, tiles)
    loads[6].wait()
    grad = (acc_ref[...].T * (head**-0.5)).astype(jnp.bfloat16)
    part_ref[...] = dot(grad, wqt_ref[...])


def key_grad_kernel(
    sizes, bits, work_ref, key_hbm, value_hbm, wq_hbm, wkt_hbm, wvt_hbm, part_hbm, mask_ref, stats_all_ref, *refs
):
    readers = sizes[0]
    count = 2 + 2 * readers
    groups, refs = refs[:count], refs[count:]
    halves, refs = (refs[:readers], refs[readers : 2 * readers]), refs[2 * readers :]
    out_ref, key_ref, value_ref, part_ref, wq_ref, wkt_ref, wvt_ref, buf, words, cot_buf, stats, bias_ref = refs[:12]
    query_stack_ref, cot_stack_ref, score_ref, d_prob_ref, key_acc, value_acc, sems, c_sems, w_sems = refs[12:]
    layout = Layout(*sizes)
    block, width = out_ref.shape
    head = width // HEADS
    rows_in = Rows(layout, groups, mask_ref, buf, words, sems, block)

    def half_copy(slot, t, k):
        into = cot_buf.at[slot, pl.ds(t * block + block // 2 * k, block // 2)]
        return lambda src: pltpu.make_async_copy(src, into, c_sems.at[slot, t, k])

    def stats_copy(slot, t, query):
        return pltpu.make_async_copy(stats_all_ref.at[query], stats.at[slot, t], c_sems.at[slot, t, 2])

    def start(slot, blocks, patterns):
        rows_in.start(slot, blocks, patterns)
        for t in range(TILES):
            stats_copy(slot, t, blocks[t]).start()
            for k in range(2):
                start_copy(layout.half_place(bits[k], blocks[t]), halves[k], half_copy(slot, t, k))

    def wait(slot):
        rows_in.wait(slot)
        for t in range(TILES):
            stats_copy(slot, t, 0).wait()
            for k in range(2):
                half_copy(slot, t, k)(halves[k][0].at[0]).wait()

    first_step(work_ref, start)
    loads = load((
        (wq_hbm, wq_ref), (key_hbm, key_ref), (value_hbm, value_ref),
        (wkt_hbm, wkt_ref), (wvt_hbm, wvt_ref), (part_hbm, part_ref),
    ), w_sems)
    key_acc[...] = jnp.zeros(key_acc.shape, jnp.float32)
    value_acc[...] = jnp.zeros(value_acc.shape, jnp.float32)
    for copy in loads[:3]:
        copy.wait()

    def tiles(slot, blocks, patterns, index):
        queries = dot(buf[slot], wq_ref[...]).astype(jnp.bfloat16) * jnp.bfloat16(head**-0.5)
        bias_ref[...] = rows_in.bias(slot, blocks, patterns)
        cots = cot_buf[slot]
        pairs = [slice(2 * head * p, 2 * head * (p + 1)) for p in range(HEADS // 2)]
        of_tile = [slice(block * t, block * (t + 1)) for t in range(TILES)]
        for p, pair in enumerate(pairs):
            query_stack_ref[p] = jnp.concatenate([pair_stack(queries[of, pair]) for of in of_tile], 0)
            cot_stack_ref[p] = jnp.concatenate([pair_stack(cots[of, pair]) for of in of_tile], 0)
            score_ref[p] = dot(key_ref[:, pair], query_stack_ref[p], NT)
            d_prob_ref[p] = dot(value_ref[:, pair], cot_stack_ref[p], NT)
        for p, pair in enumerate(pairs):
            probs, d_scores = [], []
            for t in range(TILES):
                for e in range(2):
                    h = 2 * p + e
                    of = slice(block * (2 * t + e), block * (2 * t + e + 1))
                    prob, d_score = tile_grads(
                        score_ref[p, :, of] + bias_ref[of_tile[t]], d_prob_ref[p, :, of], stats[slot, t, h : h + 1],
                        stats[slot, t, HEADS + h : HEADS + h + 1],
                    )
                    probs.append(prob)
                    d_scores.append(d_score)
            value_acc[:, pair] += dot(jnp.concatenate(probs, 1), cot_stack_ref[p])
            key_acc[:, pair] += dot(jnp.concatenate(d_scores, 1), query_stack_ref[p])

    run_steps(work_ref, start, wait, tiles)
    for copy in loads[3:]:
        copy.wait()
    grad = part_ref[...] + dot(key_acc[...].astype(jnp.bfloat16), wkt_ref[...])
    grad = grad + dot(value_acc[...].astype(jnp.bfloat16), wvt_ref[...])
    out_ref[...] = grad.astype(out_ref.dtype)


VMEM = pl.BlockSpec(memory_space=pltpu.VMEM)
SMEM = pl.BlockSpec(memory_space=pltpu.SMEM)
HBM = pl.BlockSpec(memory_space=pltpu.HBM)


def swap(block, mask):
    axes = ("reader", "blk")
    count = lax.axis_size("reader") * lax.axis_size("blk")
    return lax.ppermute(block, axes, [(i, i ^ mask) for i in range(count)])


def after(value, *others):
    return lax.optimization_barrier((value, *others))[0]


def local(features, cotangent, w_query, w_key, w_value, tile_coords, tile_count, mask_table):
    block, width = features.shape
    readers, blks, cap = lax.axis_size("reader"), lax.axis_size("blk"), tile_coords.shape[2]
    assert block == mask_table.shape[1] and 3 * cap < 128
    sizes = (readers, blks, cap)
    devices, lines = readers * blks, blks // 2
    f32, bf16, i32 = jnp.float32, jnp.bfloat16, jnp.int32
    shape = jax.ShapeDtypeStruct
    masks = mask_table.transpose(0, 2, 1)
    words = masks.shape[1]
    head = width // HEADS
    half = block // 2
    some = pltpu.CompilerParams(vmem_limit_bytes=VMEM_SOME)
    most = pltpu.CompilerParams(vmem_limit_bytes=VMEM_MOST)
    axes = ("reader", "blk")

    def cost(tiles):
        return pl.CostEstimate(flops=tiles * 200_000_000, bytes_accessed=4_000_000, transcendentals=tiles * 131072)

    packed = pl.pallas_call(
        pack_kernel,
        out_shape=shape((1, block + LIST_ROWS, width), bf16),
        in_specs=[HBM, HBM, HBM],
        out_specs=VMEM,
        scratch_shapes=[
            pltpu.SMEM((1, 3, 1, cap), i32), pltpu.SMEM((1, 1), i32), pltpu.SemaphoreType.DMA((3,)),
        ],
        compiler_params=most,
        name="pack",
    )(features, tile_coords.transpose(0, 3, 1, 2), tile_count)
    lined = [packed] + [swap(packed, 2 * k) for k in range(1, lines)]

    nearest_first = sorted(range(1, readers), key=lambda k: (k.bit_count(), k))

    def to_readers(block):
        there = {k: swap(block, blks * k) for k in nearest_first}
        return [there[k] for k in range(1, readers)]

    columns = [packed] + to_readers(packed)

    bits = (0, (readers - 1).bit_length() - 1)
    cot_parts = [cotangent[None, half * k : half * (k + 1)] for k in range(2)]
    cot_other = [swap(part, blks << bit) for part, bit in zip(cot_parts, bits)]

    column_lists = jnp.concatenate([entry[:, block:, :128] for entry in columns], 0)
    line_lists = jnp.concatenate([entry[:, block:, :128] for entry in lined], 0)
    row_lists = jnp.concatenate([line_lists, swap(line_lists, 1)], 0)

    def work(kernel, lists, count, name):
        return pl.pallas_call(
            functools.partial(kernel, sizes),
            out_shape=shape((2 * count * cap + 5,), i32),
            in_specs=[HBM],
            out_specs=SMEM,
            scratch_shapes=[pltpu.SMEM((count, 128), i32), pltpu.SemaphoreType.DMA],
            compiler_params=some,
            cost_estimate=cost(1),
            name=name,
        )(lists[:, 0].astype(i32))

    query_work = work(query_work_kernel, row_lists, blks, "query_work")
    key_work = work(key_work_kernel, column_lists, readers, "key_work")

    stacks = shape((HEADS // 2, 2 * head, 2 * block), bf16)
    own = shape((block, width), bf16)
    square = shape((width, width), bf16)
    weight = pltpu.VMEM((width, width), bf16)
    rows_low, rows_wide = pltpu.VMEM((block, width), bf16), pltpu.VMEM((block, width), f32)
    prepared = pl.pallas_call(
        prepare_kernel,
        out_shape=(stacks, stacks, own, own, square, square, square),
        in_specs=[HBM] * 5,
        out_specs=(VMEM,) * 7,
        scratch_shapes=[rows_low, rows_low, weight, weight, weight, pltpu.SemaphoreType.DMA((5,))],
        compiler_params=most,
        cost_estimate=cost(2),
        name="prepare",
    )(after(features, row_lists), cotangent, w_query, w_key, w_value)
    query_stack, cot_stack, keys, values, w_query_t, w_key_t, w_value_t = prepared

    near = jnp.concatenate([entry[:, :block] for entry in columns], 0)
    line = jnp.concatenate([entry[:, :block] for entry in lined[1:]], 0)
    line = after(line, columns, cot_other)
    here = [line] + to_readers(line)
    other_near = swap(after(near, query_work), 1)
    other_line = swap(after(line, query_work), 1)
    rows_all = [near, other_near, *here, other_line] + [swap(group, 1) for group in here[1:]]

    pairs = [part for k in range(2) for part in (cot_parts[k], cot_other[k])]
    pieces = [after(jnp.concatenate(pairs, 0), line, row_lists)]
    done_first = (query_work, key_work, prepared)
    mask = blks // 2
    while mask > 1:
        pieces += [swap(after(piece, done_first) if at else piece, mask) for at, piece in enumerate(pieces)]
        mask //= 2

    cots_here = []
    for k in range(2):
        part = jnp.concatenate([piece[2 * k : 2 * k + 2] for piece in pieces], 0)
        masks_left = [m for m in range(1, readers) if not m >> bits[k] & 1]
        cots_here.append((part, [swap(after(part, here), blks * m) for m in masks_left]))

    stack_space = pltpu.VMEM(stacks.shape, bf16)
    buffer = pltpu.VMEM((2, TILES * block, width), bf16)
    word_buffer = pltpu.VMEM((2, TILES, words, block), i32)
    bias = pltpu.VMEM((TILES * block, block), f32)
    turned = pltpu.VMEM((width, block), f32)
    per_head = pltpu.VMEM((HEADS, block), f32)
    own_stats = pltpu.VMEM((2 * HEADS, block), f32)
    met = pltpu.VMEM((HEADS, TILES * block, block), f32)
    pair_met = pltpu.VMEM((HEADS // 2, block, 2 * TILES * block), f32)
    pair_rows = pltpu.VMEM((HEADS // 2, 2 * TILES * block, 2 * head), bf16)
    row_sems = pltpu.SemaphoreType.DMA((2, TILES, 2))

    attn_out, stats = pl.pallas_call(
        functools.partial(forward_kernel, sizes),
        out_shape=(own, shape((devices, 2 * HEADS, block), f32)),
        in_specs=[SMEM] + [VMEM] * 4 + [HBM] * (3 + 2 * readers),
        out_specs=(VMEM, VMEM),
        scratch_shapes=[own_stats, buffer, word_buffer, bias, per_head, per_head, turned, met, row_sems],
        compiler_params=some,
        cost_estimate=cost(5),
        name="forward",
    )(query_work, query_stack, cotangent, w_key, w_value_t, masks, *rows_all)

    stats_all = lax.all_to_all(stats, axes, 0, 0, tiled=True)

    query_part = pl.pallas_call(
        functools.partial(query_grad_kernel, sizes),
        out_shape=shape((block, width), f32),
        in_specs=[SMEM] + [HBM] * (10 + 2 * readers),
        out_specs=VMEM,
        scratch_shapes=[
            stack_space, stack_space, own_stats, weight, weight, weight, weight, buffer, word_buffer, bias, turned,
            met, met, row_sems, pltpu.SemaphoreType.DMA((7,)),
        ],
        compiler_params=most,
        cost_estimate=cost(5),
        name="query_grad",
    )(query_work, query_stack, cot_stack, stats, w_query_t, w_key, w_key_t, w_value, masks, *rows_all)

    cots_all = []
    for first, rest in cots_here:
        cots_all += [first, *rest, swap(after(first, stats), 1)]
        cots_all += [swap(after(part, query_part), 1) for part in rest]

    grad_features = pl.pallas_call(
        functools.partial(key_grad_kernel, sizes, bits),
        out_shape=own,
        in_specs=[SMEM] + [HBM] * (10 + 4 * readers),
        out_specs=VMEM,
        scratch_shapes=[
            rows_low, rows_low, rows_wide, weight, weight, weight,
            buffer, word_buffer, buffer, pltpu.VMEM((2, TILES, 2 * HEADS, block), f32), bias,
            pair_rows, pair_rows, pair_met, pair_met, rows_wide, rows_wide,
            row_sems, pltpu.SemaphoreType.DMA((2, TILES, 3)), pltpu.SemaphoreType.DMA((6,)),
        ],
        compiler_params=most,
        cost_estimate=cost(5),
        name="key_grad",
    )(key_work, keys, values, w_query, w_key_t, w_value_t, query_part, masks, stats_all, *rows_all, *cots_all)
    return attn_out, grad_features


def solution(mesh):
    return jax.shard_map(
        local,
        mesh=mesh,
        in_specs=(
            P(("reader", "blk"), None),
            P(("reader", "blk"), None),
            P(),
            P(),
            P(),
            P("reader", "blk", None, None),
            P("reader", "blk"),
            P(),
        ),
        out_specs=(P(("reader", "blk"), None), P(("reader", "blk"), None)),
        check_vma=False,
    )
```

```python
import functools

import jax
import jax.numpy as jnp
from jax import lax
from jax.experimental import pallas as pl
from jax.experimental.pallas import tpu as pltpu
from jax.sharding import PartitionSpec as P

HEADS = 8
NEG_FILL = -1e30
NT = (((1,), (1,)), ((), ()))
NN = (((1,), (0,)), ((), ()))
TILES = 2
LIST_ROWS = 16
VMEM_SOME = 40 * 1024 * 1024
VMEM_MOST = 58 * 1024 * 1024


def dot(a, b, dims=NN):
    return lax.dot_general(a, b, dims, preferred_element_type=jnp.float32)


def pair_stack(rows):
    lane = lax.broadcasted_iota(jnp.int32, rows.shape, 1)
    half = rows.shape[1] // 2
    zero = jnp.zeros_like(rows)
    return jnp.concatenate([jnp.where(lane < half, rows, zero), jnp.where(lane >= half, rows, zero)], 0)


def tile_bias(words, pattern, diag):
    count, size = words.shape
    keys = lax.broadcasted_iota(jnp.int32, (size, size), 0)
    queries = lax.broadcasted_iota(jnp.int32, (size, size), 1)
    spread = jnp.concatenate(
        [jnp.broadcast_to(words[g : g + 1], (size // count, size)) for g in range(count)], 0
    )
    bits = jnp.right_shift(spread, keys & 31) & 1
    same = keys - queries == jnp.where(diag, 0, 2 * size)
    return jnp.where((bits == 1) | same, jnp.where(pattern < 0, NEG_FILL, 0.0), NEG_FILL)


class Layout:
    def __init__(self, readers, blks, cap):
        self.readers, self.blks, self.cap = readers, blks, cap
        self.reader, self.blk = lax.axis_index("reader"), lax.axis_index("blk")
        self.me = self.reader * blks + self.blk

    def apart(self, device):
        far = jnp.bitwise_xor(device, self.me)
        reader, blk = far // self.blks, lax.rem(far, self.blks)
        return reader, blk // 2, blk & 1

    def row_place(self, device):
        reader, line, core = self.apart(device)
        near = line == 0
        group = jnp.where(near, 0, reader) + self.readers * core
        index = jnp.where(reader == 0, self.readers, 0) + line - 1
        return group, jnp.where(near, reader, index)

    def half_place(self, bit, device):
        reader, line, core = self.apart(device)
        first = jnp.right_shift(reader, bit) & 1
        top = (self.blks // 2 - 1).bit_length() - 1
        line = sum((jnp.right_shift(line, top - at) & 1) << at for at in range(top + 1))
        low = reader & ((1 << bit) - 1)
        rest = low + (jnp.right_shift(reader, bit + 1) << bit)
        return rest + self.readers // 2 * core, 2 * line + first


def start_copy(place, refs, make):
    group, where = place
    for g, ref in enumerate(refs):

        @pl.when(group == g)
        def _():
            make(ref.at[where]).start()


def pack_kernel(own_hbm, coords_hbm, count_hbm, out_ref, coords_ref, count_ref, sems):
    block = own_hbm.shape[0]
    cap = coords_ref.shape[3]
    copies = [
        pltpu.make_async_copy(coords_hbm, coords_ref, sems.at[0]),
        pltpu.make_async_copy(count_hbm, count_ref, sems.at[1]),
        pltpu.make_async_copy(own_hbm, out_ref.at[0, pl.ds(0, block)], sems.at[2]),
    ]
    for copy in copies:
        copy.start()
    copies[0].wait()
    copies[1].wait()
    lane = lax.broadcasted_iota(jnp.int32, (LIST_ROWS, out_ref.shape[2]), 1)
    row = jnp.zeros(lane.shape, jnp.int32)
    for column in range(3):
        for slot in range(cap):
            row = jnp.where(lane == column * cap + slot, coords_ref[0, column, 0, slot], row)
    row = jnp.where(lane == 3 * cap, count_ref[0, 0], row)
    out_ref[0, block:] = row.astype(jnp.float32).astype(jnp.bfloat16)
    copies[2].wait()


def scan_list(lists_ref, cap, row, column, wanted, found, out_ref, block_of):
    def one_slot(slot, found):
        out_ref[2 * found + 1] = block_of(lists_ref[row, (1 - column) * cap + slot])
        out_ref[2 * found + 2] = lists_ref[row, 2 * cap + slot]
        return found + jnp.where(lists_ref[row, column * cap + slot] == wanted, 1, 0)

    return lax.fori_loop(0, lists_ref[row, 3 * cap], one_slot, found)


def close_work(found, out_ref):
    out_ref[2 * found + 1] = out_ref[2 * found - 1]
    out_ref[2 * found + 2] = -1
    out_ref[0] = (found + 1) // 2


def query_work_kernel(sizes, lists_hbm, work_ref, lists_ref, sem):
    readers, blks, cap = sizes
    layout = Layout(*sizes)
    copy = pltpu.make_async_copy(lists_hbm, lists_ref, sem)
    copy.start()
    copy.wait()

    def one(k, found):
        blk = jnp.bitwise_xor(k, layout.blk)
        row = k // 2 + (k & 1) * (blks // 2)
        put = lambda other: other * blks + blk
        return scan_list(lists_ref, cap, row, 0, layout.blk, found, work_ref, put)

    close_work(lax.fori_loop(0, blks, one, 0), work_ref)


def key_work_kernel(sizes, lists_hbm, work_ref, lists_ref, sem):
    readers, blks, cap = sizes
    layout = Layout(*sizes)
    copy = pltpu.make_async_copy(lists_hbm, lists_ref, sem)
    copy.start()
    copy.wait()

    def one(k, found):
        reader = jnp.bitwise_xor(k, layout.reader)
        put = lambda other: reader * blks + other
        return scan_list(lists_ref, cap, k, 1, layout.reader, found, work_ref, put)

    close_work(lax.fori_loop(0, readers, one, 0), work_ref)


def load(pairs, sems):
    copies = [pltpu.make_async_copy(src, into, sems.at[k]) for k, (src, into) in enumerate(pairs)]
    for copy in copies:
        copy.start()
    return copies


def prepare_kernel(
    own_hbm, cot_hbm, wq_hbm, wk_hbm, wv_hbm,
    query_stack_ref, cot_stack_ref, key_ref, value_ref, wqt_ref, wkt_ref, wvt_ref,
    own_ref, cot_ref, wq_ref, wk_ref, wv_ref, sems,
):
    loads = load((
        (own_hbm, own_ref), (wq_hbm, wq_ref), (wk_hbm, wk_ref), (wv_hbm, wv_ref), (cot_hbm, cot_ref),
    ), sems)
    for copy in loads:
        copy.wait()
    head = own_ref.shape[1] // HEADS
    queries = dot(own_ref[...], wq_ref[...]).astype(jnp.bfloat16) * jnp.bfloat16(head**-0.5)
    for p in range(HEADS // 2):
        pair = slice(2 * head * p, 2 * head * (p + 1))
        query_stack_ref[p] = pair_stack(queries[:, pair]).T
        cot_stack_ref[p] = pair_stack(cot_ref[:, pair]).T
    key_ref[...] = dot(own_ref[...], wk_ref[...]).astype(jnp.bfloat16)
    value_ref[...] = dot(own_ref[...], wv_ref[...]).astype(jnp.bfloat16)
    wqt_ref[...] = wq_ref[...].T
    wkt_ref[...] = wk_ref[...].T
    wvt_ref[...] = wv_ref[...].T


def step_entry(work_ref, index):
    at = 1 + 2 * TILES * index
    return [work_ref[at + 2 * t] for t in range(TILES)], [work_ref[at + 2 * t + 1] for t in range(TILES)]


def run_steps(work_ref, start, wait, body):
    total = work_ref[0]

    def step(index, carry):
        @pl.when(index + 1 < total)
        def _():
            start(lax.rem(index + 1, 2), *step_entry(work_ref, index + 1))

        slot = lax.rem(index, 2)
        wait(slot)
        body(slot, *step_entry(work_ref, index), index)
        return carry

    lax.fori_loop(0, total, step, 0)


def first_step(work_ref, start):
    start(0, *step_entry(work_ref, 0))


class Rows:
    def __init__(self, layout, groups, mask_ref, buf, words, sems, block):
        self.layout, self.groups, self.mask_ref = layout, groups, mask_ref
        self.buf, self.words, self.sems, self.block = buf, words, sems, block

    def rows(self, slot, t):
        into = self.buf.at[slot, pl.ds(t * self.block, self.block)]
        return lambda src: pltpu.make_async_copy(src, into, self.sems.at[slot, t, 0])

    def mask(self, slot, t, pattern):
        return pltpu.make_async_copy(self.mask_ref.at[pattern], self.words.at[slot, t], self.sems.at[slot, t, 1])

    def start(self, slot, blocks, patterns):
        for t in range(TILES):
            start_copy(self.layout.row_place(blocks[t]), self.groups, self.rows(slot, t))
            self.mask(slot, t, jnp.maximum(patterns[t], 0)).start()

    def wait(self, slot):
        for t in range(TILES):
            self.rows(slot, t)(self.groups[0].at[0]).wait()
            self.mask(slot, t, 0).wait()

    def bias(self, slot, blocks, patterns):
        parts = [
            tile_bias(self.words[slot, t], patterns[t], blocks[t] == self.layout.me) for t in range(TILES)
        ]
        return jnp.concatenate(parts, 0)


def forward_kernel(sizes, work_ref, stack_ref, cot_ref, wk_ref, wvt_ref, mask_ref, *refs):
    count = 2 * sizes[0]
    groups, refs = refs[:count], refs[count:]
    out_ref, sent_ref, stats_ref, buf, words, bias_ref, max_ref, sum_ref, acc_ref, score_ref, sems = refs
    layout = Layout(*sizes)
    block, width = cot_ref.shape
    head = width // HEADS
    rows_in = Rows(layout, groups, mask_ref, buf, words, sems, block)
    first_step(work_ref, rows_in.start)
    max_ref[...] = jnp.full(max_ref.shape, NEG_FILL, jnp.float32)
    sum_ref[...] = jnp.zeros(sum_ref.shape, jnp.float32)
    acc_ref[...] = jnp.zeros(acc_ref.shape, jnp.float32)

    def tiles(slot, blocks, patterns, index):
        rows = buf[slot]
        keys = dot(rows, wk_ref[...]).astype(jnp.bfloat16)
        values = dot(wvt_ref[...], rows, NT).astype(jnp.bfloat16)
        bias_ref[...] = rows_in.bias(slot, blocks, patterns)
        for p in range(HEADS // 2):
            scores = dot(keys[:, 2 * head * p : 2 * head * (p + 1)], stack_ref[p])
            for e in range(2):
                score_ref[2 * p + e] = scores[:, block * e : block * (e + 1)] + bias_ref[...]
        for h in range(HEADS):
            s = score_ref[h]
            old = max_ref[h : h + 1]
            new = jnp.maximum(old, jnp.max(s, axis=0, keepdims=True))
            fade = jnp.exp(old - new)
            expo = jnp.exp(s - new)
            max_ref[h : h + 1] = new
            sum_ref[h : h + 1] = sum_ref[h : h + 1] * fade + jnp.sum(expo, axis=0, keepdims=True)
            at = slice(head * h, head * (h + 1))
            acc_ref[at] = acc_ref[at] * fade + dot(values[at], expo.astype(jnp.bfloat16))

    run_steps(work_ref, rows_in.start, rows_in.wait, tiles)
    inverse = 1.0 / sum_ref[...]
    cot = cot_ref[...].astype(jnp.float32).T
    stats_ref[0:HEADS] = max_ref[...] + jnp.log(sum_ref[...])
    for h in range(HEADS):
        at = slice(head * h, head * (h + 1))
        outputs = acc_ref[at] * inverse[h : h + 1]
        acc_ref[at] = outputs
        stats_ref[HEADS + h : HEADS + h + 1] = jnp.sum(outputs * cot[at], axis=0, keepdims=True)
    sent_ref[...] = jnp.broadcast_to(stats_ref[...], sent_ref.shape)
    out_ref[...] = acc_ref[...].T.astype(out_ref.dtype)


def tile_grads(scores, d_probs, lse, delta):
    prob = jnp.exp(scores - lse)
    return prob.astype(jnp.bfloat16), (prob * (d_probs - delta)).astype(jnp.bfloat16)


def query_grad_kernel(
    sizes, work_ref, stack_hbm, cot_stack_hbm, stats_hbm, wqt_hbm, wk_hbm, wkt_hbm, wv_hbm, mask_ref, *refs
):
    count = 2 * sizes[0]
    groups, refs = refs[:count], refs[count:]
    part_ref, stack_ref, cot_stack_ref, stats_ref, wqt_ref, wk_ref, wkt_ref, wv_ref = refs[:8]
    buf, words, bias_ref, acc_ref, score_ref, d_prob_ref, sems, w_sems = refs[8:]
    layout = Layout(*sizes)
    block, width = part_ref.shape
    head = width // HEADS
    rows_in = Rows(layout, groups, mask_ref, buf, words, sems, block)
    first_step(work_ref, rows_in.start)
    loads = load((
        (wk_hbm, wk_ref), (stack_hbm, stack_ref), (wv_hbm, wv_ref), (cot_stack_hbm, cot_stack_ref),
        (wkt_hbm, wkt_ref), (stats_hbm.at[0], stats_ref), (wqt_hbm, wqt_ref),
    ), w_sems)
    acc_ref[...] = jnp.zeros(acc_ref.shape, jnp.float32)
    for copy in loads[:6]:
        copy.wait()

    def tiles(slot, blocks, patterns, index):
        rows = buf[slot]
        keys = dot(rows, wk_ref[...]).astype(jnp.bfloat16)
        values = dot(rows, wv_ref[...]).astype(jnp.bfloat16)
        keys_t = dot(wkt_ref[...], rows, NT).astype(jnp.bfloat16)
        bias_ref[...] = rows_in.bias(slot, blocks, patterns)
        for p in range(HEADS // 2):
            pair = slice(2 * head * p, 2 * head * (p + 1))
            scores = dot(keys[:, pair], stack_ref[p])
            d_probs = dot(values[:, pair], cot_stack_ref[p])
            for e in range(2):
                of = slice(block * e, block * (e + 1))
                score_ref[2 * p + e] = scores[:, of] + bias_ref[...]
                d_prob_ref[2 * p + e] = d_probs[:, of]
        for h in range(HEADS):
            _, d_scores = tile_grads(
                score_ref[h], d_prob_ref[h], stats_ref[h : h + 1], stats_ref[HEADS + h : HEADS + h + 1]
            )
            at = slice(head * h, head * (h + 1))
            acc_ref[at] += dot(keys_t[at], d_scores)

    run_steps(work_ref, rows_in.start, rows_in.wait, tiles)
    loads[6].wait()
    grad = (acc_ref[...].T * (head**-0.5)).astype(jnp.bfloat16)
    part_ref[...] = dot(grad, wqt_ref[...])


def key_grad_kernel(
    sizes, bits, work_ref, key_hbm, value_hbm, wq_hbm, wkt_hbm, wvt_hbm, part_hbm, mask_ref, stats_all_ref, *refs
):
    readers = sizes[0]
    count = 2 * readers
    groups, refs = refs[:count], refs[count:]
    halves, refs = (refs[:readers], refs[readers : 2 * readers]), refs[2 * readers :]
    out_ref, key_ref, value_ref, part_ref, wq_ref, wkt_ref, wvt_ref, buf, words, cot_buf, stats, bias_ref = refs[:12]
    query_stack_ref, cot_stack_ref, score_ref, d_prob_ref, key_acc, value_acc, sems, c_sems, w_sems = refs[12:]
    layout = Layout(*sizes)
    block, width = out_ref.shape
    head = width // HEADS
    rows_in = Rows(layout, groups, mask_ref, buf, words, sems, block)

    def half_copy(slot, t, k):
        into = cot_buf.at[slot, pl.ds(t * block + block // 2 * k, block // 2)]
        return lambda src: pltpu.make_async_copy(src, into, c_sems.at[slot, t, k])

    def stats_copy(slot, t, query):
        return pltpu.make_async_copy(stats_all_ref.at[query], stats.at[slot, t], c_sems.at[slot, t, 2])

    def start(slot, blocks, patterns):
        rows_in.start(slot, blocks, patterns)
        for t in range(TILES):
            stats_copy(slot, t, blocks[t]).start()
            for k in range(2):
                start_copy(layout.half_place(bits[k], blocks[t]), halves[k], half_copy(slot, t, k))

    def wait(slot):
        rows_in.wait(slot)
        for t in range(TILES):
            stats_copy(slot, t, 0).wait()
            for k in range(2):
                half_copy(slot, t, k)(halves[k][0].at[0]).wait()

    first_step(work_ref, start)
    loads = load((
        (wq_hbm, wq_ref), (key_hbm, key_ref), (value_hbm, value_ref),
        (wkt_hbm, wkt_ref), (wvt_hbm, wvt_ref), (part_hbm, part_ref),
    ), w_sems)
    key_acc[...] = jnp.zeros(key_acc.shape, jnp.float32)
    value_acc[...] = jnp.zeros(value_acc.shape, jnp.float32)
    for copy in loads[:3]:
        copy.wait()

    def tiles(slot, blocks, patterns, index):
        queries = dot(buf[slot], wq_ref[...]).astype(jnp.bfloat16) * jnp.bfloat16(head**-0.5)
        bias_ref[...] = rows_in.bias(slot, blocks, patterns)
        cots = cot_buf[slot]
        pairs = [slice(2 * head * p, 2 * head * (p + 1)) for p in range(HEADS // 2)]
        of_tile = [slice(block * t, block * (t + 1)) for t in range(TILES)]
        for p, pair in enumerate(pairs):
            query_stack_ref[p] = jnp.concatenate([pair_stack(queries[of, pair]) for of in of_tile], 0)
            cot_stack_ref[p] = jnp.concatenate([pair_stack(cots[of, pair]) for of in of_tile], 0)
            score_ref[p] = dot(key_ref[:, pair], query_stack_ref[p], NT)
            d_prob_ref[p] = dot(value_ref[:, pair], cot_stack_ref[p], NT)
        for p, pair in enumerate(pairs):
            probs, d_scores = [], []
            for t in range(TILES):
                for e in range(2):
                    h = 2 * p + e
                    of = slice(block * (2 * t + e), block * (2 * t + e + 1))
                    prob, d_score = tile_grads(
                        score_ref[p, :, of] + bias_ref[of_tile[t]], d_prob_ref[p, :, of], stats[slot, t, h : h + 1],
                        stats[slot, t, HEADS + h : HEADS + h + 1],
                    )
                    probs.append(prob)
                    d_scores.append(d_score)
            value_acc[:, pair] += dot(jnp.concatenate(probs, 1), cot_stack_ref[p])
            key_acc[:, pair] += dot(jnp.concatenate(d_scores, 1), query_stack_ref[p])

    run_steps(work_ref, start, wait, tiles)
    for copy in loads[3:]:
        copy.wait()
    grad = part_ref[...] + dot(key_acc[...].astype(jnp.bfloat16), wkt_ref[...])
    grad = grad + dot(value_acc[...].astype(jnp.bfloat16), wvt_ref[...])
    out_ref[...] = grad.astype(out_ref.dtype)


VMEM = pl.BlockSpec(memory_space=pltpu.VMEM)
SMEM = pl.BlockSpec(memory_space=pltpu.SMEM)
HBM = pl.BlockSpec(memory_space=pltpu.HBM)


def swap(block, mask):
    axes = ("reader", "blk")
    count = lax.axis_size("reader") * lax.axis_size("blk")
    return lax.ppermute(block, axes, [(i, i ^ mask) for i in range(count)])


def after(value, *others):
    return lax.optimization_barrier((value, *others))[0]


def local(features, cotangent, w_query, w_key, w_value, tile_coords, tile_count, mask_table):
    block, width = features.shape
    readers, blks, cap = lax.axis_size("reader"), lax.axis_size("blk"), tile_coords.shape[2]
    assert block == mask_table.shape[1] and 3 * cap < 128
    sizes = (readers, blks, cap)
    devices, lines = readers * blks, blks // 2
    f32, bf16, i32 = jnp.float32, jnp.bfloat16, jnp.int32
    shape = jax.ShapeDtypeStruct
    masks = mask_table.transpose(0, 2, 1)
    words = masks.shape[1]
    head = width // HEADS
    half = block // 2
    some = pltpu.CompilerParams(vmem_limit_bytes=VMEM_SOME)
    most = pltpu.CompilerParams(vmem_limit_bytes=VMEM_MOST)
    axes = ("reader", "blk")

    def cost(tiles):
        return pl.CostEstimate(flops=tiles * 200_000_000, bytes_accessed=4_000_000, transcendentals=tiles * 131072)

    packed = pl.pallas_call(
        pack_kernel,
        out_shape=shape((1, block + LIST_ROWS, width), bf16),
        in_specs=[HBM, HBM, HBM],
        out_specs=VMEM,
        scratch_shapes=[
            pltpu.SMEM((1, 3, 1, cap), i32), pltpu.SMEM((1, 1), i32), pltpu.SemaphoreType.DMA((3,)),
        ],
        compiler_params=most,
        name="pack",
    )(features, tile_coords.transpose(0, 3, 1, 2), tile_count)
    lined = [packed] + [swap(packed, 2 * k) for k in range(1, lines)]

    nearest_first = sorted(range(1, readers), key=lambda k: (k.bit_count(), k))

    def to_readers(block):
        there = {k: swap(block, blks * k) for k in nearest_first}
        return [there[k] for k in range(1, readers)]

    columns = [packed] + to_readers(packed)

    bits = (0, (readers - 1).bit_length() - 1)
    cot_parts = [cotangent[None, half * k : half * (k + 1)] for k in range(2)]
    cot_other = [swap(part, blks << bit) for part, bit in zip(cot_parts, bits)]

    column_lists = jnp.concatenate([entry[:, block:, :128] for entry in columns], 0)

    def work(kernel, lists, count, name):
        return pl.pallas_call(
            functools.partial(kernel, sizes),
            out_shape=shape((2 * count * cap + 5,), i32),
            in_specs=[HBM],
            out_specs=SMEM,
            scratch_shapes=[pltpu.SMEM((count, 128), i32), pltpu.SemaphoreType.DMA],
            compiler_params=some,
            cost_estimate=cost(1),
            name=name,
        )(lists[:, 0].astype(i32))

    key_work = work(key_work_kernel, column_lists, readers, "key_work")

    stacks = shape((HEADS // 2, 2 * head, 2 * block), bf16)
    own = shape((block, width), bf16)
    square = shape((width, width), bf16)
    weight = pltpu.VMEM((width, width), bf16)
    rows_low, rows_wide = pltpu.VMEM((block, width), bf16), pltpu.VMEM((block, width), f32)
    prepared = pl.pallas_call(
        prepare_kernel,
        out_shape=(stacks, stacks, own, own, square, square, square),
        in_specs=[HBM] * 5,
        out_specs=(VMEM,) * 7,
        scratch_shapes=[rows_low, rows_low, weight, weight, weight, pltpu.SemaphoreType.DMA((5,))],
        compiler_params=most,
        cost_estimate=cost(2),
        name="prepare",
    )(after(features, columns), cotangent, w_query, w_key, w_value)
    query_stack, cot_stack, keys, values, w_query_t, w_key_t, w_value_t = prepared

    line = jnp.concatenate([entry[:, :block] for entry in lined[1:]], 0)
    line = after(line, columns, cot_other)
    there = to_readers(line)
    near = jnp.concatenate([entry[:, :block] for entry in columns] + [line], 0)

    pairs = [part for k in range(2) for part in (cot_parts[k], cot_other[k])]
    pieces = [after(jnp.concatenate(pairs, 0), line)]
    done_first = (key_work, prepared)
    mask = blks // 2
    while mask > 1:
        pieces += [swap(after(piece, done_first) if at else piece, mask) for at, piece in enumerate(pieces)]
        mask //= 2

    line_lists = jnp.concatenate([entry[:, block:, :128] for entry in lined], 0)
    line_lists = after(line_lists, pieces[lines // 2])
    row_lists = jnp.concatenate([line_lists, swap(line_lists, 1)], 0)
    query_work = work(query_work_kernel, row_lists, blks, "query_work")
    here = [near] + there
    rows_all = here + [swap(group, 1) for group in here]

    cots_here = []
    for k in range(2):
        part = jnp.concatenate([piece[2 * k : 2 * k + 2] for piece in pieces], 0)
        masks_left = [m for m in range(1, readers) if not m >> bits[k] & 1]
        cots_here.append((part, [swap(after(part, here), blks * m) for m in masks_left]))

    stack_space = pltpu.VMEM(stacks.shape, bf16)
    buffer = pltpu.VMEM((2, TILES * block, width), bf16)
    word_buffer = pltpu.VMEM((2, TILES, words, block), i32)
    bias = pltpu.VMEM((TILES * block, block), f32)
    turned = pltpu.VMEM((width, block), f32)
    per_head = pltpu.VMEM((HEADS, block), f32)
    own_stats = pltpu.VMEM((2 * HEADS, block), f32)
    met = pltpu.VMEM((HEADS, TILES * block, block), f32)
    pair_met = pltpu.VMEM((HEADS // 2, block, 2 * TILES * block), f32)
    pair_rows = pltpu.VMEM((HEADS // 2, 2 * TILES * block, 2 * head), bf16)
    row_sems = pltpu.SemaphoreType.DMA((2, TILES, 2))

    attn_out, stats = pl.pallas_call(
        functools.partial(forward_kernel, sizes),
        out_shape=(own, shape((devices, 2 * HEADS, block), f32)),
        in_specs=[SMEM] + [VMEM] * 4 + [HBM] * (1 + 2 * readers),
        out_specs=(VMEM, VMEM),
        scratch_shapes=[own_stats, buffer, word_buffer, bias, per_head, per_head, turned, met, row_sems],
        compiler_params=some,
        cost_estimate=cost(5),
        name="forward",
    )(query_work, query_stack, cotangent, w_key, w_value_t, masks, *rows_all)

    stats_all = lax.all_to_all(stats, axes, 0, 0, tiled=True)

    query_part = pl.pallas_call(
        functools.partial(query_grad_kernel, sizes),
        out_shape=shape((block, width), f32),
        in_specs=[SMEM] + [HBM] * (8 + 2 * readers),
        out_specs=VMEM,
        scratch_shapes=[
            stack_space, stack_space, own_stats, weight, weight, weight, weight, buffer, word_buffer, bias, turned,
            met, met, row_sems, pltpu.SemaphoreType.DMA((7,)),
        ],
        compiler_params=most,
        cost_estimate=cost(5),
        name="query_grad",
    )(query_work, query_stack, cot_stack, stats, w_query_t, w_key, w_key_t, w_value, masks, *rows_all)

    cots_all = []
    for first, rest in cots_here:
        cots_all += [first, *rest, swap(after(first, stats), 1)]
        cots_all += [swap(after(part, stats_all, query_part), 1) for part in rest]

    grad_features = pl.pallas_call(
        functools.partial(key_grad_kernel, sizes, bits),
        out_shape=own,
        in_specs=[SMEM] + [HBM] * (8 + 4 * readers),
        out_specs=VMEM,
        scratch_shapes=[
            rows_low, rows_low, rows_wide, weight, weight, weight,
            buffer, word_buffer, buffer, pltpu.VMEM((2, TILES, 2 * HEADS, block), f32), bias,
            pair_rows, pair_rows, pair_met, pair_met, rows_wide, rows_wide,
            row_sems, pltpu.SemaphoreType.DMA((2, TILES, 3)), pltpu.SemaphoreType.DMA((6,)),
        ],
        compiler_params=most,
        cost_estimate=cost(5),
        name="key_grad",
    )(key_work, keys, values, w_query, w_key_t, w_value_t, query_part, masks, stats_all, *rows_all, *cots_all)
    return attn_out, grad_features


def solution(mesh):
    return jax.shard_map(
        local,
        mesh=mesh,
        in_specs=(
            P(("reader", "blk"), None),
            P(("reader", "blk"), None),
            P(),
            P(),
            P(),
            P("reader", "blk", None, None),
            P("reader", "blk"),
            P(),
        ),
        out_specs=(P(("reader", "blk"), None), P(("reader", "blk"), None)),
        check_vma=False,
    )
```

```python
import functools

import jax
import jax.numpy as jnp
from jax import lax
from jax.experimental import pallas as pl
from jax.experimental.pallas import tpu as pltpu
from jax.sharding import PartitionSpec as P

HEADS = 8
NEG_FILL = -1e30
NT = (((1,), (1,)), ((), ()))
NN = (((1,), (0,)), ((), ()))
TILES = 2
LIST_ROWS = 16
VMEM_SOME = 40 * 1024 * 1024
VMEM_MOST = 58 * 1024 * 1024


def dot(a, b, dims=NN):
    return lax.dot_general(a, b, dims, preferred_element_type=jnp.float32)


def pair_stack(rows):
    lane = lax.broadcasted_iota(jnp.int32, rows.shape, 1)
    half = rows.shape[1] // 2
    zero = jnp.zeros_like(rows)
    return jnp.concatenate([jnp.where(lane < half, rows, zero), jnp.where(lane >= half, rows, zero)], 0)


def tile_bias(words, pattern, diag):
    count, size = words.shape
    keys = lax.broadcasted_iota(jnp.int32, (size, size), 0)
    queries = lax.broadcasted_iota(jnp.int32, (size, size), 1)
    spread = jnp.concatenate(
        [jnp.broadcast_to(words[g : g + 1], (size // count, size)) for g in range(count)], 0
    )
    bits = jnp.right_shift(spread, keys & 31) & 1
    same = keys - queries == jnp.where(diag, 0, 2 * size)
    return jnp.where((bits == 1) | same, jnp.where(pattern < 0, NEG_FILL, 0.0), NEG_FILL)


class Layout:
    def __init__(self, readers, blks, cap):
        self.readers, self.blks, self.cap = readers, blks, cap
        self.reader, self.blk = lax.axis_index("reader"), lax.axis_index("blk")
        self.me = self.reader * blks + self.blk

    def apart(self, device):
        far = jnp.bitwise_xor(device, self.me)
        reader, blk = far // self.blks, lax.rem(far, self.blks)
        return reader, blk // 2, blk & 1

    def row_place(self, device):
        reader, line, core = self.apart(device)
        near = line == 0
        group = jnp.where(near, 0, reader) + self.readers * core
        index = jnp.where(reader == 0, self.readers, 0) + line - 1
        return group, jnp.where(near, reader, index)

    def half_place(self, bit, device):
        reader, line, core = self.apart(device)
        first = jnp.right_shift(reader, bit) & 1
        top = (self.blks // 2 - 1).bit_length() - 1
        line = sum((jnp.right_shift(line, top - at) & 1) << at for at in range(top + 1))
        low = reader & ((1 << bit) - 1)
        rest = low + (jnp.right_shift(reader, bit + 1) << bit)
        return rest + self.readers // 2 * core, 2 * line + first


def start_copy(place, refs, make):
    group, where = place
    for g, ref in enumerate(refs):

        @pl.when(group == g)
        def _():
            make(ref.at[where]).start()


def pack_kernel(own_hbm, coords_hbm, count_hbm, out_ref, coords_ref, count_ref, sems):
    block = own_hbm.shape[0]
    cap = coords_ref.shape[3]
    copies = [
        pltpu.make_async_copy(coords_hbm, coords_ref, sems.at[0]),
        pltpu.make_async_copy(count_hbm, count_ref, sems.at[1]),
        pltpu.make_async_copy(own_hbm, out_ref.at[0, pl.ds(0, block)], sems.at[2]),
    ]
    for copy in copies:
        copy.start()
    copies[0].wait()
    copies[1].wait()
    lane = lax.broadcasted_iota(jnp.int32, (LIST_ROWS, out_ref.shape[2]), 1)
    row = jnp.zeros(lane.shape, jnp.int32)
    for column in range(3):
        for slot in range(cap):
            row = jnp.where(lane == column * cap + slot, coords_ref[0, column, 0, slot], row)
    row = jnp.where(lane == 3 * cap, count_ref[0, 0], row)
    out_ref[0, block:] = row.astype(jnp.float32).astype(jnp.bfloat16)
    copies[2].wait()


def scan_list(lists_ref, cap, row, column, wanted, found, out_ref, block_of):
    def one_slot(slot, found):
        out_ref[2 * found + 1] = block_of(lists_ref[row, (1 - column) * cap + slot])
        out_ref[2 * found + 2] = lists_ref[row, 2 * cap + slot]
        return found + jnp.where(lists_ref[row, column * cap + slot] == wanted, 1, 0)

    return lax.fori_loop(0, lists_ref[row, 3 * cap], one_slot, found)


def close_work(found, out_ref):
    out_ref[2 * found + 1] = out_ref[2 * found - 1]
    out_ref[2 * found + 2] = -1
    out_ref[0] = (found + 1) // 2


def query_work_kernel(sizes, lists_hbm, work_ref, lists_ref, sem):
    readers, blks, cap = sizes
    layout = Layout(*sizes)
    copy = pltpu.make_async_copy(lists_hbm, lists_ref, sem)
    copy.start()
    copy.wait()

    def one(k, found):
        blk = jnp.bitwise_xor(k, layout.blk)
        row = k // 2 + (k & 1) * (blks // 2)
        put = lambda other: other * blks + blk
        return scan_list(lists_ref, cap, row, 0, layout.blk, found, work_ref, put)

    close_work(lax.fori_loop(0, blks, one, 0), work_ref)


def key_work_kernel(sizes, lists_hbm, work_ref, lists_ref, sem):
    readers, blks, cap = sizes
    layout = Layout(*sizes)
    copy = pltpu.make_async_copy(lists_hbm, lists_ref, sem)
    copy.start()
    copy.wait()

    def one(k, found):
        reader = jnp.bitwise_xor(k, layout.reader)
        put = lambda other: reader * blks + other
        return scan_list(lists_ref, cap, k, 1, layout.reader, found, work_ref, put)

    close_work(lax.fori_loop(0, readers, one, 0), work_ref)


def load(pairs, sems, first=0):
    copies = [pltpu.make_async_copy(src, into, sems.at[first + k]) for k, (src, into) in enumerate(pairs)]
    for copy in copies:
        copy.start()
    return copies


def prepare_kernel(
    own_hbm, cot_hbm, wq_hbm, wk_hbm, wv_hbm,
    query_stack_ref, cot_stack_ref, key_ref, value_ref, wqt_ref, wkt_ref, wvt_ref,
    own_ref, cot_ref, wq_ref, wk_ref, wv_ref, sems,
):
    loads = load((
        (own_hbm, own_ref), (wq_hbm, wq_ref), (wk_hbm, wk_ref), (wv_hbm, wv_ref), (cot_hbm, cot_ref),
    ), sems)
    for copy in loads:
        copy.wait()
    head = own_ref.shape[1] // HEADS
    queries = dot(own_ref[...], wq_ref[...]).astype(jnp.bfloat16) * jnp.bfloat16(head**-0.5)
    for p in range(HEADS // 2):
        pair = slice(2 * head * p, 2 * head * (p + 1))
        query_stack_ref[p] = pair_stack(queries[:, pair]).T
        cot_stack_ref[p] = pair_stack(cot_ref[:, pair]).T
    key_ref[...] = dot(own_ref[...], wk_ref[...]).astype(jnp.bfloat16)
    value_ref[...] = dot(own_ref[...], wv_ref[...]).astype(jnp.bfloat16)
    wqt_ref[...] = wq_ref[...].T
    wkt_ref[...] = wk_ref[...].T
    wvt_ref[...] = wv_ref[...].T


def step_entry(work_ref, index):
    at = 1 + 2 * TILES * index
    return [work_ref[at + 2 * t] for t in range(TILES)], [work_ref[at + 2 * t + 1] for t in range(TILES)]


def run_steps(work_ref, start, wait, body):
    total = work_ref[0]

    def step(index, carry):
        @pl.when(index + 1 < total)
        def _():
            start(lax.rem(index + 1, 2), *step_entry(work_ref, index + 1))

        slot = lax.rem(index, 2)
        wait(slot)
        body(slot, *step_entry(work_ref, index), index)
        return carry

    lax.fori_loop(0, total, step, 0)


def first_step(work_ref, start):
    start(0, *step_entry(work_ref, 0))


class Rows:
    def __init__(self, layout, groups, mask_ref, buf, words, sems, block):
        self.layout, self.groups, self.mask_ref = layout, groups, mask_ref
        self.buf, self.words, self.sems, self.block = buf, words, sems, block

    def rows(self, slot, t):
        into = self.buf.at[slot, pl.ds(t * self.block, self.block)]
        return lambda src: pltpu.make_async_copy(src, into, self.sems.at[slot, t, 0])

    def mask(self, slot, t, pattern):
        return pltpu.make_async_copy(self.mask_ref.at[pattern], self.words.at[slot, t], self.sems.at[slot, t, 1])

    def start(self, slot, blocks, patterns):
        for t in range(TILES):
            start_copy(self.layout.row_place(blocks[t]), self.groups, self.rows(slot, t))
            self.mask(slot, t, jnp.maximum(patterns[t], 0)).start()

    def wait(self, slot):
        for t in range(TILES):
            self.rows(slot, t)(self.groups[0].at[0]).wait()
            self.mask(slot, t, 0).wait()

    def bias(self, slot, blocks, patterns):
        parts = [
            tile_bias(self.words[slot, t], patterns[t], blocks[t] == self.layout.me) for t in range(TILES)
        ]
        return jnp.concatenate(parts, 0)


def forward_kernel(sizes, work_ref, stack_ref, cot_ref, wk_ref, wvt_ref, mask_ref, *refs):
    count = 2 * sizes[0]
    groups, refs = refs[:count], refs[count:]
    out_ref, sent_ref, stats_ref, buf, words, bias_ref, max_ref, sum_ref, acc_ref, score_ref, sems = refs
    layout = Layout(*sizes)
    block, width = cot_ref.shape
    head = width // HEADS
    rows_in = Rows(layout, groups, mask_ref, buf, words, sems, block)
    first_step(work_ref, rows_in.start)
    max_ref[...] = jnp.full(max_ref.shape, NEG_FILL, jnp.float32)
    sum_ref[...] = jnp.zeros(sum_ref.shape, jnp.float32)
    acc_ref[...] = jnp.zeros(acc_ref.shape, jnp.float32)

    def tiles(slot, blocks, patterns, index):
        rows = buf[slot]
        keys = dot(rows, wk_ref[...]).astype(jnp.bfloat16)
        values = dot(wvt_ref[...], rows, NT).astype(jnp.bfloat16)
        bias_ref[...] = rows_in.bias(slot, blocks, patterns)
        for p in range(HEADS // 2):
            scores = dot(keys[:, 2 * head * p : 2 * head * (p + 1)], stack_ref[p])
            for e in range(2):
                score_ref[2 * p + e] = scores[:, block * e : block * (e + 1)] + bias_ref[...]
        for h in range(HEADS):
            s = score_ref[h]
            old = max_ref[h : h + 1]
            new = jnp.maximum(old, jnp.max(s, axis=0, keepdims=True))
            fade = jnp.exp(old - new)
            expo = jnp.exp(s - new)
            max_ref[h : h + 1] = new
            sum_ref[h : h + 1] = sum_ref[h : h + 1] * fade + jnp.sum(expo, axis=0, keepdims=True)
            at = slice(head * h, head * (h + 1))
            acc_ref[at] = acc_ref[at] * fade + dot(values[at], expo.astype(jnp.bfloat16))

    run_steps(work_ref, rows_in.start, rows_in.wait, tiles)
    inverse = 1.0 / sum_ref[...]
    cot = cot_ref[...].astype(jnp.float32).T
    stats_ref[0:HEADS] = max_ref[...] + jnp.log(sum_ref[...])
    for h in range(HEADS):
        at = slice(head * h, head * (h + 1))
        outputs = acc_ref[at] * inverse[h : h + 1]
        acc_ref[at] = outputs
        stats_ref[HEADS + h : HEADS + h + 1] = jnp.sum(outputs * cot[at], axis=0, keepdims=True)
    sent_ref[...] = jnp.broadcast_to(stats_ref[...], sent_ref.shape)
    out_ref[...] = acc_ref[...].T.astype(out_ref.dtype)


def tile_grads(scores, d_probs, lse, delta):
    prob = jnp.exp(scores - lse)
    return prob.astype(jnp.bfloat16), (prob * (d_probs - delta)).astype(jnp.bfloat16)


def query_grad_kernel(
    sizes, work_ref, stack_hbm, cot_stack_hbm, stats_hbm, wqt_hbm, wk_hbm, wkt_hbm, wv_hbm, mask_ref, *refs
):
    count = 2 * sizes[0]
    groups, refs = refs[:count], refs[count:]
    part_ref, stack_ref, cot_stack_ref, stats_ref, wqt_ref, wk_ref, wkt_ref, wv_ref = refs[:8]
    buf, words, bias_ref, acc_ref, score_ref, d_prob_ref, sems, w_sems = refs[8:]
    layout = Layout(*sizes)
    block, width = part_ref.shape
    head = width // HEADS
    rows_in = Rows(layout, groups, mask_ref, buf, words, sems, block)
    first_step(work_ref, rows_in.start)
    loads = load((
        (wk_hbm, wk_ref), (stack_hbm, stack_ref), (wv_hbm, wv_ref), (cot_stack_hbm, cot_stack_ref),
        (wkt_hbm, wkt_ref), (stats_hbm.at[0], stats_ref), (wqt_hbm, wqt_ref),
    ), w_sems)
    acc_ref[...] = jnp.zeros(acc_ref.shape, jnp.float32)
    for copy in loads[:6]:
        copy.wait()

    def tiles(slot, blocks, patterns, index):
        rows = buf[slot]
        keys = dot(rows, wk_ref[...]).astype(jnp.bfloat16)
        values = dot(rows, wv_ref[...]).astype(jnp.bfloat16)
        keys_t = dot(wkt_ref[...], rows, NT).astype(jnp.bfloat16)
        bias_ref[...] = rows_in.bias(slot, blocks, patterns)
        for p in range(HEADS // 2):
            pair = slice(2 * head * p, 2 * head * (p + 1))
            scores = dot(keys[:, pair], stack_ref[p])
            d_probs = dot(values[:, pair], cot_stack_ref[p])
            for e in range(2):
                of = slice(block * e, block * (e + 1))
                score_ref[2 * p + e] = scores[:, of] + bias_ref[...]
                d_prob_ref[2 * p + e] = d_probs[:, of]
        for h in range(HEADS):
            _, d_scores = tile_grads(
                score_ref[h], d_prob_ref[h], stats_ref[h : h + 1], stats_ref[HEADS + h : HEADS + h + 1]
            )
            at = slice(head * h, head * (h + 1))
            acc_ref[at] += dot(keys_t[at], d_scores)

    run_steps(work_ref, rows_in.start, rows_in.wait, tiles)
    loads[6].wait()
    grad = (acc_ref[...].T * (head**-0.5)).astype(jnp.bfloat16)
    part_ref[...] = dot(grad, wqt_ref[...])


def key_grad_kernel(
    sizes, bits, work_ref, key_hbm, value_hbm, wq_hbm, wkt_hbm, wvt_hbm, part_hbm, mask_ref, stats_all_ref, *refs
):
    readers = sizes[0]
    count = 2 * readers
    groups, refs = refs[:count], refs[count:]
    halves, refs = (refs[:readers], refs[readers : 2 * readers]), refs[2 * readers :]
    out_ref, key_ref, value_ref, part_ref, wq_ref, wkt_ref, wvt_ref, buf, words, cot_buf, stats, bias_ref = refs[:12]
    query_stack_ref, cot_stack_ref, score_ref, d_prob_ref, key_acc, value_acc, sems, c_sems, w_sems = refs[12:]
    layout = Layout(*sizes)
    block, width = out_ref.shape
    head = width // HEADS
    rows_in = Rows(layout, groups, mask_ref, buf, words, sems, block)

    def half_copy(slot, t, k):
        into = cot_buf.at[slot, pl.ds(t * block + block // 2 * k, block // 2)]
        return lambda src: pltpu.make_async_copy(src, into, c_sems.at[slot, t, k])

    def stats_copy(slot, t, query):
        return pltpu.make_async_copy(stats_all_ref.at[query], stats.at[slot, t], c_sems.at[slot, t, 2])

    def start(slot, blocks, patterns):
        rows_in.start(slot, blocks, patterns)
        for t in range(TILES):
            stats_copy(slot, t, blocks[t]).start()
            for k in range(2):
                start_copy(layout.half_place(bits[k], blocks[t]), halves[k], half_copy(slot, t, k))

    def wait(slot):
        rows_in.wait(slot)
        for t in range(TILES):
            stats_copy(slot, t, 0).wait()
            for k in range(2):
                half_copy(slot, t, k)(halves[k][0].at[0]).wait()

    first_step(work_ref, start)
    loads = load(((wq_hbm, wq_ref), (key_hbm, key_ref), (value_hbm, value_ref)), w_sems)
    key_acc[...] = jnp.zeros(key_acc.shape, jnp.float32)
    value_acc[...] = jnp.zeros(value_acc.shape, jnp.float32)
    for copy in loads:
        copy.wait()
    loads = load(((wkt_hbm, wkt_ref), (wvt_hbm, wvt_ref), (part_hbm, part_ref)), w_sems, 3)

    def tiles(slot, blocks, patterns, index):
        queries = dot(buf[slot], wq_ref[...]).astype(jnp.bfloat16) * jnp.bfloat16(head**-0.5)
        bias_ref[...] = rows_in.bias(slot, blocks, patterns)
        cots = cot_buf[slot]
        pairs = [slice(2 * head * p, 2 * head * (p + 1)) for p in range(HEADS // 2)]
        of_tile = [slice(block * t, block * (t + 1)) for t in range(TILES)]
        for p, pair in enumerate(pairs):
            query_stack_ref[p] = jnp.concatenate([pair_stack(queries[of, pair]) for of in of_tile], 0)
            cot_stack_ref[p] = jnp.concatenate([pair_stack(cots[of, pair]) for of in of_tile], 0)
            score_ref[p] = dot(key_ref[:, pair], query_stack_ref[p], NT)
            d_prob_ref[p] = dot(value_ref[:, pair], cot_stack_ref[p], NT)
        for p, pair in enumerate(pairs):
            probs, d_scores = [], []
            for t in range(TILES):
                for e in range(2):
                    h = 2 * p + e
                    of = slice(block * (2 * t + e), block * (2 * t + e + 1))
                    prob, d_score = tile_grads(
                        score_ref[p, :, of] + bias_ref[of_tile[t]], d_prob_ref[p, :, of], stats[slot, t, h : h + 1],
                        stats[slot, t, HEADS + h : HEADS + h + 1],
                    )
                    probs.append(prob)
                    d_scores.append(d_score)
            value_acc[:, pair] += dot(jnp.concatenate(probs, 1), cot_stack_ref[p])
            key_acc[:, pair] += dot(jnp.concatenate(d_scores, 1), query_stack_ref[p])

    run_steps(work_ref, start, wait, tiles)
    for copy in loads:
        copy.wait()
    grad = part_ref[...] + dot(key_acc[...].astype(jnp.bfloat16), wkt_ref[...])
    grad = grad + dot(value_acc[...].astype(jnp.bfloat16), wvt_ref[...])
    out_ref[...] = grad.astype(out_ref.dtype)


VMEM = pl.BlockSpec(memory_space=pltpu.VMEM)
SMEM = pl.BlockSpec(memory_space=pltpu.SMEM)
HBM = pl.BlockSpec(memory_space=pltpu.HBM)


def swap(block, mask):
    axes = ("reader", "blk")
    count = lax.axis_size("reader") * lax.axis_size("blk")
    return lax.ppermute(block, axes, [(i, i ^ mask) for i in range(count)])


def after(value, *others):
    return lax.optimization_barrier((value, *others))[0]


def local(features, cotangent, w_query, w_key, w_value, tile_coords, tile_count, mask_table):
    block, width = features.shape
    readers, blks, cap = lax.axis_size("reader"), lax.axis_size("blk"), tile_coords.shape[2]
    assert block == mask_table.shape[1] and 3 * cap < 128
    sizes = (readers, blks, cap)
    devices, lines = readers * blks, blks // 2
    f32, bf16, i32 = jnp.float32, jnp.bfloat16, jnp.int32
    shape = jax.ShapeDtypeStruct
    masks = mask_table.transpose(0, 2, 1)
    words = masks.shape[1]
    head = width // HEADS
    half = block // 2
    some = pltpu.CompilerParams(vmem_limit_bytes=VMEM_SOME)
    most = pltpu.CompilerParams(vmem_limit_bytes=VMEM_MOST)
    axes = ("reader", "blk")

    def cost(tiles):
        return pl.CostEstimate(flops=tiles * 200_000_000, bytes_accessed=4_000_000, transcendentals=tiles * 131072)

    packed = pl.pallas_call(
        pack_kernel,
        out_shape=shape((1, block + LIST_ROWS, width), bf16),
        in_specs=[HBM, HBM, HBM],
        out_specs=VMEM,
        scratch_shapes=[
            pltpu.SMEM((1, 3, 1, cap), i32), pltpu.SMEM((1, 1), i32), pltpu.SemaphoreType.DMA((3,)),
        ],
        compiler_params=most,
        name="pack",
    )(features, tile_coords.transpose(0, 3, 1, 2), tile_count)
    lined = [packed] + [swap(packed, 2 * k) for k in range(1, lines)]

    nearest_first = sorted(range(1, readers), key=lambda k: (k.bit_count(), k))

    def to_readers(block):
        there = {k: swap(block, blks * k) for k in nearest_first}
        return [there[k] for k in range(1, readers)]

    columns = [packed] + to_readers(packed)

    bits = (0, (readers - 1).bit_length() - 1)
    cot_parts = [cotangent[None, half * k : half * (k + 1)] for k in range(2)]
    cot_other = [swap(part, blks << bit) for part, bit in zip(cot_parts, bits)]

    column_lists = jnp.concatenate([entry[:, block:, :128] for entry in columns], 0)

    def work(kernel, lists, count, name):
        return pl.pallas_call(
            functools.partial(kernel, sizes),
            out_shape=shape((2 * count * cap + 5,), i32),
            in_specs=[HBM],
            out_specs=SMEM,
            scratch_shapes=[pltpu.SMEM((count, 128), i32), pltpu.SemaphoreType.DMA],
            compiler_params=some,
            cost_estimate=cost(1),
            name=name,
        )(lists[:, 0].astype(i32))

    key_work = work(key_work_kernel, column_lists, readers, "key_work")

    stacks = shape((HEADS // 2, 2 * head, 2 * block), bf16)
    own = shape((block, width), bf16)
    square = shape((width, width), bf16)
    weight = pltpu.VMEM((width, width), bf16)
    rows_low, rows_wide = pltpu.VMEM((block, width), bf16), pltpu.VMEM((block, width), f32)
    prepared = pl.pallas_call(
        prepare_kernel,
        out_shape=(stacks, stacks, own, own, square, square, square),
        in_specs=[HBM] * 5,
        out_specs=(VMEM,) * 7,
        scratch_shapes=[rows_low, rows_low, weight, weight, weight, pltpu.SemaphoreType.DMA((5,))],
        compiler_params=most,
        cost_estimate=cost(2),
        name="prepare",
    )(after(features, columns), cotangent, w_query, w_key, w_value)
    query_stack, cot_stack, keys, values, w_query_t, w_key_t, w_value_t = prepared

    line = jnp.concatenate([entry[:, :block] for entry in lined[1:]], 0)
    line = after(line, columns, cot_other)
    there = to_readers(line)
    near = jnp.concatenate([entry[:, :block] for entry in columns] + [line], 0)

    pairs = [part for k in range(2) for part in (cot_parts[k], cot_other[k])]
    pieces = [after(jnp.concatenate(pairs, 0), near)]
    done_first = (key_work, prepared)
    mask = blks // 2
    while mask > 1:
        pieces += [swap(after(piece, done_first) if at else piece, mask) for at, piece in enumerate(pieces)]
        mask //= 2

    line_lists = jnp.concatenate([entry[:, block:, :128] for entry in lined], 0)
    line_lists = after(line_lists, pieces[lines // 2])
    row_lists = jnp.concatenate([line_lists, swap(line_lists, 1)], 0)
    query_work = work(query_work_kernel, row_lists, blks, "query_work")
    here = [near] + there
    rows_all = here + [swap(group, 1) for group in here]

    cots_here = []
    for k in range(2):
        part = jnp.concatenate([piece[2 * k : 2 * k + 2] for piece in pieces], 0)
        masks_left = [m for m in range(1, readers) if not m >> bits[k] & 1]
        cots_here.append((part, [swap(after(part, here), blks * m) for m in masks_left]))

    stack_space = pltpu.VMEM(stacks.shape, bf16)
    buffer = pltpu.VMEM((2, TILES * block, width), bf16)
    word_buffer = pltpu.VMEM((2, TILES, words, block), i32)
    bias = pltpu.VMEM((TILES * block, block), f32)
    turned = pltpu.VMEM((width, block), f32)
    per_head = pltpu.VMEM((HEADS, block), f32)
    own_stats = pltpu.VMEM((2 * HEADS, block), f32)
    met = pltpu.VMEM((HEADS, TILES * block, block), f32)
    pair_met = pltpu.VMEM((HEADS // 2, block, 2 * TILES * block), f32)
    pair_rows = pltpu.VMEM((HEADS // 2, 2 * TILES * block, 2 * head), bf16)
    row_sems = pltpu.SemaphoreType.DMA((2, TILES, 2))

    attn_out, stats = pl.pallas_call(
        functools.partial(forward_kernel, sizes),
        out_shape=(own, shape((devices, 2 * HEADS, block), f32)),
        in_specs=[SMEM] + [VMEM] * 4 + [HBM] * (1 + 2 * readers),
        out_specs=(VMEM, VMEM),
        scratch_shapes=[own_stats, buffer, word_buffer, bias, per_head, per_head, turned, met, row_sems],
        compiler_params=some,
        cost_estimate=cost(5),
        name="forward",
    )(query_work, query_stack, cotangent, w_key, w_value_t, masks, *rows_all)

    stats_all = lax.all_to_all(stats, axes, 0, 0, tiled=True)

    query_part = pl.pallas_call(
        functools.partial(query_grad_kernel, sizes),
        out_shape=shape((block, width), f32),
        in_specs=[SMEM] + [HBM] * (8 + 2 * readers),
        out_specs=VMEM,
        scratch_shapes=[
            stack_space, stack_space, own_stats, weight, weight, weight, weight, buffer, word_buffer, bias, turned,
            met, met, row_sems, pltpu.SemaphoreType.DMA((7,)),
        ],
        compiler_params=most,
        cost_estimate=cost(5),
        name="query_grad",
    )(query_work, query_stack, cot_stack, stats, w_query_t, w_key, w_key_t, w_value, masks, *rows_all)

    cots_all = []
    for first, rest in cots_here:
        cots_all += [first, *rest, swap(after(first, stats), 1)]
        cots_all += [swap(after(part, stats_all, query_part), 1) for part in rest]

    grad_features = pl.pallas_call(
        functools.partial(key_grad_kernel, sizes, bits),
        out_shape=own,
        in_specs=[SMEM] + [HBM] * (8 + 4 * readers),
        out_specs=VMEM,
        scratch_shapes=[
            rows_low, rows_low, rows_wide, weight, weight, weight,
            buffer, word_buffer, buffer, pltpu.VMEM((2, TILES, 2 * HEADS, block), f32), bias,
            pair_rows, pair_rows, pair_met, pair_met, rows_wide, rows_wide,
            row_sems, pltpu.SemaphoreType.DMA((2, TILES, 3)), pltpu.SemaphoreType.DMA((6,)),
        ],
        compiler_params=most,
        cost_estimate=cost(5),
        name="key_grad",
    )(key_work, keys, values, w_query, w_key_t, w_value_t, query_part, masks, stats_all, *rows_all, *cots_all)
    return attn_out, grad_features


def solution(mesh):
    return jax.shard_map(
        local,
        mesh=mesh,
        in_specs=(
            P(("reader", "blk"), None),
            P(("reader", "blk"), None),
            P(),
            P(),
            P(),
            P("reader", "blk", None, None),
            P("reader", "blk"),
            P(),
        ),
        out_specs=(P(("reader", "blk"), None), P(("reader", "blk"), None)),
        check_vma=False,
    )
```

```python
import functools

import jax
import jax.numpy as jnp
from jax import lax
from jax.experimental import pallas as pl
from jax.experimental.pallas import tpu as pltpu
from jax.sharding import PartitionSpec as P

HEADS = 8
NEG_FILL = -1e30
NT = (((1,), (1,)), ((), ()))
NN = (((1,), (0,)), ((), ()))
TILES = 2
LIST_ROWS = 16
VMEM_SOME = 40 * 1024 * 1024
VMEM_MOST = 58 * 1024 * 1024


def dot(a, b, dims=NN):
    return lax.dot_general(a, b, dims, preferred_element_type=jnp.float32)


def pair_stack(rows):
    lane = lax.broadcasted_iota(jnp.int32, rows.shape, 1)
    half = rows.shape[1] // 2
    zero = jnp.zeros_like(rows)
    return jnp.concatenate([jnp.where(lane < half, rows, zero), jnp.where(lane >= half, rows, zero)], 0)


def tile_bias(words, pattern, diag):
    count, size = words.shape
    keys = lax.broadcasted_iota(jnp.int32, (size, size), 0)
    queries = lax.broadcasted_iota(jnp.int32, (size, size), 1)
    spread = jnp.concatenate(
        [jnp.broadcast_to(words[g : g + 1], (size // count, size)) for g in range(count)], 0
    )
    bits = jnp.right_shift(spread, keys & 31) & 1
    same = keys - queries == jnp.where(diag, 0, 2 * size)
    return jnp.where((bits == 1) | same, jnp.where(pattern < 0, NEG_FILL, 0.0), NEG_FILL)


class Layout:
    def __init__(self, readers, blks, cap):
        self.readers, self.blks, self.cap = readers, blks, cap
        self.reader, self.blk = lax.axis_index("reader"), lax.axis_index("blk")
        self.me = self.reader * blks + self.blk

    def apart(self, device):
        far = jnp.bitwise_xor(device, self.me)
        reader, blk = far // self.blks, lax.rem(far, self.blks)
        return reader, blk // 2, blk & 1

    def row_place(self, device):
        reader, line, core = self.apart(device)
        near = line == 0
        group = jnp.where(near, 0, reader) + self.readers * core
        index = jnp.where(reader == 0, self.readers, 0) + line - 1
        return group, jnp.where(near, reader, index)

    def half_place(self, bit, device):
        reader, line, core = self.apart(device)
        first = jnp.right_shift(reader, bit) & 1
        top = (self.blks // 2 - 1).bit_length() - 1
        line = sum((jnp.right_shift(line, top - at) & 1) << at for at in range(top + 1))
        low = reader & ((1 << bit) - 1)
        rest = low + (jnp.right_shift(reader, bit + 1) << bit)
        return rest + self.readers // 2 * core, 2 * line + first


def start_copy(place, refs, make):
    group, where = place
    for g, ref in enumerate(refs):

        @pl.when(group == g)
        def _():
            make(ref.at[where]).start()


def pack_kernel(own_hbm, coords_hbm, count_hbm, out_ref, coords_ref, count_ref, sems):
    block = own_hbm.shape[0]
    cap = coords_ref.shape[3]
    copies = [
        pltpu.make_async_copy(coords_hbm, coords_ref, sems.at[0]),
        pltpu.make_async_copy(count_hbm, count_ref, sems.at[1]),
        pltpu.make_async_copy(own_hbm, out_ref.at[0, pl.ds(0, block)], sems.at[2]),
    ]
    for copy in copies:
        copy.start()
    copies[0].wait()
    copies[1].wait()
    lane = lax.broadcasted_iota(jnp.int32, (LIST_ROWS, out_ref.shape[2]), 1)
    row = jnp.zeros(lane.shape, jnp.int32)
    for column in range(3):
        for slot in range(cap):
            row = jnp.where(lane == column * cap + slot, coords_ref[0, column, 0, slot], row)
    row = jnp.where(lane == 3 * cap, count_ref[0, 0], row)
    out_ref[0, block:] = row.astype(jnp.float32).astype(jnp.bfloat16)
    copies[2].wait()


def scan_list(lists_ref, cap, row, column, wanted, found, out_ref, block_of):
    def one_slot(slot, found):
        out_ref[2 * found + 1] = block_of(lists_ref[row, (1 - column) * cap + slot])
        out_ref[2 * found + 2] = lists_ref[row, 2 * cap + slot]
        return found + jnp.where(lists_ref[row, column * cap + slot] == wanted, 1, 0)

    return lax.fori_loop(0, lists_ref[row, 3 * cap], one_slot, found)


def close_work(found, out_ref):
    out_ref[2 * found + 1] = out_ref[2 * found - 1]
    out_ref[2 * found + 2] = -1
    out_ref[0] = (found + 1) // 2


def query_work_kernel(sizes, lists_hbm, work_ref, lists_ref, sem):
    readers, blks, cap = sizes
    layout = Layout(*sizes)
    copy = pltpu.make_async_copy(lists_hbm, lists_ref, sem)
    copy.start()
    copy.wait()

    def one(k, found):
        blk = jnp.bitwise_xor(k, layout.blk)
        row = k // 2 + (k & 1) * (blks // 2)
        put = lambda other: other * blks + blk
        return scan_list(lists_ref, cap, row, 0, layout.blk, found, work_ref, put)

    close_work(lax.fori_loop(0, blks, one, 0), work_ref)


def key_work_kernel(sizes, lists_hbm, work_ref, lists_ref, sem):
    readers, blks, cap = sizes
    layout = Layout(*sizes)
    copy = pltpu.make_async_copy(lists_hbm, lists_ref, sem)
    copy.start()
    copy.wait()

    def one(k, found):
        reader = jnp.bitwise_xor(k, layout.reader)
        put = lambda other: reader * blks + other
        return scan_list(lists_ref, cap, k, 1, layout.reader, found, work_ref, put)

    close_work(lax.fori_loop(0, readers, one, 0), work_ref)


def load(pairs, sems, first=0):
    copies = [pltpu.make_async_copy(src, into, sems.at[first + k]) for k, (src, into) in enumerate(pairs)]
    for copy in copies:
        copy.start()
    return copies


def prepare_kernel(
    own_hbm, cot_hbm, wq_hbm, wk_hbm, wv_hbm,
    query_stack_ref, cot_stack_ref, key_ref, value_ref, wqt_ref, wkt_ref, wvt_ref,
    own_ref, cot_ref, wq_ref, wk_ref, wv_ref, sems,
):
    loads = load((
        (own_hbm, own_ref), (wq_hbm, wq_ref), (wk_hbm, wk_ref), (wv_hbm, wv_ref), (cot_hbm, cot_ref),
    ), sems)
    for copy in loads:
        copy.wait()
    head = own_ref.shape[1] // HEADS
    queries = dot(own_ref[...], wq_ref[...]).astype(jnp.bfloat16) * jnp.bfloat16(head**-0.5)
    for p in range(HEADS // 2):
        pair = slice(2 * head * p, 2 * head * (p + 1))
        query_stack_ref[p] = pair_stack(queries[:, pair]).T
        cot_stack_ref[p] = pair_stack(cot_ref[:, pair]).T
    key_ref[...] = dot(own_ref[...], wk_ref[...]).astype(jnp.bfloat16)
    value_ref[...] = dot(own_ref[...], wv_ref[...]).astype(jnp.bfloat16)
    wqt_ref[...] = wq_ref[...].T
    wkt_ref[...] = wk_ref[...].T
    wvt_ref[...] = wv_ref[...].T


def step_entry(work_ref, index):
    at = 1 + 2 * TILES * index
    return [work_ref[at + 2 * t] for t in range(TILES)], [work_ref[at + 2 * t + 1] for t in range(TILES)]


def run_steps(work_ref, start, wait, body):
    total = work_ref[0]

    def step(index, carry):
        @pl.when(index + 1 < total)
        def _():
            start(lax.rem(index + 1, 2), *step_entry(work_ref, index + 1))

        slot = lax.rem(index, 2)
        wait(slot)
        body(slot, *step_entry(work_ref, index), index)
        return carry

    lax.fori_loop(0, total, step, 0)


def first_step(work_ref, start):
    start(0, *step_entry(work_ref, 0))


class Rows:
    def __init__(self, layout, groups, mask_ref, buf, words, sems, block):
        self.layout, self.groups, self.mask_ref = layout, groups, mask_ref
        self.buf, self.words, self.sems, self.block = buf, words, sems, block

    def rows(self, slot, t):
        into = self.buf.at[slot, pl.ds(t * self.block, self.block)]
        return lambda src: pltpu.make_async_copy(src, into, self.sems.at[slot, t, 0])

    def mask(self, slot, t, pattern):
        return pltpu.make_async_copy(self.mask_ref.at[pattern], self.words.at[slot, t], self.sems.at[slot, t, 1])

    def start(self, slot, blocks, patterns):
        for t in range(TILES):
            start_copy(self.layout.row_place(blocks[t]), self.groups, self.rows(slot, t))
            self.mask(slot, t, jnp.maximum(patterns[t], 0)).start()

    def wait(self, slot):
        for t in range(TILES):
            self.rows(slot, t)(self.groups[0].at[0]).wait()
            self.mask(slot, t, 0).wait()

    def bias(self, slot, blocks, patterns):
        parts = [
            tile_bias(self.words[slot, t], patterns[t], blocks[t] == self.layout.me) for t in range(TILES)
        ]
        return jnp.concatenate(parts, 0)


def forward_kernel(sizes, work_ref, stack_ref, cot_ref, wk_ref, wvt_ref, mask_ref, *refs):
    count = 2 * sizes[0]
    groups, refs = refs[:count], refs[count:]
    out_ref, sent_ref, stats_ref, buf, words, bias_ref, max_ref, sum_ref, acc_ref, score_ref, sems = refs
    layout = Layout(*sizes)
    block, width = cot_ref.shape
    head = width // HEADS
    rows_in = Rows(layout, groups, mask_ref, buf, words, sems, block)
    first_step(work_ref, rows_in.start)
    max_ref[...] = jnp.full(max_ref.shape, NEG_FILL, jnp.float32)
    sum_ref[...] = jnp.zeros(sum_ref.shape, jnp.float32)
    acc_ref[...] = jnp.zeros(acc_ref.shape, jnp.float32)

    def tiles(slot, blocks, patterns, index):
        rows = buf[slot]
        keys = dot(rows, wk_ref[...]).astype(jnp.bfloat16)
        values = dot(wvt_ref[...], rows, NT).astype(jnp.bfloat16)
        bias_ref[...] = rows_in.bias(slot, blocks, patterns)
        for p in range(HEADS // 2):
            scores = dot(keys[:, 2 * head * p : 2 * head * (p + 1)], stack_ref[p])
            for e in range(2):
                score_ref[2 * p + e] = scores[:, block * e : block * (e + 1)] + bias_ref[...]
        for h in range(HEADS):
            s = score_ref[h]
            old = max_ref[h : h + 1]
            new = jnp.maximum(old, jnp.max(s, axis=0, keepdims=True))
            fade = jnp.exp(old - new)
            expo = jnp.exp(s - new)
            max_ref[h : h + 1] = new
            sum_ref[h : h + 1] = sum_ref[h : h + 1] * fade + jnp.sum(expo, axis=0, keepdims=True)
            at = slice(head * h, head * (h + 1))
            acc_ref[at] = acc_ref[at] * fade + dot(values[at], expo.astype(jnp.bfloat16))

    run_steps(work_ref, rows_in.start, rows_in.wait, tiles)
    inverse = 1.0 / sum_ref[...]
    cot = cot_ref[...].astype(jnp.float32).T
    stats_ref[0:HEADS] = max_ref[...] + jnp.log(sum_ref[...])
    for h in range(HEADS):
        at = slice(head * h, head * (h + 1))
        outputs = acc_ref[at] * inverse[h : h + 1]
        acc_ref[at] = outputs
        stats_ref[HEADS + h : HEADS + h + 1] = jnp.sum(outputs * cot[at], axis=0, keepdims=True)
    sent_ref[...] = jnp.broadcast_to(stats_ref[...], sent_ref.shape)
    out_ref[...] = acc_ref[...].T.astype(out_ref.dtype)


def tile_grads(scores, d_probs, lse, delta):
    prob = jnp.exp(scores - lse)
    return prob.astype(jnp.bfloat16), (prob * (d_probs - delta)).astype(jnp.bfloat16)


def query_grad_kernel(
    sizes, work_ref, stack_hbm, cot_stack_hbm, stats_hbm, wqt_hbm, wk_hbm, wkt_hbm, wv_hbm, mask_ref, *refs
):
    count = 2 * sizes[0]
    groups, refs = refs[:count], refs[count:]
    part_ref, stack_ref, cot_stack_ref, stats_ref, wqt_ref, wk_ref, wkt_ref, wv_ref = refs[:8]
    buf, words, bias_ref, acc_ref, score_ref, d_prob_ref, sems, w_sems = refs[8:]
    layout = Layout(*sizes)
    block, width = part_ref.shape
    head = width // HEADS
    rows_in = Rows(layout, groups, mask_ref, buf, words, sems, block)
    first_step(work_ref, rows_in.start)
    loads = load((
        (wk_hbm, wk_ref), (stack_hbm, stack_ref), (wv_hbm, wv_ref), (cot_stack_hbm, cot_stack_ref),
        (wkt_hbm, wkt_ref), (stats_hbm.at[0], stats_ref), (wqt_hbm, wqt_ref),
    ), w_sems)
    acc_ref[...] = jnp.zeros(acc_ref.shape, jnp.float32)
    for copy in loads[:6]:
        copy.wait()

    def tiles(slot, blocks, patterns, index):
        rows = buf[slot]
        keys = dot(rows, wk_ref[...]).astype(jnp.bfloat16)
        values = dot(rows, wv_ref[...]).astype(jnp.bfloat16)
        keys_t = dot(wkt_ref[...], rows, NT).astype(jnp.bfloat16)
        bias_ref[...] = rows_in.bias(slot, blocks, patterns)
        for p in range(HEADS // 2):
            pair = slice(2 * head * p, 2 * head * (p + 1))
            scores = dot(keys[:, pair], stack_ref[p])
            d_probs = dot(values[:, pair], cot_stack_ref[p])
            for e in range(2):
                of = slice(block * e, block * (e + 1))
                score_ref[2 * p + e] = scores[:, of] + bias_ref[...]
                d_prob_ref[2 * p + e] = d_probs[:, of]
        for h in range(HEADS):
            _, d_scores = tile_grads(
                score_ref[h], d_prob_ref[h], stats_ref[h : h + 1], stats_ref[HEADS + h : HEADS + h + 1]
            )
            at = slice(head * h, head * (h + 1))
            acc_ref[at] += dot(keys_t[at], d_scores)

    run_steps(work_ref, rows_in.start, rows_in.wait, tiles)
    loads[6].wait()
    grad = (acc_ref[...].T * (head**-0.5)).astype(jnp.bfloat16)
    part_ref[...] = dot(grad, wqt_ref[...])


def key_grad_kernel(
    sizes, bits, work_ref, key_hbm, value_hbm, wq_hbm, wkt_hbm, wvt_hbm, part_hbm, mask_ref, stats_all_ref, *refs
):
    readers = sizes[0]
    count = 2 * readers
    groups, refs = refs[:count], refs[count:]
    halves, refs = (refs[:readers], refs[readers : 2 * readers]), refs[2 * readers :]
    out_ref, key_ref, value_ref, part_ref, wq_ref, wkt_ref, wvt_ref, buf, words, cot_buf, stats, bias_ref = refs[:12]
    query_stack_ref, cot_stack_ref, score_ref, d_prob_ref, key_acc, value_acc, sems, c_sems, w_sems = refs[12:]
    layout = Layout(*sizes)
    block, width = out_ref.shape
    head = width // HEADS
    rows_in = Rows(layout, groups, mask_ref, buf, words, sems, block)

    def half_copy(slot, t, k):
        into = cot_buf.at[slot, pl.ds(t * block + block // 2 * k, block // 2)]
        return lambda src: pltpu.make_async_copy(src, into, c_sems.at[slot, t, k])

    def stats_copy(slot, t, query):
        return pltpu.make_async_copy(stats_all_ref.at[query], stats.at[slot, t], c_sems.at[slot, t, 2])

    def start(slot, blocks, patterns):
        rows_in.start(slot, blocks, patterns)
        for t in range(TILES):
            stats_copy(slot, t, blocks[t]).start()
            for k in range(2):
                start_copy(layout.half_place(bits[k], blocks[t]), halves[k], half_copy(slot, t, k))

    def wait(slot):
        rows_in.wait(slot)
        for t in range(TILES):
            stats_copy(slot, t, 0).wait()
            for k in range(2):
                half_copy(slot, t, k)(halves[k][0].at[0]).wait()

    first_step(work_ref, start)
    loads = load(((wq_hbm, wq_ref), (key_hbm, key_ref), (value_hbm, value_ref)), w_sems)
    key_acc[...] = jnp.zeros(key_acc.shape, jnp.float32)
    value_acc[...] = jnp.zeros(value_acc.shape, jnp.float32)
    for copy in loads:
        copy.wait()
    loads = load(((wkt_hbm, wkt_ref), (wvt_hbm, wvt_ref), (part_hbm, part_ref)), w_sems, 3)

    def tiles(slot, blocks, patterns, index):
        queries = dot(buf[slot], wq_ref[...]).astype(jnp.bfloat16) * jnp.bfloat16(head**-0.5)
        bias_ref[...] = rows_in.bias(slot, blocks, patterns)
        cots = cot_buf[slot]
        pairs = [slice(2 * head * p, 2 * head * (p + 1)) for p in range(HEADS // 2)]
        of_tile = [slice(block * t, block * (t + 1)) for t in range(TILES)]
        for p, pair in enumerate(pairs):
            query_stack_ref[p] = jnp.concatenate([pair_stack(queries[of, pair]) for of in of_tile], 0)
            cot_stack_ref[p] = jnp.concatenate([pair_stack(cots[of, pair]) for of in of_tile], 0)
            score_ref[p] = dot(key_ref[:, pair], query_stack_ref[p], NT)
            d_prob_ref[p] = dot(value_ref[:, pair], cot_stack_ref[p], NT)
        for p, pair in enumerate(pairs):
            probs, d_scores = [], []
            for t in range(TILES):
                for e in range(2):
                    h = 2 * p + e
                    of = slice(block * (2 * t + e), block * (2 * t + e + 1))
                    prob, d_score = tile_grads(
                        score_ref[p, :, of] + bias_ref[of_tile[t]], d_prob_ref[p, :, of], stats[slot, t, h : h + 1],
                        stats[slot, t, HEADS + h : HEADS + h + 1],
                    )
                    probs.append(prob)
                    d_scores.append(d_score)
            value_acc[:, pair] += dot(jnp.concatenate(probs, 1), cot_stack_ref[p])
            key_acc[:, pair] += dot(jnp.concatenate(d_scores, 1), query_stack_ref[p])

    run_steps(work_ref, start, wait, tiles)
    for copy in loads:
        copy.wait()
    grad = part_ref[...] + dot(key_acc[...].astype(jnp.bfloat16), wkt_ref[...])
    grad = grad + dot(value_acc[...].astype(jnp.bfloat16), wvt_ref[...])
    out_ref[...] = grad.astype(out_ref.dtype)


VMEM = pl.BlockSpec(memory_space=pltpu.VMEM)
SMEM = pl.BlockSpec(memory_space=pltpu.SMEM)
HBM = pl.BlockSpec(memory_space=pltpu.HBM)


def swap(block, mask):
    axes = ("reader", "blk")
    count = lax.axis_size("reader") * lax.axis_size("blk")
    return lax.ppermute(block, axes, [(i, i ^ mask) for i in range(count)])


def after(value, *others):
    return lax.optimization_barrier((value, *others))[0]


def local(features, cotangent, w_query, w_key, w_value, tile_coords, tile_count, mask_table):
    block, width = features.shape
    readers, blks, cap = lax.axis_size("reader"), lax.axis_size("blk"), tile_coords.shape[2]
    assert block == mask_table.shape[1] and 3 * cap < 128
    sizes = (readers, blks, cap)
    devices, lines = readers * blks, blks // 2
    f32, bf16, i32 = jnp.float32, jnp.bfloat16, jnp.int32
    shape = jax.ShapeDtypeStruct
    masks = mask_table.transpose(0, 2, 1)
    words = masks.shape[1]
    head = width // HEADS
    half = block // 2
    some = pltpu.CompilerParams(vmem_limit_bytes=VMEM_SOME)
    most = pltpu.CompilerParams(vmem_limit_bytes=VMEM_MOST)
    axes = ("reader", "blk")

    def cost(tiles):
        return pl.CostEstimate(flops=tiles * 200_000_000, bytes_accessed=4_000_000, transcendentals=tiles * 131072)

    packed = pl.pallas_call(
        pack_kernel,
        out_shape=shape((1, block + LIST_ROWS, width), bf16),
        in_specs=[HBM, HBM, HBM],
        out_specs=VMEM,
        scratch_shapes=[
            pltpu.SMEM((1, 3, 1, cap), i32), pltpu.SMEM((1, 1), i32), pltpu.SemaphoreType.DMA((3,)),
        ],
        compiler_params=most,
        name="pack",
    )(features, tile_coords.transpose(0, 3, 1, 2), tile_count)
    lined = [packed] + [swap(packed, 2 * k) for k in range(1, lines)]

    nearest_first = sorted(range(1, readers), key=lambda k: (k.bit_count(), k))

    def to_readers(block):
        there = {k: swap(block, blks * k) for k in nearest_first}
        return [there[k] for k in range(1, readers)]

    columns = [packed] + to_readers(packed)

    bits = (0, (readers - 1).bit_length() - 1)
    cot_parts = [cotangent[None, half * k : half * (k + 1)] for k in range(2)]
    cot_other = [swap(part, blks << bit) for part, bit in zip(cot_parts, bits)]

    column_lists = jnp.concatenate([entry[:, block:, :128] for entry in columns], 0)

    def work(kernel, lists, count, name):
        return pl.pallas_call(
            functools.partial(kernel, sizes),
            out_shape=shape((2 * count * cap + 5,), i32),
            in_specs=[HBM],
            out_specs=SMEM,
            scratch_shapes=[pltpu.SMEM((count, 128), i32), pltpu.SemaphoreType.DMA],
            compiler_params=some,
            cost_estimate=cost(1),
            name=name,
        )(lists[:, 0].astype(i32))

    key_work = work(key_work_kernel, column_lists, readers, "key_work")

    stacks = shape((HEADS // 2, 2 * head, 2 * block), bf16)
    own = shape((block, width), bf16)
    square = shape((width, width), bf16)
    weight = pltpu.VMEM((width, width), bf16)
    rows_low, rows_wide = pltpu.VMEM((block, width), bf16), pltpu.VMEM((block, width), f32)
    prepared = pl.pallas_call(
        prepare_kernel,
        out_shape=(stacks, stacks, own, own, square, square, square),
        in_specs=[HBM] * 5,
        out_specs=(VMEM,) * 7,
        scratch_shapes=[rows_low, rows_low, weight, weight, weight, pltpu.SemaphoreType.DMA((5,))],
        compiler_params=most,
        cost_estimate=cost(2),
        name="prepare",
    )(after(features, columns), cotangent, w_query, w_key, w_value)
    query_stack, cot_stack, keys, values, w_query_t, w_key_t, w_value_t = prepared

    line = jnp.concatenate([entry[:, :block] for entry in lined[1:]], 0)
    line = after(line, columns, cot_other)
    there = to_readers(line)
    near = jnp.concatenate([entry[:, :block] for entry in columns] + [line], 0)

    pairs = [part for k in range(2) for part in (cot_parts[k], cot_other[k])]
    pieces = [after(jnp.concatenate(pairs, 0), near)]
    done_first = (key_work, prepared)
    mask = blks // 2
    while mask > 1:
        pieces += [swap(after(piece, done_first) if at else piece, mask) for at, piece in enumerate(pieces)]
        mask //= 2

    line_lists = jnp.concatenate([entry[:, block:, :128] for entry in lined], 0)
    line_lists = after(line_lists, pieces[lines // 2])
    row_lists = jnp.concatenate([line_lists, swap(line_lists, 1)], 0)
    query_work = work(query_work_kernel, row_lists, blks, "query_work")
    here = [near] + there
    rows_all = here + [swap(after(near, pieces[lines // 2]), 1)] + [swap(group, 1) for group in there]

    stack_space = pltpu.VMEM(stacks.shape, bf16)
    buffer = pltpu.VMEM((2, TILES * block, width), bf16)
    word_buffer = pltpu.VMEM((2, TILES, words, block), i32)
    bias = pltpu.VMEM((TILES * block, block), f32)
    turned = pltpu.VMEM((width, block), f32)
    per_head = pltpu.VMEM((HEADS, block), f32)
    own_stats = pltpu.VMEM((2 * HEADS, block), f32)
    met = pltpu.VMEM((HEADS, TILES * block, block), f32)
    pair_met = pltpu.VMEM((HEADS // 2, block, 2 * TILES * block), f32)
    pair_rows = pltpu.VMEM((HEADS // 2, 2 * TILES * block, 2 * head), bf16)
    row_sems = pltpu.SemaphoreType.DMA((2, TILES, 2))

    attn_out, stats = pl.pallas_call(
        functools.partial(forward_kernel, sizes),
        out_shape=(own, shape((devices, 2 * HEADS, block), f32)),
        in_specs=[SMEM] + [VMEM] * 4 + [HBM] * (1 + 2 * readers),
        out_specs=(VMEM, VMEM),
        scratch_shapes=[own_stats, buffer, word_buffer, bias, per_head, per_head, turned, met, row_sems],
        compiler_params=some,
        cost_estimate=cost(5),
        name="forward",
    )(query_work, query_stack, cotangent, w_key, w_value_t, masks, *rows_all)

    pieces[-1] = after(pieces[-1], stats)
    cots_here = []
    for k in range(2):
        part = jnp.concatenate([piece[2 * k : 2 * k + 2] for piece in pieces], 0)
        masks_left = [m for m in range(1, readers) if not m >> bits[k] & 1]
        cots_here.append((part, [swap(part, blks * m) for m in masks_left]))

    stats_all = lax.all_to_all(stats, axes, 0, 0, tiled=True)

    query_part = pl.pallas_call(
        functools.partial(query_grad_kernel, sizes),
        out_shape=shape((block, width), f32),
        in_specs=[SMEM] + [HBM] * (8 + 2 * readers),
        out_specs=VMEM,
        scratch_shapes=[
            stack_space, stack_space, own_stats, weight, weight, weight, weight, buffer, word_buffer, bias, turned,
            met, met, row_sems, pltpu.SemaphoreType.DMA((7,)),
        ],
        compiler_params=most,
        cost_estimate=cost(5),
        name="query_grad",
    )(query_work, query_stack, cot_stack, stats, w_query_t, w_key, w_key_t, w_value, masks, *rows_all)

    cots_all = []
    for first, rest in cots_here:
        cots_all += [first, *rest, swap(after(first, stats), 1)]
        cots_all += [swap(after(part, stats_all, query_part), 1) for part in rest]

    grad_features = pl.pallas_call(
        functools.partial(key_grad_kernel, sizes, bits),
        out_shape=own,
        in_specs=[SMEM] + [HBM] * (8 + 4 * readers),
        out_specs=VMEM,
        scratch_shapes=[
            rows_low, rows_low, rows_wide, weight, weight, weight,
            buffer, word_buffer, buffer, pltpu.VMEM((2, TILES, 2 * HEADS, block), f32), bias,
            pair_rows, pair_rows, pair_met, pair_met, rows_wide, rows_wide,
            row_sems, pltpu.SemaphoreType.DMA((2, TILES, 3)), pltpu.SemaphoreType.DMA((6,)),
        ],
        compiler_params=most,
        cost_estimate=cost(5),
        name="key_grad",
    )(key_work, keys, values, w_query, w_key_t, w_value_t, query_part, masks, stats_all, *rows_all, *cots_all)
    return attn_out, grad_features


def solution(mesh):
    return jax.shard_map(
        local,
        mesh=mesh,
        in_specs=(
            P(("reader", "blk"), None),
            P(("reader", "blk"), None),
            P(),
            P(),
            P(),
            P("reader", "blk", None, None),
            P("reader", "blk"),
            P(),
        ),
        out_specs=(P(("reader", "blk"), None), P(("reader", "blk"), None)),
        check_vma=False,
    )
```

```python
import functools

import jax
import jax.numpy as jnp
from jax import lax
from jax.experimental import pallas as pl
from jax.experimental.pallas import tpu as pltpu
from jax.sharding import PartitionSpec as P

HEADS = 8
NEG_FILL = -1e30
NT = (((1,), (1,)), ((), ()))
NN = (((1,), (0,)), ((), ()))
TILES = 2
LIST_ROWS = 16
VMEM_SOME = 40 * 1024 * 1024
VMEM_MOST = 58 * 1024 * 1024


def dot(a, b, dims=NN):
    return lax.dot_general(a, b, dims, preferred_element_type=jnp.float32)


def pair_stack(rows):
    lane = lax.broadcasted_iota(jnp.int32, rows.shape, 1)
    half = rows.shape[1] // 2
    zero = jnp.zeros_like(rows)
    return jnp.concatenate([jnp.where(lane < half, rows, zero), jnp.where(lane >= half, rows, zero)], 0)


def tile_bias(words, pattern, diag):
    count, size = words.shape
    keys = lax.broadcasted_iota(jnp.int32, (size, size), 0)
    queries = lax.broadcasted_iota(jnp.int32, (size, size), 1)
    spread = jnp.concatenate(
        [jnp.broadcast_to(words[g : g + 1], (size // count, size)) for g in range(count)], 0
    )
    bits = jnp.right_shift(spread, keys & 31) & 1
    same = keys - queries == jnp.where(diag, 0, 2 * size)
    return jnp.where((bits == 1) | same, jnp.where(pattern < 0, NEG_FILL, 0.0), NEG_FILL)


class Layout:
    def __init__(self, readers, blks, cap):
        self.readers, self.blks, self.cap = readers, blks, cap
        self.reader, self.blk = lax.axis_index("reader"), lax.axis_index("blk")
        self.me = self.reader * blks + self.blk

    def apart(self, device):
        far = jnp.bitwise_xor(device, self.me)
        reader, blk = far // self.blks, lax.rem(far, self.blks)
        return reader, blk // 2, blk & 1

    def row_place(self, device):
        reader, line, core = self.apart(device)
        near = line == 0
        group = jnp.where(near, 0, reader) + self.readers * core
        index = jnp.where(reader == 0, self.readers, 0) + line - 1
        return group, jnp.where(near, reader, index)

    def half_place(self, bit, device):
        reader, line, core = self.apart(device)
        first = jnp.right_shift(reader, bit) & 1
        top = (self.blks // 2 - 1).bit_length() - 1
        line = sum((jnp.right_shift(line, top - at) & 1) << at for at in range(top + 1))
        low = reader & ((1 << bit) - 1)
        rest = low + (jnp.right_shift(reader, bit + 1) << bit)
        return rest + self.readers // 2 * core, 2 * line + first


def start_copy(place, refs, make):
    group, where = place
    for g, ref in enumerate(refs):

        @pl.when(group == g)
        def _():
            make(ref.at[where]).start()


def pack_kernel(own_hbm, coords_hbm, count_hbm, out_ref, coords_ref, count_ref, sems):
    block = own_hbm.shape[0]
    cap = coords_ref.shape[3]
    copies = [
        pltpu.make_async_copy(coords_hbm, coords_ref, sems.at[0]),
        pltpu.make_async_copy(count_hbm, count_ref, sems.at[1]),
        pltpu.make_async_copy(own_hbm, out_ref.at[0, pl.ds(0, block)], sems.at[2]),
    ]
    for copy in copies:
        copy.start()
    copies[0].wait()
    copies[1].wait()
    lane = lax.broadcasted_iota(jnp.int32, (LIST_ROWS, out_ref.shape[2]), 1)
    row = jnp.zeros(lane.shape, jnp.int32)
    for column in range(3):
        for slot in range(cap):
            row = jnp.where(lane == column * cap + slot, coords_ref[0, column, 0, slot], row)
    row = jnp.where(lane == 3 * cap, count_ref[0, 0], row)
    out_ref[0, block:] = row.astype(jnp.float32).astype(jnp.bfloat16)
    copies[2].wait()


def scan_list(lists_ref, cap, row, column, wanted, found, out_ref, block_of):
    def one_slot(slot, found):
        out_ref[2 * found + 1] = block_of(lists_ref[row, (1 - column) * cap + slot])
        out_ref[2 * found + 2] = lists_ref[row, 2 * cap + slot]
        return found + jnp.where(lists_ref[row, column * cap + slot] == wanted, 1, 0)

    return lax.fori_loop(0, lists_ref[row, 3 * cap], one_slot, found)


def close_work(found, out_ref):
    out_ref[2 * found + 1] = out_ref[2 * found - 1]
    out_ref[2 * found + 2] = -1
    out_ref[0] = (found + 1) // 2


def query_work_kernel(sizes, lists_hbm, work_ref, lists_ref, sem):
    readers, blks, cap = sizes
    layout = Layout(*sizes)
    copy = pltpu.make_async_copy(lists_hbm, lists_ref, sem)
    copy.start()
    copy.wait()

    def one(k, found):
        blk = jnp.bitwise_xor(k, layout.blk)
        row = k // 2 + (k & 1) * (blks // 2)
        put = lambda other: other * blks + blk
        return scan_list(lists_ref, cap, row, 0, layout.blk, found, work_ref, put)

    close_work(lax.fori_loop(0, blks, one, 0), work_ref)


def key_work_kernel(sizes, lists_hbm, work_ref, lists_ref, sem):
    readers, blks, cap = sizes
    layout = Layout(*sizes)
    copy = pltpu.make_async_copy(lists_hbm, lists_ref, sem)
    copy.start()
    copy.wait()

    def one(k, found):
        reader = jnp.bitwise_xor(k, layout.reader)
        put = lambda other: reader * blks + other
        return scan_list(lists_ref, cap, k, 1, layout.reader, found, work_ref, put)

    close_work(lax.fori_loop(0, readers, one, 0), work_ref)


def load(pairs, sems, first=0):
    copies = [pltpu.make_async_copy(src, into, sems.at[first + k]) for k, (src, into) in enumerate(pairs)]
    for copy in copies:
        copy.start()
    return copies


def prepare_kernel(
    own_hbm, cot_hbm, wq_hbm, wk_hbm, wv_hbm,
    query_stack_ref, cot_stack_ref, key_ref, value_ref, wqt_ref, wkt_ref, wvt_ref,
    own_ref, cot_ref, wq_ref, wk_ref, wv_ref, sems,
):
    loads = load((
        (own_hbm, own_ref), (wq_hbm, wq_ref), (wk_hbm, wk_ref), (wv_hbm, wv_ref), (cot_hbm, cot_ref),
    ), sems)
    for copy in loads:
        copy.wait()
    head = own_ref.shape[1] // HEADS
    queries = dot(own_ref[...], wq_ref[...]).astype(jnp.bfloat16) * jnp.bfloat16(head**-0.5)
    for p in range(HEADS // 2):
        pair = slice(2 * head * p, 2 * head * (p + 1))
        query_stack_ref[p] = pair_stack(queries[:, pair]).T
        cot_stack_ref[p] = pair_stack(cot_ref[:, pair]).T
    key_ref[...] = dot(own_ref[...], wk_ref[...]).astype(jnp.bfloat16)
    value_ref[...] = dot(own_ref[...], wv_ref[...]).astype(jnp.bfloat16)
    wqt_ref[...] = wq_ref[...].T
    wkt_ref[...] = wk_ref[...].T
    wvt_ref[...] = wv_ref[...].T


def step_entry(work_ref, index):
    at = 1 + 2 * TILES * index
    return [work_ref[at + 2 * t] for t in range(TILES)], [work_ref[at + 2 * t + 1] for t in range(TILES)]


def run_steps(work_ref, start, wait, body):
    total = work_ref[0]

    def step(index, carry):
        @pl.when(index + 1 < total)
        def _():
            start(lax.rem(index + 1, 2), *step_entry(work_ref, index + 1))

        slot = lax.rem(index, 2)
        wait(slot)
        body(slot, *step_entry(work_ref, index), index)
        return carry

    lax.fori_loop(0, total, step, 0)


def first_step(work_ref, start):
    start(0, *step_entry(work_ref, 0))


class Rows:
    def __init__(self, layout, groups, mask_ref, buf, words, sems, block):
        self.layout, self.groups, self.mask_ref = layout, groups, mask_ref
        self.buf, self.words, self.sems, self.block = buf, words, sems, block

    def rows(self, slot, t):
        into = self.buf.at[slot, pl.ds(t * self.block, self.block)]
        return lambda src: pltpu.make_async_copy(src, into, self.sems.at[slot, t, 0])

    def mask(self, slot, t, pattern):
        return pltpu.make_async_copy(self.mask_ref.at[pattern], self.words.at[slot, t], self.sems.at[slot, t, 1])

    def start(self, slot, blocks, patterns):
        for t in range(TILES):
            start_copy(self.layout.row_place(blocks[t]), self.groups, self.rows(slot, t))
            self.mask(slot, t, jnp.maximum(patterns[t], 0)).start()

    def wait(self, slot):
        for t in range(TILES):
            self.rows(slot, t)(self.groups[0].at[0]).wait()
            self.mask(slot, t, 0).wait()

    def bias(self, slot, blocks, patterns):
        parts = [
            tile_bias(self.words[slot, t], patterns[t], blocks[t] == self.layout.me) for t in range(TILES)
        ]
        return jnp.concatenate(parts, 0)


def forward_kernel(sizes, work_ref, stack_ref, cot_ref, wk_ref, wvt_ref, mask_ref, *refs):
    count = 2 * sizes[0]
    groups, refs = refs[:count], refs[count:]
    out_ref, sent_ref, stats_ref, buf, words, bias_ref, max_ref, sum_ref, acc_ref, score_ref, expo_ref, sems = refs
    layout = Layout(*sizes)
    block, width = cot_ref.shape
    head = width // HEADS
    rows_in = Rows(layout, groups, mask_ref, buf, words, sems, block)
    first_step(work_ref, rows_in.start)
    max_ref[...] = jnp.full(max_ref.shape, NEG_FILL, jnp.float32)
    sum_ref[...] = jnp.zeros(sum_ref.shape, jnp.float32)
    acc_ref[...] = jnp.zeros(acc_ref.shape, jnp.float32)

    def tiles(slot, blocks, patterns, index):
        rows = buf[slot]
        keys = dot(rows, wk_ref[...]).astype(jnp.bfloat16)
        values = dot(wvt_ref[...], rows, NT).astype(jnp.bfloat16)
        bias_ref[...] = rows_in.bias(slot, blocks, patterns)
        for p in range(HEADS // 2):
            scores = dot(keys[:, 2 * head * p : 2 * head * (p + 1)], stack_ref[p])
            for e in range(2):
                score_ref[2 * p + e] = scores[:, block * e : block * (e + 1)] + bias_ref[...]
        old = max_ref[...]
        tops = [jnp.max(score_ref[h], axis=0, keepdims=True) for h in range(HEADS)]
        new = jnp.maximum(old, jnp.concatenate(tops, 0))
        fade = jnp.exp(old - new)
        max_ref[...] = new
        sums = []
        for h in range(HEADS):
            expo = jnp.exp(score_ref[h] - new[h : h + 1])
            sums.append(jnp.sum(expo, axis=0, keepdims=True))
            expo_ref[h] = expo.astype(jnp.bfloat16)
        sum_ref[...] = sum_ref[...] * fade + jnp.concatenate(sums, 0)
        for h in range(HEADS):
            at = slice(head * h, head * (h + 1))
            acc_ref[at] = acc_ref[at] * fade[h : h + 1] + dot(values[at], expo_ref[h])

    run_steps(work_ref, rows_in.start, rows_in.wait, tiles)
    inverse = 1.0 / sum_ref[...]
    cot = cot_ref[...].astype(jnp.float32).T
    stats_ref[0:HEADS] = max_ref[...] + jnp.log(sum_ref[...])
    for h in range(HEADS):
        at = slice(head * h, head * (h + 1))
        outputs = acc_ref[at] * inverse[h : h + 1]
        acc_ref[at] = outputs
        stats_ref[HEADS + h : HEADS + h + 1] = jnp.sum(outputs * cot[at], axis=0, keepdims=True)
    sent_ref[...] = jnp.broadcast_to(stats_ref[...], sent_ref.shape)
    out_ref[...] = acc_ref[...].T.astype(out_ref.dtype)


def tile_grads(scores, d_probs, lse, delta):
    prob = jnp.exp(scores - lse)
    return prob.astype(jnp.bfloat16), (prob * (d_probs - delta)).astype(jnp.bfloat16)


def query_grad_kernel(
    sizes, work_ref, stack_hbm, cot_stack_hbm, stats_hbm, wqt_hbm, wk_hbm, wkt_hbm, wv_hbm, mask_ref, *refs
):
    count = 2 * sizes[0]
    groups, refs = refs[:count], refs[count:]
    part_ref, stack_ref, cot_stack_ref, stats_ref, wqt_ref, wk_ref, wkt_ref, wv_ref = refs[:8]
    buf, words, bias_ref, acc_ref, score_ref, d_prob_ref, sems, w_sems = refs[8:]
    layout = Layout(*sizes)
    block, width = part_ref.shape
    head = width // HEADS
    rows_in = Rows(layout, groups, mask_ref, buf, words, sems, block)
    first_step(work_ref, rows_in.start)
    loads = load((
        (wk_hbm, wk_ref), (stack_hbm, stack_ref), (wv_hbm, wv_ref), (cot_stack_hbm, cot_stack_ref),
        (wkt_hbm, wkt_ref), (stats_hbm.at[0], stats_ref), (wqt_hbm, wqt_ref),
    ), w_sems)
    acc_ref[...] = jnp.zeros(acc_ref.shape, jnp.float32)
    for copy in loads[:6]:
        copy.wait()

    def tiles(slot, blocks, patterns, index):
        rows = buf[slot]
        keys = dot(rows, wk_ref[...]).astype(jnp.bfloat16)
        values = dot(rows, wv_ref[...]).astype(jnp.bfloat16)
        keys_t = dot(wkt_ref[...], rows, NT).astype(jnp.bfloat16)
        bias_ref[...] = rows_in.bias(slot, blocks, patterns)
        for p in range(HEADS // 2):
            pair = slice(2 * head * p, 2 * head * (p + 1))
            scores = dot(keys[:, pair], stack_ref[p])
            d_probs = dot(values[:, pair], cot_stack_ref[p])
            for e in range(2):
                of = slice(block * e, block * (e + 1))
                score_ref[2 * p + e] = scores[:, of] + bias_ref[...]
                d_prob_ref[2 * p + e] = d_probs[:, of]
        for h in range(HEADS):
            _, d_scores = tile_grads(
                score_ref[h], d_prob_ref[h], stats_ref[h : h + 1], stats_ref[HEADS + h : HEADS + h + 1]
            )
            at = slice(head * h, head * (h + 1))
            acc_ref[at] += dot(keys_t[at], d_scores)

    run_steps(work_ref, rows_in.start, rows_in.wait, tiles)
    loads[6].wait()
    grad = (acc_ref[...].T * (head**-0.5)).astype(jnp.bfloat16)
    part_ref[...] = dot(grad, wqt_ref[...])


def key_grad_kernel(
    sizes, bits, work_ref, key_hbm, value_hbm, wq_hbm, wkt_hbm, wvt_hbm, part_hbm, mask_ref, stats_all_ref, *refs
):
    readers = sizes[0]
    count = 2 * readers
    groups, refs = refs[:count], refs[count:]
    halves, refs = (refs[:readers], refs[readers : 2 * readers]), refs[2 * readers :]
    out_ref, key_ref, value_ref, part_ref, wq_ref, wkt_ref, wvt_ref, buf, words, cot_buf, stats, bias_ref = refs[:12]
    query_stack_ref, cot_stack_ref, score_ref, d_prob_ref, prob_ref, d_score_ref = refs[12:18]
    key_acc, value_acc, sems, c_sems, w_sems = refs[18:]
    layout = Layout(*sizes)
    block, width = out_ref.shape
    head = width // HEADS
    rows_in = Rows(layout, groups, mask_ref, buf, words, sems, block)

    def half_copy(slot, t, k):
        into = cot_buf.at[slot, pl.ds(t * block + block // 2 * k, block // 2)]
        return lambda src: pltpu.make_async_copy(src, into, c_sems.at[slot, t, k])

    def stats_copy(slot, t, query):
        return pltpu.make_async_copy(stats_all_ref.at[query], stats.at[slot, t], c_sems.at[slot, t, 2])

    def start(slot, blocks, patterns):
        rows_in.start(slot, blocks, patterns)
        for t in range(TILES):
            stats_copy(slot, t, blocks[t]).start()
            for k in range(2):
                start_copy(layout.half_place(bits[k], blocks[t]), halves[k], half_copy(slot, t, k))

    def wait(slot):
        rows_in.wait(slot)
        for t in range(TILES):
            stats_copy(slot, t, 0).wait()
            for k in range(2):
                half_copy(slot, t, k)(halves[k][0].at[0]).wait()

    first_step(work_ref, start)
    loads = load(((wq_hbm, wq_ref), (key_hbm, key_ref), (value_hbm, value_ref)), w_sems)
    key_acc[...] = jnp.zeros(key_acc.shape, jnp.float32)
    value_acc[...] = jnp.zeros(value_acc.shape, jnp.float32)
    for copy in loads:
        copy.wait()
    loads = load(((wkt_hbm, wkt_ref), (wvt_hbm, wvt_ref), (part_hbm, part_ref)), w_sems, 3)

    def tiles(slot, blocks, patterns, index):
        queries = dot(buf[slot], wq_ref[...]).astype(jnp.bfloat16) * jnp.bfloat16(head**-0.5)
        bias_ref[...] = rows_in.bias(slot, blocks, patterns)
        cots = cot_buf[slot]
        pairs = [slice(2 * head * p, 2 * head * (p + 1)) for p in range(HEADS // 2)]
        of_tile = [slice(block * t, block * (t + 1)) for t in range(TILES)]
        for p, pair in enumerate(pairs):
            query_stack_ref[p] = jnp.concatenate([pair_stack(queries[of, pair]) for of in of_tile], 0)
            cot_stack_ref[p] = jnp.concatenate([pair_stack(cots[of, pair]) for of in of_tile], 0)
            score_ref[p] = dot(key_ref[:, pair], query_stack_ref[p], NT)
            d_prob_ref[p] = dot(value_ref[:, pair], cot_stack_ref[p], NT)
        for p in range(HEADS // 2):
            for t in range(TILES):
                for e in range(2):
                    h = 2 * p + e
                    of = slice(block * (2 * t + e), block * (2 * t + e + 1))
                    prob_ref[p, :, of], d_score_ref[p, :, of] = tile_grads(
                        score_ref[p, :, of] + bias_ref[of_tile[t]], d_prob_ref[p, :, of], stats[slot, t, h : h + 1],
                        stats[slot, t, HEADS + h : HEADS + h + 1],
                    )
        for p, pair in enumerate(pairs):
            value_acc[:, pair] += dot(prob_ref[p], cot_stack_ref[p])
            key_acc[:, pair] += dot(d_score_ref[p], query_stack_ref[p])

    run_steps(work_ref, start, wait, tiles)
    for copy in loads:
        copy.wait()
    grad = part_ref[...] + dot(key_acc[...].astype(jnp.bfloat16), wkt_ref[...])
    grad = grad + dot(value_acc[...].astype(jnp.bfloat16), wvt_ref[...])
    out_ref[...] = grad.astype(out_ref.dtype)


VMEM = pl.BlockSpec(memory_space=pltpu.VMEM)
SMEM = pl.BlockSpec(memory_space=pltpu.SMEM)
HBM = pl.BlockSpec(memory_space=pltpu.HBM)


def swap(block, mask):
    axes = ("reader", "blk")
    count = lax.axis_size("reader") * lax.axis_size("blk")
    return lax.ppermute(block, axes, [(i, i ^ mask) for i in range(count)])


def after(value, *others):
    return lax.optimization_barrier((value, *others))[0]


def local(features, cotangent, w_query, w_key, w_value, tile_coords, tile_count, mask_table):
    block, width = features.shape
    readers, blks, cap = lax.axis_size("reader"), lax.axis_size("blk"), tile_coords.shape[2]
    assert block == mask_table.shape[1] and 3 * cap < 128
    sizes = (readers, blks, cap)
    devices, lines = readers * blks, blks // 2
    f32, bf16, i32 = jnp.float32, jnp.bfloat16, jnp.int32
    shape = jax.ShapeDtypeStruct
    masks = mask_table.transpose(0, 2, 1)
    words = masks.shape[1]
    head = width // HEADS
    half = block // 2
    some = pltpu.CompilerParams(vmem_limit_bytes=VMEM_SOME)
    most = pltpu.CompilerParams(vmem_limit_bytes=VMEM_MOST)
    axes = ("reader", "blk")

    def cost(tiles):
        return pl.CostEstimate(flops=tiles * 200_000_000, bytes_accessed=4_000_000, transcendentals=tiles * 131072)

    packed = pl.pallas_call(
        pack_kernel,
        out_shape=shape((1, block + LIST_ROWS, width), bf16),
        in_specs=[HBM, HBM, HBM],
        out_specs=VMEM,
        scratch_shapes=[
            pltpu.SMEM((1, 3, 1, cap), i32), pltpu.SMEM((1, 1), i32), pltpu.SemaphoreType.DMA((3,)),
        ],
        compiler_params=most,
        name="pack",
    )(features, tile_coords.transpose(0, 3, 1, 2), tile_count)
    lined = [packed] + [swap(packed, 2 * k) for k in range(1, lines)]

    nearest_first = sorted(range(1, readers), key=lambda k: (k.bit_count(), k))

    def to_readers(block):
        there = {k: swap(block, blks * k) for k in nearest_first}
        return [there[k] for k in range(1, readers)]

    columns = [packed] + to_readers(packed)

    bits = (0, (readers - 1).bit_length() - 1)
    cot_parts = [cotangent[None, half * k : half * (k + 1)] for k in range(2)]
    cot_other = [swap(part, blks << bit) for part, bit in zip(cot_parts, bits)]

    column_lists = jnp.concatenate([entry[:, block:, :128] for entry in columns], 0)

    def work(kernel, lists, count, name):
        return pl.pallas_call(
            functools.partial(kernel, sizes),
            out_shape=shape((2 * count * cap + 5,), i32),
            in_specs=[HBM],
            out_specs=SMEM,
            scratch_shapes=[pltpu.SMEM((count, 128), i32), pltpu.SemaphoreType.DMA],
            compiler_params=some,
            cost_estimate=cost(1),
            name=name,
        )(lists[:, 0].astype(i32))

    key_work = work(key_work_kernel, column_lists, readers, "key_work")

    stacks = shape((HEADS // 2, 2 * head, 2 * block), bf16)
    own = shape((block, width), bf16)
    square = shape((width, width), bf16)
    weight = pltpu.VMEM((width, width), bf16)
    rows_low, rows_wide = pltpu.VMEM((block, width), bf16), pltpu.VMEM((block, width), f32)
    prepared = pl.pallas_call(
        prepare_kernel,
        out_shape=(stacks, stacks, own, own, square, square, square),
        in_specs=[HBM] * 5,
        out_specs=(VMEM,) * 7,
        scratch_shapes=[rows_low, rows_low, weight, weight, weight, pltpu.SemaphoreType.DMA((5,))],
        compiler_params=most,
        cost_estimate=cost(2),
        name="prepare",
    )(after(features, columns), cotangent, w_query, w_key, w_value)
    query_stack, cot_stack, keys, values, w_query_t, w_key_t, w_value_t = prepared

    line = jnp.concatenate([entry[:, :block] for entry in lined[1:]], 0)
    line = after(line, columns, cot_other)
    there = to_readers(line)
    near = jnp.concatenate([entry[:, :block] for entry in columns] + [line], 0)

    pairs = [part for k in range(2) for part in (cot_parts[k], cot_other[k])]
    pieces = [after(jnp.concatenate(pairs, 0), line)]
    done_first = (key_work, prepared)
    mask = blks // 2
    while mask > 1:
        pieces += [swap(after(piece, done_first) if at else piece, mask) for at, piece in enumerate(pieces)]
        mask //= 2

    line_lists = jnp.concatenate([entry[:, block:, :128] for entry in lined], 0)
    line_lists = after(line_lists, there[-1])
    row_lists = jnp.concatenate([line_lists, swap(line_lists, 1)], 0)
    query_work = work(query_work_kernel, row_lists, blks, "query_work")
    here = [near] + there
    rows_all = here + [swap(after(near, there[-1]), 1)] + [swap(group, 1) for group in there]

    cots_here = []
    for k in range(2):
        part = jnp.concatenate([piece[2 * k : 2 * k + 2] for piece in pieces], 0)
        masks_left = [m for m in range(1, readers) if not m >> bits[k] & 1]
        cots_here.append((part, [swap(after(part, here), blks * m) for m in masks_left]))

    stack_space = pltpu.VMEM(stacks.shape, bf16)
    buffer = pltpu.VMEM((2, TILES * block, width), bf16)
    word_buffer = pltpu.VMEM((2, TILES, words, block), i32)
    bias = pltpu.VMEM((TILES * block, block), f32)
    turned = pltpu.VMEM((width, block), f32)
    per_head = pltpu.VMEM((HEADS, block), f32)
    own_stats = pltpu.VMEM((2 * HEADS, block), f32)
    met = pltpu.VMEM((HEADS, TILES * block, block), f32)
    met_low = pltpu.VMEM((HEADS, TILES * block, block), bf16)
    pair_low = pltpu.VMEM((HEADS // 2, block, 2 * TILES * block), bf16)
    pair_met = pltpu.VMEM((HEADS // 2, block, 2 * TILES * block), f32)
    pair_rows = pltpu.VMEM((HEADS // 2, 2 * TILES * block, 2 * head), bf16)
    row_sems = pltpu.SemaphoreType.DMA((2, TILES, 2))

    attn_out, stats = pl.pallas_call(
        functools.partial(forward_kernel, sizes),
        out_shape=(own, shape((devices, 2 * HEADS, block), f32)),
        in_specs=[SMEM] + [VMEM] * 4 + [HBM] * (1 + 2 * readers),
        out_specs=(VMEM, VMEM),
        scratch_shapes=[
            own_stats, buffer, word_buffer, bias, per_head, per_head, turned, met, met_low, row_sems,
        ],
        compiler_params=some,
        cost_estimate=cost(5),
        name="forward",
    )(query_work, query_stack, cotangent, w_key, w_value_t, masks, *rows_all)

    stats_all = lax.all_to_all(stats, axes, 0, 0, tiled=True)

    query_part = pl.pallas_call(
        functools.partial(query_grad_kernel, sizes),
        out_shape=shape((block, width), f32),
        in_specs=[SMEM] + [HBM] * (8 + 2 * readers),
        out_specs=VMEM,
        scratch_shapes=[
            stack_space, stack_space, own_stats, weight, weight, weight, weight, buffer, word_buffer, bias, turned,
            met, met, row_sems, pltpu.SemaphoreType.DMA((7,)),
        ],
        compiler_params=most,
        cost_estimate=cost(5),
        name="query_grad",
    )(query_work, query_stack, cot_stack, stats, w_query_t, w_key, w_key_t, w_value, masks, *rows_all)

    cots_all = []
    for first, rest in cots_here:
        cots_all += [first, *rest, swap(after(first, stats), 1)]
        cots_all += [swap(after(part, stats_all, query_part), 1) for part in rest]

    grad_features = pl.pallas_call(
        functools.partial(key_grad_kernel, sizes, bits),
        out_shape=own,
        in_specs=[SMEM] + [HBM] * (8 + 4 * readers),
        out_specs=VMEM,
        scratch_shapes=[
            rows_low, rows_low, rows_wide, weight, weight, weight,
            buffer, word_buffer, buffer, pltpu.VMEM((2, TILES, 2 * HEADS, block), f32), bias,
            pair_rows, pair_rows, pair_met, pair_met, pair_low, pair_low, rows_wide, rows_wide,
            row_sems, pltpu.SemaphoreType.DMA((2, TILES, 3)), pltpu.SemaphoreType.DMA((6,)),
        ],
        compiler_params=most,
        cost_estimate=cost(5),
        name="key_grad",
    )(key_work, keys, values, w_query, w_key_t, w_value_t, query_part, masks, stats_all, *rows_all, *cots_all)
    return attn_out, grad_features


def solution(mesh):
    return jax.shard_map(
        local,
        mesh=mesh,
        in_specs=(
            P(("reader", "blk"), None),
            P(("reader", "blk"), None),
            P(),
            P(),
            P(),
            P("reader", "blk", None, None),
            P("reader", "blk"),
            P(),
        ),
        out_specs=(P(("reader", "blk"), None), P(("reader", "blk"), None)),
        check_vma=False,
    )
```

```python
import functools

import jax
import jax.numpy as jnp
from jax import lax
from jax.experimental import pallas as pl
from jax.experimental.pallas import tpu as pltpu
from jax.sharding import PartitionSpec as P

HEADS = 8
NEG_FILL = -1e30
NT = (((1,), (1,)), ((), ()))
NN = (((1,), (0,)), ((), ()))
TILES = 2
LIST_ROWS = 16
VMEM_SOME = 40 * 1024 * 1024
VMEM_MOST = 58 * 1024 * 1024


def dot(a, b, dims=NN):
    return lax.dot_general(a, b, dims, preferred_element_type=jnp.float32)


def pair_stack(rows):
    lane = lax.broadcasted_iota(jnp.int32, rows.shape, 1)
    half = rows.shape[1] // 2
    zero = jnp.zeros_like(rows)
    return jnp.concatenate([jnp.where(lane < half, rows, zero), jnp.where(lane >= half, rows, zero)], 0)


def tile_bias(words, pattern, diag):
    count, size = words.shape
    keys = lax.broadcasted_iota(jnp.int32, (size, size), 0)
    queries = lax.broadcasted_iota(jnp.int32, (size, size), 1)
    spread = jnp.concatenate(
        [jnp.broadcast_to(words[g : g + 1], (size // count, size)) for g in range(count)], 0
    )
    bits = jnp.right_shift(spread, keys & 31) & 1
    same = keys - queries == jnp.where(diag, 0, 2 * size)
    return jnp.where((bits == 1) | same, jnp.where(pattern < 0, NEG_FILL, 0.0), NEG_FILL)


class Layout:
    def __init__(self, readers, blks, cap):
        self.readers, self.blks, self.cap = readers, blks, cap
        self.reader, self.blk = lax.axis_index("reader"), lax.axis_index("blk")
        self.me = self.reader * blks + self.blk

    def apart(self, device):
        far = jnp.bitwise_xor(device, self.me)
        reader, blk = far // self.blks, lax.rem(far, self.blks)
        return reader, blk // 2, blk & 1

    def row_place(self, device):
        reader, line, core = self.apart(device)
        near = line == 0
        group = jnp.where(near, 0, reader) + self.readers * core
        index = jnp.where(reader == 0, self.readers, 0) + line - 1
        return group, jnp.where(near, reader, index)

    def cot_place(self, device):
        reader, line, core = self.apart(device)
        lines = self.blks // 2
        top = (lines - 1).bit_length() - 1
        piece = sum((jnp.right_shift(line, top - at) & 1) << at for at in range(top + 1))
        return piece + lines * core, reader


def start_copy(place, refs, make):
    group, where = place
    for g, ref in enumerate(refs):

        @pl.when(group == g)
        def _():
            make(ref.at[where]).start()


def pack_kernel(own_hbm, coords_hbm, count_hbm, out_ref, coords_ref, count_ref, sems):
    block = own_hbm.shape[0]
    cap = coords_ref.shape[3]
    copies = [
        pltpu.make_async_copy(coords_hbm, coords_ref, sems.at[0]),
        pltpu.make_async_copy(count_hbm, count_ref, sems.at[1]),
        pltpu.make_async_copy(own_hbm, out_ref.at[0, pl.ds(0, block)], sems.at[2]),
    ]
    for copy in copies:
        copy.start()
    copies[0].wait()
    copies[1].wait()
    lane = lax.broadcasted_iota(jnp.int32, (LIST_ROWS, out_ref.shape[2]), 1)
    row = jnp.zeros(lane.shape, jnp.int32)
    for column in range(3):
        for slot in range(cap):
            row = jnp.where(lane == column * cap + slot, coords_ref[0, column, 0, slot], row)
    row = jnp.where(lane == 3 * cap, count_ref[0, 0], row)
    out_ref[0, block:] = row.astype(jnp.float32).astype(jnp.bfloat16)
    copies[2].wait()


def scan_list(lists_ref, cap, row, column, wanted, found, out_ref, block_of):
    def one_slot(slot, found):
        out_ref[2 * found + 1] = block_of(lists_ref[row, (1 - column) * cap + slot])
        out_ref[2 * found + 2] = lists_ref[row, 2 * cap + slot]
        return found + jnp.where(lists_ref[row, column * cap + slot] == wanted, 1, 0)

    return lax.fori_loop(0, lists_ref[row, 3 * cap], one_slot, found)


def close_work(found, out_ref):
    out_ref[2 * found + 1] = out_ref[2 * found - 1]
    out_ref[2 * found + 2] = -1
    out_ref[0] = (found + 1) // 2


def query_work_kernel(sizes, lists_hbm, work_ref, lists_ref, sem):
    readers, blks, cap = sizes
    layout = Layout(*sizes)
    copy = pltpu.make_async_copy(lists_hbm, lists_ref, sem)
    copy.start()
    copy.wait()

    def one(k, found):
        blk = jnp.bitwise_xor(k, layout.blk)
        row = k // 2 + (k & 1) * (blks // 2)
        put = lambda other: other * blks + blk
        return scan_list(lists_ref, cap, row, 0, layout.blk, found, work_ref, put)

    close_work(lax.fori_loop(0, blks, one, 0), work_ref)


def key_work_kernel(sizes, lists_hbm, work_ref, lists_ref, sem):
    readers, blks, cap = sizes
    layout = Layout(*sizes)
    copy = pltpu.make_async_copy(lists_hbm, lists_ref, sem)
    copy.start()
    copy.wait()

    def one(k, found):
        reader = jnp.bitwise_xor(k, layout.reader)
        put = lambda other: reader * blks + other
        return scan_list(lists_ref, cap, k, 1, layout.reader, found, work_ref, put)

    close_work(lax.fori_loop(0, readers, one, 0), work_ref)


def load(pairs, sems):
    copies = [pltpu.make_async_copy(src, into, sems.at[k]) for k, (src, into) in enumerate(pairs)]
    for copy in copies:
        copy.start()
    return copies


def prepare_kernel(
    own_hbm, cot_hbm, wq_hbm, wk_hbm, wv_hbm,
    query_stack_ref, cot_stack_ref, key_ref, value_ref, wqt_ref, wkt_ref, wvt_ref,
    own_ref, cot_ref, wq_ref, wk_ref, wv_ref, sems,
):
    loads = load((
        (own_hbm, own_ref), (wq_hbm, wq_ref), (wk_hbm, wk_ref), (wv_hbm, wv_ref), (cot_hbm, cot_ref),
    ), sems)
    for copy in loads:
        copy.wait()
    head = own_ref.shape[1] // HEADS
    queries = dot(own_ref[...], wq_ref[...]).astype(jnp.bfloat16) * jnp.bfloat16(head**-0.5)
    for p in range(HEADS // 2):
        pair = slice(2 * head * p, 2 * head * (p + 1))
        query_stack_ref[p] = pair_stack(queries[:, pair]).T
        cot_stack_ref[p] = pair_stack(cot_ref[:, pair]).T
    key_ref[...] = dot(own_ref[...], wk_ref[...]).astype(jnp.bfloat16)
    value_ref[...] = dot(own_ref[...], wv_ref[...]).astype(jnp.bfloat16)
    wqt_ref[...] = wq_ref[...].T
    wkt_ref[...] = wk_ref[...].T
    wvt_ref[...] = wv_ref[...].T


def step_entry(work_ref, index):
    at = 1 + 2 * TILES * index
    return [work_ref[at + 2 * t] for t in range(TILES)], [work_ref[at + 2 * t + 1] for t in range(TILES)]


def run_steps(work_ref, start, wait, body):
    total = work_ref[0]

    def step(index, carry):
        @pl.when(index + 1 < total)
        def _():
            start(lax.rem(index + 1, 2), *step_entry(work_ref, index + 1))

        slot = lax.rem(index, 2)
        wait(slot)
        body(slot, *step_entry(work_ref, index), index)
        return carry

    lax.fori_loop(0, total, step, 0)


def first_step(work_ref, start):
    start(0, *step_entry(work_ref, 0))


class Rows:
    def __init__(self, layout, groups, mask_ref, buf, words, sems, block):
        self.layout, self.groups, self.mask_ref = layout, groups, mask_ref
        self.buf, self.words, self.sems, self.block = buf, words, sems, block

    def rows(self, slot, t):
        into = self.buf.at[slot, pl.ds(t * self.block, self.block)]
        return lambda src: pltpu.make_async_copy(src, into, self.sems.at[slot, t, 0])

    def mask(self, slot, t, pattern):
        return pltpu.make_async_copy(self.mask_ref.at[pattern], self.words.at[slot, t], self.sems.at[slot, t, 1])

    def start(self, slot, blocks, patterns):
        for t in range(TILES):
            start_copy(self.layout.row_place(blocks[t]), self.groups, self.rows(slot, t))
            self.mask(slot, t, jnp.maximum(patterns[t], 0)).start()

    def wait(self, slot):
        for t in range(TILES):
            self.rows(slot, t)(self.groups[0].at[0]).wait()
            self.mask(slot, t, 0).wait()

    def bias(self, slot, blocks, patterns):
        parts = [
            tile_bias(self.words[slot, t], patterns[t], blocks[t] == self.layout.me) for t in range(TILES)
        ]
        return jnp.concatenate(parts, 0)


def forward_kernel(sizes, work_ref, stack_ref, cot_ref, wk_ref, wvt_ref, mask_ref, *refs):
    count = 2 * sizes[0]
    groups, refs = refs[:count], refs[count:]
    out_ref, sent_ref, stats_ref, buf, words, bias_ref, max_ref, sum_ref, acc_ref, score_ref, sems = refs
    layout = Layout(*sizes)
    block, width = cot_ref.shape
    head = width // HEADS
    rows_in = Rows(layout, groups, mask_ref, buf, words, sems, block)
    first_step(work_ref, rows_in.start)
    max_ref[...] = jnp.full(max_ref.shape, NEG_FILL, jnp.float32)
    sum_ref[...] = jnp.zeros(sum_ref.shape, jnp.float32)
    acc_ref[...] = jnp.zeros(acc_ref.shape, jnp.float32)

    def tiles(slot, blocks, patterns, index):
        rows = buf[slot]
        keys = dot(rows, wk_ref[...]).astype(jnp.bfloat16)
        values = dot(wvt_ref[...], rows, NT).astype(jnp.bfloat16)
        bias_ref[...] = rows_in.bias(slot, blocks, patterns)
        for p in range(HEADS // 2):
            scores = dot(keys[:, 2 * head * p : 2 * head * (p + 1)], stack_ref[p])
            for e in range(2):
                score_ref[2 * p + e] = scores[:, block * e : block * (e + 1)] + bias_ref[...]
        for h in range(HEADS):
            s = score_ref[h]
            old = max_ref[h : h + 1]
            new = jnp.maximum(old, jnp.max(s, axis=0, keepdims=True))
            fade = jnp.exp(old - new)
            expo = jnp.exp(s - new)
            max_ref[h : h + 1] = new
            sum_ref[h : h + 1] = sum_ref[h : h + 1] * fade + jnp.sum(expo, axis=0, keepdims=True)
            at = slice(head * h, head * (h + 1))
            acc_ref[at] = acc_ref[at] * fade + dot(values[at], expo.astype(jnp.bfloat16))

    run_steps(work_ref, rows_in.start, rows_in.wait, tiles)
    inverse = 1.0 / sum_ref[...]
    cot = cot_ref[...].astype(jnp.float32).T
    stats_ref[0:HEADS] = max_ref[...] + jnp.log(sum_ref[...])
    for h in range(HEADS):
        at = slice(head * h, head * (h + 1))
        outputs = acc_ref[at] * inverse[h : h + 1]
        acc_ref[at] = outputs
        stats_ref[HEADS + h : HEADS + h + 1] = jnp.sum(outputs * cot[at], axis=0, keepdims=True)
    sent_ref[...] = jnp.broadcast_to(stats_ref[...], sent_ref.shape)
    out_ref[...] = acc_ref[...].T.astype(out_ref.dtype)


def tile_grads(scores, d_probs, lse, delta):
    prob = jnp.exp(scores - lse)
    return prob.astype(jnp.bfloat16), (prob * (d_probs - delta)).astype(jnp.bfloat16)


def query_grad_kernel(
    sizes, work_ref, stack_hbm, cot_stack_hbm, stats_hbm, wqt_hbm, wk_hbm, wkt_hbm, wv_hbm, mask_ref, *refs
):
    count = 2 * sizes[0]
    groups, refs = refs[:count], refs[count:]
    part_ref, stack_ref, cot_stack_ref, stats_ref, wqt_ref, wk_ref, wkt_ref, wv_ref = refs[:8]
    buf, words, bias_ref, acc_ref, score_ref, d_prob_ref, sems, w_sems = refs[8:]
    layout = Layout(*sizes)
    block, width = part_ref.shape
    head = width // HEADS
    rows_in = Rows(layout, groups, mask_ref, buf, words, sems, block)
    first_step(work_ref, rows_in.start)
    loads = load((
        (wk_hbm, wk_ref), (stack_hbm, stack_ref), (wv_hbm, wv_ref), (cot_stack_hbm, cot_stack_ref),
        (wkt_hbm, wkt_ref), (stats_hbm.at[0], stats_ref), (wqt_hbm, wqt_ref),
    ), w_sems)
    acc_ref[...] = jnp.zeros(acc_ref.shape, jnp.float32)
    for copy in loads[:6]:
        copy.wait()

    def tiles(slot, blocks, patterns, index):
        rows = buf[slot]
        keys = dot(rows, wk_ref[...]).astype(jnp.bfloat16)
        values = dot(rows, wv_ref[...]).astype(jnp.bfloat16)
        keys_t = dot(wkt_ref[...], rows, NT).astype(jnp.bfloat16)
        bias_ref[...] = rows_in.bias(slot, blocks, patterns)
        for p in range(HEADS // 2):
            pair = slice(2 * head * p, 2 * head * (p + 1))
            scores = dot(keys[:, pair], stack_ref[p])
            d_probs = dot(values[:, pair], cot_stack_ref[p])
            for e in range(2):
                of = slice(block * e, block * (e + 1))
                score_ref[2 * p + e] = scores[:, of] + bias_ref[...]
                d_prob_ref[2 * p + e] = d_probs[:, of]
        for h in range(HEADS):
            _, d_scores = tile_grads(
                score_ref[h], d_prob_ref[h], stats_ref[h : h + 1], stats_ref[HEADS + h : HEADS + h + 1]
            )
            at = slice(head * h, head * (h + 1))
            acc_ref[at] += dot(keys_t[at], d_scores)

    run_steps(work_ref, rows_in.start, rows_in.wait, tiles)
    loads[6].wait()
    grad = (acc_ref[...].T * (head**-0.5)).astype(jnp.bfloat16)
    part_ref[...] = dot(grad, wqt_ref[...])


def key_grad_kernel(
    sizes, work_ref, key_hbm, value_hbm, wq_hbm, wkt_hbm, wvt_hbm, part_hbm, mask_ref, stats_all_ref, *refs
):
    readers = sizes[0]
    count = 2 * readers
    groups, refs = refs[:count], refs[count:]
    cots, refs = refs[: sizes[1]], refs[sizes[1] :]
    out_ref, key_ref, value_ref, part_ref, wq_ref, wkt_ref, wvt_ref, buf, words, cot_buf, stats, bias_ref = refs[:12]
    query_stack_ref, cot_stack_ref, score_ref, d_prob_ref, key_acc, value_acc, sems, c_sems, w_sems = refs[12:]
    layout = Layout(*sizes)
    block, width = out_ref.shape
    head = width // HEADS
    rows_in = Rows(layout, groups, mask_ref, buf, words, sems, block)

    def cot_copy(slot, t):
        into = cot_buf.at[slot, pl.ds(t * block, block)]
        return lambda src: pltpu.make_async_copy(src, into, c_sems.at[slot, t, 0])

    def stats_copy(slot, t, query):
        return pltpu.make_async_copy(stats_all_ref.at[query], stats.at[slot, t], c_sems.at[slot, t, 1])

    def start(slot, blocks, patterns):
        rows_in.start(slot, blocks, patterns)
        for t in range(TILES):
            stats_copy(slot, t, blocks[t]).start()
            start_copy(layout.cot_place(blocks[t]), cots, cot_copy(slot, t))

    def wait(slot):
        rows_in.wait(slot)
        for t in range(TILES):
            stats_copy(slot, t, 0).wait()
            cot_copy(slot, t)(cots[0].at[0]).wait()

    first_step(work_ref, start)
    loads = load((
        (wq_hbm, wq_ref), (key_hbm, key_ref), (value_hbm, value_ref),
        (wkt_hbm, wkt_ref), (wvt_hbm, wvt_ref), (part_hbm, part_ref),
    ), w_sems)
    key_acc[...] = jnp.zeros(key_acc.shape, jnp.float32)
    value_acc[...] = jnp.zeros(value_acc.shape, jnp.float32)
    for copy in loads[:3]:
        copy.wait()

    def tiles(slot, blocks, patterns, index):
        queries = dot(buf[slot], wq_ref[...]).astype(jnp.bfloat16) * jnp.bfloat16(head**-0.5)
        bias_ref[...] = rows_in.bias(slot, blocks, patterns)
        cots = cot_buf[slot]
        pairs = [slice(2 * head * p, 2 * head * (p + 1)) for p in range(HEADS // 2)]
        of_tile = [slice(block * t, block * (t + 1)) for t in range(TILES)]
        for p, pair in enumerate(pairs):
            query_stack_ref[p] = jnp.concatenate([pair_stack(queries[of, pair]) for of in of_tile], 0)
            cot_stack_ref[p] = jnp.concatenate([pair_stack(cots[of, pair]) for of in of_tile], 0)
            score_ref[p] = dot(key_ref[:, pair], query_stack_ref[p], NT)
            d_prob_ref[p] = dot(value_ref[:, pair], cot_stack_ref[p], NT)
        for p, pair in enumerate(pairs):
            probs, d_scores = [], []
            for t in range(TILES):
                for e in range(2):
                    h = 2 * p + e
                    of = slice(block * (2 * t + e), block * (2 * t + e + 1))
                    prob, d_score = tile_grads(
                        score_ref[p, :, of] + bias_ref[of_tile[t]], d_prob_ref[p, :, of], stats[slot, t, h : h + 1],
                        stats[slot, t, HEADS + h : HEADS + h + 1],
                    )
                    probs.append(prob)
                    d_scores.append(d_score)
            value_acc[:, pair] += dot(jnp.concatenate(probs, 1), cot_stack_ref[p])
            key_acc[:, pair] += dot(jnp.concatenate(d_scores, 1), query_stack_ref[p])

    run_steps(work_ref, start, wait, tiles)
    for copy in loads[3:]:
        copy.wait()
    grad = part_ref[...] + dot(key_acc[...].astype(jnp.bfloat16), wkt_ref[...])
    grad = grad + dot(value_acc[...].astype(jnp.bfloat16), wvt_ref[...])
    out_ref[...] = grad.astype(out_ref.dtype)


VMEM = pl.BlockSpec(memory_space=pltpu.VMEM)
SMEM = pl.BlockSpec(memory_space=pltpu.SMEM)
HBM = pl.BlockSpec(memory_space=pltpu.HBM)


def swap(block, mask):
    axes = ("reader", "blk")
    count = lax.axis_size("reader") * lax.axis_size("blk")
    return lax.ppermute(block, axes, [(i, i ^ mask) for i in range(count)])


def after(value, *others):
    return lax.optimization_barrier((value, *others))[0]


def local(features, cotangent, w_query, w_key, w_value, tile_coords, tile_count, mask_table):
    block, width = features.shape
    readers, blks, cap = lax.axis_size("reader"), lax.axis_size("blk"), tile_coords.shape[2]
    assert block == mask_table.shape[1] and 3 * cap < 128
    sizes = (readers, blks, cap)
    devices, lines = readers * blks, blks // 2
    f32, bf16, i32 = jnp.float32, jnp.bfloat16, jnp.int32
    shape = jax.ShapeDtypeStruct
    masks = mask_table.transpose(0, 2, 1)
    words = masks.shape[1]
    head = width // HEADS
    some = pltpu.CompilerParams(vmem_limit_bytes=VMEM_SOME)
    most = pltpu.CompilerParams(vmem_limit_bytes=VMEM_MOST)
    axes = ("reader", "blk")

    def cost(tiles):
        return pl.CostEstimate(flops=tiles * 200_000_000, bytes_accessed=4_000_000, transcendentals=tiles * 131072)

    packed = pl.pallas_call(
        pack_kernel,
        out_shape=shape((1, block + LIST_ROWS, width), bf16),
        in_specs=[HBM, HBM, HBM],
        out_specs=VMEM,
        scratch_shapes=[
            pltpu.SMEM((1, 3, 1, cap), i32), pltpu.SMEM((1, 1), i32), pltpu.SemaphoreType.DMA((3,)),
        ],
        compiler_params=most,
        name="pack",
    )(features, tile_coords.transpose(0, 3, 1, 2), tile_count)
    lined = [packed] + [swap(packed, 2 * k) for k in range(1, lines)]

    nearest_first = sorted(range(1, readers), key=lambda k: (k.bit_count(), k))

    def to_readers(block):
        there = {k: swap(block, blks * k) for k in nearest_first}
        return [there[k] for k in range(1, readers)]

    own_rows = jnp.concatenate([packed, cotangent[None]], 1)
    columns = [own_rows] + to_readers(own_rows)
    column_lists = jnp.concatenate([entry[:, block : block + LIST_ROWS, :128] for entry in columns], 0)

    def work(kernel, lists, count, name):
        return pl.pallas_call(
            functools.partial(kernel, sizes),
            out_shape=shape((2 * count * cap + 5,), i32),
            in_specs=[HBM],
            out_specs=SMEM,
            scratch_shapes=[pltpu.SMEM((count, 128), i32), pltpu.SemaphoreType.DMA],
            compiler_params=some,
            cost_estimate=cost(1),
            name=name,
        )(lists[:, 0].astype(i32))

    key_work = work(key_work_kernel, column_lists, readers, "key_work")

    stacks = shape((HEADS // 2, 2 * head, 2 * block), bf16)
    own = shape((block, width), bf16)
    square = shape((width, width), bf16)
    weight = pltpu.VMEM((width, width), bf16)
    rows_low, rows_wide = pltpu.VMEM((block, width), bf16), pltpu.VMEM((block, width), f32)
    prepared = pl.pallas_call(
        prepare_kernel,
        out_shape=(stacks, stacks, own, own, square, square, square),
        in_specs=[HBM] * 5,
        out_specs=(VMEM,) * 7,
        scratch_shapes=[rows_low, rows_low, weight, weight, weight, pltpu.SemaphoreType.DMA((5,))],
        compiler_params=most,
        cost_estimate=cost(2),
        name="prepare",
    )(after(features, columns), cotangent, w_query, w_key, w_value)
    query_stack, cot_stack, keys, values, w_query_t, w_key_t, w_value_t = prepared

    line = jnp.concatenate([entry[:, :block] for entry in lined[1:]], 0)
    line = after(line, columns)
    there = to_readers(line)
    near = jnp.concatenate([entry[:, :block] for entry in columns] + [line], 0)

    pieces = [after(jnp.concatenate([entry[:, block + LIST_ROWS :] for entry in columns], 0), line)]
    done_first = (key_work, prepared)
    mask = blks // 2
    while mask > 1:
        pieces += [swap(after(piece, done_first) if at else piece, mask) for at, piece in enumerate(pieces)]
        mask //= 2

    line_lists = jnp.concatenate([entry[:, block:, :128] for entry in lined], 0)
    line_lists = after(line_lists, there[0])
    row_lists = jnp.concatenate([line_lists, swap(line_lists, 1)], 0)
    query_work = work(query_work_kernel, row_lists, blks, "query_work")
    here = [near] + there
    near_last = (there, pieces[1], pieces[lines // 2], key_work, prepared, query_work)
    rows_all = here + [swap(after(near, near_last), 1)] + [swap(group, 1) for group in there]

    stack_space = pltpu.VMEM(stacks.shape, bf16)
    buffer = pltpu.VMEM((2, TILES * block, width), bf16)
    word_buffer = pltpu.VMEM((2, TILES, words, block), i32)
    bias = pltpu.VMEM((TILES * block, block), f32)
    turned = pltpu.VMEM((width, block), f32)
    per_head = pltpu.VMEM((HEADS, block), f32)
    own_stats = pltpu.VMEM((2 * HEADS, block), f32)
    met = pltpu.VMEM((HEADS, TILES * block, block), f32)
    pair_met = pltpu.VMEM((HEADS // 2, block, 2 * TILES * block), f32)
    pair_rows = pltpu.VMEM((HEADS // 2, 2 * TILES * block, 2 * head), bf16)
    row_sems = pltpu.SemaphoreType.DMA((2, TILES, 2))

    attn_out, stats = pl.pallas_call(
        functools.partial(forward_kernel, sizes),
        out_shape=(own, shape((devices, 2 * HEADS, block), f32)),
        in_specs=[SMEM] + [VMEM] * 4 + [HBM] * (1 + 2 * readers),
        out_specs=(VMEM, VMEM),
        scratch_shapes=[own_stats, buffer, word_buffer, bias, per_head, per_head, turned, met, row_sems],
        compiler_params=some,
        cost_estimate=cost(5),
        name="forward",
    )(query_work, query_stack, cotangent, w_key, w_value_t, masks, *rows_all)

    stats_all = lax.all_to_all(stats, axes, 0, 0, tiled=True)

    query_part = pl.pallas_call(
        functools.partial(query_grad_kernel, sizes),
        out_shape=shape((block, width), f32),
        in_specs=[SMEM] + [HBM] * (8 + 2 * readers),
        out_specs=VMEM,
        scratch_shapes=[
            stack_space, stack_space, own_stats, weight, weight, weight, weight, buffer, word_buffer, bias, turned,
            met, met, row_sems, pltpu.SemaphoreType.DMA((7,)),
        ],
        compiler_params=most,
        cost_estimate=cost(5),
        name="query_grad",
    )(query_work, query_stack, cot_stack, stats, w_query_t, w_key, w_key_t, w_value, masks, *rows_all)

    cots_all = pieces + [swap(after(piece, stats), 1) for piece in pieces[:-1]]
    cots_all += [swap(after(pieces[-1], stats_all, query_part), 1)]

    grad_features = pl.pallas_call(
        functools.partial(key_grad_kernel, sizes),
        out_shape=own,
        in_specs=[SMEM] + [HBM] * (8 + 2 * readers + blks),
        out_specs=VMEM,
        scratch_shapes=[
            rows_low, rows_low, rows_wide, weight, weight, weight,
            buffer, word_buffer, buffer, pltpu.VMEM((2, TILES, 2 * HEADS, block), f32), bias,
            pair_rows, pair_rows, pair_met, pair_met, rows_wide, rows_wide,
            row_sems, pltpu.SemaphoreType.DMA((2, TILES, 2)), pltpu.SemaphoreType.DMA((6,)),
        ],
        compiler_params=most,
        cost_estimate=cost(5),
        name="key_grad",
    )(key_work, keys, values, w_query, w_key_t, w_value_t, query_part, masks, stats_all, *rows_all, *cots_all)
    return attn_out, grad_features


def solution(mesh):
    return jax.shard_map(
        local,
        mesh=mesh,
        in_specs=(
            P(("reader", "blk"), None),
            P(("reader", "blk"), None),
            P(),
            P(),
            P(),
            P("reader", "blk", None, None),
            P("reader", "blk"),
            P(),
        ),
        out_specs=(P(("reader", "blk"), None), P(("reader", "blk"), None)),
        check_vma=False,
    )
```

```python
import functools

import jax
import jax.numpy as jnp
from jax import lax
from jax.experimental import pallas as pl
from jax.experimental.pallas import tpu as pltpu
from jax.sharding import PartitionSpec as P

HEADS = 8
NEG_FILL = -1e30
NT = (((1,), (1,)), ((), ()))
NN = (((1,), (0,)), ((), ()))
TILES = 2
LIST_ROWS = 16
VMEM_SOME = 40 * 1024 * 1024
VMEM_MOST = 58 * 1024 * 1024


def dot(a, b, dims=NN):
    return lax.dot_general(a, b, dims, preferred_element_type=jnp.float32)


def pair_stack(rows):
    lane = lax.broadcasted_iota(jnp.int32, rows.shape, 1)
    half = rows.shape[1] // 2
    zero = jnp.zeros_like(rows)
    return jnp.concatenate([jnp.where(lane < half, rows, zero), jnp.where(lane >= half, rows, zero)], 0)


def tile_bias(words, pattern, diag):
    count, size = words.shape
    keys = lax.broadcasted_iota(jnp.int32, (size, size), 0)
    queries = lax.broadcasted_iota(jnp.int32, (size, size), 1)
    spread = jnp.concatenate(
        [jnp.broadcast_to(words[g : g + 1], (size // count, size)) for g in range(count)], 0
    )
    bits = jnp.right_shift(spread, keys & 31) & 1
    same = keys - queries == jnp.where(diag, 0, 2 * size)
    return jnp.where((bits == 1) | same, jnp.where(pattern < 0, NEG_FILL, 0.0), NEG_FILL)


class Layout:
    def __init__(self, readers, blks, cap):
        self.readers, self.blks, self.cap = readers, blks, cap
        self.reader, self.blk = lax.axis_index("reader"), lax.axis_index("blk")
        self.me = self.reader * blks + self.blk

    def apart(self, device):
        far = jnp.bitwise_xor(device, self.me)
        reader, blk = far // self.blks, lax.rem(far, self.blks)
        return reader, blk // 2, blk & 1

    def row_place(self, device):
        reader, line, core = self.apart(device)
        near = line == 0
        group = jnp.where(near, 0, reader) + self.readers * core
        index = jnp.where(reader == 0, self.readers, 0) + line - 1
        return group, jnp.where(near, reader, index)

    def half_place(self, bit, device):
        reader, line, core = self.apart(device)
        first = jnp.right_shift(reader, bit) & 1
        top = (self.blks // 2 - 1).bit_length() - 1
        line = sum((jnp.right_shift(line, top - at) & 1) << at for at in range(top + 1))
        low = reader & ((1 << bit) - 1)
        rest = low + (jnp.right_shift(reader, bit + 1) << bit)
        return rest + self.readers // 2 * core, 2 * line + first


def start_copy(place, refs, make):
    group, where = place
    for g, ref in enumerate(refs):

        @pl.when(group == g)
        def _():
            make(ref.at[where]).start()


def pack_kernel(own_hbm, coords_hbm, count_hbm, out_ref, coords_ref, count_ref, sems):
    block = own_hbm.shape[0]
    cap = coords_ref.shape[3]
    copies = [
        pltpu.make_async_copy(coords_hbm, coords_ref, sems.at[0]),
        pltpu.make_async_copy(count_hbm, count_ref, sems.at[1]),
        pltpu.make_async_copy(own_hbm, out_ref.at[0, pl.ds(0, block)], sems.at[2]),
    ]
    for copy in copies:
        copy.start()
    copies[0].wait()
    copies[1].wait()
    lane = lax.broadcasted_iota(jnp.int32, (LIST_ROWS, out_ref.shape[2]), 1)
    row = jnp.zeros(lane.shape, jnp.int32)
    for column in range(3):
        for slot in range(cap):
            row = jnp.where(lane == column * cap + slot, coords_ref[0, column, 0, slot], row)
    row = jnp.where(lane == 3 * cap, count_ref[0, 0], row)
    out_ref[0, block:] = row.astype(jnp.float32).astype(jnp.bfloat16)
    copies[2].wait()


def scan_list(lists_ref, cap, row, column, wanted, found, out_ref, block_of):
    def one_slot(slot, found):
        out_ref[2 * found + 1] = block_of(lists_ref[row, (1 - column) * cap + slot])
        out_ref[2 * found + 2] = lists_ref[row, 2 * cap + slot]
        return found + jnp.where(lists_ref[row, column * cap + slot] == wanted, 1, 0)

    return lax.fori_loop(0, lists_ref[row, 3 * cap], one_slot, found)


def close_work(found, out_ref):
    out_ref[2 * found + 1] = out_ref[2 * found - 1]
    out_ref[2 * found + 2] = -1
    out_ref[0] = (found + 1) // 2


def query_work_kernel(sizes, lists_hbm, work_ref, lists_ref, sem):
    readers, blks, cap = sizes
    layout = Layout(*sizes)
    copy = pltpu.make_async_copy(lists_hbm, lists_ref, sem)
    copy.start()
    copy.wait()

    def one(k, found):
        blk = jnp.bitwise_xor(k, layout.blk)
        row = k // 2 + (k & 1) * (blks // 2)
        put = lambda other: other * blks + blk
        return scan_list(lists_ref, cap, row, 0, layout.blk, found, work_ref, put)

    close_work(lax.fori_loop(0, blks, one, 0), work_ref)


def key_work_kernel(sizes, lists_hbm, work_ref, lists_ref, sem):
    readers, blks, cap = sizes
    layout = Layout(*sizes)
    copy = pltpu.make_async_copy(lists_hbm, lists_ref, sem)
    copy.start()
    copy.wait()

    def one(k, found):
        reader = jnp.bitwise_xor(k, layout.reader)
        put = lambda other: reader * blks + other
        return scan_list(lists_ref, cap, k, 1, layout.reader, found, work_ref, put)

    close_work(lax.fori_loop(0, readers, one, 0), work_ref)


def load(pairs, sems, first=0):
    copies = [pltpu.make_async_copy(src, into, sems.at[first + k]) for k, (src, into) in enumerate(pairs)]
    for copy in copies:
        copy.start()
    return copies


def prepare_kernel(
    own_hbm, cot_hbm, wq_hbm, wk_hbm, wv_hbm,
    query_stack_ref, cot_stack_ref, key_ref, value_ref, wqt_ref, wkt_ref, wvt_ref,
    own_ref, cot_ref, wq_ref, wk_ref, wv_ref, sems,
):
    loads = load((
        (own_hbm, own_ref), (wq_hbm, wq_ref), (wk_hbm, wk_ref), (wv_hbm, wv_ref), (cot_hbm, cot_ref),
    ), sems)
    for copy in loads:
        copy.wait()
    head = own_ref.shape[1] // HEADS
    queries = dot(own_ref[...], wq_ref[...]).astype(jnp.bfloat16) * jnp.bfloat16(head**-0.5)
    for p in range(HEADS // 2):
        pair = slice(2 * head * p, 2 * head * (p + 1))
        query_stack_ref[p] = pair_stack(queries[:, pair]).T
        cot_stack_ref[p] = pair_stack(cot_ref[:, pair]).T
    key_ref[...] = dot(own_ref[...], wk_ref[...]).astype(jnp.bfloat16)
    value_ref[...] = dot(own_ref[...], wv_ref[...]).astype(jnp.bfloat16)
    wqt_ref[...] = wq_ref[...].T
    wkt_ref[...] = wk_ref[...].T
    wvt_ref[...] = wv_ref[...].T


def step_entry(work_ref, index):
    at = 1 + 2 * TILES * index
    return [work_ref[at + 2 * t] for t in range(TILES)], [work_ref[at + 2 * t + 1] for t in range(TILES)]


def run_steps(work_ref, start, wait, body):
    total = work_ref[0]

    def step(index, carry):
        @pl.when(index + 1 < total)
        def _():
            start(lax.rem(index + 1, 2), *step_entry(work_ref, index + 1))

        slot = lax.rem(index, 2)
        wait(slot)
        body(slot, *step_entry(work_ref, index), index)
        return carry

    lax.fori_loop(0, total, step, 0)


def first_step(work_ref, start):
    start(0, *step_entry(work_ref, 0))


class Rows:
    def __init__(self, layout, groups, mask_ref, buf, words, sems, block):
        self.layout, self.groups, self.mask_ref = layout, groups, mask_ref
        self.buf, self.words, self.sems, self.block = buf, words, sems, block

    def rows(self, slot, t):
        into = self.buf.at[slot, pl.ds(t * self.block, self.block)]
        return lambda src: pltpu.make_async_copy(src, into, self.sems.at[slot, t, 0])

    def mask(self, slot, t, pattern):
        return pltpu.make_async_copy(self.mask_ref.at[pattern], self.words.at[slot, t], self.sems.at[slot, t, 1])

    def start(self, slot, blocks, patterns):
        for t in range(TILES):
            start_copy(self.layout.row_place(blocks[t]), self.groups, self.rows(slot, t))
            self.mask(slot, t, jnp.maximum(patterns[t], 0)).start()

    def wait(self, slot):
        for t in range(TILES):
            self.rows(slot, t)(self.groups[0].at[0]).wait()
            self.mask(slot, t, 0).wait()

    def bias(self, slot, blocks, patterns):
        parts = [
            tile_bias(self.words[slot, t], patterns[t], blocks[t] == self.layout.me) for t in range(TILES)
        ]
        return jnp.concatenate(parts, 0)


def forward_kernel(sizes, work_ref, stack_ref, cot_ref, wk_ref, wvt_ref, mask_ref, *refs):
    count = 2 * sizes[0]
    groups, refs = refs[:count], refs[count:]
    out_ref, sent_ref, stats_ref, buf, words, bias_ref, max_ref, sum_ref, acc_ref, score_ref, sems = refs
    layout = Layout(*sizes)
    block, width = cot_ref.shape
    head = width // HEADS
    rows_in = Rows(layout, groups, mask_ref, buf, words, sems, block)
    first_step(work_ref, rows_in.start)
    max_ref[...] = jnp.full(max_ref.shape, NEG_FILL, jnp.float32)
    sum_ref[...] = jnp.zeros(sum_ref.shape, jnp.float32)
    acc_ref[...] = jnp.zeros(acc_ref.shape, jnp.float32)

    def tiles(slot, blocks, patterns, index):
        rows = buf[slot]
        keys = dot(rows, wk_ref[...]).astype(jnp.bfloat16)
        values = dot(wvt_ref[...], rows, NT).astype(jnp.bfloat16)
        bias_ref[...] = rows_in.bias(slot, blocks, patterns)
        for p in range(HEADS // 2):
            scores = dot(keys[:, 2 * head * p : 2 * head * (p + 1)], stack_ref[p])
            for e in range(2):
                score_ref[2 * p + e] = scores[:, block * e : block * (e + 1)] + bias_ref[...]
        for h in range(HEADS):
            s = score_ref[h]
            old = max_ref[h : h + 1]
            new = jnp.maximum(old, jnp.max(s, axis=0, keepdims=True))
            fade = jnp.exp(old - new)
            expo = jnp.exp(s - new)
            max_ref[h : h + 1] = new
            sum_ref[h : h + 1] = sum_ref[h : h + 1] * fade + jnp.sum(expo, axis=0, keepdims=True)
            at = slice(head * h, head * (h + 1))
            acc_ref[at] = acc_ref[at] * fade + dot(values[at], expo.astype(jnp.bfloat16))

    run_steps(work_ref, rows_in.start, rows_in.wait, tiles)
    inverse = 1.0 / sum_ref[...]
    cot = cot_ref[...].astype(jnp.float32).T
    stats_ref[0:HEADS] = max_ref[...] + jnp.log(sum_ref[...])
    for h in range(HEADS):
        at = slice(head * h, head * (h + 1))
        outputs = acc_ref[at] * inverse[h : h + 1]
        acc_ref[at] = outputs
        stats_ref[HEADS + h : HEADS + h + 1] = jnp.sum(outputs * cot[at], axis=0, keepdims=True)
    sent_ref[...] = jnp.broadcast_to(stats_ref[...], sent_ref.shape)
    out_ref[...] = acc_ref[...].T.astype(out_ref.dtype)


def tile_grads(scores, d_probs, lse, delta):
    prob = jnp.exp(scores - lse)
    return prob.astype(jnp.bfloat16), (prob * (d_probs - delta)).astype(jnp.bfloat16)


def query_grad_kernel(
    sizes, work_ref, stack_hbm, cot_stack_hbm, stats_hbm, wqt_hbm, wk_hbm, wkt_hbm, wv_hbm, mask_ref, *refs
):
    count = 2 * sizes[0]
    groups, refs = refs[:count], refs[count:]
    part_ref, stack_ref, cot_stack_ref, stats_ref, wqt_ref, wk_ref, wkt_ref, wv_ref = refs[:8]
    buf, words, bias_ref, acc_ref, score_ref, d_prob_ref, sems, w_sems = refs[8:]
    layout = Layout(*sizes)
    block, width = part_ref.shape
    head = width // HEADS
    rows_in = Rows(layout, groups, mask_ref, buf, words, sems, block)
    first_step(work_ref, rows_in.start)
    loads = load((
        (wk_hbm, wk_ref), (stack_hbm, stack_ref), (wv_hbm, wv_ref), (cot_stack_hbm, cot_stack_ref),
        (wkt_hbm, wkt_ref), (stats_hbm.at[0], stats_ref), (wqt_hbm, wqt_ref),
    ), w_sems)
    acc_ref[...] = jnp.zeros(acc_ref.shape, jnp.float32)
    for copy in loads[:6]:
        copy.wait()

    def tiles(slot, blocks, patterns, index):
        rows = buf[slot]
        keys = dot(rows, wk_ref[...]).astype(jnp.bfloat16)
        values = dot(rows, wv_ref[...]).astype(jnp.bfloat16)
        keys_t = dot(wkt_ref[...], rows, NT).astype(jnp.bfloat16)
        bias_ref[...] = rows_in.bias(slot, blocks, patterns)
        for p in range(HEADS // 2):
            pair = slice(2 * head * p, 2 * head * (p + 1))
            scores = dot(keys[:, pair], stack_ref[p])
            d_probs = dot(values[:, pair], cot_stack_ref[p])
            for e in range(2):
                of = slice(block * e, block * (e + 1))
                score_ref[2 * p + e] = scores[:, of] + bias_ref[...]
                d_prob_ref[2 * p + e] = d_probs[:, of]
        for h in range(HEADS):
            _, d_scores = tile_grads(
                score_ref[h], d_prob_ref[h], stats_ref[h : h + 1], stats_ref[HEADS + h : HEADS + h + 1]
            )
            at = slice(head * h, head * (h + 1))
            acc_ref[at] += dot(keys_t[at], d_scores)

    run_steps(work_ref, rows_in.start, rows_in.wait, tiles)
    loads[6].wait()
    grad = (acc_ref[...].T * (head**-0.5)).astype(jnp.bfloat16)
    part_ref[...] = dot(grad, wqt_ref[...])


def key_grad_kernel(
    sizes, bits, work_ref, key_hbm, value_hbm, wq_hbm, wkt_hbm, wvt_hbm, part_hbm, mask_ref, stats_all_ref, *refs
):
    readers = sizes[0]
    count = 2 * readers
    groups, refs = refs[:count], refs[count:]
    halves, refs = (refs[:readers], refs[readers : 2 * readers]), refs[2 * readers :]
    out_ref, key_ref, value_ref, part_ref, wq_ref, wkt_ref, wvt_ref, buf, words, cot_buf, stats, bias_ref = refs[:12]
    query_stack_ref, cot_stack_ref, score_ref, d_prob_ref, key_acc, value_acc, sems, c_sems, w_sems = refs[12:]
    layout = Layout(*sizes)
    block, width = out_ref.shape
    head = width // HEADS
    rows_in = Rows(layout, groups, mask_ref, buf, words, sems, block)

    def half_copy(slot, t, k):
        into = cot_buf.at[slot, pl.ds(t * block + block // 2 * k, block // 2)]
        return lambda src: pltpu.make_async_copy(src, into, c_sems.at[slot, t, k])

    def stats_copy(slot, t, query):
        return pltpu.make_async_copy(stats_all_ref.at[query], stats.at[slot, t], c_sems.at[slot, t, 2])

    def start(slot, blocks, patterns):
        rows_in.start(slot, blocks, patterns)
        for t in range(TILES):
            stats_copy(slot, t, blocks[t]).start()
            for k in range(2):
                start_copy(layout.half_place(bits[k], blocks[t]), halves[k], half_copy(slot, t, k))

    def wait(slot):
        rows_in.wait(slot)
        for t in range(TILES):
            stats_copy(slot, t, 0).wait()
            for k in range(2):
                half_copy(slot, t, k)(halves[k][0].at[0]).wait()

    first_step(work_ref, start)
    loads = load(((wq_hbm, wq_ref), (key_hbm, key_ref), (value_hbm, value_ref)), w_sems)
    key_acc[...] = jnp.zeros(key_acc.shape, jnp.float32)
    value_acc[...] = jnp.zeros(value_acc.shape, jnp.float32)
    for copy in loads:
        copy.wait()
    loads = load(((wkt_hbm, wkt_ref), (wvt_hbm, wvt_ref), (part_hbm, part_ref)), w_sems, 3)

    def tiles(slot, blocks, patterns, index):
        queries = dot(buf[slot], wq_ref[...]).astype(jnp.bfloat16) * jnp.bfloat16(head**-0.5)
        bias_ref[...] = rows_in.bias(slot, blocks, patterns)
        cots = cot_buf[slot]
        pairs = [slice(2 * head * p, 2 * head * (p + 1)) for p in range(HEADS // 2)]
        of_tile = [slice(block * t, block * (t + 1)) for t in range(TILES)]
        for p, pair in enumerate(pairs):
            query_stack_ref[p] = jnp.concatenate([pair_stack(queries[of, pair]) for of in of_tile], 0)
            cot_stack_ref[p] = jnp.concatenate([pair_stack(cots[of, pair]) for of in of_tile], 0)
            score_ref[p] = dot(key_ref[:, pair], query_stack_ref[p], NT)
            d_prob_ref[p] = dot(value_ref[:, pair], cot_stack_ref[p], NT)
        for p, pair in enumerate(pairs):
            probs, d_scores = [], []
            for t in range(TILES):
                for e in range(2):
                    h = 2 * p + e
                    of = slice(block * (2 * t + e), block * (2 * t + e + 1))
                    prob, d_score = tile_grads(
                        score_ref[p, :, of] + bias_ref[of_tile[t]], d_prob_ref[p, :, of], stats[slot, t, h : h + 1],
                        stats[slot, t, HEADS + h : HEADS + h + 1],
                    )
                    probs.append(prob)
                    d_scores.append(d_score)
            value_acc[:, pair] += dot(jnp.concatenate(probs, 1), cot_stack_ref[p])
            key_acc[:, pair] += dot(jnp.concatenate(d_scores, 1), query_stack_ref[p])

    run_steps(work_ref, start, wait, tiles)
    for copy in loads:
        copy.wait()
    grad = part_ref[...] + dot(key_acc[...].astype(jnp.bfloat16), wkt_ref[...])
    grad = grad + dot(value_acc[...].astype(jnp.bfloat16), wvt_ref[...])
    out_ref[...] = grad.astype(out_ref.dtype)


VMEM = pl.BlockSpec(memory_space=pltpu.VMEM)
SMEM = pl.BlockSpec(memory_space=pltpu.SMEM)
HBM = pl.BlockSpec(memory_space=pltpu.HBM)


def swap(block, mask):
    axes = ("reader", "blk")
    count = lax.axis_size("reader") * lax.axis_size("blk")
    return lax.ppermute(block, axes, [(i, i ^ mask) for i in range(count)])


def after(value, *others):
    return lax.optimization_barrier((value, *others))[0]


def local(features, cotangent, w_query, w_key, w_value, tile_coords, tile_count, mask_table):
    block, width = features.shape
    readers, blks, cap = lax.axis_size("reader"), lax.axis_size("blk"), tile_coords.shape[2]
    assert block == mask_table.shape[1] and 3 * cap < 128
    sizes = (readers, blks, cap)
    devices, lines = readers * blks, blks // 2
    f32, bf16, i32 = jnp.float32, jnp.bfloat16, jnp.int32
    shape = jax.ShapeDtypeStruct
    masks = mask_table.transpose(0, 2, 1)
    words = masks.shape[1]
    head = width // HEADS
    half = block // 2
    some = pltpu.CompilerParams(vmem_limit_bytes=VMEM_SOME)
    most = pltpu.CompilerParams(vmem_limit_bytes=VMEM_MOST)
    axes = ("reader", "blk")

    def cost(tiles):
        return pl.CostEstimate(flops=tiles * 200_000_000, bytes_accessed=4_000_000, transcendentals=tiles * 131072)

    packed = pl.pallas_call(
        pack_kernel,
        out_shape=shape((1, block + LIST_ROWS, width), bf16),
        in_specs=[HBM, HBM, HBM],
        out_specs=VMEM,
        scratch_shapes=[
            pltpu.SMEM((1, 3, 1, cap), i32), pltpu.SMEM((1, 1), i32), pltpu.SemaphoreType.DMA((3,)),
        ],
        compiler_params=most,
        name="pack",
    )(features, tile_coords.transpose(0, 3, 1, 2), tile_count)
    lined = [packed] + [swap(packed, 2 * k) for k in range(1, lines)]

    nearest_first = sorted(range(1, readers), key=lambda k: (k.bit_count(), k))

    def to_readers(block):
        there = {k: swap(block, blks * k) for k in nearest_first}
        return [there[k] for k in range(1, readers)]

    columns = [packed] + to_readers(packed)

    bits = (0, (readers - 1).bit_length() - 1)
    cot_parts = [cotangent[None, half * k : half * (k + 1)] for k in range(2)]
    cot_other = [swap(part, blks << bit) for part, bit in zip(cot_parts, bits)]

    column_lists = jnp.concatenate([entry[:, block:, :128] for entry in columns], 0)

    def work(kernel, lists, count, name):
        return pl.pallas_call(
            functools.partial(kernel, sizes),
            out_shape=shape((2 * count * cap + 5,), i32),
            in_specs=[HBM],
            out_specs=SMEM,
            scratch_shapes=[pltpu.SMEM((count, 128), i32), pltpu.SemaphoreType.DMA],
            compiler_params=some,
            cost_estimate=cost(1),
            name=name,
        )(lists[:, 0].astype(i32))

    key_work = work(key_work_kernel, column_lists, readers, "key_work")

    stacks = shape((HEADS // 2, 2 * head, 2 * block), bf16)
    own = shape((block, width), bf16)
    square = shape((width, width), bf16)
    weight = pltpu.VMEM((width, width), bf16)
    rows_low, rows_wide = pltpu.VMEM((block, width), bf16), pltpu.VMEM((block, width), f32)
    prepared = pl.pallas_call(
        prepare_kernel,
        out_shape=(stacks, stacks, own, own, square, square, square),
        in_specs=[HBM] * 5,
        out_specs=(VMEM,) * 7,
        scratch_shapes=[rows_low, rows_low, weight, weight, weight, pltpu.SemaphoreType.DMA((5,))],
        compiler_params=most,
        cost_estimate=cost(2),
        name="prepare",
    )(after(features, columns), cotangent, w_query, w_key, w_value)
    query_stack, cot_stack, keys, values, w_query_t, w_key_t, w_value_t = prepared

    line = jnp.concatenate(lined[1:], 0)[:, :block]
    line = after(line, columns, cot_other)
    there = to_readers(line)
    near = jnp.concatenate([entry[:, :block] for entry in columns] + [line], 0)

    pairs = [part for k in range(2) for part in (cot_parts[k], cot_other[k])]
    pieces = [after(jnp.concatenate(pairs, 0), line)]
    done_first = (key_work, prepared)
    mask = blks // 2
    while mask > 1:
        pieces += [swap(after(piece, done_first) if at else piece, mask) for at, piece in enumerate(pieces)]
        mask //= 2

    line_lists = jnp.concatenate([entry[:, block:, :128] for entry in lined], 0)
    line_lists = after(line_lists, pieces[lines // 2])
    row_lists = jnp.concatenate([line_lists, swap(line_lists, 1)], 0)
    query_work = work(query_work_kernel, row_lists, blks, "query_work")
    here = [near] + there
    rows_all = here + [swap(group, 1) for group in here]

    cots_here = []
    for k in range(2):
        part = jnp.concatenate([piece[2 * k : 2 * k + 2] for piece in pieces], 0)
        masks_left = [m for m in range(1, readers) if not m >> bits[k] & 1]
        cots_here.append((part, [swap(after(part, here), blks * m) for m in masks_left]))

    stack_space = pltpu.VMEM(stacks.shape, bf16)
    buffer = pltpu.VMEM((2, TILES * block, width), bf16)
    word_buffer = pltpu.VMEM((2, TILES, words, block), i32)
    bias = pltpu.VMEM((TILES * block, block), f32)
    turned = pltpu.VMEM((width, block), f32)
    per_head = pltpu.VMEM((HEADS, block), f32)
    own_stats = pltpu.VMEM((2 * HEADS, block), f32)
    met = pltpu.VMEM((HEADS, TILES * block, block), f32)
    pair_met = pltpu.VMEM((HEADS // 2, block, 2 * TILES * block), f32)
    pair_rows = pltpu.VMEM((HEADS // 2, 2 * TILES * block, 2 * head), bf16)
    row_sems = pltpu.SemaphoreType.DMA((2, TILES, 2))

    attn_out, stats = pl.pallas_call(
        functools.partial(forward_kernel, sizes),
        out_shape=(own, shape((devices, 2 * HEADS, block), f32)),
        in_specs=[SMEM] + [VMEM] * 4 + [HBM] * (1 + 2 * readers),
        out_specs=(VMEM, VMEM),
        scratch_shapes=[own_stats, buffer, word_buffer, bias, per_head, per_head, turned, met, row_sems],
        compiler_params=some,
        cost_estimate=cost(5),
        name="forward",
    )(query_work, query_stack, cotangent, w_key, w_value_t, masks, *rows_all)

    stats_all = lax.all_to_all(stats, axes, 0, 0, tiled=True)

    query_part = pl.pallas_call(
        functools.partial(query_grad_kernel, sizes),
        out_shape=shape((block, width), f32),
        in_specs=[SMEM] + [HBM] * (8 + 2 * readers),
        out_specs=VMEM,
        scratch_shapes=[
            stack_space, stack_space, own_stats, weight, weight, weight, weight, buffer, word_buffer, bias, turned,
            met, met, row_sems, pltpu.SemaphoreType.DMA((7,)),
        ],
        compiler_params=most,
        cost_estimate=cost(5),
        name="query_grad",
    )(query_work, query_stack, cot_stack, stats, w_query_t, w_key, w_key_t, w_value, masks, *rows_all)

    cots_all = []
    for first, rest in cots_here:
        cots_all += [first, *rest, swap(after(first, stats), 1)]
        cots_all += [swap(after(part, stats_all, query_part), 1) for part in rest]

    grad_features = pl.pallas_call(
        functools.partial(key_grad_kernel, sizes, bits),
        out_shape=own,
        in_specs=[SMEM] + [HBM] * (8 + 4 * readers),
        out_specs=VMEM,
        scratch_shapes=[
            rows_low, rows_low, rows_wide, weight, weight, weight,
            buffer, word_buffer, buffer, pltpu.VMEM((2, TILES, 2 * HEADS, block), f32), bias,
            pair_rows, pair_rows, pair_met, pair_met, rows_wide, rows_wide,
            row_sems, pltpu.SemaphoreType.DMA((2, TILES, 3)), pltpu.SemaphoreType.DMA((6,)),
        ],
        compiler_params=most,
        cost_estimate=cost(5),
        name="key_grad",
    )(key_work, keys, values, w_query, w_key_t, w_value_t, query_part, masks, stats_all, *rows_all, *cots_all)
    return attn_out, grad_features


def solution(mesh):
    return jax.shard_map(
        local,
        mesh=mesh,
        in_specs=(
            P(("reader", "blk"), None),
            P(("reader", "blk"), None),
            P(),
            P(),
            P(),
            P("reader", "blk", None, None),
            P("reader", "blk"),
            P(),
        ),
        out_specs=(P(("reader", "blk"), None), P(("reader", "blk"), None)),
        check_vma=False,
    )
```

```python
import functools

import jax
import jax.numpy as jnp
from jax import lax
from jax.experimental import pallas as pl
from jax.experimental.pallas import tpu as pltpu
from jax.sharding import PartitionSpec as P

HEADS = 8
NEG_FILL = -1e30
NT = (((1,), (1,)), ((), ()))
NN = (((1,), (0,)), ((), ()))
TILES = 2
LIST_ROWS = 16
VMEM_SOME = 40 * 1024 * 1024
VMEM_MOST = 58 * 1024 * 1024


def dot(a, b, dims=NN):
    return lax.dot_general(a, b, dims, preferred_element_type=jnp.float32)


def pair_stack(rows):
    lane = lax.broadcasted_iota(jnp.int32, rows.shape, 1)
    half = rows.shape[1] // 2
    zero = jnp.zeros_like(rows)
    return jnp.concatenate([jnp.where(lane < half, rows, zero), jnp.where(lane >= half, rows, zero)], 0)


def tile_bias(words, pattern, diag):
    count, size = words.shape
    keys = lax.broadcasted_iota(jnp.int32, (size, size), 0)
    queries = lax.broadcasted_iota(jnp.int32, (size, size), 1)
    spread = jnp.concatenate(
        [jnp.broadcast_to(words[g : g + 1], (size // count, size)) for g in range(count)], 0
    )
    bits = jnp.right_shift(spread, keys & 31) & 1
    same = keys - queries == jnp.where(diag, 0, 2 * size)
    return jnp.where((bits == 1) | same, jnp.where(pattern < 0, NEG_FILL, 0.0), NEG_FILL)


class Layout:
    def __init__(self, readers, blks, cap):
        self.readers, self.blks, self.cap = readers, blks, cap
        self.reader, self.blk = lax.axis_index("reader"), lax.axis_index("blk")
        self.me = self.reader * blks + self.blk

    def apart(self, device):
        far = jnp.bitwise_xor(device, self.me)
        reader, blk = far // self.blks, lax.rem(far, self.blks)
        return reader, blk // 2, blk & 1

    def row_place(self, device):
        reader, line, core = self.apart(device)
        near = line == 0
        group = jnp.where(near, 0, reader) + self.readers * core
        index = jnp.where(reader == 0, self.readers, 0) + line - 1
        return group, jnp.where(near, reader, index)

    def half_place(self, bit, device):
        reader, line, core = self.apart(device)
        first = jnp.right_shift(reader, bit) & 1
        top = (self.blks // 2 - 1).bit_length() - 1
        line = sum((jnp.right_shift(line, top - at) & 1) << at for at in range(top + 1))
        low = reader & ((1 << bit) - 1)
        rest = low + (jnp.right_shift(reader, bit + 1) << bit)
        return rest + self.readers // 2 * core, 2 * line + first


def start_copy(place, refs, make):
    group, where = place
    for g, ref in enumerate(refs):

        @pl.when(group == g)
        def _():
            make(ref.at[where]).start()


def pack_kernel(own_hbm, coords_hbm, count_hbm, out_ref, coords_ref, count_ref, sems):
    block = own_hbm.shape[0]
    cap = coords_ref.shape[3]
    copies = [
        pltpu.make_async_copy(coords_hbm, coords_ref, sems.at[0]),
        pltpu.make_async_copy(count_hbm, count_ref, sems.at[1]),
        pltpu.make_async_copy(own_hbm, out_ref.at[0, pl.ds(0, block)], sems.at[2]),
    ]
    for copy in copies:
        copy.start()
    copies[0].wait()
    copies[1].wait()
    lane = lax.broadcasted_iota(jnp.int32, (LIST_ROWS, out_ref.shape[2]), 1)
    row = jnp.zeros(lane.shape, jnp.int32)
    for column in range(3):
        for slot in range(cap):
            row = jnp.where(lane == column * cap + slot, coords_ref[0, column, 0, slot], row)
    row = jnp.where(lane == 3 * cap, count_ref[0, 0], row)
    out_ref[0, block:] = row.astype(jnp.float32).astype(jnp.bfloat16)
    copies[2].wait()


def scan_list(lists_ref, cap, row, column, wanted, found, out_ref, block_of):
    def one_slot(slot, found):
        out_ref[2 * found + 1] = block_of(lists_ref[row, (1 - column) * cap + slot])
        out_ref[2 * found + 2] = lists_ref[row, 2 * cap + slot]
        return found + jnp.where(lists_ref[row, column * cap + slot] == wanted, 1, 0)

    return lax.fori_loop(0, lists_ref[row, 3 * cap], one_slot, found)


def close_work(found, out_ref):
    out_ref[2 * found + 1] = out_ref[2 * found - 1]
    out_ref[2 * found + 2] = -1
    out_ref[0] = (found + 1) // 2


def query_work_kernel(sizes, lists_hbm, work_ref, lists_ref, sem):
    readers, blks, cap = sizes
    layout = Layout(*sizes)
    copy = pltpu.make_async_copy(lists_hbm, lists_ref, sem)
    copy.start()
    copy.wait()

    def one(k, found):
        blk = jnp.bitwise_xor(k, layout.blk)
        row = k // 2 + (k & 1) * (blks // 2)
        put = lambda other: other * blks + blk
        return scan_list(lists_ref, cap, row, 0, layout.blk, found, work_ref, put)

    close_work(lax.fori_loop(0, blks, one, 0), work_ref)


def key_work_kernel(sizes, lists_hbm, work_ref, lists_ref, sem):
    readers, blks, cap = sizes
    layout = Layout(*sizes)
    copy = pltpu.make_async_copy(lists_hbm, lists_ref, sem)
    copy.start()
    copy.wait()

    def one(k, found):
        reader = jnp.bitwise_xor(k, layout.reader)
        put = lambda other: reader * blks + other
        return scan_list(lists_ref, cap, k, 1, layout.reader, found, work_ref, put)

    close_work(lax.fori_loop(0, readers, one, 0), work_ref)


def load(pairs, sems, first=0):
    copies = [pltpu.make_async_copy(src, into, sems.at[first + k]) for k, (src, into) in enumerate(pairs)]
    for copy in copies:
        copy.start()
    return copies


def prepare_kernel(
    own_hbm, cot_hbm, wq_hbm, wk_hbm, wv_hbm,
    query_stack_ref, cot_stack_ref, key_ref, value_ref, wqt_ref, wkt_ref, wvt_ref,
    own_ref, cot_ref, wq_ref, wk_ref, wv_ref, sems,
):
    loads = load((
        (own_hbm, own_ref), (wq_hbm, wq_ref), (wk_hbm, wk_ref), (wv_hbm, wv_ref), (cot_hbm, cot_ref),
    ), sems)
    for copy in loads:
        copy.wait()
    head = own_ref.shape[1] // HEADS
    queries = dot(own_ref[...], wq_ref[...]).astype(jnp.bfloat16) * jnp.bfloat16(head**-0.5)
    for p in range(HEADS // 2):
        pair = slice(2 * head * p, 2 * head * (p + 1))
        query_stack_ref[p] = pair_stack(queries[:, pair]).T
        cot_stack_ref[p] = pair_stack(cot_ref[:, pair]).T
    key_ref[...] = dot(own_ref[...], wk_ref[...]).astype(jnp.bfloat16)
    value_ref[...] = dot(own_ref[...], wv_ref[...]).astype(jnp.bfloat16)
    wqt_ref[...] = wq_ref[...].T
    wkt_ref[...] = wk_ref[...].T
    wvt_ref[...] = wv_ref[...].T


def step_entry(work_ref, index):
    at = 1 + 2 * TILES * index
    return [work_ref[at + 2 * t] for t in range(TILES)], [work_ref[at + 2 * t + 1] for t in range(TILES)]


def run_steps(work_ref, start, wait, body):
    total = work_ref[0]

    def step(index, carry):
        @pl.when(index + 1 < total)
        def _():
            start(lax.rem(index + 1, 2), *step_entry(work_ref, index + 1))

        slot = lax.rem(index, 2)
        wait(slot)
        body(slot, *step_entry(work_ref, index), index)
        return carry

    lax.fori_loop(0, total, step, 0)


def first_step(work_ref, start):
    start(0, *step_entry(work_ref, 0))


class Rows:
    def __init__(self, layout, groups, mask_ref, buf, words, sems, block):
        self.layout, self.groups, self.mask_ref = layout, groups, mask_ref
        self.buf, self.words, self.sems, self.block = buf, words, sems, block

    def rows(self, slot, t):
        into = self.buf.at[slot, pl.ds(t * self.block, self.block)]
        return lambda src: pltpu.make_async_copy(src, into, self.sems.at[slot, t, 0])

    def mask(self, slot, t, pattern):
        return pltpu.make_async_copy(self.mask_ref.at[pattern], self.words.at[slot, t], self.sems.at[slot, t, 1])

    def start(self, slot, blocks, patterns):
        for t in range(TILES):
            start_copy(self.layout.row_place(blocks[t]), self.groups, self.rows(slot, t))
            self.mask(slot, t, jnp.maximum(patterns[t], 0)).start()

    def wait(self, slot):
        for t in range(TILES):
            self.rows(slot, t)(self.groups[0].at[0]).wait()
            self.mask(slot, t, 0).wait()

    def bias(self, slot, blocks, patterns):
        parts = [
            tile_bias(self.words[slot, t], patterns[t], blocks[t] == self.layout.me) for t in range(TILES)
        ]
        return jnp.concatenate(parts, 0)


def forward_kernel(sizes, work_ref, stack_ref, cot_ref, wk_ref, wvt_ref, mask_ref, *refs):
    count = 2 * sizes[0]
    groups, refs = refs[:count], refs[count:]
    out_ref, sent_ref, stats_ref, buf, words, bias_ref, max_ref, sum_ref, acc_ref, score_ref, sems = refs
    layout = Layout(*sizes)
    block, width = cot_ref.shape
    head = width // HEADS
    rows_in = Rows(layout, groups, mask_ref, buf, words, sems, block)
    first_step(work_ref, rows_in.start)
    max_ref[...] = jnp.full(max_ref.shape, NEG_FILL, jnp.float32)
    sum_ref[...] = jnp.zeros(sum_ref.shape, jnp.float32)
    acc_ref[...] = jnp.zeros(acc_ref.shape, jnp.float32)

    def tiles(slot, blocks, patterns, index):
        rows = buf[slot]
        keys = dot(rows, wk_ref[...]).astype(jnp.bfloat16)
        values = dot(wvt_ref[...], rows, NT).astype(jnp.bfloat16)
        bias_ref[...] = rows_in.bias(slot, blocks, patterns)
        for p in range(HEADS // 2):
            scores = dot(keys[:, 2 * head * p : 2 * head * (p + 1)], stack_ref[p])
            for e in range(2):
                score_ref[2 * p + e] = scores[:, block * e : block * (e + 1)] + bias_ref[...]
        for h in range(HEADS):
            s = score_ref[h]
            old = max_ref[h : h + 1]
            new = jnp.maximum(old, jnp.max(s, axis=0, keepdims=True))
            fade = jnp.exp(old - new)
            expo = jnp.exp(s - new)
            max_ref[h : h + 1] = new
            sum_ref[h : h + 1] = sum_ref[h : h + 1] * fade + jnp.sum(expo, axis=0, keepdims=True)
            at = slice(head * h, head * (h + 1))
            acc_ref[at] = acc_ref[at] * fade + dot(values[at], expo.astype(jnp.bfloat16))

    run_steps(work_ref, rows_in.start, rows_in.wait, tiles)
    inverse = 1.0 / sum_ref[...]
    cot = cot_ref[...].astype(jnp.float32).T
    stats_ref[0:HEADS] = max_ref[...] + jnp.log(sum_ref[...])
    for h in range(HEADS):
        at = slice(head * h, head * (h + 1))
        outputs = acc_ref[at] * inverse[h : h + 1]
        acc_ref[at] = outputs
        stats_ref[HEADS + h : HEADS + h + 1] = jnp.sum(outputs * cot[at], axis=0, keepdims=True)
    sent_ref[...] = jnp.broadcast_to(stats_ref[...], sent_ref.shape)
    out_ref[...] = acc_ref[...].T.astype(out_ref.dtype)


def tile_grads(scores, d_probs, lse, delta):
    prob = jnp.exp(scores - lse)
    return prob.astype(jnp.bfloat16), (prob * (d_probs - delta)).astype(jnp.bfloat16)


def query_grad_kernel(
    sizes, work_ref, stack_hbm, cot_stack_hbm, stats_hbm, wqt_hbm, wk_hbm, wkt_hbm, wv_hbm, mask_ref, *refs
):
    count = 2 * sizes[0]
    groups, refs = refs[:count], refs[count:]
    part_ref, stack_ref, cot_stack_ref, stats_ref, wqt_ref, wk_ref, wkt_ref, wv_ref = refs[:8]
    buf, words, bias_ref, acc_ref, score_ref, d_prob_ref, sems, w_sems = refs[8:]
    layout = Layout(*sizes)
    block, width = part_ref.shape
    head = width // HEADS
    rows_in = Rows(layout, groups, mask_ref, buf, words, sems, block)
    first_step(work_ref, rows_in.start)
    loads = load((
        (wk_hbm, wk_ref), (stack_hbm, stack_ref), (wv_hbm, wv_ref), (cot_stack_hbm, cot_stack_ref),
        (wkt_hbm, wkt_ref), (stats_hbm.at[0], stats_ref), (wqt_hbm, wqt_ref),
    ), w_sems)
    acc_ref[...] = jnp.zeros(acc_ref.shape, jnp.float32)
    for copy in loads[:6]:
        copy.wait()

    def tiles(slot, blocks, patterns, index):
        rows = buf[slot]
        keys = dot(rows, wk_ref[...]).astype(jnp.bfloat16)
        values = dot(rows, wv_ref[...]).astype(jnp.bfloat16)
        keys_t = dot(wkt_ref[...], rows, NT).astype(jnp.bfloat16)
        bias_ref[...] = rows_in.bias(slot, blocks, patterns)
        for p in range(HEADS // 2):
            pair = slice(2 * head * p, 2 * head * (p + 1))
            scores = dot(keys[:, pair], stack_ref[p])
            d_probs = dot(values[:, pair], cot_stack_ref[p])
            for e in range(2):
                of = slice(block * e, block * (e + 1))
                score_ref[2 * p + e] = scores[:, of] + bias_ref[...]
                d_prob_ref[2 * p + e] = d_probs[:, of]
        for h in range(HEADS):
            _, d_scores = tile_grads(
                score_ref[h], d_prob_ref[h], stats_ref[h : h + 1], stats_ref[HEADS + h : HEADS + h + 1]
            )
            at = slice(head * h, head * (h + 1))
            acc_ref[at] += dot(keys_t[at], d_scores)

    run_steps(work_ref, rows_in.start, rows_in.wait, tiles)
    loads[6].wait()
    grad = (acc_ref[...].T * (head**-0.5)).astype(jnp.bfloat16)
    part_ref[...] = dot(grad, wqt_ref[...])


def key_grad_kernel(
    sizes, bits, work_ref, key_hbm, value_hbm, wq_hbm, wkt_hbm, wvt_hbm, part_hbm, mask_ref, stats_all_ref, *refs
):
    readers = sizes[0]
    count = 2 * readers
    groups, refs = refs[:count], refs[count:]
    halves, refs = (refs[:readers], refs[readers : 2 * readers]), refs[2 * readers :]
    out_ref, key_ref, value_ref, part_ref, wq_ref, wkt_ref, wvt_ref, buf, words, cot_buf, stats, bias_ref = refs[:12]
    query_stack_ref, cot_stack_ref, score_ref, d_prob_ref, key_acc, value_acc, sems, c_sems, w_sems = refs[12:]
    layout = Layout(*sizes)
    block, width = out_ref.shape
    head = width // HEADS
    rows_in = Rows(layout, groups, mask_ref, buf, words, sems, block)

    def half_copy(slot, t, k):
        into = cot_buf.at[slot, pl.ds(t * block + block // 2 * k, block // 2)]
        return lambda src: pltpu.make_async_copy(src, into, c_sems.at[slot, t, k])

    def stats_copy(slot, t, query):
        return pltpu.make_async_copy(stats_all_ref.at[query], stats.at[slot, t], c_sems.at[slot, t, 2])

    def start(slot, blocks, patterns):
        rows_in.start(slot, blocks, patterns)
        for t in range(TILES):
            stats_copy(slot, t, blocks[t]).start()
            for k in range(2):
                start_copy(layout.half_place(bits[k], blocks[t]), halves[k], half_copy(slot, t, k))

    def wait(slot):
        rows_in.wait(slot)
        for t in range(TILES):
            stats_copy(slot, t, 0).wait()
            for k in range(2):
                half_copy(slot, t, k)(halves[k][0].at[0]).wait()

    first_step(work_ref, start)
    loads = load(((wq_hbm, wq_ref), (key_hbm, key_ref), (value_hbm, value_ref)), w_sems)
    key_acc[...] = jnp.zeros(key_acc.shape, jnp.float32)
    value_acc[...] = jnp.zeros(value_acc.shape, jnp.float32)
    for copy in loads:
        copy.wait()
    loads = load(((wkt_hbm, wkt_ref), (wvt_hbm, wvt_ref), (part_hbm, part_ref)), w_sems, 3)

    def tiles(slot, blocks, patterns, index):
        queries = dot(buf[slot], wq_ref[...]).astype(jnp.bfloat16) * jnp.bfloat16(head**-0.5)
        bias_ref[...] = rows_in.bias(slot, blocks, patterns)
        cots = cot_buf[slot]
        pairs = [slice(2 * head * p, 2 * head * (p + 1)) for p in range(HEADS // 2)]
        of_tile = [slice(block * t, block * (t + 1)) for t in range(TILES)]
        for p, pair in enumerate(pairs):
            query_stack_ref[p] = jnp.concatenate([pair_stack(queries[of, pair]) for of in of_tile], 0)
            cot_stack_ref[p] = jnp.concatenate([pair_stack(cots[of, pair]) for of in of_tile], 0)
            score_ref[p] = dot(key_ref[:, pair], query_stack_ref[p], NT)
            d_prob_ref[p] = dot(value_ref[:, pair], cot_stack_ref[p], NT)
        for p, pair in enumerate(pairs):
            probs, d_scores = [], []
            for t in range(TILES):
                for e in range(2):
                    h = 2 * p + e
                    of = slice(block * (2 * t + e), block * (2 * t + e + 1))
                    prob, d_score = tile_grads(
                        score_ref[p, :, of] + bias_ref[of_tile[t]], d_prob_ref[p, :, of], stats[slot, t, h : h + 1],
                        stats[slot, t, HEADS + h : HEADS + h + 1],
                    )
                    probs.append(prob)
                    d_scores.append(d_score)
            value_acc[:, pair] += dot(jnp.concatenate(probs, 1), cot_stack_ref[p])
            key_acc[:, pair] += dot(jnp.concatenate(d_scores, 1), query_stack_ref[p])

    run_steps(work_ref, start, wait, tiles)
    for copy in loads:
        copy.wait()
    grad = part_ref[...] + dot(key_acc[...].astype(jnp.bfloat16), wkt_ref[...])
    grad = grad + dot(value_acc[...].astype(jnp.bfloat16), wvt_ref[...])
    out_ref[...] = grad.astype(out_ref.dtype)


VMEM = pl.BlockSpec(memory_space=pltpu.VMEM)
SMEM = pl.BlockSpec(memory_space=pltpu.SMEM)
HBM = pl.BlockSpec(memory_space=pltpu.HBM)


def swap(block, mask):
    axes = ("reader", "blk")
    count = lax.axis_size("reader") * lax.axis_size("blk")
    return lax.ppermute(block, axes, [(i, i ^ mask) for i in range(count)])


def after(value, *others):
    return lax.optimization_barrier((value, *others))[0]


def local(features, cotangent, w_query, w_key, w_value, tile_coords, tile_count, mask_table):
    block, width = features.shape
    readers, blks, cap = lax.axis_size("reader"), lax.axis_size("blk"), tile_coords.shape[2]
    assert block == mask_table.shape[1] and 3 * cap < 128
    sizes = (readers, blks, cap)
    devices, lines = readers * blks, blks // 2
    f32, bf16, i32 = jnp.float32, jnp.bfloat16, jnp.int32
    shape = jax.ShapeDtypeStruct
    masks = mask_table.transpose(0, 2, 1)
    words = masks.shape[1]
    head = width // HEADS
    half = block // 2
    some = pltpu.CompilerParams(vmem_limit_bytes=VMEM_SOME)
    most = pltpu.CompilerParams(vmem_limit_bytes=VMEM_MOST)
    axes = ("reader", "blk")

    def cost(tiles):
        return pl.CostEstimate(flops=tiles * 200_000_000, bytes_accessed=4_000_000, transcendentals=tiles * 131072)

    packed = pl.pallas_call(
        pack_kernel,
        out_shape=shape((1, block + LIST_ROWS, width), bf16),
        in_specs=[HBM, HBM, HBM],
        out_specs=VMEM,
        scratch_shapes=[
            pltpu.SMEM((1, 3, 1, cap), i32), pltpu.SMEM((1, 1), i32), pltpu.SemaphoreType.DMA((3,)),
        ],
        compiler_params=most,
        name="pack",
    )(features, tile_coords.transpose(0, 3, 1, 2), tile_count)
    lined = [packed] + [swap(packed, 2 * k) for k in range(1, lines)]

    nearest_first = sorted(range(1, readers), key=lambda k: (k.bit_count(), k))

    def to_readers(block):
        there = {k: swap(block, blks * k) for k in nearest_first}
        return [there[k] for k in range(1, readers)]

    columns = [packed] + to_readers(packed)

    bits = (0, (readers - 1).bit_length() - 1)
    cot_parts = [cotangent[None, half * k : half * (k + 1)] for k in range(2)]
    cot_other = [swap(part, blks << bit) for part, bit in zip(cot_parts, bits)]

    column_lists = jnp.concatenate([entry[:, block:, :128] for entry in columns], 0)

    def work(kernel, lists, count, name):
        return pl.pallas_call(
            functools.partial(kernel, sizes),
            out_shape=shape((2 * count * cap + 5,), i32),
            in_specs=[HBM],
            out_specs=SMEM,
            scratch_shapes=[pltpu.SMEM((count, 128), i32), pltpu.SemaphoreType.DMA],
            compiler_params=some,
            cost_estimate=cost(1),
            name=name,
        )(lists[:, 0].astype(i32))

    key_work = work(key_work_kernel, column_lists, readers, "key_work")

    stacks = shape((HEADS // 2, 2 * head, 2 * block), bf16)
    own = shape((block, width), bf16)
    square = shape((width, width), bf16)
    weight = pltpu.VMEM((width, width), bf16)
    rows_low, rows_wide = pltpu.VMEM((block, width), bf16), pltpu.VMEM((block, width), f32)
    prepared = pl.pallas_call(
        prepare_kernel,
        out_shape=(stacks, stacks, own, own, square, square, square),
        in_specs=[HBM] * 5,
        out_specs=(VMEM,) * 7,
        scratch_shapes=[rows_low, rows_low, weight, weight, weight, pltpu.SemaphoreType.DMA((5,))],
        compiler_params=most,
        cost_estimate=cost(2),
        name="prepare",
    )(after(features, columns), cotangent, w_query, w_key, w_value)
    query_stack, cot_stack, keys, values, w_query_t, w_key_t, w_value_t = prepared

    line = jnp.concatenate(lined[1:], 0)[:, :block]
    line = after(line, columns, cot_other)
    there = to_readers(line)
    near = jnp.concatenate([entry[:, :block] for entry in columns] + [line], 0)

    pairs = [part for k in range(2) for part in (cot_parts[k], cot_other[k])]
    pieces = [after(jnp.concatenate(pairs, 0), line)]
    done_first = (key_work, prepared)
    mask = blks // 2
    while mask > 1:
        pieces += [swap(after(piece, done_first) if at else piece, mask) for at, piece in enumerate(pieces)]
        mask //= 2

    line_lists = jnp.concatenate([entry[:, block:, :128] for entry in lined], 0)
    other_near = swap(after(near, pieces[lines // 2]), 1)
    line_lists = after(line_lists, other_near)
    row_lists = jnp.concatenate([line_lists, swap(line_lists, 1)], 0)
    query_work = work(query_work_kernel, row_lists, blks, "query_work")
    here = [near] + there
    rows_all = here + [other_near] + [swap(group, 1) for group in there]

    cots_here = []
    for k in range(2):
        part = jnp.concatenate([piece[2 * k : 2 * k + 2] for piece in pieces], 0)
        masks_left = [m for m in range(1, readers) if not m >> bits[k] & 1]
        cots_here.append((part, [swap(after(part, here), blks * m) for m in masks_left]))

    stack_space = pltpu.VMEM(stacks.shape, bf16)
    buffer = pltpu.VMEM((2, TILES * block, width), bf16)
    word_buffer = pltpu.VMEM((2, TILES, words, block), i32)
    bias = pltpu.VMEM((TILES * block, block), f32)
    turned = pltpu.VMEM((width, block), f32)
    per_head = pltpu.VMEM((HEADS, block), f32)
    own_stats = pltpu.VMEM((2 * HEADS, block), f32)
    met = pltpu.VMEM((HEADS, TILES * block, block), f32)
    pair_met = pltpu.VMEM((HEADS // 2, block, 2 * TILES * block), f32)
    pair_rows = pltpu.VMEM((HEADS // 2, 2 * TILES * block, 2 * head), bf16)
    row_sems = pltpu.SemaphoreType.DMA((2, TILES, 2))

    attn_out, stats = pl.pallas_call(
        functools.partial(forward_kernel, sizes),
        out_shape=(own, shape((devices, 2 * HEADS, block), f32)),
        in_specs=[SMEM] + [VMEM] * 4 + [HBM] * (1 + 2 * readers),
        out_specs=(VMEM, VMEM),
        scratch_shapes=[own_stats, buffer, word_buffer, bias, per_head, per_head, turned, met, row_sems],
        compiler_params=some,
        cost_estimate=cost(5),
        name="forward",
    )(query_work, query_stack, cotangent, w_key, w_value_t, masks, *rows_all)

    stats_all = lax.all_to_all(stats, axes, 0, 0, tiled=True)

    query_part = pl.pallas_call(
        functools.partial(query_grad_kernel, sizes),
        out_shape=shape((block, width), f32),
        in_specs=[SMEM] + [HBM] * (8 + 2 * readers),
        out_specs=VMEM,
        scratch_shapes=[
            stack_space, stack_space, own_stats, weight, weight, weight, weight, buffer, word_buffer, bias, turned,
            met, met, row_sems, pltpu.SemaphoreType.DMA((7,)),
        ],
        compiler_params=most,
        cost_estimate=cost(5),
        name="query_grad",
    )(query_work, query_stack, cot_stack, stats, w_query_t, w_key, w_key_t, w_value, masks, *rows_all)

    cots_all = []
    for first, rest in cots_here:
        cots_all += [first, *rest, swap(after(first, stats), 1)]
        cots_all += [swap(after(part, stats_all, query_part), 1) for part in rest]

    grad_features = pl.pallas_call(
        functools.partial(key_grad_kernel, sizes, bits),
        out_shape=own,
        in_specs=[SMEM] + [HBM] * (8 + 4 * readers),
        out_specs=VMEM,
        scratch_shapes=[
            rows_low, rows_low, rows_wide, weight, weight, weight,
            buffer, word_buffer, buffer, pltpu.VMEM((2, TILES, 2 * HEADS, block), f32), bias,
            pair_rows, pair_rows, pair_met, pair_met, rows_wide, rows_wide,
            row_sems, pltpu.SemaphoreType.DMA((2, TILES, 3)), pltpu.SemaphoreType.DMA((6,)),
        ],
        compiler_params=most,
        cost_estimate=cost(5),
        name="key_grad",
    )(key_work, keys, values, w_query, w_key_t, w_value_t, query_part, masks, stats_all, *rows_all, *cots_all)
    return attn_out, grad_features


def solution(mesh):
    return jax.shard_map(
        local,
        mesh=mesh,
        in_specs=(
            P(("reader", "blk"), None),
            P(("reader", "blk"), None),
            P(),
            P(),
            P(),
            P("reader", "blk", None, None),
            P("reader", "blk"),
            P(),
        ),
        out_specs=(P(("reader", "blk"), None), P(("reader", "blk"), None)),
        check_vma=False,
    )
```

```python
import functools

import jax
import jax.numpy as jnp
from jax import lax
from jax.experimental import pallas as pl
from jax.experimental.pallas import tpu as pltpu
from jax.sharding import PartitionSpec as P

HEADS = 8
NEG_FILL = -1e30
NT = (((1,), (1,)), ((), ()))
NN = (((1,), (0,)), ((), ()))
TILES = 2
LIST_ROWS = 16
VMEM_SOME = 40 * 1024 * 1024
VMEM_MOST = 58 * 1024 * 1024


def dot(a, b, dims=NN):
    return lax.dot_general(a, b, dims, preferred_element_type=jnp.float32)


def pair_stack(rows):
    lane = lax.broadcasted_iota(jnp.int32, rows.shape, 1)
    half = rows.shape[1] // 2
    zero = jnp.zeros_like(rows)
    return jnp.concatenate([jnp.where(lane < half, rows, zero), jnp.where(lane >= half, rows, zero)], 0)


def tile_bias(words, pattern, diag):
    count, size = words.shape
    keys = lax.broadcasted_iota(jnp.int32, (size, size), 0)
    queries = lax.broadcasted_iota(jnp.int32, (size, size), 1)
    spread = jnp.concatenate(
        [jnp.broadcast_to(words[g : g + 1], (size // count, size)) for g in range(count)], 0
    )
    bits = jnp.right_shift(spread, keys & 31) & 1
    same = keys - queries == jnp.where(diag, 0, 2 * size)
    return jnp.where((bits == 1) | same, jnp.where(pattern < 0, NEG_FILL, 0.0), NEG_FILL)


class Layout:
    def __init__(self, readers, blks, cap):
        self.readers, self.blks, self.cap = readers, blks, cap
        self.reader, self.blk = lax.axis_index("reader"), lax.axis_index("blk")
        self.me = self.reader * blks + self.blk

    def apart(self, device):
        far = jnp.bitwise_xor(device, self.me)
        reader, blk = far // self.blks, lax.rem(far, self.blks)
        return reader, blk // 2, blk & 1

    def row_place(self, device):
        reader, line, core = self.apart(device)
        near = line == 0
        group = jnp.where(near, 0, reader) + self.readers * core
        index = jnp.where(reader == 0, self.readers, 0) + line - 1
        return group, jnp.where(near, reader, index)

    def half_place(self, bit, device):
        reader, line, core = self.apart(device)
        first = jnp.right_shift(reader, bit) & 1
        top = (self.blks // 2 - 1).bit_length() - 1
        line = sum((jnp.right_shift(line, top - at) & 1) << at for at in range(top + 1))
        low = reader & ((1 << bit) - 1)
        rest = low + (jnp.right_shift(reader, bit + 1) << bit)
        return rest + self.readers // 2 * core, 2 * line + first


def start_copy(place, refs, make):
    group, where = place
    for g, ref in enumerate(refs):

        @pl.when(group == g)
        def _():
            make(ref.at[where]).start()


def pack_kernel(own_hbm, coords_hbm, count_hbm, out_ref, coords_ref, count_ref, sems):
    block = own_hbm.shape[0]
    cap = coords_ref.shape[3]
    copies = [
        pltpu.make_async_copy(coords_hbm, coords_ref, sems.at[0]),
        pltpu.make_async_copy(count_hbm, count_ref, sems.at[1]),
        pltpu.make_async_copy(own_hbm, out_ref.at[0, pl.ds(0, block)], sems.at[2]),
    ]
    for copy in copies:
        copy.start()
    copies[0].wait()
    copies[1].wait()
    lane = lax.broadcasted_iota(jnp.int32, (LIST_ROWS, out_ref.shape[2]), 1)
    row = jnp.zeros(lane.shape, jnp.int32)
    for column in range(3):
        for slot in range(cap):
            row = jnp.where(lane == column * cap + slot, coords_ref[0, column, 0, slot], row)
    row = jnp.where(lane == 3 * cap, count_ref[0, 0], row)
    out_ref[0, block:] = row.astype(jnp.float32).astype(jnp.bfloat16)
    copies[2].wait()


def scan_list(lists_ref, cap, row, column, wanted, found, out_ref, block_of):
    def one_slot(slot, found):
        out_ref[2 * found + 1] = block_of(lists_ref[row, (1 - column) * cap + slot])
        out_ref[2 * found + 2] = lists_ref[row, 2 * cap + slot]
        return found + jnp.where(lists_ref[row, column * cap + slot] == wanted, 1, 0)

    return lax.fori_loop(0, lists_ref[row, 3 * cap], one_slot, found)


def close_work(found, out_ref):
    out_ref[2 * found + 1] = out_ref[2 * found - 1]
    out_ref[2 * found + 2] = -1
    out_ref[0] = (found + 1) // 2


def query_work_kernel(sizes, lists_hbm, work_ref, lists_ref, sem):
    readers, blks, cap = sizes
    layout = Layout(*sizes)
    copy = pltpu.make_async_copy(lists_hbm, lists_ref, sem)
    copy.start()
    copy.wait()

    def one(k, found):
        blk = jnp.bitwise_xor(k, layout.blk)
        row = k // 2 + (k & 1) * (blks // 2)
        put = lambda other: other * blks + blk
        return scan_list(lists_ref, cap, row, 0, layout.blk, found, work_ref, put)

    close_work(lax.fori_loop(0, blks, one, 0), work_ref)


def key_work_kernel(sizes, lists_hbm, work_ref, lists_ref, sem):
    readers, blks, cap = sizes
    layout = Layout(*sizes)
    copy = pltpu.make_async_copy(lists_hbm, lists_ref, sem)
    copy.start()
    copy.wait()

    def one(k, found):
        reader = jnp.bitwise_xor(k, layout.reader)
        put = lambda other: reader * blks + other
        return scan_list(lists_ref, cap, k, 1, layout.reader, found, work_ref, put)

    close_work(lax.fori_loop(0, readers, one, 0), work_ref)


def load(pairs, sems, first=0):
    copies = [pltpu.make_async_copy(src, into, sems.at[first + k]) for k, (src, into) in enumerate(pairs)]
    for copy in copies:
        copy.start()
    return copies


def prepare_kernel(
    own_hbm, cot_hbm, wq_hbm, wk_hbm, wv_hbm,
    query_stack_ref, cot_stack_ref, key_ref, value_ref, wqt_ref, wkt_ref, wvt_ref,
    own_ref, cot_ref, wq_ref, wk_ref, wv_ref, sems,
):
    loads = load((
        (own_hbm, own_ref), (wq_hbm, wq_ref), (wk_hbm, wk_ref), (wv_hbm, wv_ref), (cot_hbm, cot_ref),
    ), sems)
    for copy in loads:
        copy.wait()
    head = own_ref.shape[1] // HEADS
    queries = dot(own_ref[...], wq_ref[...]).astype(jnp.bfloat16) * jnp.bfloat16(head**-0.5)
    for p in range(HEADS // 2):
        pair = slice(2 * head * p, 2 * head * (p + 1))
        query_stack_ref[p] = pair_stack(queries[:, pair]).T
        cot_stack_ref[p] = pair_stack(cot_ref[:, pair]).T
    key_ref[...] = dot(own_ref[...], wk_ref[...]).astype(jnp.bfloat16)
    value_ref[...] = dot(own_ref[...], wv_ref[...]).astype(jnp.bfloat16)
    wqt_ref[...] = wq_ref[...].T
    wkt_ref[...] = wk_ref[...].T
    wvt_ref[...] = wv_ref[...].T


def step_entry(work_ref, index):
    at = 1 + 2 * TILES * index
    return [work_ref[at + 2 * t] for t in range(TILES)], [work_ref[at + 2 * t + 1] for t in range(TILES)]


def run_steps(work_ref, start, wait, body):
    total = work_ref[0]

    def step(index, carry):
        @pl.when(index + 1 < total)
        def _():
            start(lax.rem(index + 1, 2), *step_entry(work_ref, index + 1))

        slot = lax.rem(index, 2)
        wait(slot)
        body(slot, *step_entry(work_ref, index), index)
        return carry

    lax.fori_loop(0, total, step, 0)


def first_step(work_ref, start):
    start(0, *step_entry(work_ref, 0))


class Rows:
    def __init__(self, layout, groups, mask_ref, buf, words, sems, block):
        self.layout, self.groups, self.mask_ref = layout, groups, mask_ref
        self.buf, self.words, self.sems, self.block = buf, words, sems, block

    def rows(self, slot, t):
        into = self.buf.at[slot, pl.ds(t * self.block, self.block)]
        return lambda src: pltpu.make_async_copy(src, into, self.sems.at[slot, t, 0])

    def mask(self, slot, t, pattern):
        return pltpu.make_async_copy(self.mask_ref.at[pattern], self.words.at[slot, t], self.sems.at[slot, t, 1])

    def start(self, slot, blocks, patterns):
        for t in range(TILES):
            start_copy(self.layout.row_place(blocks[t]), self.groups, self.rows(slot, t))
            self.mask(slot, t, jnp.maximum(patterns[t], 0)).start()

    def wait(self, slot):
        for t in range(TILES):
            self.rows(slot, t)(self.groups[0].at[0]).wait()
            self.mask(slot, t, 0).wait()

    def bias(self, slot, blocks, patterns):
        parts = [
            tile_bias(self.words[slot, t], patterns[t], blocks[t] == self.layout.me) for t in range(TILES)
        ]
        return jnp.concatenate(parts, 0)


def forward_kernel(sizes, work_ref, stack_ref, cot_ref, wk_ref, wvt_ref, mask_ref, *refs):
    count = 2 * sizes[0]
    groups, refs = refs[:count], refs[count:]
    out_ref, sent_ref, stats_ref, buf, words, bias_ref, max_ref, sum_ref, acc_ref, score_ref, sems = refs
    layout = Layout(*sizes)
    block, width = cot_ref.shape
    head = width // HEADS
    rows_in = Rows(layout, groups, mask_ref, buf, words, sems, block)
    first_step(work_ref, rows_in.start)
    max_ref[...] = jnp.full(max_ref.shape, NEG_FILL, jnp.float32)
    sum_ref[...] = jnp.zeros(sum_ref.shape, jnp.float32)
    acc_ref[...] = jnp.zeros(acc_ref.shape, jnp.float32)

    def tiles(slot, blocks, patterns, index):
        rows = buf[slot]
        keys = dot(rows, wk_ref[...]).astype(jnp.bfloat16)
        values = dot(wvt_ref[...], rows, NT).astype(jnp.bfloat16)
        bias_ref[...] = rows_in.bias(slot, blocks, patterns)
        for p in range(HEADS // 2):
            scores = dot(keys[:, 2 * head * p : 2 * head * (p + 1)], stack_ref[p])
            for e in range(2):
                score_ref[2 * p + e] = scores[:, block * e : block * (e + 1)] + bias_ref[...]
        for h in range(HEADS):
            s = score_ref[h]
            old = max_ref[h : h + 1]
            new = jnp.maximum(old, jnp.max(s, axis=0, keepdims=True))
            fade = jnp.exp(old - new)
            expo = jnp.exp(s - new)
            max_ref[h : h + 1] = new
            sum_ref[h : h + 1] = sum_ref[h : h + 1] * fade + jnp.sum(expo, axis=0, keepdims=True)
            at = slice(head * h, head * (h + 1))
            acc_ref[at] = acc_ref[at] * fade + dot(values[at], expo.astype(jnp.bfloat16))

    run_steps(work_ref, rows_in.start, rows_in.wait, tiles)
    inverse = 1.0 / sum_ref[...]
    cot = cot_ref[...].astype(jnp.float32).T
    stats_ref[0:HEADS] = max_ref[...] + jnp.log(sum_ref[...])
    for h in range(HEADS):
        at = slice(head * h, head * (h + 1))
        outputs = acc_ref[at] * inverse[h : h + 1]
        acc_ref[at] = outputs
        stats_ref[HEADS + h : HEADS + h + 1] = jnp.sum(outputs * cot[at], axis=0, keepdims=True)
    sent_ref[...] = jnp.broadcast_to(stats_ref[...], sent_ref.shape)
    out_ref[...] = acc_ref[...].T.astype(out_ref.dtype)


def tile_grads(scores, d_probs, lse, delta):
    prob = jnp.exp(scores - lse)
    return prob.astype(jnp.bfloat16), (prob * (d_probs - delta)).astype(jnp.bfloat16)


def query_grad_kernel(
    sizes, work_ref, stack_hbm, cot_stack_hbm, stats_hbm, wqt_hbm, wk_hbm, wkt_hbm, wv_hbm, mask_ref, *refs
):
    count = 2 * sizes[0]
    groups, refs = refs[:count], refs[count:]
    part_ref, stack_ref, cot_stack_ref, stats_ref, wqt_ref, wk_ref, wkt_ref, wv_ref = refs[:8]
    buf, words, bias_ref, acc_ref, score_ref, d_prob_ref, sems, w_sems = refs[8:]
    layout = Layout(*sizes)
    block, width = part_ref.shape
    head = width // HEADS
    rows_in = Rows(layout, groups, mask_ref, buf, words, sems, block)
    first_step(work_ref, rows_in.start)
    loads = load((
        (wk_hbm, wk_ref), (stack_hbm, stack_ref), (wv_hbm, wv_ref), (cot_stack_hbm, cot_stack_ref),
        (wkt_hbm, wkt_ref), (stats_hbm.at[0], stats_ref), (wqt_hbm, wqt_ref),
    ), w_sems)
    acc_ref[...] = jnp.zeros(acc_ref.shape, jnp.float32)
    for copy in loads[:6]:
        copy.wait()

    def tiles(slot, blocks, patterns, index):
        rows = buf[slot]
        keys = dot(rows, wk_ref[...]).astype(jnp.bfloat16)
        values = dot(rows, wv_ref[...]).astype(jnp.bfloat16)
        keys_t = dot(wkt_ref[...], rows, NT).astype(jnp.bfloat16)
        bias_ref[...] = rows_in.bias(slot, blocks, patterns)
        for p in range(HEADS // 2):
            pair = slice(2 * head * p, 2 * head * (p + 1))
            scores = dot(keys[:, pair], stack_ref[p])
            d_probs = dot(values[:, pair], cot_stack_ref[p])
            for e in range(2):
                of = slice(block * e, block * (e + 1))
                score_ref[2 * p + e] = scores[:, of] + bias_ref[...]
                d_prob_ref[2 * p + e] = d_probs[:, of]
        for h in range(HEADS):
            _, d_scores = tile_grads(
                score_ref[h], d_prob_ref[h], stats_ref[h : h + 1], stats_ref[HEADS + h : HEADS + h + 1]
            )
            at = slice(head * h, head * (h + 1))
            acc_ref[at] += dot(keys_t[at], d_scores)

    run_steps(work_ref, rows_in.start, rows_in.wait, tiles)
    loads[6].wait()
    grad = (acc_ref[...].T * (head**-0.5)).astype(jnp.bfloat16)
    part_ref[...] = dot(grad, wqt_ref[...])


def key_grad_kernel(
    sizes, bits, work_ref, key_hbm, value_hbm, wq_hbm, wkt_hbm, wvt_hbm, part_hbm, mask_ref, stats_all_ref, *refs
):
    readers = sizes[0]
    count = 2 * readers
    groups, refs = refs[:count], refs[count:]
    halves, refs = (refs[:readers], refs[readers : 2 * readers]), refs[2 * readers :]
    out_ref, key_ref, value_ref, part_ref, wq_ref, wkt_ref, wvt_ref, buf, words, cot_buf, stats, bias_ref = refs[:12]
    query_stack_ref, cot_stack_ref, score_ref, d_prob_ref, key_acc, value_acc, sems, c_sems, w_sems = refs[12:]
    layout = Layout(*sizes)
    block, width = out_ref.shape
    head = width // HEADS
    rows_in = Rows(layout, groups, mask_ref, buf, words, sems, block)

    def half_copy(slot, t, k):
        into = cot_buf.at[slot, pl.ds(t * block + block // 2 * k, block // 2)]
        return lambda src: pltpu.make_async_copy(src, into, c_sems.at[slot, t, k])

    def stats_copy(slot, t, query):
        return pltpu.make_async_copy(stats_all_ref.at[query], stats.at[slot, t], c_sems.at[slot, t, 2])

    def start(slot, blocks, patterns):
        rows_in.start(slot, blocks, patterns)
        for t in range(TILES):
            stats_copy(slot, t, blocks[t]).start()
            for k in range(2):
                start_copy(layout.half_place(bits[k], blocks[t]), halves[k], half_copy(slot, t, k))

    def wait(slot):
        rows_in.wait(slot)
        for t in range(TILES):
            stats_copy(slot, t, 0).wait()
            for k in range(2):
                half_copy(slot, t, k)(halves[k][0].at[0]).wait()

    first_step(work_ref, start)
    loads = load(((wq_hbm, wq_ref), (key_hbm, key_ref), (value_hbm, value_ref)), w_sems)
    key_acc[...] = jnp.zeros(key_acc.shape, jnp.float32)
    value_acc[...] = jnp.zeros(value_acc.shape, jnp.float32)
    for copy in loads:
        copy.wait()
    loads = load(((wkt_hbm, wkt_ref), (wvt_hbm, wvt_ref), (part_hbm, part_ref)), w_sems, 3)

    def tiles(slot, blocks, patterns, index):
        queries = dot(buf[slot], wq_ref[...]).astype(jnp.bfloat16) * jnp.bfloat16(head**-0.5)
        bias_ref[...] = rows_in.bias(slot, blocks, patterns)
        cots = cot_buf[slot]
        pairs = [slice(2 * head * p, 2 * head * (p + 1)) for p in range(HEADS // 2)]
        of_tile = [slice(block * t, block * (t + 1)) for t in range(TILES)]
        for p, pair in enumerate(pairs):
            query_stack_ref[p] = jnp.concatenate([pair_stack(queries[of, pair]) for of in of_tile], 0)
            cot_stack_ref[p] = jnp.concatenate([pair_stack(cots[of, pair]) for of in of_tile], 0)
            score_ref[p] = dot(key_ref[:, pair], query_stack_ref[p], NT)
            d_prob_ref[p] = dot(value_ref[:, pair], cot_stack_ref[p], NT)
        for p, pair in enumerate(pairs):
            probs, d_scores = [], []
            for t in range(TILES):
                for e in range(2):
                    h = 2 * p + e
                    of = slice(block * (2 * t + e), block * (2 * t + e + 1))
                    prob, d_score = tile_grads(
                        score_ref[p, :, of] + bias_ref[of_tile[t]], d_prob_ref[p, :, of], stats[slot, t, h : h + 1],
                        stats[slot, t, HEADS + h : HEADS + h + 1],
                    )
                    probs.append(prob)
                    d_scores.append(d_score)
            value_acc[:, pair] += dot(jnp.concatenate(probs, 1), cot_stack_ref[p])
            key_acc[:, pair] += dot(jnp.concatenate(d_scores, 1), query_stack_ref[p])

    run_steps(work_ref, start, wait, tiles)
    for copy in loads:
        copy.wait()
    grad = part_ref[...] + dot(key_acc[...].astype(jnp.bfloat16), wkt_ref[...])
    grad = grad + dot(value_acc[...].astype(jnp.bfloat16), wvt_ref[...])
    out_ref[...] = grad.astype(out_ref.dtype)


VMEM = pl.BlockSpec(memory_space=pltpu.VMEM)
SMEM = pl.BlockSpec(memory_space=pltpu.SMEM)
HBM = pl.BlockSpec(memory_space=pltpu.HBM)


def swap(block, mask):
    axes = ("reader", "blk")
    count = lax.axis_size("reader") * lax.axis_size("blk")
    return lax.ppermute(block, axes, [(i, i ^ mask) for i in range(count)])


def after(value, *others):
    return lax.optimization_barrier((value, *others))[0]


def local(features, cotangent, w_query, w_key, w_value, tile_coords, tile_count, mask_table):
    block, width = features.shape
    readers, blks, cap = lax.axis_size("reader"), lax.axis_size("blk"), tile_coords.shape[2]
    assert block == mask_table.shape[1] and 3 * cap < 128
    sizes = (readers, blks, cap)
    devices, lines = readers * blks, blks // 2
    f32, bf16, i32 = jnp.float32, jnp.bfloat16, jnp.int32
    shape = jax.ShapeDtypeStruct
    masks = mask_table.transpose(0, 2, 1)
    words = masks.shape[1]
    head = width // HEADS
    half = block // 2
    some = pltpu.CompilerParams(vmem_limit_bytes=VMEM_SOME)
    most = pltpu.CompilerParams(vmem_limit_bytes=VMEM_MOST)
    axes = ("reader", "blk")

    def cost(tiles):
        return pl.CostEstimate(flops=tiles * 200_000_000, bytes_accessed=4_000_000, transcendentals=tiles * 131072)

    packed = pl.pallas_call(
        pack_kernel,
        out_shape=shape((1, block + LIST_ROWS, width), bf16),
        in_specs=[HBM, HBM, HBM],
        out_specs=VMEM,
        scratch_shapes=[
            pltpu.SMEM((1, 3, 1, cap), i32), pltpu.SMEM((1, 1), i32), pltpu.SemaphoreType.DMA((3,)),
        ],
        compiler_params=most,
        name="pack",
    )(features, tile_coords.transpose(0, 3, 1, 2), tile_count)
    lined = [packed] + [swap(packed, 2 * k) for k in range(1, lines)]

    nearest_first = sorted(range(1, readers), key=lambda k: (k.bit_count(), k))

    def to_readers(block):
        there = {k: swap(block, blks * k) for k in nearest_first}
        return [there[k] for k in range(1, readers)]

    columns = [packed] + to_readers(packed)

    bits = (0, (readers - 1).bit_length() - 1)
    cot_parts = [cotangent[None, half * k : half * (k + 1)] for k in range(2)]
    cot_other = [swap(part, blks << bit) for part, bit in zip(cot_parts, bits)]

    column_lists = jnp.concatenate([entry[:, block:, :128] for entry in columns], 0)

    def work(kernel, lists, count, name):
        return pl.pallas_call(
            functools.partial(kernel, sizes),
            out_shape=shape((2 * count * cap + 5,), i32),
            in_specs=[HBM],
            out_specs=SMEM,
            scratch_shapes=[pltpu.SMEM((count, 128), i32), pltpu.SemaphoreType.DMA],
            compiler_params=some,
            cost_estimate=cost(1),
            name=name,
        )(lists[:, 0].astype(i32))

    key_work = work(key_work_kernel, column_lists, readers, "key_work")

    stacks = shape((HEADS // 2, 2 * head, 2 * block), bf16)
    own = shape((block, width), bf16)
    square = shape((width, width), bf16)
    weight = pltpu.VMEM((width, width), bf16)
    rows_low, rows_wide = pltpu.VMEM((block, width), bf16), pltpu.VMEM((block, width), f32)
    prepared = pl.pallas_call(
        prepare_kernel,
        out_shape=(stacks, stacks, own, own, square, square, square),
        in_specs=[HBM] * 5,
        out_specs=(VMEM,) * 7,
        scratch_shapes=[rows_low, rows_low, weight, weight, weight, pltpu.SemaphoreType.DMA((5,))],
        compiler_params=most,
        cost_estimate=cost(2),
        name="prepare",
    )(after(features, columns), cotangent, w_query, w_key, w_value)
    query_stack, cot_stack, keys, values, w_query_t, w_key_t, w_value_t = prepared

    line = jnp.concatenate(lined[1:], 0)[:, :block]
    line = after(line, columns, cot_other)
    there = to_readers(line)
    near = jnp.concatenate([entry[:, :block] for entry in columns] + [line], 0)

    pairs = [part for k in range(2) for part in (cot_parts[k], cot_other[k])]
    pieces = [after(jnp.concatenate(pairs, 0), line)]
    done_first = (key_work, prepared)
    mask = blks // 2
    while mask > 1:
        pieces += [swap(after(piece, done_first) if at else piece, mask) for at, piece in enumerate(pieces)]
        mask //= 2

    line_lists = jnp.concatenate([entry[:, block:, :128] for entry in lined], 0)
    other_near = swap(after(near, pieces[lines // 2]), 1)
    line_lists = after(line_lists, pieces[1])
    row_lists = jnp.concatenate([line_lists, swap(line_lists, 1)], 0)
    query_work = work(query_work_kernel, row_lists, blks, "query_work")
    here = [near] + there
    rows_all = here + [other_near] + [swap(group, 1) for group in there]

    cots_here = []
    for k in range(2):
        part = jnp.concatenate([piece[2 * k : 2 * k + 2] for piece in pieces], 0)
        masks_left = [m for m in range(1, readers) if not m >> bits[k] & 1]
        cots_here.append((part, [swap(after(part, here), blks * m) for m in masks_left]))

    stack_space = pltpu.VMEM(stacks.shape, bf16)
    buffer = pltpu.VMEM((2, TILES * block, width), bf16)
    word_buffer = pltpu.VMEM((2, TILES, words, block), i32)
    bias = pltpu.VMEM((TILES * block, block), f32)
    turned = pltpu.VMEM((width, block), f32)
    per_head = pltpu.VMEM((HEADS, block), f32)
    own_stats = pltpu.VMEM((2 * HEADS, block), f32)
    met = pltpu.VMEM((HEADS, TILES * block, block), f32)
    pair_met = pltpu.VMEM((HEADS // 2, block, 2 * TILES * block), f32)
    pair_rows = pltpu.VMEM((HEADS // 2, 2 * TILES * block, 2 * head), bf16)
    row_sems = pltpu.SemaphoreType.DMA((2, TILES, 2))

    attn_out, stats = pl.pallas_call(
        functools.partial(forward_kernel, sizes),
        out_shape=(own, shape((devices, 2 * HEADS, block), f32)),
        in_specs=[SMEM] + [VMEM] * 4 + [HBM] * (1 + 2 * readers),
        out_specs=(VMEM, VMEM),
        scratch_shapes=[own_stats, buffer, word_buffer, bias, per_head, per_head, turned, met, row_sems],
        compiler_params=some,
        cost_estimate=cost(5),
        name="forward",
    )(query_work, query_stack, cotangent, w_key, w_value_t, masks, *rows_all)

    stats_all = lax.all_to_all(stats, axes, 0, 0, tiled=True)

    query_part = pl.pallas_call(
        functools.partial(query_grad_kernel, sizes),
        out_shape=shape((block, width), f32),
        in_specs=[SMEM] + [HBM] * (8 + 2 * readers),
        out_specs=VMEM,
        scratch_shapes=[
            stack_space, stack_space, own_stats, weight, weight, weight, weight, buffer, word_buffer, bias, turned,
            met, met, row_sems, pltpu.SemaphoreType.DMA((7,)),
        ],
        compiler_params=most,
        cost_estimate=cost(5),
        name="query_grad",
    )(query_work, query_stack, cot_stack, stats, w_query_t, w_key, w_key_t, w_value, masks, *rows_all)

    cots_all = []
    for first, rest in cots_here:
        cots_all += [first, *rest, swap(after(first, stats), 1)]
        cots_all += [swap(after(part, stats_all, query_part), 1) for part in rest]

    grad_features = pl.pallas_call(
        functools.partial(key_grad_kernel, sizes, bits),
        out_shape=own,
        in_specs=[SMEM] + [HBM] * (8 + 4 * readers),
        out_specs=VMEM,
        scratch_shapes=[
            rows_low, rows_low, rows_wide, weight, weight, weight,
            buffer, word_buffer, buffer, pltpu.VMEM((2, TILES, 2 * HEADS, block), f32), bias,
            pair_rows, pair_rows, pair_met, pair_met, rows_wide, rows_wide,
            row_sems, pltpu.SemaphoreType.DMA((2, TILES, 3)), pltpu.SemaphoreType.DMA((6,)),
        ],
        compiler_params=most,
        cost_estimate=cost(5),
        name="key_grad",
    )(key_work, keys, values, w_query, w_key_t, w_value_t, query_part, masks, stats_all, *rows_all, *cots_all)
    return attn_out, grad_features


def solution(mesh):
    return jax.shard_map(
        local,
        mesh=mesh,
        in_specs=(
            P(("reader", "blk"), None),
            P(("reader", "blk"), None),
            P(),
            P(),
            P(),
            P("reader", "blk", None, None),
            P("reader", "blk"),
            P(),
        ),
        out_specs=(P(("reader", "blk"), None), P(("reader", "blk"), None)),
        check_vma=False,
    )
```
